32 devices in a mesh: gx: 4 (over z), gy: 8 (over y, x, core).
Axes of the slice: x: 2, y: 2, z: 4, core: 2. Of those that a mesh axis runs over, the one named last changes fastest.
Arguments:
- tokens: bfloat16 [64, 216, 512], P(('gx', 'gy')), may hold values from -6 to 6
- segment_ids: int32 [64, 216], P(('gx', 'gy')), may hold values from 0 to 3, never falling along the last dimension, each value on 1 to 108 neighbouring positions
- pack_task: int32 [64], replicated, may hold values from 0 to 23
- task_experts: int32 [24, 2], replicated, may hold values from 0 to 31, all different within a row
- w_qkv: bfloat16 [512, 1536], P(('gx', 'gy')), may hold values from -0.25 to 0.25
- w_attn_out: bfloat16 [512, 512], P(('gx', 'gy')), may hold values from -2 to 2
- w_router: bfloat16 [512, 32], P(('gx', 'gy')), may hold values from -0.1875 to 0.1875
- w_expert_in: bfloat16 [32, 512, 2048], P(None, ('gx', 'gy')), may hold values from -0.25 to 0.25
- w_expert_out: bfloat16 [32, 2048, 512], P(None, ('gx', 'gy')), may hold values from -0.125 to 0.125
- norm1_gain: bfloat16 [512], P(('gx', 'gy')), may hold values from 0.099609375 to 1.8984375
- norm1_bias: bfloat16 [512], P(('gx', 'gy')), may hold values from -3 to 3
- norm2_gain: bfloat16 [512], P(('gx', 'gy')), may hold values from 0.099609375 to 1.8984375
- norm2_bias: bfloat16 [512], P(('gx', 'gy')), may hold values from -3 to 3
- cotangent: bfloat16 [64, 216, 512], P(('gx', 'gy')), may hold values from -6 to 6
Outputs:
- mixed: bfloat16 [64, 216, 512], P(('gx', 'gy'))
- d_tokens: bfloat16 [64, 216, 512], P(('gx', 'gy'))
- d_qkv: float32 [512, 1536], P(('gx', 'gy'))
- d_attn_out: float32 [512, 512], P(('gx', 'gy'))
- d_router: float32 [512, 32], P(('gx', 'gy'))
- d_expert_in: float32 [32, 512, 2048], P(None, ('gx', 'gy'))
- d_expert_out: float32 [32, 2048, 512], P(None, ('gx', 'gy'))
- d_gain1: float32 [512], P(('gx', 'gy'))
- d_bias1: float32 [512], P(('gx', 'gy'))
- d_gain2: float32 [512], P(('gx', 'gy'))
- d_bias2: float32 [512], P(('gx', 'gy'))
The draws below stay inside these ranges and needn't reach their ends.
Inputs may be any that keep to these rules, and one draw needn't show every extreme that they name: `segment_ids`: within a pack the ids never fall, the pack has 4 segments of 1 to 108 tokens, one of exactly that many. `task_experts`: each task names two different experts; every expert is named by some task.
All inputs are finite; a program needn't handle non-finite values.
Results may differ from the reference program's by a relative error of at most 0.012.
Values may be sent and summed in bfloat16 or wider, within the bound.
A program may use at most 192 MiB of HBM per device.

```python
import math
import jax
import jax.numpy as jnp
import numpy as np
from jax import lax

D = 512
HEADS = 8
FF = 2048
EXPERTS = 32
TASKS = 24
PACK = 216
PACKS = 64


def with_ends(array, stream_key, smallest, largest):
    index_at = [jax.random.randint(jax.random.fold_in(stream_key, axis), (), 0, length) for axis, length in enumerate(array.shape)]
    widest = array.shape.index(max(array.shape))
    next_to = index_at[:widest] + [(index_at[widest] + 1) % array.shape[widest]] + index_at[widest + 1:]
    return array.at[tuple(index_at)].set(smallest).at[tuple(next_to)].set(largest)


def levels(own_key, extent, shards, smallest, largest):
    def one(position, shards_of):
        steps = jax.random.uniform(jax.random.fold_in(jax.random.fold_in(own_key, 6), position), (shards_of,), jnp.float32, smallest / len(shards), largest / len(shards))
        return jnp.repeat(jnp.exp(steps), extent[position] // shards_of).reshape((-1,) + (1,) * (len(extent) - position - 1))

    factor_of = one(*shards[0])
    for cut in shards[1:]:
        factor_of = factor_of * one(*cut)
    return factor_of


def distinct(stream_key, rows, number_of, top, lift):
    order = jax.random.permutation(jax.random.fold_in(stream_key, 1), number_of)
    favour = order
    for power in range(3):
        favour = favour * favour // number_of
    favour = favour * lift // number_of
    tickets = jax.random.randint(jax.random.fold_in(stream_key, 2), (rows, number_of), 0, 4096) + favour
    holders = jax.random.permutation(jax.random.fold_in(stream_key, 3), rows)[jnp.arange(number_of) % rows]
    tickets = jnp.where(jnp.arange(rows)[:, None] == holders[None, :], 1 << 14, tickets)
    score = tickets * number_of + jnp.arange(number_of)
    return lax.top_k(score.astype(jnp.int32), top)[1].astype(jnp.int32)


def length_profile(count, total, reach, lean):
    portions = [(1 << 20) // math.isqrt(rank ** lean) + 1 for rank in range(2, count + 1)]
    spare, holding = total - reach - (count - 1), [1] * (count - 1)
    while spare > 0:
        free = [i for i in range(count - 1) if holding[i] < reach]
        whole, remaining = sum([portions[i] for i in free]), spare
        for i in free:
            addition = min(reach - holding[i], max(1, remaining * portions[i] // whole), spare)
            holding[i] = holding[i] + addition
            spare = spare - addition
    return np.array([reach] + holding)


def ragged(stream_key, number_of, total, limit, lean):
    if number_of == 2:
        one = jax.random.randint(stream_key, (), max(1, total - limit), min(limit, total - 1) + 1)
        return jnp.stack([one, total - one])
    lengths = jnp.asarray(length_profile(number_of, total, limit, lean), jnp.int32)
    twos = (number_of - 1) // 2
    source_of, sink = lengths[1:1 + 2 * twos:2], lengths[2:2 + 2 * twos:2]
    room = jnp.minimum(source_of - 1, limit - sink)
    passed = jax.random.randint(jax.random.fold_in(stream_key, 1), (twos,), 0, 1 << 20) % (room + 1)
    lengths = lengths.at[1:1 + 2 * twos:2].set(source_of - passed).at[2:2 + 2 * twos:2].set(sink + passed)
    return lengths[jax.random.permutation(jax.random.fold_in(stream_key, 2), number_of)]


def scatter_about(rng, extent, scale, most, shards=(), held_as=jnp.bfloat16):
    factor_of = levels(rng, extent, shards, -0.22, 0.18) if shards else 1.0
    values = jax.random.normal(rng, extent, jnp.float32) * scale * factor_of
    return jnp.minimum(jnp.maximum(values, -most), most).astype(held_as)


def setup_inputs(seed: int = 0) -> dict:
    seeds = jax.random.split(jax.random.key(seed), 15)
    return {
        "tokens": scatter_about(seeds[0], (PACKS, PACK, D), 1.0, 6.0, ((0, 32),)),
        "segment_ids": jax.vmap(lambda own: jnp.searchsorted(jnp.cumsum(ragged(own, 4, PACK, PACK // 2, 0)), jnp.arange(PACK), side="right"))(jax.random.split(seeds[1], PACKS)).reshape((PACKS, PACK)).astype(jnp.int32),
        "pack_task": with_ends(jax.random.randint(seeds[2], (PACKS,), 0, TASKS), jax.random.fold_in(seeds[2], 1), 0, TASKS - 1).astype(jnp.int32),
        "task_experts": distinct(seeds[3], TASKS, EXPERTS, 2, 0),
        "w_qkv": scatter_about(seeds[4], (D, 3 * D), D ** -0.5, 0.25, ((0, 32),)),
        "w_attn_out": scatter_about(seeds[5], (D, D), (D // 48) ** -0.5, 2.0, ((0, 32),)),
        "w_router": scatter_about(seeds[6], (D, EXPERTS), (2 * D) ** -0.5, 0.1875, ((0, 32),)),
        "w_expert_in": scatter_about(seeds[7], (EXPERTS, D, FF), D ** -0.5, 0.25, ((1, 32),)),
        "w_expert_out": scatter_about(seeds[8], (EXPERTS, FF, D), FF ** -0.5, 0.125, ((1, 32),)),
        "norm1_gain": jnp.clip(1.0 + 0.18 * jax.random.normal(seeds[9], (D,), jnp.float32), 0.099609375, 1.8984375).astype(jnp.bfloat16),
        "norm1_bias": scatter_about(seeds[10], (D,), 0.3, 3.0, ((0, 32),)),
        "norm2_gain": jnp.clip(1.0 + 0.18 * jax.random.normal(seeds[11], (D,), jnp.float32), 0.099609375, 1.8984375).astype(jnp.bfloat16),
        "norm2_bias": scatter_about(seeds[12], (D,), 0.3, 3.0, ((0, 32),)),
        "cotangent": scatter_about(seeds[13], (PACKS, PACK, D), 1.0, 6.0, ((0, 32),)),
    }


EPS = 1e-05
MASK_FILL = -1e+30
HIGH = lax.Precision.HIGHEST

@jax.custom_vjp
def low(v):
    return lax.optimization_barrier(v.astype(jnp.bfloat16)).astype(jnp.float32)

@jax.custom_vjp
def low_back(v):
    return v

def low_keep(v):
    return (low(v), None)

def low_pass(kept, grad):
    return (grad,)

def back_keep(v):
    return (v, None)

def back_low(kept, grad):
    return (low(grad),)
low.defvjp(low_keep, low_pass)
low_back.defvjp(back_keep, back_low)

def layer_norm(values, gain, bias):
    center = values - lax.optimization_barrier(jnp.mean(values, -1, keepdims=True))
    spread = lax.optimization_barrier(jnp.mean(center * center, -1, keepdims=True))
    return center * lax.rsqrt(spread + EPS) * gain + bias

def softmax_last(scores):
    raised = jnp.exp(scores - lax.optimization_barrier(jnp.max(scores, -1, keepdims=True)))
    return raised / lax.optimization_barrier(jnp.sum(raised, -1, keepdims=True))

def pack_layer(params, inputs):
    w_qkv, w_attn, w_route, w_in, w_out, gain_one, bias_one, gain_two, bias_two = params
    block, segment, pair = inputs
    length = block.shape[0]
    head_size = D // HEADS
    normed = low(layer_norm(block, gain_one, bias_one))
    project = low_back(low(jnp.dot(normed, w_qkv, precision=HIGH)))
    queries = project[:, :D].reshape(length, HEADS, head_size)
    keys_all = project[:, D:2 * D].reshape(length, HEADS, head_size)
    values_all = project[:, 2 * D:].reshape(length, HEADS, head_size)
    scores = low_back(jnp.einsum('qhd,khd->hqk', queries, keys_all, precision=HIGH) * (1.0 / math.sqrt(head_size)))
    same_doc = segment[:, None] == segment[None, :]
    attn_probs = low(softmax_last(jnp.where(same_doc[None], scores, MASK_FILL)))
    heads_out = jnp.einsum('hqk,khd->qhd', attn_probs, values_all, precision=HIGH).reshape(length, D)
    heads_out = low_back(low(heads_out))
    attended = low_back(jnp.dot(heads_out, w_attn, precision=HIGH))
    middle = block + attended
    routed = low(layer_norm(middle, gain_two, bias_two))
    logits = jnp.dot(routed, w_route, precision=HIGH)
    gates = softmax_last(logits[:, pair])
    hidden_pre = low_back(jnp.einsum('ld,kdf->klf', routed, w_in[pair], precision=HIGH))
    hidden_act = low(jax.nn.gelu(hidden_pre))
    expert_out = low_back(jnp.einsum('klf,kfd->kld', hidden_act, w_out[pair], precision=HIGH))
    return middle + gates[:, 0:1] * expert_out[0] + gates[:, 1:2] * expert_out[1]

def reference(tokens, segment_ids, pack_task, task_experts, w_qkv, w_attn_out, w_router, w_expert_in, w_expert_out, norm1_gain, norm1_bias, norm2_gain, norm2_bias, cotangent):
    params = tuple((piece.astype(jnp.float32) for piece in (w_qkv, w_attn_out, w_router, w_expert_in, w_expert_out, norm1_gain, norm1_bias, norm2_gain, norm2_bias)))
    pairs = task_experts[pack_task].astype(jnp.int32)

    def whole_layer(weights, inputs_float):

        def one_pack(entry):
            return pack_layer(weights, entry)
        return lax.map(jax.checkpoint(one_pack), (inputs_float, segment_ids, pairs))
    mixed, backward = jax.vjp(whole_layer, params, tokens.astype(jnp.float32))
    grad_params, grad_tokens = backward(cotangent.astype(jnp.float32))
    return (mixed.astype(jnp.bfloat16), grad_tokens.astype(jnp.bfloat16), grad_params[0], grad_params[1], grad_params[2], grad_params[3], grad_params[4], grad_params[5], grad_params[6], grad_params[7], grad_params[8])
```

```python
import functools
import math

import jax
import jax.numpy as jnp
from jax import lax
from jax.experimental import pallas as pl
from jax.experimental.pallas import tpu as pltpu
from jax.sharding import PartitionSpec as P

HEADS = 8
HEAD = 64
PACK = 216
GAIN_ONE = 32


EPS = 1e-05
MASK_FILL = -1e30
HIGH = lax.Precision.HIGHEST


def shortened(value):

    def short(part):
        return part.astype(jnp.bfloat16) if part.dtype == jnp.float32 else part

    return jax.tree.map(short, value)


def layer_norm(values, gain, bias):
    center = values - jnp.mean(values, -1, keepdims=True)
    spread = jnp.mean(center * center, -1, keepdims=True)
    return center * lax.rsqrt(spread + EPS) * gain + bias


def contract_rows(left, right):
    return lax.dot_general(
        left, right, (((0,), (0,)), ((), ())), preferred_element_type=jnp.float32
    )


def contract_cols(left, right):
    return lax.dot_general(
        left, right, (((1,), (1,)), ((), ())), preferred_element_type=jnp.float32
    )


def shards_any(
    tokens,
    segment_ids,
    pack_task,
    task_experts,
    w_qkv,
    w_attn_out,
    w_router,
    w_expert_in,
    w_expert_out,
    norm1_gain,
    norm1_bias,
    norm2_gain,
    norm2_bias,
    cotangent,
):
    outer = lax.axis_size("gx")
    inner = lax.axis_size("gy")
    devices = outer * inner
    micro, length, width = tokens.shape
    experts, slab_in, hidden = w_expert_in.shape
    slab_out = w_expert_out.shape[1]
    head_size = width // HEADS
    scale = 1.0 / math.sqrt(head_size)
    device = lax.axis_index("gx") * inner + lax.axis_index("gy")
    gathered = (
        lax.all_gather(w_qkv, ("gx", "gy"), axis=0, tiled=True),
        lax.all_gather(w_attn_out, ("gx", "gy"), axis=0, tiled=True),
        lax.all_gather(w_router, ("gx", "gy"), axis=0, tiled=True),
        lax.all_gather(norm1_gain, ("gx", "gy"), axis=0, tiled=True),
        lax.all_gather(norm1_bias, ("gx", "gy"), axis=0, tiled=True),
        lax.all_gather(norm2_gain, ("gx", "gy"), axis=0, tiled=True),
        lax.all_gather(norm2_bias, ("gx", "gy"), axis=0, tiled=True),
    )
    qkv_full, attn_full, route_full = (gathered[0], gathered[1], gathered[2])
    gain_one, bias_one, gain_two, bias_two = tuple(
        (piece.astype(jnp.float32) for piece in gathered[3:])
    )
    route_float = route_full.astype(jnp.float32)
    pack_pairs = task_experts[pack_task]
    needs = jnp.transpose(pack_pairs.reshape(outer, inner, micro, 2), (2, 3, 0, 1))
    route_pairs = jnp.transpose(pack_pairs.reshape(devices, micro, 2), (1, 0, 2))
    own_pairs = lax.dynamic_slice_in_dim(pack_pairs, device * micro, micro, 0)
    expert_ids = jnp.arange(experts, dtype=jnp.int32)

    def slabs(need):
        return (w_expert_in[need], w_expert_out[need])

    def joined(pieces):
        return (
            pieces[0].reshape(pieces[0].shape[0], width, hidden),
            pieces[1].reshape(pieces[1].shape[0], hidden, width),
        )

    def attention_probs(project, segment):
        queries = project[:, :width].reshape(length, HEADS, head_size)
        keys_all = project[:, width : 2 * width].reshape(length, HEADS, head_size)
        scores = (
            jnp.einsum("qhd,khd->hqk", queries, keys_all, preferred_element_type=jnp.float32)
            * scale
        )
        same_doc = segment[:, None] == segment[None, :]
        return jnp.where(same_doc[None], scores, MASK_FILL)

    def forward_step(carry, inputs):
        block, segment, need, pair, senders = inputs
        block_float = block.astype(jnp.float32)
        normed = layer_norm(block_float, gain_one, bias_one).astype(jnp.bfloat16)
        project = jnp.dot(normed, qkv_full, preferred_element_type=jnp.float32).astype(jnp.bfloat16)
        masked = attention_probs(project, segment)
        peak = jnp.max(masked, -1, keepdims=True)
        raised = jnp.exp(masked - peak)
        totals = jnp.sum(raised, -1, keepdims=True)
        log_total = peak + jnp.log(totals)
        attn_low = (raised / totals).astype(jnp.bfloat16)
        values_all = project[:, 2 * width :].reshape(length, HEADS, head_size)
        heads_out = (
            jnp.einsum("hqk,khd->qhd", attn_low, values_all, preferred_element_type=jnp.float32)
            .reshape(length, width)
            .astype(jnp.bfloat16)
        )
        middle = block_float + jnp.dot(heads_out, attn_full, preferred_element_type=jnp.float32)
        routed = layer_norm(middle, gain_two, bias_two).astype(jnp.bfloat16)
        logits = jnp.dot(routed, route_full, preferred_element_type=jnp.float32)
        select = (expert_ids[None, :] == pair[:, None]).astype(jnp.float32)
        chosen = jnp.sum(logits[:, None, :] * select[None], -1)
        raised_gate = jnp.exp(chosen - jnp.max(chosen, -1, keepdims=True))
        gates = raised_gate / jnp.sum(raised_gate, -1, keepdims=True)
        weights_in, weights_out = joined(
            lax.all_to_all(
                lax.all_to_all(
                    shortened(slabs(need)), "gx", split_axis=1, concat_axis=1, tiled=True
                ),
                "gy",
                split_axis=2,
                concat_axis=2,
                tiled=True,
            )
        )
        hidden_pre = jnp.einsum(
            "ld,kdf->klf", routed, weights_in, preferred_element_type=jnp.float32
        )
        hidden_low = jax.nn.gelu(hidden_pre).astype(jnp.bfloat16)
        expert_out = jnp.einsum(
            "klf,kfd->kld", hidden_low, weights_out, preferred_element_type=jnp.float32
        )
        saved = ()
        mixed = middle + gates[:, 0:1] * expert_out[0] + gates[:, 1:2] * expert_out[1]
        kept = (
            normed,
            project,
            log_total,
            heads_out,
            middle,
            routed,
            gates,
            hidden_pre,
            hidden_low,
            expert_out,
            saved,
        )
        return (carry, (mixed.astype(jnp.bfloat16), kept))

    start = jnp.zeros((), jnp.float32)
    unused, (mixed_all, kept_all) = lax.scan(
        forward_step, start, (tokens, segment_ids, needs, own_pairs, route_pairs)
    )

    def backward_step(carry, inputs):
        dense_acc, shard_in, shard_out, holding = carry
        block, grad_top, segment, need, pair, kept = inputs
        (
            normed,
            project,
            log_total,
            heads_out,
            middle,
            routed,
            gates,
            hidden_pre,
            hidden_low,
            expert_out,
            saved,
        ) = kept
        grad_float = grad_top.astype(jnp.float32)
        grad_gate = jnp.sum(grad_float[None] * expert_out, -1).T
        grad_chosen = gates * (grad_gate - jnp.sum(gates * grad_gate, -1, keepdims=True))
        select = (expert_ids[None, :] == pair[:, None]).astype(jnp.float32)
        grad_logits = jnp.sum(grad_chosen[:, :, None] * select[None], 1)
        routed_float = routed.astype(jnp.float32)
        grad_route = jnp.dot(routed_float.T, grad_logits, precision=HIGH)
        grad_routed = jnp.dot(grad_logits, route_float.T, precision=HIGH)
        grad_eout = (gates.T[:, :, None] * grad_float[None]).astype(jnp.bfloat16)
        slot = ()
        weights_in, weights_out = joined(
            lax.all_to_all(
                lax.all_to_all(
                    shortened(slabs(need)), "gx", split_axis=1, concat_axis=1, tiled=True
                ),
                "gy",
                split_axis=2,
                concat_axis=2,
                tiled=True,
            )
        )
        grad_act = jnp.einsum(
            "kld,kfd->klf", grad_eout, weights_out, preferred_element_type=jnp.float32
        )
        unused_act, gelu_back = jax.vjp(jax.nn.gelu, hidden_pre)
        grad_pre = gelu_back(grad_act)[0].astype(jnp.bfloat16)
        grad_in = jnp.einsum("ld,klf->kdf", routed, grad_pre, preferred_element_type=jnp.float32)
        grad_out = jnp.einsum(
            "klf,kld->kfd", hidden_low, grad_eout, preferred_element_type=jnp.float32
        )
        grad_routed = grad_routed + jnp.einsum(
            "klf,kdf->ld", grad_pre, weights_in, preferred_element_type=jnp.float32
        )
        slot = (grad_in, grad_out)
        unused_two, norm_two_back = jax.vjp(layer_norm, middle, gain_two, bias_two)
        grad_mid_norm, grad_gain_two, grad_bias_two = norm_two_back(grad_routed)
        grad_middle = grad_float + grad_mid_norm
        grad_attended = grad_middle.astype(jnp.bfloat16)
        grad_attn_w = contract_rows(heads_out, grad_attended)
        grad_heads = (
            contract_cols(grad_attended, attn_full)
            .astype(jnp.bfloat16)
            .reshape(length, HEADS, head_size)
        )
        masked = attention_probs(project, segment)
        probs_float = jnp.exp(masked - log_total)
        probs_low = probs_float.astype(jnp.bfloat16)
        queries = project[:, :width].reshape(length, HEADS, head_size)
        keys_all = project[:, width : 2 * width].reshape(length, HEADS, head_size)
        values_all = project[:, 2 * width :].reshape(length, HEADS, head_size)
        grad_values = jnp.einsum(
            "hqk,qhd->khd", probs_low, grad_heads, preferred_element_type=jnp.float32
        )
        grad_probs = jnp.einsum(
            "qhd,khd->hqk", grad_heads, values_all, preferred_element_type=jnp.float32
        )
        row_dot = jnp.sum(probs_float * grad_probs, -1, keepdims=True)
        grad_scores = (probs_float * (grad_probs - row_dot)).astype(jnp.bfloat16)
        grad_queries = (
            jnp.einsum("hqk,khd->qhd", grad_scores, keys_all, preferred_element_type=jnp.float32)
            * scale
        )
        grad_keys = (
            jnp.einsum("hqk,qhd->khd", grad_scores, queries, preferred_element_type=jnp.float32)
            * scale
        )
        grad_qkv = jnp.concatenate(
            [
                grad_queries.reshape(length, width),
                grad_keys.reshape(length, width),
                grad_values.reshape(length, width),
            ],
            -1,
        ).astype(jnp.bfloat16)
        grad_qkv_w = contract_rows(normed, grad_qkv)
        grad_normed = contract_cols(grad_qkv, qkv_full)
        unused_one, norm_one_back = jax.vjp(
            layer_norm, block.astype(jnp.float32), gain_one, bias_one
        )
        grad_in_norm, grad_gain_one, grad_bias_one = norm_one_back(grad_normed)
        grad_tokens = (grad_middle + grad_in_norm).astype(jnp.bfloat16)
        terms = (
            grad_qkv_w,
            grad_attn_w,
            grad_route,
            grad_gain_one,
            grad_bias_one,
            grad_gain_two,
            grad_bias_two,
        )
        dense_acc = tuple((total + term for total, term in zip(dense_acc, terms)))
        return ((dense_acc, shard_in, shard_out, holding), (grad_tokens, slot))

    dense_zero = (
        jnp.zeros((width, 3 * width), jnp.float32),
        jnp.zeros((width, width), jnp.float32),
        jnp.zeros((width, experts), jnp.float32),
        jnp.zeros((width,), jnp.float32),
        jnp.zeros((width,), jnp.float32),
        jnp.zeros((width,), jnp.float32),
        jnp.zeros((width,), jnp.float32),
    )
    shard_zero_in = jnp.zeros((experts, slab_in, hidden), jnp.float32)
    shard_zero_out = jnp.zeros((experts, slab_out, width), jnp.float32)
    holding_zero = ()
    (dense_acc, shard_in, shard_out, holding), (grad_tokens_all, slots) = lax.scan(
        backward_step,
        (dense_zero, shard_zero_in, shard_zero_out, holding_zero),
        (tokens, cotangent, segment_ids, needs, own_pairs, kept_all),
    )
    slot_in = slots[0].reshape(micro * 2, width, hidden)
    slot_out = slots[1].reshape(micro * 2, hidden, width)
    amount = slot_in.shape[0]
    returned = lax.all_to_all(
        lax.all_to_all(
            shortened(
                (
                    slot_in.reshape(amount, outer, inner, slab_in, hidden),
                    slot_out.reshape(amount, outer, inner, slab_out, width),
                )
            ),
            "gx",
            split_axis=1,
            concat_axis=1,
            tiled=True,
        ),
        "gy",
        split_axis=2,
        concat_axis=2,
        tiled=True,
    )
    onehot = (
        needs.reshape(micro * 2, outer, inner)[None] == expert_ids[:, None, None, None]
    ).astype(jnp.float32)
    added = tuple(
        (jnp.einsum("esab,sabrc->erc", onehot, piece, precision=HIGH) for piece in returned)
    )
    shard_in = shard_in + added[0]
    shard_out = shard_out + added[1]
    dense_shards = (
        lax.psum_scatter(dense_acc[0], ("gx", "gy"), scatter_dimension=0, tiled=True),
        lax.psum_scatter(dense_acc[1], ("gx", "gy"), scatter_dimension=0, tiled=True),
        lax.psum_scatter(dense_acc[2], ("gx", "gy"), scatter_dimension=0, tiled=True),
        lax.psum_scatter(dense_acc[3], ("gx", "gy"), scatter_dimension=0, tiled=True),
        lax.psum_scatter(dense_acc[4], ("gx", "gy"), scatter_dimension=0, tiled=True),
        lax.psum_scatter(dense_acc[5], ("gx", "gy"), scatter_dimension=0, tiled=True),
        lax.psum_scatter(dense_acc[6], ("gx", "gy"), scatter_dimension=0, tiled=True),
    )
    return (
        mixed_all,
        grad_tokens_all,
        dense_shards[0],
        dense_shards[1],
        dense_shards[2],
        shard_in,
        shard_out,
        dense_shards[3],
        dense_shards[4],
        dense_shards[5],
        dense_shards[6],
    )


MESH = pl.DeviceIdType.MESH
ROWS = 224
SIDE = 128
ROOT2PI = math.sqrt(2.0 / math.pi)


def dot(left, right):
    return jnp.dot(left, right, preferred_element_type=jnp.float32)


class Place:
    def __init__(self):
        self.z = lax.axis_index("gx")
        g = lax.axis_index("gy")
        self.core = g % 2
        across_x = g + 2 - 4 * ((g // 2) % 2)
        across_y = g + 4 - 8 * (g // 4)
        across_both = across_x + 4 - 8 * (across_x // 4)
        self.at = (g, across_x, across_y, across_both)
        self.sibling = (self.z, g + 1 - 2 * self.core)

    def plane(self, k):
        return (self.z + k) % 4

    def device(self, rel, k):
        return (self.plane(k), self.at[rel])

    def chip(self, rel, k):
        return self.plane(k) * 4 + self.at[rel] // 2

    def index(self, rel, k):
        return self.plane(k) * 8 + self.at[rel]

    def greet(self):
        barrier = pltpu.get_barrier_semaphore()
        others = [(rel, k) for rel in range(4) for k in range(4) if (rel, k) != (0, 0)]
        for rel, k in others:
            pl.semaphore_signal(
                barrier, inc=1, device_id=self.device(rel, k), device_id_type=MESH
            )
        pl.semaphore_signal(barrier, inc=1, device_id=self.sibling, device_id_type=MESH)
        pl.semaphore_wait(barrier, len(others) + 1)


def send(started, src, dst, send_sem, recv_sem, device):
    copy = pltpu.make_async_remote_copy(
        src_ref=src,
        dst_ref=dst,
        send_sem=send_sem,
        recv_sem=recv_sem,
        device_id=device,
        device_id_type=MESH,
    )
    copy.start()
    started.append(copy)


def arrived(ref, sem):
    pltpu.make_async_copy(ref, ref, sem).wait()


def back(k):
    return (4 - k) % 4


class Spread:
    def __init__(self, place, here, there, packs, half, sems):
        self.place, self.here, self.there = place, here, there
        self.packs, self.half, self.started = packs, half, []
        self.send_sem, self.recv_sem = sems

    def go(self, kind, k_sem, k_there, rel, k, p, src, rel_there, device):
        send(
            self.started,
            src,
            self.there(rel_there, k_there, p, rel, k),
            self.send_sem.at[kind, k_sem * self.packs + p],
            self.recv_sem.at[kind, k_there * self.packs + p],
            device,
        )

    def wait(self, kind, rel, k, p):
        arrived(self.here(rel, k, p), self.recv_sem.at[kind, k * self.packs + p])

    def own(self, p, src, planes=True):
        if planes:
            for k in (1, 2, 3):
                self.go(0, k, back(k), 0, 0, p, src, 0, self.place.device(0, k))
        self.go(1, 0, 0, 0, 0, p, src, 1, self.place.device(1, 0))
        self.go(2, 0, 0, 0, 0, p, src, 2, self.place.device(2, 0))

    def plane(self, k, p):
        if k:
            self.wait(0, 0, k, p)
            src = self.here(0, k, p)
            self.go(1, k, k, 0, k, p, src, 1, self.place.device(1, 0))
            self.go(2, k, k, 0, k, p, src, 2, self.place.device(2, 0))

    def corner(self, k, p):
        self.wait(1, 1, k, p)
        self.wait(2, 2, k, p)
        if self.half(k, p) == 0:
            self.go(3, k, k, 1, k, p, self.here(1, k, p), 3, self.place.device(2, 0))
        else:
            self.go(3, k, k, 2, k, p, self.here(2, k, p), 3, self.place.device(1, 0))

    def last(self, k, p):
        self.wait(3, 3, k, p)

    def finish(self):
        for copy in self.started:
            copy.wait_send()


def norm_parts(values):
    center = values - jnp.mean(values, -1, keepdims=True)
    spread = jnp.mean(center * center, -1, keepdims=True)
    rise = lax.rsqrt(spread + EPS)
    return center * rise, rise


def real_rows():
    return lax.broadcasted_iota(jnp.int32, (ROWS, 1), 0) < PACK


def head_lanes(h):
    lane = lax.broadcasted_iota(jnp.int32, (1, SIDE), 1)
    inside = (lane >= h * HEAD) & (lane < (h + 1) * HEAD)
    return inside.astype(jnp.bfloat16)


def softmax_rows(queries, keys, same):
    scores = contract_cols(queries, keys) * (1.0 / math.sqrt(HEAD))
    scores = jnp.where(same, scores, MASK_FILL)
    raised = jnp.exp(scores - jnp.max(scores, -1, keepdims=True))
    return raised * (1.0 / jnp.sum(raised, -1, keepdims=True))


def pick(logits, expert):
    lane = lax.broadcasted_iota(jnp.int32, logits.shape, 1)
    return jnp.sum(jnp.where(lane == expert, logits, 0.0), -1, keepdims=True)


def two_gates(logits, first, second):
    gap = pick(logits, second) - pick(logits, first)
    return 1.0 / (1.0 + jnp.exp(gap)), 1.0 / (1.0 + jnp.exp(-gap))


def front_kernel(
    tok, seg_col, seg_row, own_dense, cot, w_in, w_out,
    routed_all, cot_all, w_in_all, w_out_all, dense_out, proj, heads, middle,
    dense, routed, turned,
    cot_send, cot_recv, routed_send, routed_recv, dense_send, dense_recv,
    core_send, core_recv, in_send, in_recv, pair_send, pair_recv, local_sem,
):
    place = Place()
    width = tok.shape[2]
    place.greet()

    def block_here(ref):
        return lambda rel, k, p: ref.at[rel, k * 2 + p]

    def block_there(ref):
        return lambda rel_there, k_there, p, rel, k: ref.at[rel_there, k_there * 2 + p]

    dense_tree = Spread(
        place,
        lambda rel, k, p: dense.at[place.index(rel, k)],
        lambda rel_there, k_there, p, rel, k: dense.at[place.index(rel, k)],
        1,
        lambda k, p: k % 2,
        (dense_send, dense_recv),
    )
    core_started = []

    def to_core(rel, k):
        slot = dense.at[place.index(rel, k)]
        send(
            core_started, slot, slot, core_send.at[rel, k], core_recv.at[rel, k], place.sibling
        )

    dense[place.index(0, 0)] = own_dense[...]
    dense_tree.own(0, dense.at[place.index(0, 0)])
    to_core(0, 0)
    for k in (1, 2, 3):
        dense_tree.plane(k, 0)
        to_core(0, k)
    for k in range(4):
        dense_tree.corner(k, 0)
        to_core(1, k)
        to_core(2, k)

    local = []

    def local_copy(src, dst):
        copy = pltpu.make_async_copy(src, dst, local_sem.at[len(local)])
        copy.start()
        local.append(copy)

    cot_tree = Spread(
        place, block_here(cot_all), block_there(cot_all), 2, lambda k, p: p, (cot_send, cot_recv)
    )
    for p in range(2):
        cot_tree.own(p, cot.at[p])
        local_copy(cot.at[p], cot_all.at[0, p])
    for k in range(4):
        dense_tree.last(k, 0)
        to_core(3, k)
    in_started = []
    for rel in (3, 1, 2, 0):
        for k in (2, 1, 3, 0):
            columns = pl.ds(pl.multiple_of(place.chip(rel, k) * SIDE, SIDE), SIDE)
            src = w_in.at[:, :, columns]
            dst = w_in_all.at[place.chip(0, 0), place.core]
            if (rel, k) == (0, 0):
                local_copy(src, dst)
            else:
                send(
                    in_started, src, dst, in_send.at[rel, k], in_recv.at[rel, back(k)],
                    place.device(rel, k),
                )
    pair_started = []
    local_copy(w_out, w_out_all.at[place.core])
    send(
        pair_started, w_out, w_out_all.at[place.core], pair_send.at[0], pair_recv.at[0],
        place.sibling,
    )
    for k in range(4):
        for rel in range(4):
            slot = dense.at[place.plane(k) * 8 + place.at[rel] + 1 - 2 * place.core]
            arrived(slot, core_recv.at[rel, k])
    local_copy(dense, dense_out)

    small = dense[:, :, 4 * width : 4 * width + SIDE].reshape(width, SIDE)
    turned[...] = jnp.transpose(small.astype(jnp.float32))
    gain_one, bias_one = turned[GAIN_ONE : GAIN_ONE + 1, :], turned[GAIN_ONE + 1 : GAIN_ONE + 2, :]
    gain_two, bias_two = turned[GAIN_ONE + 2 : GAIN_ONE + 3, :], turned[GAIN_ONE + 3 : GAIN_ONE + 4, :]

    routed_tree = Spread(
        place,
        block_here(routed_all),
        block_there(routed_all),
        2,
        lambda k, p: p,
        (routed_send, routed_recv),
    )

    for p in range(2):
        block = tok[p].astype(jnp.float32)
        unit, unused = norm_parts(block)
        normed = (unit * gain_one + bias_one).astype(jnp.bfloat16)
        w_qkv = dense[:, :, : 3 * width].reshape(width, 3 * width)
        proj[p] = dot(normed, w_qkv).astype(jnp.bfloat16)
        same = seg_col[p] == seg_row[p]

        def pair_of_heads(j, carry, p=p, same=same):
            at = pl.multiple_of(j * SIDE, SIDE)
            queries = proj[p, :, pl.ds(at, SIDE)]
            keys = proj[p, :, pl.ds(at + width, SIDE)]
            values = proj[p, :, pl.ds(at + 2 * width, SIDE)]
            out = jnp.zeros((ROWS, SIDE), jnp.float32)
            for h in range(2):
                lanes = head_lanes(h)
                probs = softmax_rows(queries * lanes, keys, same).astype(jnp.bfloat16)
                out = out + dot(probs, values * lanes)
            heads[p, :, pl.ds(at, SIDE)] = out.astype(jnp.bfloat16)
            return carry

        lax.fori_loop(0, width // SIDE, pair_of_heads, 0)
        w_attn = dense[:, :, 3 * width : 4 * width].reshape(width, width)
        mid = block + dot(heads[p], w_attn)
        middle[p] = mid
        unit, unused = norm_parts(mid)
        routed[p] = jnp.where(real_rows(), unit * gain_two + bias_two, 0.0).astype(jnp.bfloat16)
        routed_tree.own(p, routed.at[p])
        local_copy(routed.at[p], routed_all.at[0, p])

    for k in (1, 2, 3):
        for p in range(2):
            cot_tree.plane(k, p)
    for k in range(4):
        for p in range(2):
            cot_tree.corner(k, p)
    for k in (1, 2, 3):
        for p in range(2):
            routed_tree.plane(k, p)
    for rel in range(4):
        for k in range(4):
            if (rel, k) != (0, 0):
                arrived(w_in_all.at[place.chip(rel, k), place.core], in_recv.at[rel, k])
    local[2 + 0].wait()
    mine = w_in_all.at[:, place.core]
    send(pair_started, mine, mine, pair_send.at[1], pair_recv.at[1], place.sibling)
    for k in range(4):
        for p in range(2):
            routed_tree.corner(k, p)
    for k in range(4):
        for p in range(2):
            cot_tree.last(k, p)
            routed_tree.last(k, p)
    other = 1 - place.core
    arrived(w_out_all.at[other], pair_recv.at[0])
    arrived(w_in_all.at[:, other], pair_recv.at[1])
    for copy in local[:2] + local[3:]:
        copy.wait()
    for tree in (dense_tree, cot_tree, routed_tree):
        tree.finish()
    for copy in core_started + in_started + pair_started:
        copy.wait_send()


def expert_kernel(
    pairs, core, routed, cot, w_in_all, w_out_all, dense,
    mixed, grad, d_in, d_out_own, d_out_far,
    acc_in, acc_out, gate_row,
):
    step = pl.program_id(0)
    width, slab = routed.shape[3], 2 * SIDE
    experts = acc_in.shape[0]

    @pl.when(step == 0)
    def clear():
        def one(e, carry):
            acc_in[e] = jnp.zeros(acc_in.shape[1:], jnp.float32)
            acc_out[e] = jnp.zeros(acc_out.shape[1:], jnp.float32)
            return carry

        lax.fori_loop(0, experts, one, 0)
        gate_row[...] = jnp.zeros_like(gate_row)

    first, second = pairs[2 * step], pairs[2 * step + 1]
    rows, cots = routed[0, 0], cot[0, 0]
    w_in = jnp.concatenate(
        [w_in_all[:, :, e].reshape(width, SIDE) for e in (first, second)], axis=1
    )
    w_out = jnp.concatenate(
        [w_out_all[:, e].reshape(SIDE, width) for e in (first, second)], axis=0
    )
    route = dense[:, :, 4 * width : 4 * width + SIDE].reshape(width, SIDE)
    gate_a, gate_b = two_gates(dot(rows, route), first, second)
    lane = lax.broadcasted_iota(jnp.int32, (1, slab), 1)
    gates = jnp.where(lane < SIDE, gate_a, gate_b)
    hidden = dot(rows, w_in)
    back_act = contract_cols(cots, w_out)
    square = hidden * hidden
    bend = jnp.tanh(ROOT2PI * hidden * (1.0 + 0.044715 * square))
    half = 0.5 * (1.0 + bend)
    act = (hidden * half).astype(jnp.bfloat16).astype(jnp.float32)
    slope = half + 0.5 * hidden * (1.0 - bend * bend) * (ROOT2PI * (1.0 + 0.134145 * square))
    gated = (gates * act).astype(jnp.bfloat16)
    grad_pre = (gates * back_act * slope).astype(jnp.bfloat16)
    product = (act * back_act).astype(jnp.bfloat16)
    sign = jnp.where(lane < SIDE, 1.0, -1.0)
    signs = jnp.broadcast_to(sign, (8, slab)).astype(jnp.bfloat16)
    gate_row[:, :ROWS] = contract_cols(signs, product)
    mixed[0, 0] = dot(gated, w_out).astype(jnp.bfloat16)
    grads = contract_cols(grad_pre, w_in)
    grad[0, 0] = jnp.concatenate([grads[:PACK], gate_row[...]], axis=0).astype(jnp.bfloat16)
    new_in = contract_rows(rows, grad_pre)
    acc_in[first] += new_in[:, :SIDE]
    acc_in[second] += new_in[:, SIDE:]
    new_out = contract_rows(gated, cots)
    acc_out[first] += new_out[:SIDE]
    acc_out[second] += new_out[SIDE:]

    @pl.when(step == pl.num_programs(0) - 1)
    def emit():
        own = pl.multiple_of(core[0] * HEAD, HEAD)
        far = pl.multiple_of((1 - core[0]) * HEAD, HEAD)

        def one(e, carry):
            total = acc_in[e].astype(jnp.bfloat16).reshape(16, 2, 16, SIDE)
            d_in[0, :, e] = total[:, 0]
            d_in[1, :, e] = total[:, 1]
            d_out_own[e] = acc_out[e, pl.ds(own, HEAD)]
            d_out_far[e] = acc_out[e, pl.ds(far, HEAD)].astype(jnp.bfloat16)
            return carry

        lax.fori_loop(0, experts, one, 0)


class Collect:
    def __init__(self, place, part, corner, from_x, from_y, from_z, packs, half, sems):
        self.place, self.part = place, part
        self.corner, self.from_x, self.from_y, self.from_z = corner, from_x, from_y, from_z
        self.packs, self.half, self.started = packs, half, []
        self.send_sem, self.recv_sem = sems

    def go(self, kind, src, dst, at_send, at_recv, device):
        send(
            self.started, src, dst, self.send_sem.at[kind, at_send],
            self.recv_sem.at[kind, at_recv], device,
        )

    def opposite(self, k, p):
        at = k * self.packs + p
        towards = 2 if self.half(k, p) == 0 else 1
        self.go(3, self.part(3, k, p), self.corner.at[at], at, at, self.place.device(towards, 0))

    def straight(self, k, p):
        at = k * self.packs + p
        if self.half(k, p) == 0:
            self.go(2, self.part(2, k, p), self.from_y.at[at], at, at, self.place.device(2, 0))
        else:
            self.go(1, self.part(1, k, p), self.from_x.at[at], at, at, self.place.device(1, 0))

    def helped(self, k, p, mine):
        at = k * self.packs + p
        ref = self.corner.at[at]
        arrived(ref, self.recv_sem.at[3, at])
        total = ref[...].astype(jnp.float32) + mine().astype(jnp.float32)
        ref[...] = total.astype(jnp.bfloat16)
        if self.half(k, p) == 0:
            self.go(1, ref, self.from_x.at[at], at, at, self.place.device(1, 0))
        else:
            self.go(2, ref, self.from_y.at[at], at, at, self.place.device(2, 0))

    def plane(self, k, p, mine):
        at = k * self.packs + p
        arrived(self.from_x.at[at], self.recv_sem.at[1, at])
        arrived(self.from_y.at[at], self.recv_sem.at[2, at])
        total = self.from_x[at].astype(jnp.float32) + self.from_y[at].astype(jnp.float32)
        total = total + mine().astype(jnp.float32)
        if k:
            self.from_x[at] = total.astype(jnp.bfloat16)
            there = back(k) * self.packs + p
            self.go(
                0, self.from_x.at[at], self.from_z.at[there], at, there, self.place.device(0, k)
            )
            return None
        for other in (1, 2, 3):
            at = other * self.packs + p
            arrived(self.from_z.at[at], self.recv_sem.at[0, at])
            total = total + self.from_z[at].astype(jnp.float32)
        return total

    def finish(self):
        for copy in self.started:
            copy.wait_send()


def tail_kernel(
    pairs, tok, cot, seg_col, seg_row, proj, heads, middle, dense, grad_part, mixed_part, d_in,
    d_out_far,
    mixed, d_tok, d_dense, d_in_all, d_out_all,
    g_own, g_corner, g_x, g_y, g_z, m_own, m_corner, m_x, m_y, m_z,
    total_grad, grad_mid, grad_heads, grad_qkv, acc, small_rows, turned,
    in_far, in_mine, far_dense, got_dense, part_dense, s_corner, s_x, s_y, s_z,
    g_send, g_recv, m_send, m_recv, s_send, s_recv, in_send, in_recv,
    pair_send, pair_recv, load_sem,
):
    place = Place()
    width = tok.shape[2]
    place.greet()

    def by_pack(k, p):
        return p

    def part_of(ref):
        return lambda rel, k, p: ref.at[rel, k * 2 + p]

    grads = Collect(
        place, part_of(grad_part), g_corner, g_x, g_y, g_z, 2, by_pack, (g_send, g_recv)
    )
    mixes = Collect(
        place, part_of(mixed_part), m_corner, m_x, m_y, m_z, 2, by_pack, (m_send, m_recv)
    )
    order = [(k, p) for k in (2, 1, 3, 0) for p in range(2)]
    for k, p in order:
        grads.opposite(k, p)
    for k, p in order:
        grads.straight(k, p)

    loads = []

    def load(src, dst):
        copy = pltpu.make_async_copy(src, dst, load_sem.at[len(loads)])
        copy.start()
        loads.append(copy)
        return copy

    def load_parts(ref, own):
        waits = {}
        for k, p in order:
            at = k * 2 + p
            waits["helped", k, p] = load(ref.at[1 + p, at], own.at[1, at])
        for k, p in order:
            at = k * 2 + p
            waits["plane", k, p] = load(ref.at[0, at], own.at[0, at])
        return waits

    g_waits = load_parts(grad_part, g_own)
    pair_started = []
    send(
        pair_started, d_in.at[1 - place.core], in_far, pair_send.at[0], pair_recv.at[0],
        place.sibling,
    )
    send(
        pair_started, d_out_far, d_out_all, pair_send.at[1], pair_recv.at[1], place.sibling
    )
    in_load = load(d_in.at[place.core], in_mine)
    m_waits = load_parts(mixed_part, m_own)

    def mine(waits, own, kind, k, p):
        def get():
            waits[kind, k, p].wait()
            return own[0 if kind == "plane" else 1, k * 2 + p]

        return get

    in_load.wait()
    arrived(in_far, pair_recv.at[0])

    def add_pair(i, carry):
        total = in_mine[i].astype(jnp.float32) + in_far[i].astype(jnp.float32)
        in_mine[i] = total.astype(jnp.bfloat16)
        return carry

    lax.fori_loop(0, in_mine.shape[0], add_pair, 0)

    for k, p in order:
        grads.helped(k, p, mine(g_waits, g_own, "helped", k, p))
    for k, p in order:
        mixes.opposite(k, p)
    for k, p in order:
        mixes.straight(k, p)
    for k, p in order:
        if k:
            grads.plane(k, p, mine(g_waits, g_own, "plane", k, p))
    in_started = []
    columns = pl.ds(pl.multiple_of(place.chip(0, 0) * SIDE, SIDE), SIDE)
    for rel in (3, 1, 2, 0):
        for k in (2, 1, 3, 0):
            src = in_mine.at[place.chip(rel, k)]
            dst = d_in_all.at[:, :, columns]
            if (rel, k) == (0, 0):
                in_local = load(src, dst)
            else:
                send(
                    in_started, src, dst, in_send.at[rel, k], in_recv.at[rel, back(k)],
                    place.device(rel, k),
                )
    for p in range(2):
        total_grad[p] = grads.plane(0, p, mine(g_waits, g_own, "plane", 0, p))

    small = dense[:, :, 4 * width : 4 * width + SIDE].reshape(width, SIDE)
    turned[...] = jnp.transpose(small.astype(jnp.float32))
    small_rows[...] = jnp.zeros_like(small_rows)
    gain_one, bias_one = turned[GAIN_ONE : GAIN_ONE + 1, :], turned[GAIN_ONE + 1 : GAIN_ONE + 2, :]
    gain_two, bias_two = turned[GAIN_ONE + 2 : GAIN_ONE + 3, :], turned[GAIN_ONE + 3 : GAIN_ONE + 4, :]

    def add_to(p, columns, value):
        if p == 0:
            acc[:, columns] = value
        else:
            acc[:, columns] += value

    def add_row(at, value):
        small_rows[at : at + 1, :] += jnp.sum(value, 0, keepdims=True)

    for p in range(2):
        first, second = pairs[2 * p], pairs[2 * p + 1]
        got = total_grad[p]
        tall = jnp.concatenate(
            [got[PACK:, : 2 * SIDE], jnp.zeros((SIDE - 8, 2 * SIDE), jnp.float32)], axis=0
        )
        gap_grad = jnp.transpose(tall)[:ROWS, 0:1]
        got = jnp.where(real_rows(), got, 0.0)
        mid = middle[p]
        unit, rise = norm_parts(mid)
        routed = jnp.where(real_rows(), unit * gain_two + bias_two, 0.0).astype(jnp.bfloat16)
        route = dense[:, :, 4 * width : 4 * width + SIDE].reshape(width, SIDE)
        gate_a, gate_b = two_gates(dot(routed, route), first, second)
        grad_a = gate_a * gate_b * gap_grad
        lane = lax.broadcasted_iota(jnp.int32, (ROWS, SIDE), 1)
        grad_logits = jnp.where(lane == first, grad_a, jnp.where(lane == second, -grad_a, 0.0))
        grad_logits = jnp.where(real_rows(), grad_logits, 0.0).astype(jnp.bfloat16)
        add_to(p, pl.ds(4 * width, SIDE), contract_rows(routed, grad_logits))
        got = got + contract_cols(grad_logits, route)
        add_row(2, got * unit)
        add_row(3, got)
        u = got * gain_two
        grad_middle = cot[p].astype(jnp.float32) + rise * (
            u - jnp.mean(u, -1, keepdims=True) - unit * jnp.mean(u * unit, -1, keepdims=True)
        )
        grad_mid[...] = grad_middle
        attended = grad_middle.astype(jnp.bfloat16)
        add_to(p, pl.ds(3 * width, width), contract_rows(heads[p], attended))
        w_attn = dense[:, :, 3 * width : 4 * width].reshape(width, width)
        grad_heads[...] = contract_cols(attended, w_attn).astype(jnp.bfloat16)
        same = seg_col[p] == seg_row[p]

        def pair_of_heads(j, carry, p=p, same=same):
            at = pl.multiple_of(j * SIDE, SIDE)
            queries = proj[p, :, pl.ds(at, SIDE)]
            keys = proj[p, :, pl.ds(at + width, SIDE)]
            values = proj[p, :, pl.ds(at + 2 * width, SIDE)]
            out_grad = grad_heads[:, pl.ds(at, SIDE)]
            zero = jnp.zeros((ROWS, SIDE), jnp.float32)
            grad_q, grad_k, grad_v = zero, zero, zero
            for h in range(2):
                lanes = head_lanes(h)
                probs = softmax_rows(queries * lanes, keys, same)
                mine_grad = out_grad * lanes
                grad_v = grad_v + contract_rows(probs.astype(jnp.bfloat16), mine_grad)
                grad_probs = contract_cols(mine_grad, values)
                row_dot = jnp.sum(probs * grad_probs, -1, keepdims=True)
                grad_scores = (probs * (grad_probs - row_dot)).astype(jnp.bfloat16)
                grad_q = grad_q + dot(grad_scores, keys * lanes)
                grad_k = grad_k + contract_rows(grad_scores, queries * lanes)
            scale = 1.0 / math.sqrt(HEAD)
            grad_qkv[:, pl.ds(at, SIDE)] = (grad_q * scale).astype(jnp.bfloat16)
            grad_qkv[:, pl.ds(at + width, SIDE)] = (grad_k * scale).astype(jnp.bfloat16)
            grad_qkv[:, pl.ds(at + 2 * width, SIDE)] = grad_v.astype(jnp.bfloat16)
            return carry

        lax.fori_loop(0, width // SIDE, pair_of_heads, 0)
        for k, q in order[4 * p : 4 * p + 4]:
            mixes.helped(k, q, mine(m_waits, m_own, "helped", k, q))
        unit, rise = norm_parts(tok[p].astype(jnp.float32))
        normed = (unit * gain_one + bias_one).astype(jnp.bfloat16)
        add_to(p, pl.ds(0, 3 * width), contract_rows(normed, grad_qkv[...]))
        w_qkv = dense[:, :, : 3 * width].reshape(width, 3 * width)
        grad_normed = contract_cols(grad_qkv[...], w_qkv)
        add_row(0, grad_normed * unit)
        add_row(1, grad_normed)
        u = grad_normed * gain_one
        d_tok[p] = (
            grad_mid[...]
            + rise
            * (u - jnp.mean(u, -1, keepdims=True) - unit * jnp.mean(u * unit, -1, keepdims=True))
        ).astype(jnp.bfloat16)

    tall = jnp.concatenate(
        [
            jnp.zeros((GAIN_ONE, width), jnp.float32),
            small_rows[...],
            jnp.zeros((SIDE - GAIN_ONE - 8, width), jnp.float32),
        ],
        axis=0,
    )
    acc[:, 4 * width :] += jnp.transpose(tall)
    columns_all = acc.shape[1]

    def cut(i, carry):
        own_rows = pl.ds(pl.multiple_of(i * 32 + place.core * 16, 16), 16)
        far_rows = pl.ds(pl.multiple_of(i * 32 + 16 - place.core * 16, 16), 16)
        far_dense[i] = acc[far_rows, :].astype(jnp.bfloat16)
        part_dense[i] = acc[own_rows, :]
        return carry

    lax.fori_loop(0, 16, cut, 0)
    send(
        pair_started, far_dense, got_dense, pair_send.at[2], pair_recv.at[2], place.sibling
    )
    arrived(got_dense, pair_recv.at[2])

    def join(i, carry):
        far_dense_sum = part_dense[i] + got_dense[i].astype(jnp.float32)
        got_dense[i] = far_dense_sum.astype(jnp.bfloat16)
        return carry

    lax.fori_loop(0, 16, join, 0)

    def dense_part(rel, k, p):
        return got_dense.at[place.chip(rel, k)]

    sums = Collect(
        place, dense_part, s_corner, s_x, s_y, s_z, 1, lambda k, p: k % 2, (s_send, s_recv)
    )
    for k in (2, 1, 3, 0):
        sums.opposite(k, 0)
    for k in (2, 1, 3, 0):
        sums.straight(k, 0)
    for k in (2, 1, 3, 0):
        sums.helped(k, 0, lambda k=k: got_dense[place.chip(1 + k % 2, k)])
    for k in (2, 1, 3):
        sums.plane(k, 0, lambda k=k: got_dense[place.chip(0, k)])
    d_dense[...] = sums.plane(0, 0, lambda: got_dense[place.chip(0, 0)])

    for k, p in order:
        if k:
            mixes.plane(k, p, mine(m_waits, m_own, "plane", k, p))
    for p in range(2):
        summed = mixes.plane(0, p, mine(m_waits, m_own, "plane", 0, p))
        mixed[p] = (middle[p] + summed).astype(jnp.bfloat16)

    for rel in range(4):
        for k in range(4):
            if (rel, k) != (0, 0):
                place_columns = pl.ds(pl.multiple_of(place.chip(rel, k) * SIDE, SIDE), SIDE)
                arrived(d_in_all.at[:, :, place_columns], in_recv.at[rel, k])
    in_local.wait()
    arrived(d_out_all, pair_recv.at[1])
    for tree in (grads, mixes, sums):
        tree.finish()
    for copy in pair_started + in_started:
        copy.wait_send()


def shards_fast(
    tokens,
    segment_ids,
    pack_task,
    task_experts,
    w_qkv,
    w_attn_out,
    w_router,
    w_expert_in,
    w_expert_out,
    norm1_gain,
    norm1_bias,
    norm2_gain,
    norm2_bias,
    cotangent,
):
    packs, length, width = tokens.shape
    experts, slab_in, hidden = w_expert_in.shape
    slab_out = w_expert_out.shape[1]
    dense_width = 4 * width + SIDE
    any_space = pl.BlockSpec(memory_space=pl.ANY)
    vmem = pl.BlockSpec(memory_space=pltpu.VMEM)
    smem = pl.BlockSpec(memory_space=pltpu.SMEM)
    low = jnp.bfloat16
    flat = jax.ShapeDtypeStruct
    dma = pltpu.SemaphoreType.DMA

    def tall(array, fill=0):
        return jnp.pad(
            array,
            ((0, 0), (0, ROWS - length)) + ((0, 0),) * (array.ndim - 2),
            constant_values=fill,
        )

    tok, cot = tall(tokens), tall(cotangent)
    segments = tall(segment_ids, -1)
    seg_col, seg_row = segments[:, :, None], segments[:, None, :]
    norms = jnp.stack([norm1_gain, norm1_bias, norm2_gain, norm2_bias], axis=1)
    small = jnp.concatenate([w_router, norms], axis=1)
    small = jnp.pad(small, ((0, 0), (0, SIDE - small.shape[1])))
    own_dense = jnp.concatenate([w_qkv, w_attn_out, small], axis=1)

    pack_pairs = task_experts[pack_task]
    z, g = lax.axis_index("gx"), lax.axis_index("gy")
    core = g % 2
    slot_devices = []
    for rel in range(4):
        at = g + (2 - 4 * ((g // 2) % 2)) * (rel % 2) + (4 - 8 * (g // 4)) * (rel // 2)
        for k in range(4):
            slot_devices.append(((z + k) % 4) * 8 + at)
    slots = jnp.stack(slot_devices)
    slot_pairs = pack_pairs.reshape(32, packs * 2)[slots].reshape(-1)

    blocks = flat((4, 4 * packs, ROWS, width), low)
    (
        routed_all, cot_all, w_in_all, w_out_all, dense, proj, heads, middle,
    ) = pl.pallas_call(
        front_kernel,
        out_shape=(
            blocks,
            blocks,
            flat((16, 2, experts, slab_in, SIDE), low),
            flat((2, experts, slab_out, width), low),
            flat((32, slab_in, dense_width), low),
            flat((packs, ROWS, 3 * width), low),
            flat((packs, ROWS, width), low),
            flat((packs, ROWS, width), jnp.float32),
        ),
        in_specs=[vmem] * 4 + [any_space] * 3,
        out_specs=(any_space,) * 5 + (vmem,) * 3,
        scratch_shapes=[
            pltpu.VMEM((32, slab_in, dense_width), low),
            pltpu.VMEM((packs, ROWS, width), low),
            pltpu.VMEM((SIDE, width), jnp.float32),
            dma((4, 8)), dma((4, 8)), dma((4, 8)), dma((4, 8)), dma((4, 4)), dma((4, 4)),
            dma((4, 4)), dma((4, 4)), dma((4, 4)), dma((4, 4)), dma((2,)), dma((2,)), dma((8,)),
        ],
        compiler_params=pltpu.CompilerParams(
            collective_id=0, has_side_effects=True, vmem_limit_bytes=40 << 20
        ),
        name="front",
    )(tok, seg_col, seg_row, own_dense, cot, w_expert_in, w_expert_out)

    steps = 4 * 4 * packs
    one_block = pl.BlockSpec(
        (1, 1, ROWS, width), lambda i, *unused: (i // (4 * packs), i % (4 * packs), 0, 0)
    )
    mixed_part, grad_part, d_in, d_out_own, d_out_far = pl.pallas_call(
        expert_kernel,
        grid_spec=pltpu.PrefetchScalarGridSpec(
            num_scalar_prefetch=2,
            grid=(steps,),
            in_specs=[one_block, one_block, vmem, vmem, vmem],
            out_specs=[one_block, one_block, vmem, vmem, vmem],
            scratch_shapes=[
                pltpu.VMEM((experts, width, SIDE), jnp.float32),
                pltpu.VMEM((experts, SIDE, width), jnp.float32),
                pltpu.VMEM((8, width), jnp.float32),
            ],
        ),
        out_shape=(
            blocks,
            blocks,
            flat((2, 16, experts, slab_in, SIDE), low),
            flat((experts, slab_out, width), jnp.float32),
            flat((experts, slab_out, width), low),
        ),
        compiler_params=pltpu.CompilerParams(vmem_limit_bytes=56 << 20),
        name="experts",
    )(slot_pairs, core[None], routed_all, cot_all, w_in_all, w_out_all, dense)

    parts = pltpu.VMEM((4 * packs, ROWS, width), low)
    slices = pltpu.VMEM((4, slab_in, dense_width), low)
    sliced = pltpu.VMEM((16, slab_in, dense_width), low)
    mixed, d_tok, d_dense, d_in_all, d_out_all = pl.pallas_call(
        tail_kernel,
        out_shape=(
            flat((packs, ROWS, width), low),
            flat((packs, ROWS, width), low),
            flat((slab_in, dense_width), jnp.float32),
            flat((experts, slab_in, hidden), low),
            flat((experts, slab_out, width), low),
        ),
        in_specs=[smem] + [vmem] * 8 + [any_space] * 4,
        out_specs=(vmem,) * 3 + (any_space,) * 2,
        scratch_shapes=[
            pltpu.VMEM((2, 4 * packs, ROWS, width), low), parts, parts, parts, parts,
            pltpu.VMEM((2, 4 * packs, ROWS, width), low), parts, parts, parts, parts,
            pltpu.VMEM((packs, ROWS, width), jnp.float32),
            pltpu.VMEM((ROWS, width), jnp.float32),
            pltpu.VMEM((ROWS, width), low),
            pltpu.VMEM((ROWS, 3 * width), low),
            pltpu.VMEM((width, dense_width), jnp.float32),
            pltpu.VMEM((8, width), jnp.float32),
            pltpu.VMEM((SIDE, width), jnp.float32),
            pltpu.VMEM((16, experts, slab_in, SIDE), low),
            pltpu.VMEM((16, experts, slab_in, SIDE), low),
            sliced, sliced,
            pltpu.VMEM((16, slab_in, dense_width), jnp.float32),
            slices, slices, slices, slices,
            dma((4, 8)), dma((4, 8)), dma((4, 8)), dma((4, 8)), dma((4, 4)), dma((4, 4)),
            dma((4, 4)), dma((4, 4)), dma((3,)), dma((3,)), dma((40,)),
        ],
        compiler_params=pltpu.CompilerParams(
            collective_id=1, has_side_effects=True, vmem_limit_bytes=60 << 20
        ),
        name="tail",
    )(
        slot_pairs[: 2 * packs], tok, cot, seg_col, seg_row, proj, heads, middle, dense,
        grad_part, mixed_part, d_in, d_out_far,
    )
    norm_at = 4 * width + GAIN_ONE
    return (
        mixed[:, :length],
        d_tok[:, :length],
        d_dense[:, : 3 * width],
        d_dense[:, 3 * width : 4 * width],
        d_dense[:, 4 * width : 4 * width + experts],
        d_in_all.astype(jnp.float32),
        d_out_own + d_out_all.astype(jnp.float32),
        d_dense[:, norm_at],
        d_dense[:, norm_at + 1],
        d_dense[:, norm_at + 2],
        d_dense[:, norm_at + 3],
    )


def solution(mesh):
    outer, inner = mesh.shape["gx"], mesh.shape["gy"]

    def shards(*arrays):
        packs, length, width = arrays[0].shape
        experts, slab_in, hidden = arrays[7].shape
        fits = (
            (outer, inner) == (4, 8)
            and packs == 2
            and length == PACK
            and experts == GAIN_ONE
            and width == HEADS * HEAD
            and slab_in == 16
            and hidden == 16 * SIDE
        )
        return (shards_fast if fits else shards_any)(*arrays)

    placed = (
        P(("gx", "gy"), None, None),
        P(("gx", "gy"), None),
        P(),
        P(),
        P(("gx", "gy"), None),
        P(("gx", "gy"), None),
        P(("gx", "gy"), None),
        P(None, ("gx", "gy"), None),
        P(None, ("gx", "gy"), None),
        P(("gx", "gy")),
        P(("gx", "gy")),
        P(("gx", "gy")),
        P(("gx", "gy")),
        P(("gx", "gy"), None, None),
    )
    return jax.shard_map(
        shards,
        mesh=mesh,
        in_specs=placed,
        out_specs=(
            P(("gx", "gy"), None, None),
            P(("gx", "gy"), None, None),
            P(("gx", "gy"), None),
            P(("gx", "gy"), None),
            P(("gx", "gy"), None),
            P(None, ("gx", "gy"), None),
            P(None, ("gx", "gy"), None),
            P(("gx", "gy")),
            P(("gx", "gy")),
            P(("gx", "gy")),
            P(("gx", "gy")),
        ),
        check_vma=False,
    )
```

```python
import functools
import math

import jax
import jax.numpy as jnp
from jax import lax
from jax.experimental import pallas as pl
from jax.experimental.pallas import tpu as pltpu
from jax.sharding import PartitionSpec as P

HEADS = 8
HEAD = 64
PACK = 216
GAIN_ONE = 32


EPS = 1e-05
MASK_FILL = -1e30
HIGH = lax.Precision.HIGHEST


def shortened(value):

    def short(part):
        return part.astype(jnp.bfloat16) if part.dtype == jnp.float32 else part

    return jax.tree.map(short, value)


def layer_norm(values, gain, bias):
    center = values - jnp.mean(values, -1, keepdims=True)
    spread = jnp.mean(center * center, -1, keepdims=True)
    return center * lax.rsqrt(spread + EPS) * gain + bias


def contract_rows(left, right):
    return lax.dot_general(
        left, right, (((0,), (0,)), ((), ())), preferred_element_type=jnp.float32
    )


def contract_cols(left, right):
    return lax.dot_general(
        left, right, (((1,), (1,)), ((), ())), preferred_element_type=jnp.float32
    )


def shards_any(
    tokens,
    segment_ids,
    pack_task,
    task_experts,
    w_qkv,
    w_attn_out,
    w_router,
    w_expert_in,
    w_expert_out,
    norm1_gain,
    norm1_bias,
    norm2_gain,
    norm2_bias,
    cotangent,
):
    outer = lax.axis_size("gx")
    inner = lax.axis_size("gy")
    devices = outer * inner
    micro, length, width = tokens.shape
    experts, slab_in, hidden = w_expert_in.shape
    slab_out = w_expert_out.shape[1]
    head_size = width // HEADS
    scale = 1.0 / math.sqrt(head_size)
    device = lax.axis_index("gx") * inner + lax.axis_index("gy")
    gathered = (
        lax.all_gather(w_qkv, ("gx", "gy"), axis=0, tiled=True),
        lax.all_gather(w_attn_out, ("gx", "gy"), axis=0, tiled=True),
        lax.all_gather(w_router, ("gx", "gy"), axis=0, tiled=True),
        lax.all_gather(norm1_gain, ("gx", "gy"), axis=0, tiled=True),
        lax.all_gather(norm1_bias, ("gx", "gy"), axis=0, tiled=True),
        lax.all_gather(norm2_gain, ("gx", "gy"), axis=0, tiled=True),
        lax.all_gather(norm2_bias, ("gx", "gy"), axis=0, tiled=True),
    )
    qkv_full, attn_full, route_full = (gathered[0], gathered[1], gathered[2])
    gain_one, bias_one, gain_two, bias_two = tuple(
        (piece.astype(jnp.float32) for piece in gathered[3:])
    )
    route_float = route_full.astype(jnp.float32)
    pack_pairs = task_experts[pack_task]
    needs = jnp.transpose(pack_pairs.reshape(outer, inner, micro, 2), (2, 3, 0, 1))
    route_pairs = jnp.transpose(pack_pairs.reshape(devices, micro, 2), (1, 0, 2))
    own_pairs = lax.dynamic_slice_in_dim(pack_pairs, device * micro, micro, 0)
    expert_ids = jnp.arange(experts, dtype=jnp.int32)

    def slabs(need):
        return (w_expert_in[need], w_expert_out[need])

    def joined(pieces):
        return (
            pieces[0].reshape(pieces[0].shape[0], width, hidden),
            pieces[1].reshape(pieces[1].shape[0], hidden, width),
        )

    def attention_probs(project, segment):
        queries = project[:, :width].reshape(length, HEADS, head_size)
        keys_all = project[:, width : 2 * width].reshape(length, HEADS, head_size)
        scores = (
            jnp.einsum("qhd,khd->hqk", queries, keys_all, preferred_element_type=jnp.float32)
            * scale
        )
        same_doc = segment[:, None] == segment[None, :]
        return jnp.where(same_doc[None], scores, MASK_FILL)

    def forward_step(carry, inputs):
        block, segment, need, pair, senders = inputs
        block_float = block.astype(jnp.float32)
        normed = layer_norm(block_float, gain_one, bias_one).astype(jnp.bfloat16)
        project = jnp.dot(normed, qkv_full, preferred_element_type=jnp.float32).astype(jnp.bfloat16)
        masked = attention_probs(project, segment)
        peak = jnp.max(masked, -1, keepdims=True)
        raised = jnp.exp(masked - peak)
        totals = jnp.sum(raised, -1, keepdims=True)
        log_total = peak + jnp.log(totals)
        attn_low = (raised / totals).astype(jnp.bfloat16)
        values_all = project[:, 2 * width :].reshape(length, HEADS, head_size)
        heads_out = (
            jnp.einsum("hqk,khd->qhd", attn_low, values_all, preferred_element_type=jnp.float32)
            .reshape(length, width)
            .astype(jnp.bfloat16)
        )
        middle = block_float + jnp.dot(heads_out, attn_full, preferred_element_type=jnp.float32)
        routed = layer_norm(middle, gain_two, bias_two).astype(jnp.bfloat16)
        logits = jnp.dot(routed, route_full, preferred_element_type=jnp.float32)
        select = (expert_ids[None, :] == pair[:, None]).astype(jnp.float32)
        chosen = jnp.sum(logits[:, None, :] * select[None], -1)
        raised_gate = jnp.exp(chosen - jnp.max(chosen, -1, keepdims=True))
        gates = raised_gate / jnp.sum(raised_gate, -1, keepdims=True)
        weights_in, weights_out = joined(
            lax.all_to_all(
                lax.all_to_all(
                    shortened(slabs(need)), "gx", split_axis=1, concat_axis=1, tiled=True
                ),
                "gy",
                split_axis=2,
                concat_axis=2,
                tiled=True,
            )
        )
        hidden_pre = jnp.einsum(
            "ld,kdf->klf", routed, weights_in, preferred_element_type=jnp.float32
        )
        hidden_low = jax.nn.gelu(hidden_pre).astype(jnp.bfloat16)
        expert_out = jnp.einsum(
            "klf,kfd->kld", hidden_low, weights_out, preferred_element_type=jnp.float32
        )
        saved = ()
        mixed = middle + gates[:, 0:1] * expert_out[0] + gates[:, 1:2] * expert_out[1]
        kept = (
            normed,
            project,
            log_total,
            heads_out,
            middle,
            routed,
            gates,
            hidden_pre,
            hidden_low,
            expert_out,
            saved,
        )
        return (carry, (mixed.astype(jnp.bfloat16), kept))

    start = jnp.zeros((), jnp.float32)
    unused, (mixed_all, kept_all) = lax.scan(
        forward_step, start, (tokens, segment_ids, needs, own_pairs, route_pairs)
    )

    def backward_step(carry, inputs):
        dense_acc, shard_in, shard_out, holding = carry
        block, grad_top, segment, need, pair, kept = inputs
        (
            normed,
            project,
            log_total,
            heads_out,
            middle,
            routed,
            gates,
            hidden_pre,
            hidden_low,
            expert_out,
            saved,
        ) = kept
        grad_float = grad_top.astype(jnp.float32)
        grad_gate = jnp.sum(grad_float[None] * expert_out, -1).T
        grad_chosen = gates * (grad_gate - jnp.sum(gates * grad_gate, -1, keepdims=True))
        select = (expert_ids[None, :] == pair[:, None]).astype(jnp.float32)
        grad_logits = jnp.sum(grad_chosen[:, :, None] * select[None], 1)
        routed_float = routed.astype(jnp.float32)
        grad_route = jnp.dot(routed_float.T, grad_logits, precision=HIGH)
        grad_routed = jnp.dot(grad_logits, route_float.T, precision=HIGH)
        grad_eout = (gates.T[:, :, None] * grad_float[None]).astype(jnp.bfloat16)
        slot = ()
        weights_in, weights_out = joined(
            lax.all_to_all(
                lax.all_to_all(
                    shortened(slabs(need)), "gx", split_axis=1, concat_axis=1, tiled=True
                ),
                "gy",
                split_axis=2,
                concat_axis=2,
                tiled=True,
            )
        )
        grad_act = jnp.einsum(
            "kld,kfd->klf", grad_eout, weights_out, preferred_element_type=jnp.float32
        )
        unused_act, gelu_back = jax.vjp(jax.nn.gelu, hidden_pre)
        grad_pre = gelu_back(grad_act)[0].astype(jnp.bfloat16)
        grad_in = jnp.einsum("ld,klf->kdf", routed, grad_pre, preferred_element_type=jnp.float32)
        grad_out = jnp.einsum(
            "klf,kld->kfd", hidden_low, grad_eout, preferred_element_type=jnp.float32
        )
        grad_routed = grad_routed + jnp.einsum(
            "klf,kdf->ld", grad_pre, weights_in, preferred_element_type=jnp.float32
        )
        slot = (grad_in, grad_out)
        unused_two, norm_two_back = jax.vjp(layer_norm, middle, gain_two, bias_two)
        grad_mid_norm, grad_gain_two, grad_bias_two = norm_two_back(grad_routed)
        grad_middle = grad_float + grad_mid_norm
        grad_attended = grad_middle.astype(jnp.bfloat16)
        grad_attn_w = contract_rows(heads_out, grad_attended)
        grad_heads = (
            contract_cols(grad_attended, attn_full)
            .astype(jnp.bfloat16)
            .reshape(length, HEADS, head_size)
        )
        masked = attention_probs(project, segment)
        probs_float = jnp.exp(masked - log_total)
        probs_low = probs_float.astype(jnp.bfloat16)
        queries = project[:, :width].reshape(length, HEADS, head_size)
        keys_all = project[:, width : 2 * width].reshape(length, HEADS, head_size)
        values_all = project[:, 2 * width :].reshape(length, HEADS, head_size)
        grad_values = jnp.einsum(
            "hqk,qhd->khd", probs_low, grad_heads, preferred_element_type=jnp.float32
        )
        grad_probs = jnp.einsum(
            "qhd,khd->hqk", grad_heads, values_all, preferred_element_type=jnp.float32
        )
        row_dot = jnp.sum(probs_float * grad_probs, -1, keepdims=True)
        grad_scores = (probs_float * (grad_probs - row_dot)).astype(jnp.bfloat16)
        grad_queries = (
            jnp.einsum("hqk,khd->qhd", grad_scores, keys_all, preferred_element_type=jnp.float32)
            * scale
        )
        grad_keys = (
            jnp.einsum("hqk,qhd->khd", grad_scores, queries, preferred_element_type=jnp.float32)
            * scale
        )
        grad_qkv = jnp.concatenate(
            [
                grad_queries.reshape(length, width),
                grad_keys.reshape(length, width),
                grad_values.reshape(length, width),
            ],
            -1,
        ).astype(jnp.bfloat16)
        grad_qkv_w = contract_rows(normed, grad_qkv)
        grad_normed = contract_cols(grad_qkv, qkv_full)
        unused_one, norm_one_back = jax.vjp(
            layer_norm, block.astype(jnp.float32), gain_one, bias_one
        )
        grad_in_norm, grad_gain_one, grad_bias_one = norm_one_back(grad_normed)
        grad_tokens = (grad_middle + grad_in_norm).astype(jnp.bfloat16)
        terms = (
            grad_qkv_w,
            grad_attn_w,
            grad_route,
            grad_gain_one,
            grad_bias_one,
            grad_gain_two,
            grad_bias_two,
        )
        dense_acc = tuple((total + term for total, term in zip(dense_acc, terms)))
        return ((dense_acc, shard_in, shard_out, holding), (grad_tokens, slot))

    dense_zero = (
        jnp.zeros((width, 3 * width), jnp.float32),
        jnp.zeros((width, width), jnp.float32),
        jnp.zeros((width, experts), jnp.float32),
        jnp.zeros((width,), jnp.float32),
        jnp.zeros((width,), jnp.float32),
        jnp.zeros((width,), jnp.float32),
        jnp.zeros((width,), jnp.float32),
    )
    shard_zero_in = jnp.zeros((experts, slab_in, hidden), jnp.float32)
    shard_zero_out = jnp.zeros((experts, slab_out, width), jnp.float32)
    holding_zero = ()
    (dense_acc, shard_in, shard_out, holding), (grad_tokens_all, slots) = lax.scan(
        backward_step,
        (dense_zero, shard_zero_in, shard_zero_out, holding_zero),
        (tokens, cotangent, segment_ids, needs, own_pairs, kept_all),
    )
    slot_in = slots[0].reshape(micro * 2, width, hidden)
    slot_out = slots[1].reshape(micro * 2, hidden, width)
    amount = slot_in.shape[0]
    returned = lax.all_to_all(
        lax.all_to_all(
            shortened(
                (
                    slot_in.reshape(amount, outer, inner, slab_in, hidden),
                    slot_out.reshape(amount, outer, inner, slab_out, width),
                )
            ),
            "gx",
            split_axis=1,
            concat_axis=1,
            tiled=True,
        ),
        "gy",
        split_axis=2,
        concat_axis=2,
        tiled=True,
    )
    onehot = (
        needs.reshape(micro * 2, outer, inner)[None] == expert_ids[:, None, None, None]
    ).astype(jnp.float32)
    added = tuple(
        (jnp.einsum("esab,sabrc->erc", onehot, piece, precision=HIGH) for piece in returned)
    )
    shard_in = shard_in + added[0]
    shard_out = shard_out + added[1]
    dense_shards = (
        lax.psum_scatter(dense_acc[0], ("gx", "gy"), scatter_dimension=0, tiled=True),
        lax.psum_scatter(dense_acc[1], ("gx", "gy"), scatter_dimension=0, tiled=True),
        lax.psum_scatter(dense_acc[2], ("gx", "gy"), scatter_dimension=0, tiled=True),
        lax.psum_scatter(dense_acc[3], ("gx", "gy"), scatter_dimension=0, tiled=True),
        lax.psum_scatter(dense_acc[4], ("gx", "gy"), scatter_dimension=0, tiled=True),
        lax.psum_scatter(dense_acc[5], ("gx", "gy"), scatter_dimension=0, tiled=True),
        lax.psum_scatter(dense_acc[6], ("gx", "gy"), scatter_dimension=0, tiled=True),
    )
    return (
        mixed_all,
        grad_tokens_all,
        dense_shards[0],
        dense_shards[1],
        dense_shards[2],
        shard_in,
        shard_out,
        dense_shards[3],
        dense_shards[4],
        dense_shards[5],
        dense_shards[6],
    )


MESH = pl.DeviceIdType.MESH
ROWS = 224
SIDE = 128
ROOT2PI = math.sqrt(2.0 / math.pi)


(
    DOWN, DPLANE, DCORNER, DLAST, DWAIT, ATT, WIN, WO, WINWAIT, WSIBWAIT, WAVE, COWN,
    CPLANE, CCORNER, RPLANE, RCORNER, GFIRST, MFIRST, GHELP, MHELP, GPLANE, MPLANE, PAIR, ADDPAIR, DENSE,
) = range(25)

FRONT_STEPS = (
    (WIN, 2, 1), (COWN, 0), (DOWN,), (WO,), (WIN, 2, 0), (WIN, 3, 1), (COWN, 1), (DPLANE, 2), (WIN, 3, 2),
    (DPLANE, 3), (WIN, 1, 3), (DCORNER, 2), (DCORNER, 0), (DPLANE, 1), (CPLANE, 1, 1), (WIN, 2, 2),
    (WIN, 1, 2), (DLAST, 2), (DCORNER, 1), (CPLANE, 1, 0), (DCORNER, 3), (WIN, 1, 1), (CPLANE, 2, 1),
    (CCORNER, 1, 0), (DLAST, 1), (DLAST, 3), (CPLANE, 2, 0), (DLAST, 0), (CPLANE, 3, 1), (WIN, 0, 1),
    (DWAIT,), (ATT, 0), (WIN, 0, 3), (ATT, 1), (RPLANE, 1, 0), (WIN, 2, 3), (WIN, 1, 0), (WIN, 0, 2),
    (CCORNER, 0, 0), (WIN, 3, 3), (WIN, 3, 0), (RPLANE, 1, 1), (RPLANE, 2, 0), (CCORNER, 2, 0),
    (CCORNER, 2, 1), (WINWAIT,), (CCORNER, 0, 1), (RCORNER, 0, 1), (RCORNER, 1, 0), (WSIBWAIT,),
    (CCORNER, 1, 1), (RCORNER, 0, 0), (WAVE, 0, 1), (RCORNER, 2, 0), (RCORNER, 1, 1), (CPLANE, 3, 0),
    (WAVE, 1, 0), (RPLANE, 2, 1), (RPLANE, 3, 0), (CCORNER, 3, 0), (WAVE, 1, 1), (RPLANE, 3, 1), (WAVE, 2, 0),
    (RCORNER, 3, 0), (RCORNER, 2, 1), (WAVE, 0, 0), (CCORNER, 3, 1), (WAVE, 2, 1), (RCORNER, 3, 1),
    (WAVE, 3, 0), (WAVE, 3, 1),
)
TAIL_STEPS = (
    (GFIRST, 0, 0), (GFIRST, 0, 1), (GHELP, 0, 0), (PAIR,), (GFIRST, 1, 0), (GHELP, 1, 0), (GFIRST, 2, 1),
    (ADDPAIR,), (GHELP, 0, 1), (WIN, 0, 2), (GPLANE, 1, 0), (GFIRST, 2, 0), (GPLANE, 0, 0), (GFIRST, 1, 1),
    (MFIRST, 0, 0), (WIN, 0, 1), (WIN, 2, 0), (MHELP, 0, 0), (GHELP, 2, 0), (WIN, 3, 1), (WIN, 0, 0),
    (GHELP, 1, 1), (WIN, 1, 1), (GHELP, 2, 1), (GPLANE, 0, 1), (MFIRST, 0, 1), (GFIRST, 3, 0), (WIN, 3, 0),
    (WIN, 2, 1), (GPLANE, 2, 0), (GPLANE, 1, 1), (GPLANE, 2, 1), (GFIRST, 3, 1), (GHELP, 3, 0), (MHELP, 0, 1),
    (MFIRST, 1, 0), (WIN, 3, 2), (WIN, 2, 2), (WIN, 1, 2), (GHELP, 3, 1), (MHELP, 1, 0), (MPLANE, 0, 0),
    (GPLANE, 3, 0), (MFIRST, 1, 1), (GPLANE, 3, 1), (MFIRST, 2, 1), (MFIRST, 2, 0), (ATT, 0), (MHELP, 1, 1),
    (ATT, 1), (ATT, 2), (ATT, 3), (ATT, 4), (MFIRST, 3, 0), (MHELP, 2, 0), (MPLANE, 1, 0), (MPLANE, 1, 1),
    (MPLANE, 0, 1), (WIN, 1, 0), (MFIRST, 3, 1), (ATT, 5), (MHELP, 2, 1), (DENSE,), (MPLANE, 2, 0),
    (MHELP, 3, 0), (MHELP, 3, 1), (WIN, 3, 3), (MPLANE, 2, 1), (WIN, 1, 3), (WIN, 2, 3), (MPLANE, 3, 0),
    (MPLANE, 3, 1),
)


def dot(left, right):
    return jnp.dot(left, right, preferred_element_type=jnp.float32)


class Place:
    def __init__(self):
        self.z = lax.axis_index("gx")
        g = lax.axis_index("gy")
        self.core = g % 2
        across_x = g + 2 - 4 * ((g // 2) % 2)
        across_y = g + 4 - 8 * (g // 4)
        across_both = across_x + 4 - 8 * (across_x // 4)
        self.at = (g, across_x, across_y, across_both)
        self.step_x, self.step_y = across_x - g, across_y - g
        self.sibling = (self.z, g + 1 - 2 * self.core)

    def plane(self, k):
        return (self.z + k) % 4

    def nearest(self, j):
        z = self.z
        return (0, 1 + 2 * (z // 2), 2 + z - 3 * (z // 2), 3 - z + z // 2)[j]

    def device(self, rel, k):
        return (self.plane(k), self.at[rel])

    def chip(self, rel, k):
        return self.plane(k) * 4 + self.at[rel] // 2

    def index(self, rel, k):
        return self.plane(k) * 8 + self.at[rel]

    def pair(self, pack_task, task_experts, rel, k, p):
        at = self.at[0] + self.step_x * (rel % 2) + self.step_y * (rel // 2)
        task = pack_task[(self.plane(k) * 8 + at) * 2 + p]
        return task_experts[task, 0], task_experts[task, 1]

    def greet(self):
        barrier = pltpu.get_barrier_semaphore()
        others = [(rel, k) for rel in range(4) for k in range(4) if (rel, k) != (0, 0)]
        for rel, k in others:
            pl.semaphore_signal(
                barrier, inc=1, device_id=self.device(rel, k), device_id_type=MESH
            )
        pl.semaphore_signal(barrier, inc=1, device_id=self.sibling, device_id_type=MESH)
        pl.semaphore_wait(barrier, len(others) + 1)


def send(started, src, dst, send_sem, recv_sem, device):
    copy = pltpu.make_async_remote_copy(
        src_ref=src,
        dst_ref=dst,
        send_sem=send_sem,
        recv_sem=recv_sem,
        device_id=device,
        device_id_type=MESH,
    )
    copy.start()
    started.append(copy)


def arrived(ref, sem):
    pltpu.make_async_copy(ref, ref, sem).wait()


def back(k):
    return (4 - k) % 4


class Spread:
    def __init__(self, place, here, there, packs, half, chained, sems):
        self.place, self.here, self.there = place, here, there
        self.packs, self.half, self.chained, self.started = packs, half, chained, []
        self.send_sem, self.recv_sem = sems

    def go(self, kind, at_send, k_there, rel, k, p, src, rel_there, device, only_if=None):
        copy = pltpu.make_async_remote_copy(
            src_ref=src,
            dst_ref=self.there(rel_there, k_there, p, rel, k),
            send_sem=self.send_sem.at[kind, at_send * self.packs + p],
            recv_sem=self.recv_sem.at[kind % 4, k_there * self.packs + p],
            device_id=device,
            device_id_type=MESH,
        )
        if only_if is None:
            copy.start()
        else:
            pl.when(only_if)(copy.start)
        self.started.append((copy, only_if))

    def wait(self, kind, rel, k, p):
        arrived(self.here(rel, k, p), self.recv_sem.at[kind, k * self.packs + p])

    def own(self, p, src):
        place = self.place
        if self.chained:
            self.go(0, 0, 3, 0, 0, p, src, 0, place.device(0, 1), place.z < 3)
            self.go(4, 0, 1, 0, 0, p, src, 0, place.device(0, 3), place.z > 0)
        else:
            for k in (1, 2, 3):
                self.go(0, k, back(k), 0, 0, p, src, 0, place.device(0, k))
        self.go(1, 0, 0, 0, 0, p, src, 1, place.device(1, 0))
        self.go(2, 0, 0, 0, 0, p, src, 2, place.device(2, 0))

    def plane(self, j, p):
        place = self.place
        k = place.nearest(j)
        self.wait(0, 0, k, p)
        src = self.here(0, k, p)
        if self.chained:
            step = 2 * ((place.z - place.plane(k) + 3) // 4) - 1
            goes = (place.z + step >= 0) & (place.z + step <= 3)
            on = (place.plane(step + 4), place.at[0])
            self.go(0, k, (k - step + 4) % 4, 0, k, p, src, 0, on, goes)
        self.go(1, k, k, 0, k, p, src, 1, place.device(1, 0))
        self.go(2, k, k, 0, k, p, src, 2, place.device(2, 0))

    def corner(self, j, p):
        k = self.place.nearest(j)
        rel = 1 + self.half(j, p)
        self.wait(rel, rel, k, p)
        self.go(3, k, k, rel, k, p, self.here(rel, k, p), 3, self.place.device(3 - rel, 0))

    def last(self, j, p):
        k = self.place.nearest(j)
        rel = 2 - self.half(j, p)
        self.wait(rel, rel, k, p)
        self.wait(3, 3, k, p)

    def finish(self):
        for copy, only_if in self.started:
            if only_if is None:
                copy.wait_send()
            else:
                pl.when(only_if)(copy.wait_send)


def norm_parts(values):
    center = values - jnp.mean(values, -1, keepdims=True)
    spread = jnp.mean(center * center, -1, keepdims=True)
    rise = lax.rsqrt(spread + EPS)
    return center * rise, rise


def real_rows():
    return lax.broadcasted_iota(jnp.int32, (ROWS, 1), 0) < PACK


def head_lanes(h):
    lane = lax.broadcasted_iota(jnp.int32, (1, SIDE), 1)
    inside = (lane >= h * HEAD) & (lane < (h + 1) * HEAD)
    return inside.astype(jnp.bfloat16)


def softmax_rows(queries, keys, same):
    scores = contract_cols(queries, keys) * (1.0 / math.sqrt(HEAD))
    scores = jnp.where(same, scores, MASK_FILL)
    raised = jnp.exp(scores - jnp.max(scores, -1, keepdims=True))
    return raised * (1.0 / jnp.sum(raised, -1, keepdims=True))


def pick(logits, expert):
    lane = lax.broadcasted_iota(jnp.int32, logits.shape, 1)
    return jnp.sum(jnp.where(lane == expert, logits, 0.0), -1, keepdims=True)


def two_gates(logits, first, second):
    gap = pick(logits, second) - pick(logits, first)
    return 1.0 / (1.0 + jnp.exp(gap)), 1.0 / (1.0 + jnp.exp(-gap))


def lengthened(ref, p):
    rows = ref[p].astype(jnp.float32)
    return jnp.concatenate([rows, jnp.zeros((ROWS - PACK, rows.shape[1]), jnp.float32)], axis=0)


def same_documents(segments, flat_ids, tall_ids):
    flat_ids[...] = jnp.full(flat_ids.shape, -1.0, jnp.float32)
    flat_ids[: segments.shape[0], :PACK] = segments[...].astype(jnp.float32)
    tall_ids[...] = jnp.transpose(flat_ids[...])


def same_document(flat_ids, tall_ids, p):
    return tall_ids[:ROWS, p : p + 1] == flat_ids[p : p + 1, :ROWS]


def front_kernel(
    pack_task, task_experts, tok, segments, w_qkv_own, w_attn_own, route_own,
    gain_one_own, bias_one_own, gain_two_own, bias_two_own, cot_own, w_in, w_out,
    in_terms, out_terms, mixed_out, grad_out, dense_out, proj, heads, middle,
    dense, routed_all, cot_all, w_in_all, w_out_all, in_stage, out_stage, mixed_all, grad_all,
    turned, square, flat_ids, tall_ids, gate_row,
    cot_send, cot_recv, routed_send, routed_recv, dense_send, dense_recv,
    core_send, core_recv, in_send, in_recv, pair_send, pair_recv, local_sem, out_sem,
):
    place = Place()
    width, experts = tok.shape[2], route_own.shape[1]
    other = 1 - place.core

    def block_here(ref):
        return lambda rel, k, p: ref.at[rel, k * 2 + p]

    def block_there(ref):
        return lambda rel_there, k_there, p, rel, k: ref.at[rel_there, k_there * 2 + p]

    own = place.index(0, 0)
    dense[own, :, : 3 * width] = w_qkv_own[...]
    dense[own, :, 3 * width : 4 * width] = w_attn_own[...]
    square[...] = jnp.zeros_like(square)
    for i, ref in enumerate((gain_one_own, bias_one_own, gain_two_own, bias_two_own)):
        square[GAIN_ONE + i : GAIN_ONE + i + 1, : ref.shape[0]] = (
            ref[...].astype(jnp.float32).reshape(1, ref.shape[0])
        )
    columns = jnp.transpose(square[...])[: gain_one_own.shape[0]]
    square[: gain_one_own.shape[0], :] = columns
    square[: gain_one_own.shape[0], :experts] = route_own[...].astype(jnp.float32)
    dense[own, :, 4 * width :] = square[: gain_one_own.shape[0], :].astype(jnp.bfloat16)
    for p in range(2):
        cot_all[0, p] = lengthened(cot_own, p).astype(jnp.bfloat16)
    place.greet()

    dense_tree = Spread(
        place,
        lambda rel, k, p: dense.at[place.index(rel, k)],
        lambda rel_there, k_there, p, rel, k: dense.at[place.index(rel, k)],
        1,
        lambda j, p: j % 2,
        False,
        (dense_send, dense_recv),
    )
    core_started, in_started, pair_started, local, outs = [], [], [], [], []

    def to_core(rel, k):
        slot = dense.at[place.index(rel, k)]
        send(
            core_started, slot, slot, core_send.at[rel, k], core_recv.at[rel, k], place.sibling
        )

    def tree(ref, sems):
        return Spread(place, block_here(ref), block_there(ref), 2, lambda j, p: p, True, sems)

    cot_tree = tree(cot_all, (cot_send, cot_recv))
    routed_tree = tree(routed_all, (routed_send, routed_recv))

    def local_copy(src, dst):
        copy = pltpu.make_async_copy(src, dst, local_sem.at[len(local)])
        copy.start()
        local.append(copy)

    def down():
        dense_tree.own(0, dense.at[own])
        to_core(0, 0)
        local_copy(w_in.at[:, :, pl.ds(pl.multiple_of(place.chip(0, 0) * SIDE, SIDE), SIDE)],
                   w_in_all.at[place.chip(0, 0), place.core])
        same_documents(segments, flat_ids, tall_ids)
        gate_row[...] = jnp.zeros_like(gate_row)

    def dplane(j):
        dense_tree.plane(j, 0)
        to_core(0, place.nearest(j))

    def dcorner(j):
        k = place.nearest(j)
        dense_tree.corner(j, 0)
        other_side = 2 - j % 2
        dense_tree.wait(other_side, other_side, k, 0)
        to_core(1, k)
        to_core(2, k)

    def dlast(j):
        k = place.nearest(j)
        dense_tree.wait(3, 3, k, 0)
        to_core(3, k)

    def dwait():
        for k in range(4):
            for rel in range(4):
                slot = dense.at[place.plane(k) * 8 + place.at[rel] + 1 - 2 * place.core]
                arrived(slot, core_recv.at[rel, k])
        local_copy(dense, dense_out)
        small = dense[:, :, 4 * width : 4 * width + SIDE].reshape(width, SIDE)
        turned[...] = jnp.transpose(small.astype(jnp.float32))

    def att(p):
        row = [turned[GAIN_ONE + i : GAIN_ONE + i + 1, :] for i in range(4)]
        block = lengthened(tok, p)
        unit, unused = norm_parts(block)
        normed = (unit * row[0] + row[1]).astype(jnp.bfloat16)
        w_qkv = dense[:, :, : 3 * width].reshape(width, 3 * width)
        proj[p] = dot(normed, w_qkv).astype(jnp.bfloat16)
        same = same_document(flat_ids, tall_ids, p)

        def pair_of_heads(j, carry):
            at = pl.multiple_of(j * SIDE, SIDE)
            queries = proj[p, :, pl.ds(at, SIDE)]
            keys = proj[p, :, pl.ds(at + width, SIDE)]
            values = proj[p, :, pl.ds(at + 2 * width, SIDE)]
            out = jnp.zeros((ROWS, SIDE), jnp.float32)
            for h in range(2):
                lanes = head_lanes(h)
                probs = softmax_rows(queries * lanes, keys, same).astype(jnp.bfloat16)
                out = out + dot(probs, values * lanes)
            heads[p, :, pl.ds(at, SIDE)] = out.astype(jnp.bfloat16)
            return carry

        lax.fori_loop(0, width // SIDE, pair_of_heads, 0)
        w_attn = dense[:, :, 3 * width : 4 * width].reshape(width, width)
        mid = block + dot(heads[p], w_attn)
        middle[p] = mid
        unit, unused = norm_parts(mid)
        routed_all[0, p] = jnp.where(real_rows(), unit * row[2] + row[3], 0.0).astype(jnp.bfloat16)
        routed_tree.own(p, routed_all.at[0, p])

    def win(rel, j):
        k = place.nearest(j)
        columns = pl.ds(pl.multiple_of(place.chip(rel, k) * SIDE, SIDE), SIDE)
        send(
            in_started, w_in.at[:, :, columns], w_in_all.at[place.chip(0, 0), place.core],
            in_send.at[rel, k], in_recv.at[rel, (4 - k) % 4], place.device(rel, k),
        )

    def wo():
        local_copy(w_out, w_out_all.at[place.core])
        send(
            pair_started, w_out, w_out_all.at[place.core], pair_send.at[0], pair_recv.at[0],
            place.sibling,
        )

    def winwait():
        for rel in range(4):
            for k in range(4):
                if (rel, k) != (0, 0):
                    arrived(w_in_all.at[place.chip(rel, k), place.core], in_recv.at[rel, k])
        local[0].wait()
        mine = w_in_all.at[:, place.core]
        send(pair_started, mine, mine, pair_send.at[1], pair_recv.at[1], place.sibling)

    def wsibwait():
        for copy in local[1:]:
            copy.wait()
        arrived(w_out_all.at[other], pair_recv.at[0])
        arrived(w_in_all.at[:, other], pair_recv.at[1])

    def put(src, dst):
        copy = pltpu.make_async_copy(src, dst, out_sem.at[len(outs)])
        copy.start()
        outs.append(copy)

    def wave(j, p):
        at = place.nearest(j) * 2 + p
        cot_tree.last(j, p)
        routed_tree.last(j, p)
        count = len(outs) // 4
        stage = count % 2
        if count >= 2:
            outs[4 * count - 8].wait()
            outs[4 * count - 7].wait()

        def one_block(rel, carry):
            pair = place.pair(pack_task, task_experts, rel, place.nearest(j), p)
            rows, cots = routed_all[rel, at], cot_all[rel, at]
            gated, grad_pre, mixed, grad = expert_block(
                pair, rows, cots, w_in_all, w_out_all, dense, gate_row
            )
            mixed_all[rel, at] = mixed
            grad_all[rel, at] = grad
            in_stage[stage, rel] = contract_rows(rows, grad_pre).astype(jnp.bfloat16)
            out_stage[stage, rel] = contract_rows(gated, cots).astype(jnp.bfloat16)
            return carry

        lax.fori_loop(0, 4, one_block, 0)
        put(in_stage.at[stage], in_terms.at[:, at])
        put(out_stage.at[stage], out_terms.at[:, at])
        put(grad_all.at[:, at], grad_out.at[:, at])
        put(mixed_all.at[:, at], mixed_out.at[:, at])

    steps = {
        DOWN: down, DPLANE: dplane, DCORNER: dcorner, DLAST: dlast, DWAIT: dwait,
        ATT: att, WIN: win, WO: wo, WINWAIT: winwait, WSIBWAIT: wsibwait, WAVE: wave,
        COWN: lambda p: cot_tree.own(p, cot_all.at[0, p]),
        CPLANE: cot_tree.plane, CCORNER: cot_tree.corner,
        RPLANE: routed_tree.plane, RCORNER: routed_tree.corner,
    }
    for name, *where in FRONT_STEPS:
        steps[name](*where)
    for i, copy in enumerate(outs):
        if i % 4 >= 2 or i >= len(outs) - 8:
            copy.wait()
    for each in (dense_tree, cot_tree, routed_tree):
        each.finish()
    for copy in core_started + in_started + pair_started:
        copy.wait_send()


def expert_block(pair, rows, cots, w_in_all, w_out_all, dense, gate_row):
    width, slab = rows.shape[1], 2 * SIDE
    first, second = pair
    w_in = jnp.concatenate([w_in_all[:, :, e].reshape(width, SIDE) for e in pair], axis=1)
    w_out = jnp.concatenate([w_out_all[:, e].reshape(SIDE, width) for e in pair], axis=0)
    route = dense[:, :, 4 * width : 4 * width + SIDE].reshape(width, SIDE)
    gate_a, gate_b = two_gates(dot(rows, route), first, second)
    lane = lax.broadcasted_iota(jnp.int32, (1, slab), 1)
    gates = jnp.where(lane < SIDE, gate_a, gate_b)
    hidden = dot(rows, w_in)
    back_act = contract_cols(cots, w_out)
    square = hidden * hidden
    bend = jnp.tanh(ROOT2PI * hidden * (1.0 + 0.044715 * square))
    half = 0.5 * (1.0 + bend)
    act = (hidden * half).astype(jnp.bfloat16).astype(jnp.float32)
    slope = half + 0.5 * hidden * (1.0 - bend * bend) * (ROOT2PI * (1.0 + 0.134145 * square))
    gated = (gates * act).astype(jnp.bfloat16)
    grad_pre = (gates * back_act * slope).astype(jnp.bfloat16)
    product = (act * back_act).astype(jnp.bfloat16)
    signs = jnp.broadcast_to(jnp.where(lane < SIDE, 1.0, -1.0), (8, slab)).astype(jnp.bfloat16)
    gate_row[:, :ROWS] = contract_cols(signs, product)
    mixed = dot(gated, w_out).astype(jnp.bfloat16)
    grads = contract_cols(grad_pre, w_in)
    grad = jnp.concatenate([grads[:PACK], gate_row[...]], axis=0).astype(jnp.bfloat16)
    return gated, grad_pre, mixed, grad


def sum_kernel(
    pack_task, task_experts, where, in_terms, out_terms, d_in, d_out_own, d_out_far, heads, nexts,
    total_in, total_out,
):
    group = d_out_own.shape[0]
    experts = group * pl.num_programs(0)
    slots = in_terms.shape[0] * in_terms.shape[1]

    @pl.when(pl.program_id(0) == 0)
    def list_uses():
        def clear(e, carry):
            heads[e] = -1
            return carry

        lax.fori_loop(0, experts, clear, 0)
        g = where[1]
        step_x, step_y = 2 - 4 * ((g // 2) % 2), 4 - 8 * (g // 4)

        def one(slot, carry):
            rel, k, p = slot // 8, (slot // 2) % 4, slot % 2
            at = g + step_x * (rel % 2) + step_y * (rel // 2)
            task = pack_task[(((where[0] + k) % 4) * 8 + at) * 2 + p]
            for i in range(2):
                e = task_experts[task, i]
                nexts[slot * 2 + i] = heads[e]
                heads[e] = slot * 2 + i
            return carry

        lax.fori_loop(0, slots, one, 0)

    def terms(use):
        slot = use // 2
        rel, at, half = slot // 8, slot % 8, pl.multiple_of((use % 2) * SIDE, SIDE)
        return (
            in_terms[rel, at, :, pl.ds(half, SIDE)].astype(jnp.float32),
            out_terms[rel, at, pl.ds(half, SIDE), :].astype(jnp.float32),
        )

    def add_terms(use):
        new_in, new_out = terms(use)
        total_in[...] += new_in
        total_out[...] += new_out
        return nexts[use]

    own = pl.ds(pl.multiple_of(where[2] * HEAD, HEAD), HEAD)
    far = pl.ds(pl.multiple_of((1 - where[2]) * HEAD, HEAD), HEAD)

    def one_expert(i, carry):
        head = heads[pl.program_id(0) * group + i]

        @pl.when(head < 0)
        def unused():
            total_in[...] = jnp.zeros_like(total_in)
            total_out[...] = jnp.zeros_like(total_out)

        @pl.when(head >= 0)
        def used():
            total_in[...], total_out[...] = terms(head)
            lax.while_loop(lambda use: use >= 0, add_terms, nexts[head])

        low = total_in[...].astype(jnp.bfloat16).reshape(16, 2, 16, SIDE)
        d_in[0, :, i] = low[:, 0]
        d_in[1, :, i] = low[:, 1]
        d_out_own[i] = total_out[own, :]
        d_out_far[i] = total_out[far, :].astype(jnp.bfloat16)
        return carry

    lax.fori_loop(0, group, one_expert, 0)


class Collect:
    def __init__(self, place, part, corner, from_x, from_y, from_z, packs, half, sems):
        self.place, self.part = place, part
        self.corner, self.from_x, self.from_y, self.from_z = corner, from_x, from_y, from_z
        self.packs, self.half, self.started = packs, half, []
        self.send_sem, self.recv_sem = sems

    def go(self, kind, src, dst, at_send, at_recv, device):
        send(
            self.started, src, dst, self.send_sem.at[kind, at_send],
            self.recv_sem.at[kind, at_recv], device,
        )

    def opposite(self, k, p):
        at = k * self.packs + p
        towards = 2 if self.half(k, p) == 0 else 1
        self.go(3, self.part(3, k, p), self.corner.at[at], at, at, self.place.device(towards, 0))

    def straight(self, k, p):
        at = k * self.packs + p
        if self.half(k, p) == 0:
            self.go(2, self.part(2, k, p), self.from_y.at[at], at, at, self.place.device(2, 0))
        else:
            self.go(1, self.part(1, k, p), self.from_x.at[at], at, at, self.place.device(1, 0))

    def helped(self, k, p, mine):
        at = k * self.packs + p
        ref = self.corner.at[at]
        arrived(ref, self.recv_sem.at[3, at])
        total = ref[...].astype(jnp.float32) + mine().astype(jnp.float32)
        ref[...] = total.astype(jnp.bfloat16)
        if self.half(k, p) == 0:
            self.go(1, ref, self.from_x.at[at], at, at, self.place.device(1, 0))
        else:
            self.go(2, ref, self.from_y.at[at], at, at, self.place.device(2, 0))

    def plane(self, k, p, mine):
        at = k * self.packs + p
        arrived(self.from_x.at[at], self.recv_sem.at[1, at])
        arrived(self.from_y.at[at], self.recv_sem.at[2, at])
        total = self.from_x[at].astype(jnp.float32) + self.from_y[at].astype(jnp.float32)
        total = total + mine().astype(jnp.float32)
        if k:
            self.from_x[at] = total.astype(jnp.bfloat16)
            there = back(k) * self.packs + p
            self.go(
                0, self.from_x.at[at], self.from_z.at[there], at, there, self.place.device(0, k)
            )
            return None
        for other in (1, 2, 3):
            at = other * self.packs + p
            arrived(self.from_z.at[at], self.recv_sem.at[0, at])
            total = total + self.from_z[at].astype(jnp.float32)
        return total

    def finish(self):
        for copy in self.started:
            copy.wait_send()


def tail_kernel(
    pack_task, task_experts, tok, cot, segments, proj, heads, middle, dense, grad_part, mixed_part,
    d_in, d_out_far,
    mixed, d_tok, d_dense, d_in_all, d_out_all,
    g_own, g_corner, g_x, g_y, g_z, m_own, m_corner, m_x, m_y, m_z,
    total_grad, grad_mid, grad_heads, grad_qkv, acc, small_rows, turned, flat_ids, tall_ids,
    in_far, in_mine, far_dense, got_dense, part_dense, s_corner, s_x, s_y, s_z,
    g_send, g_recv, m_send, m_recv, s_send, s_recv, in_send, in_recv,
    pair_send, pair_recv, load_sem,
):
    place = Place()
    width = tok.shape[2]
    place.greet()

    def by_pack(k, p):
        return p

    def part_of(ref):
        return lambda rel, k, p: ref.at[rel, k * 2 + p]

    grads = Collect(
        place, part_of(grad_part), g_corner, g_x, g_y, g_z, 2, by_pack, (g_send, g_recv)
    )
    mixes = Collect(
        place, part_of(mixed_part), m_corner, m_x, m_y, m_z, 2, by_pack, (m_send, m_recv)
    )
    planes = (2, 1, 3, 0)
    order = [(k, p) for k in planes for p in range(2)]
    loads = []

    def load(src, dst):
        copy = pltpu.make_async_copy(src, dst, load_sem.at[len(loads)])
        copy.start()
        loads.append(copy)
        return copy

    def load_parts(ref, own):
        waits = {}
        for k, p in order:
            at = k * 2 + p
            waits["helped", k, p] = load(ref.at[1 + p, at], own.at[1, at])
        for k, p in order:
            at = k * 2 + p
            waits["plane", k, p] = load(ref.at[0, at], own.at[0, at])
        return waits

    g_waits = load_parts(grad_part, g_own)
    in_load = load(d_in.at[place.core], in_mine)
    m_waits = load_parts(mixed_part, m_own)
    pair_started, in_started, kept = [], [], {}

    def mine(waits, own, kind, k, p):
        def get():
            waits[kind, k, p].wait()
            return own[0 if kind == "plane" else 1, k * 2 + p]

        return get

    same_documents(segments, flat_ids, tall_ids)
    small = dense[:, :, 4 * width : 4 * width + SIDE].reshape(width, SIDE)
    turned[...] = jnp.transpose(small.astype(jnp.float32))
    small_rows[...] = jnp.zeros_like(small_rows)
    gain_one, bias_one, gain_two, bias_two = (
        turned[GAIN_ONE + i : GAIN_ONE + i + 1, :] for i in range(4)
    )

    def pair():
        send(
            pair_started, d_in.at[1 - place.core], in_far, pair_send.at[0], pair_recv.at[0],
            place.sibling,
        )
        send(
            pair_started, d_out_far, d_out_all, pair_send.at[1], pair_recv.at[1], place.sibling
        )

    def addpair():
        in_load.wait()
        arrived(in_far, pair_recv.at[0])

        def one(i, carry):
            total = in_mine[i].astype(jnp.float32) + in_far[i].astype(jnp.float32)
            in_mine[i] = total.astype(jnp.bfloat16)
            return carry

        lax.fori_loop(0, in_mine.shape[0], one, 0)
        columns = pl.ds(pl.multiple_of(place.chip(0, 0) * SIDE, SIDE), SIDE)
        kept["local"] = load(in_mine.at[place.chip(0, 0)], d_in_all.at[:, :, columns])

    def win(rel, j):
        k = planes[j]
        columns = pl.ds(pl.multiple_of(place.chip(0, 0) * SIDE, SIDE), SIDE)
        send(
            in_started, in_mine.at[place.chip(rel, k)], d_in_all.at[:, :, columns],
            in_send.at[rel, k], in_recv.at[rel, back(k)], place.device(rel, k),
        )

    def plane_of(tree, waits, own_parts, keep):
        def run(j, p):
            got = tree.plane(planes[j], p, mine(waits, own_parts, "plane", planes[j], p))
            if got is not None:
                keep(p, got)

        return run

    def keep_grad(p, got):
        total_grad[p] = got

    def keep_mixed(p, got):
        mixed[p] = (middle[p] + got).astype(jnp.bfloat16)

    def add_to(p, columns, value):
        if p == 0:
            acc[:, columns] = value
        else:
            acc[:, columns] += value

    def add_row(at, value):
        small_rows[at : at + 1, :] += jnp.sum(value, 0, keepdims=True)

    def att(part):
        p = part // 3
        (att_routed, att_heads, att_normed)[part % 3](p)

    def att_routed(p):
        first, second = place.pair(pack_task, task_experts, 0, 0, p)
        got = total_grad[p]
        tall = jnp.concatenate(
            [got[PACK:, : 2 * SIDE], jnp.zeros((SIDE - 8, 2 * SIDE), jnp.float32)], axis=0
        )
        gap_grad = jnp.transpose(tall)[:ROWS, 0:1]
        got = jnp.where(real_rows(), got, 0.0)
        mid = middle[p]
        unit, rise = norm_parts(mid)
        routed = jnp.where(real_rows(), unit * gain_two + bias_two, 0.0).astype(jnp.bfloat16)
        route = dense[:, :, 4 * width : 4 * width + SIDE].reshape(width, SIDE)
        gate_a, gate_b = two_gates(dot(routed, route), first, second)
        grad_a = gate_a * gate_b * gap_grad
        lane = lax.broadcasted_iota(jnp.int32, (ROWS, SIDE), 1)
        grad_logits = jnp.where(lane == first, grad_a, jnp.where(lane == second, -grad_a, 0.0))
        grad_logits = jnp.where(real_rows(), grad_logits, 0.0).astype(jnp.bfloat16)
        add_to(p, pl.ds(4 * width, SIDE), contract_rows(routed, grad_logits))
        got = got + contract_cols(grad_logits, route)
        add_row(2, got * unit)
        add_row(3, got)
        u = got * gain_two
        grad_middle = lengthened(cot, p) + rise * (
            u - jnp.mean(u, -1, keepdims=True) - unit * jnp.mean(u * unit, -1, keepdims=True)
        )
        grad_mid[...] = grad_middle
        attended = grad_middle.astype(jnp.bfloat16)
        add_to(p, pl.ds(3 * width, width), contract_rows(heads[p], attended))
        w_attn = dense[:, :, 3 * width : 4 * width].reshape(width, width)
        grad_heads[...] = contract_cols(attended, w_attn).astype(jnp.bfloat16)

    def att_heads(p):
        same = same_document(flat_ids, tall_ids, p)

        def pair_of_heads(j, carry):
            at = pl.multiple_of(j * SIDE, SIDE)
            queries = proj[p, :, pl.ds(at, SIDE)]
            keys = proj[p, :, pl.ds(at + width, SIDE)]
            values = proj[p, :, pl.ds(at + 2 * width, SIDE)]
            out_grad = grad_heads[:, pl.ds(at, SIDE)]
            zero = jnp.zeros((ROWS, SIDE), jnp.float32)
            grad_q, grad_k, grad_v = zero, zero, zero
            for h in range(2):
                lanes = head_lanes(h)
                probs = softmax_rows(queries * lanes, keys, same)
                mine_grad = out_grad * lanes
                grad_v = grad_v + contract_rows(probs.astype(jnp.bfloat16), mine_grad)
                grad_probs = contract_cols(mine_grad, values)
                row_dot = jnp.sum(probs * grad_probs, -1, keepdims=True)
                grad_scores = (probs * (grad_probs - row_dot)).astype(jnp.bfloat16)
                grad_q = grad_q + dot(grad_scores, keys * lanes)
                grad_k = grad_k + contract_rows(grad_scores, queries * lanes)
            scale = 1.0 / math.sqrt(HEAD)
            grad_qkv[:, pl.ds(at, SIDE)] = (grad_q * scale).astype(jnp.bfloat16)
            grad_qkv[:, pl.ds(at + width, SIDE)] = (grad_k * scale).astype(jnp.bfloat16)
            grad_qkv[:, pl.ds(at + 2 * width, SIDE)] = grad_v.astype(jnp.bfloat16)
            return carry

        lax.fori_loop(0, width // SIDE, pair_of_heads, 0)

    def att_normed(p):
        unit, rise = norm_parts(lengthened(tok, p))
        normed = (unit * gain_one + bias_one).astype(jnp.bfloat16)
        add_to(p, pl.ds(0, 3 * width), contract_rows(normed, grad_qkv[...]))
        w_qkv = dense[:, :, : 3 * width].reshape(width, 3 * width)
        grad_normed = contract_cols(grad_qkv[...], w_qkv)
        add_row(0, grad_normed * unit)
        add_row(1, grad_normed)
        u = grad_normed * gain_one
        d_tok[p] = (
            grad_mid[...]
            + rise
            * (u - jnp.mean(u, -1, keepdims=True) - unit * jnp.mean(u * unit, -1, keepdims=True))
        ).astype(jnp.bfloat16)

    def dense_part(rel, k, p):
        return got_dense.at[place.chip(rel, k)]

    sums = Collect(
        place, dense_part, s_corner, s_x, s_y, s_z, 1, lambda k, p: k % 2, (s_send, s_recv)
    )
    def dense_step():
        tall = jnp.concatenate(
            [
                jnp.zeros((GAIN_ONE, width), jnp.float32),
                small_rows[...],
                jnp.zeros((SIDE - GAIN_ONE - 8, width), jnp.float32),
            ],
            axis=0,
        )
        acc[:, 4 * width :] += jnp.transpose(tall)
        columns_all = acc.shape[1]

        def cut(i, carry):
            own_rows = pl.ds(pl.multiple_of(i * 32 + place.core * 16, 16), 16)
            far_rows = pl.ds(pl.multiple_of(i * 32 + 16 - place.core * 16, 16), 16)
            far_dense[i] = acc[far_rows, :].astype(jnp.bfloat16)
            part_dense[i] = acc[own_rows, :]
            return carry

        lax.fori_loop(0, 16, cut, 0)
        send(
            pair_started, far_dense, got_dense, pair_send.at[2], pair_recv.at[2], place.sibling
        )
        arrived(got_dense, pair_recv.at[2])

        def join(i, carry):
            far_dense_sum = part_dense[i] + got_dense[i].astype(jnp.float32)
            got_dense[i] = far_dense_sum.astype(jnp.bfloat16)
            return carry

        lax.fori_loop(0, 16, join, 0)

        for k in (2, 1, 3, 0):
            sums.opposite(k, 0)
        for k in (2, 1, 3, 0):
            sums.straight(k, 0)
        for k in (2, 1, 3, 0):
            sums.helped(k, 0, lambda k=k: got_dense[place.chip(1 + k % 2, k)])
        for k in (2, 1, 3):
            sums.plane(k, 0, lambda k=k: got_dense[place.chip(0, k)])
        d_dense[...] = sums.plane(0, 0, lambda: got_dense[place.chip(0, 0)])

    steps = {
        GFIRST: lambda j, p: (grads.opposite(planes[j], p), grads.straight(planes[j], p)),
        MFIRST: lambda j, p: (mixes.opposite(planes[j], p), mixes.straight(planes[j], p)),
        GHELP: lambda j, p: grads.helped(
            planes[j], p, mine(g_waits, g_own, "helped", planes[j], p)
        ),
        MHELP: lambda j, p: mixes.helped(
            planes[j], p, mine(m_waits, m_own, "helped", planes[j], p)
        ),
        GPLANE: plane_of(grads, g_waits, g_own, keep_grad),
        MPLANE: plane_of(mixes, m_waits, m_own, keep_mixed),
        PAIR: pair, ADDPAIR: addpair, WIN: win, ATT: att, DENSE: dense_step,
    }
    for name, *where in TAIL_STEPS:
        steps[name](*where)

    for rel in range(4):
        for k in range(4):
            if (rel, k) != (0, 0):
                place_columns = pl.ds(pl.multiple_of(place.chip(rel, k) * SIDE, SIDE), SIDE)
                arrived(d_in_all.at[:, :, place_columns], in_recv.at[rel, k])
    kept["local"].wait()
    arrived(d_out_all, pair_recv.at[1])
    for tree in (grads, mixes, sums):
        tree.finish()
    for copy in pair_started + in_started:
        copy.wait_send()


def last_kernel(
    mixed_tall, d_tok_tall, d_dense, d_in_low, d_out_own, d_out_far,
    mixed, d_tok, d_qkv, d_attn, d_route, d_in, d_out, gain_one, bias_one, gain_two, bias_two,
):
    width, experts = mixed.shape[2], d_route.shape[1]

    @pl.when(pl.program_id(0) == 0)
    def small():
        for p in range(mixed.shape[0]):
            mixed[p] = mixed_tall[p, :PACK]
            d_tok[p] = d_tok_tall[p, :PACK]
        d_qkv[...] = d_dense[:, : 3 * width]
        d_attn[...] = d_dense[:, 3 * width : 4 * width]
        d_route[...] = d_dense[:, 4 * width : 4 * width + experts]
        rows = jnp.transpose(d_dense[:, 4 * width :])
        for i, ref in enumerate((gain_one, bias_one, gain_two, bias_two)):
            ref[...] = rows[GAIN_ONE + i]

    d_in[...] = d_in_low[...].astype(jnp.float32)
    d_out[...] = d_out_own[...] + d_out_far[...].astype(jnp.float32)


def shards_fast(
    tokens,
    segment_ids,
    pack_task,
    task_experts,
    w_qkv,
    w_attn_out,
    w_router,
    w_expert_in,
    w_expert_out,
    norm1_gain,
    norm1_bias,
    norm2_gain,
    norm2_bias,
    cotangent,
):
    packs, length, width = tokens.shape
    experts, slab_in, hidden = w_expert_in.shape
    slab_out = w_expert_out.shape[1]
    dense_width = 4 * width + SIDE
    any_space = pl.BlockSpec(memory_space=pl.ANY)
    vmem = pl.BlockSpec(memory_space=pltpu.VMEM)
    smem = pl.BlockSpec(memory_space=pltpu.SMEM)
    low, full = jnp.bfloat16, jnp.float32
    flat = jax.ShapeDtypeStruct
    dma = pltpu.SemaphoreType.DMA

    z, g = lax.axis_index("gx"), lax.axis_index("gy")
    where = jnp.stack([z, g, g % 2])

    blocks = flat((4, 4 * packs, ROWS, width), low)
    in_sums = flat((4, 4 * packs, width, 2 * SIDE), low)
    out_sums = flat((4, 4 * packs, 2 * SIDE, width), low)

    def held(shape):
        return pltpu.VMEM(shape.shape, shape.dtype)

    in_terms, out_terms, mixed_part, grad_part, dense, proj, heads, middle = pl.pallas_call(
        front_kernel,
        out_shape=(
            in_sums, out_sums, blocks, blocks,
            flat((32, slab_in, dense_width), low),
            flat((packs, ROWS, 3 * width), low),
            flat((packs, ROWS, width), low),
            flat((packs, ROWS, width), full),
        ),
        in_specs=[smem] * 2 + [vmem] * 10 + [any_space] * 2,
        out_specs=(any_space,) * 5 + (vmem,) * 3,
        scratch_shapes=[
            pltpu.VMEM((32, slab_in, dense_width), low),
            held(blocks), held(blocks),
            pltpu.VMEM((16, 2, experts, slab_in, SIDE), low),
            pltpu.VMEM((2, experts, slab_out, width), low),
            pltpu.VMEM((2, 4, width, 2 * SIDE), low),
            pltpu.VMEM((2, 4, 2 * SIDE, width), low),
            held(blocks), held(blocks),
            pltpu.VMEM((SIDE, width), full),
            pltpu.VMEM((SIDE, SIDE), full),
            pltpu.VMEM((8, 2 * SIDE), full),
            pltpu.VMEM((2 * SIDE, 8), full),
            pltpu.VMEM((8, width), full),
            dma((5, 8)), dma((4, 8)), dma((5, 8)), dma((4, 8)), dma((5, 4)), dma((4, 4)),
            dma((4, 4)), dma((4, 4)), dma((4, 4)), dma((4, 4)), dma((2,)), dma((2,)), dma((3,)),
            dma((32,)),
        ],
        compiler_params=pltpu.CompilerParams(
            collective_id=0, has_side_effects=True, vmem_limit_bytes=60 << 20
        ),
        name="front",
    )(
        pack_task, task_experts, tokens, segment_ids, w_qkv, w_attn_out, w_router,
        norm1_gain, norm1_bias, norm2_gain, norm2_bias, cotangent, w_expert_in, w_expert_out,
    )

    def by_expert(rows):
        return pl.BlockSpec((experts // 8, rows, width), lambda e, *unused: (e, 0, 0))

    d_in, d_out_own, d_out_far = pl.pallas_call(
        sum_kernel,
        grid_spec=pltpu.PrefetchScalarGridSpec(
            num_scalar_prefetch=3,
            grid=(8,),
            in_specs=[vmem] * 2,
            out_specs=[
                pl.BlockSpec((2, 16, experts // 8, slab_in, SIDE), lambda e, *unused: (0, 0, e, 0, 0)),
                by_expert(slab_out), by_expert(slab_out),
            ],
            scratch_shapes=[
                pltpu.SMEM((experts,), jnp.int32),
                pltpu.SMEM((32 * packs,), jnp.int32),
                pltpu.VMEM((width, SIDE), full),
                pltpu.VMEM((SIDE, width), full),
            ],
        ),
        out_shape=(
            flat((2, 16, experts, slab_in, SIDE), low),
            flat((experts, slab_out, width), full),
            flat((experts, slab_out, width), low),
        ),
        compiler_params=pltpu.CompilerParams(vmem_limit_bytes=60 << 20),
        name="sums",
    )(pack_task, task_experts, where, in_terms, out_terms)

    parts = pltpu.VMEM((4 * packs, ROWS, width), low)
    slices = pltpu.VMEM((4, slab_in, dense_width), low)
    sliced = pltpu.VMEM((16, slab_in, dense_width), low)
    mixed_tall, d_tok_tall, d_dense, d_in_all, d_out_all = pl.pallas_call(
        tail_kernel,
        out_shape=(
            flat((packs, ROWS, width), low),
            flat((packs, ROWS, width), low),
            flat((slab_in, dense_width), full),
            flat((experts, slab_in, hidden), low),
            flat((experts, slab_out, width), low),
        ),
        in_specs=[smem] * 2 + [vmem] * 7 + [any_space] * 4,
        out_specs=(vmem,) * 3 + (any_space,) * 2,
        scratch_shapes=[
            pltpu.VMEM((2, 4 * packs, ROWS, width), low), parts, parts, parts, parts,
            pltpu.VMEM((2, 4 * packs, ROWS, width), low), parts, parts, parts, parts,
            pltpu.VMEM((packs, ROWS, width), full),
            pltpu.VMEM((ROWS, width), full),
            pltpu.VMEM((ROWS, width), low),
            pltpu.VMEM((ROWS, 3 * width), low),
            pltpu.VMEM((width, dense_width), full),
            pltpu.VMEM((8, width), full),
            pltpu.VMEM((SIDE, width), full),
            pltpu.VMEM((8, 2 * SIDE), full),
            pltpu.VMEM((2 * SIDE, 8), full),
            pltpu.VMEM((16, experts, slab_in, SIDE), low),
            pltpu.VMEM((16, experts, slab_in, SIDE), low),
            sliced, sliced,
            pltpu.VMEM((16, slab_in, dense_width), full),
            slices, slices, slices, slices,
            dma((4, 8)), dma((4, 8)), dma((4, 8)), dma((4, 8)), dma((4, 4)), dma((4, 4)),
            dma((4, 4)), dma((4, 4)), dma((3,)), dma((3,)), dma((40,)),
        ],
        compiler_params=pltpu.CompilerParams(
            collective_id=1, has_side_effects=True, vmem_limit_bytes=60 << 20
        ),
        name="tail",
    )(
        pack_task, task_experts, tokens, cotangent, segment_ids, proj, heads, middle, dense,
        grad_part, mixed_part, d_in, d_out_far,
    )

    group = experts // 2

    def some(rows, columns):
        return pl.BlockSpec((group, rows, columns), lambda i: (i, 0, 0))

    def whole(*shape):
        return pl.BlockSpec(shape, lambda i: (0,) * len(shape))

    return pl.pallas_call(
        last_kernel,
        grid=(2,),
        in_specs=[
            whole(packs, ROWS, width), whole(packs, ROWS, width), whole(slab_in, dense_width),
            some(slab_in, hidden), some(slab_out, width), some(slab_out, width),
        ],
        out_specs=(
            whole(packs, length, width), whole(packs, length, width),
            whole(slab_in, 3 * width), whole(slab_in, width), whole(slab_in, experts),
            some(slab_in, hidden), some(slab_out, width),
        ) + (whole(slab_in),) * 4,
        out_shape=(
            flat((packs, length, width), low), flat((packs, length, width), low),
            flat((slab_in, 3 * width), full), flat((slab_in, width), full),
            flat((slab_in, experts), full),
            flat((experts, slab_in, hidden), full), flat((experts, slab_out, width), full),
        ) + (flat((slab_in,), full),) * 4,
        compiler_params=pltpu.CompilerParams(vmem_limit_bytes=60 << 20),
        name="last",
    )(mixed_tall, d_tok_tall, d_dense, d_in_all, d_out_own, d_out_all)


def solution(mesh):
    outer, inner = mesh.shape["gx"], mesh.shape["gy"]

    def shards(*arrays):
        packs, length, width = arrays[0].shape
        experts, slab_in, hidden = arrays[7].shape
        fits = (
            (outer, inner) == (4, 8)
            and packs == 2
            and length == PACK
            and experts == GAIN_ONE
            and width == HEADS * HEAD
            and slab_in == 16
            and hidden == 16 * SIDE
        )
        return (shards_fast if fits else shards_any)(*arrays)

    placed = (
        P(("gx", "gy"), None, None),
        P(("gx", "gy"), None),
        P(),
        P(),
        P(("gx", "gy"), None),
        P(("gx", "gy"), None),
        P(("gx", "gy"), None),
        P(None, ("gx", "gy"), None),
        P(None, ("gx", "gy"), None),
        P(("gx", "gy")),
        P(("gx", "gy")),
        P(("gx", "gy")),
        P(("gx", "gy")),
        P(("gx", "gy"), None, None),
    )
    return jax.shard_map(
        shards,
        mesh=mesh,
        in_specs=placed,
        out_specs=(
            P(("gx", "gy"), None, None),
            P(("gx", "gy"), None, None),
            P(("gx", "gy"), None),
            P(("gx", "gy"), None),
            P(("gx", "gy"), None),
            P(None, ("gx", "gy"), None),
            P(None, ("gx", "gy"), None),
            P(("gx", "gy")),
            P(("gx", "gy")),
            P(("gx", "gy")),
            P(("gx", "gy")),
        ),
        check_vma=False,
    )
```

```python
import functools
import math

import jax
import jax.numpy as jnp
from jax import lax
from jax.experimental import pallas as pl
from jax.experimental.pallas import tpu as pltpu
from jax.sharding import PartitionSpec as P

HEADS = 8
HEAD = 64
PACK = 216
GAIN_ONE = 32


EPS = 1e-05
MASK_FILL = -1e30
HIGH = lax.Precision.HIGHEST


def shortened(value):

    def short(part):
        return part.astype(jnp.bfloat16) if part.dtype == jnp.float32 else part

    return jax.tree.map(short, value)


def layer_norm(values, gain, bias):
    center = values - jnp.mean(values, -1, keepdims=True)
    spread = jnp.mean(center * center, -1, keepdims=True)
    return center * lax.rsqrt(spread + EPS) * gain + bias


def contract_rows(left, right):
    return lax.dot_general(
        left, right, (((0,), (0,)), ((), ())), preferred_element_type=jnp.float32
    )


def contract_cols(left, right):
    return lax.dot_general(
        left, right, (((1,), (1,)), ((), ())), preferred_element_type=jnp.float32
    )


def shards_any(
    tokens,
    segment_ids,
    pack_task,
    task_experts,
    w_qkv,
    w_attn_out,
    w_router,
    w_expert_in,
    w_expert_out,
    norm1_gain,
    norm1_bias,
    norm2_gain,
    norm2_bias,
    cotangent,
):
    outer = lax.axis_size("gx")
    inner = lax.axis_size("gy")
    devices = outer * inner
    micro, length, width = tokens.shape
    experts, slab_in, hidden = w_expert_in.shape
    slab_out = w_expert_out.shape[1]
    head_size = width // HEADS
    scale = 1.0 / math.sqrt(head_size)
    device = lax.axis_index("gx") * inner + lax.axis_index("gy")
    gathered = (
        lax.all_gather(w_qkv, ("gx", "gy"), axis=0, tiled=True),
        lax.all_gather(w_attn_out, ("gx", "gy"), axis=0, tiled=True),
        lax.all_gather(w_router, ("gx", "gy"), axis=0, tiled=True),
        lax.all_gather(norm1_gain, ("gx", "gy"), axis=0, tiled=True),
        lax.all_gather(norm1_bias, ("gx", "gy"), axis=0, tiled=True),
        lax.all_gather(norm2_gain, ("gx", "gy"), axis=0, tiled=True),
        lax.all_gather(norm2_bias, ("gx", "gy"), axis=0, tiled=True),
    )
    qkv_full, attn_full, route_full = (gathered[0], gathered[1], gathered[2])
    gain_one, bias_one, gain_two, bias_two = tuple(
        (piece.astype(jnp.float32) for piece in gathered[3:])
    )
    route_float = route_full.astype(jnp.float32)
    pack_pairs = task_experts[pack_task]
    needs = jnp.transpose(pack_pairs.reshape(outer, inner, micro, 2), (2, 3, 0, 1))
    route_pairs = jnp.transpose(pack_pairs.reshape(devices, micro, 2), (1, 0, 2))
    own_pairs = lax.dynamic_slice_in_dim(pack_pairs, device * micro, micro, 0)
    expert_ids = jnp.arange(experts, dtype=jnp.int32)

    def slabs(need):
        return (w_expert_in[need], w_expert_out[need])

    def joined(pieces):
        return (
            pieces[0].reshape(pieces[0].shape[0], width, hidden),
            pieces[1].reshape(pieces[1].shape[0], hidden, width),
        )

    def attention_probs(project, segment):
        queries = project[:, :width].reshape(length, HEADS, head_size)
        keys_all = project[:, width : 2 * width].reshape(length, HEADS, head_size)
        scores = (
            jnp.einsum("qhd,khd->hqk", queries, keys_all, preferred_element_type=jnp.float32)
            * scale
        )
        same_doc = segment[:, None] == segment[None, :]
        return jnp.where(same_doc[None], scores, MASK_FILL)

    def forward_step(carry, inputs):
        block, segment, need, pair, senders = inputs
        block_float = block.astype(jnp.float32)
        normed = layer_norm(block_float, gain_one, bias_one).astype(jnp.bfloat16)
        project = jnp.dot(normed, qkv_full, preferred_element_type=jnp.float32).astype(jnp.bfloat16)
        masked = attention_probs(project, segment)
        peak = jnp.max(masked, -1, keepdims=True)
        raised = jnp.exp(masked - peak)
        totals = jnp.sum(raised, -1, keepdims=True)
        log_total = peak + jnp.log(totals)
        attn_low = (raised / totals).astype(jnp.bfloat16)
        values_all = project[:, 2 * width :].reshape(length, HEADS, head_size)
        heads_out = (
            jnp.einsum("hqk,khd->qhd", attn_low, values_all, preferred_element_type=jnp.float32)
            .reshape(length, width)
            .astype(jnp.bfloat16)
        )
        middle = block_float + jnp.dot(heads_out, attn_full, preferred_element_type=jnp.float32)
        routed = layer_norm(middle, gain_two, bias_two).astype(jnp.bfloat16)
        logits = jnp.dot(routed, route_full, preferred_element_type=jnp.float32)
        select = (expert_ids[None, :] == pair[:, None]).astype(jnp.float32)
        chosen = jnp.sum(logits[:, None, :] * select[None], -1)
        raised_gate = jnp.exp(chosen - jnp.max(chosen, -1, keepdims=True))
        gates = raised_gate / jnp.sum(raised_gate, -1, keepdims=True)
        weights_in, weights_out = joined(
            lax.all_to_all(
                lax.all_to_all(
                    shortened(slabs(need)), "gx", split_axis=1, concat_axis=1, tiled=True
                ),
                "gy",
                split_axis=2,
                concat_axis=2,
                tiled=True,
            )
        )
        hidden_pre = jnp.einsum(
            "ld,kdf->klf", routed, weights_in, preferred_element_type=jnp.float32
        )
        hidden_low = jax.nn.gelu(hidden_pre).astype(jnp.bfloat16)
        expert_out = jnp.einsum(
            "klf,kfd->kld", hidden_low, weights_out, preferred_element_type=jnp.float32
        )
        saved = ()
        mixed = middle + gates[:, 0:1] * expert_out[0] + gates[:, 1:2] * expert_out[1]
        kept = (
            normed,
            project,
            log_total,
            heads_out,
            middle,
            routed,
            gates,
            hidden_pre,
            hidden_low,
            expert_out,
            saved,
        )
        return (carry, (mixed.astype(jnp.bfloat16), kept))

    start = jnp.zeros((), jnp.float32)
    unused, (mixed_all, kept_all) = lax.scan(
        forward_step, start, (tokens, segment_ids, needs, own_pairs, route_pairs)
    )

    def backward_step(carry, inputs):
        dense_acc, shard_in, shard_out, holding = carry
        block, grad_top, segment, need, pair, kept = inputs
        (
            normed,
            project,
            log_total,
            heads_out,
            middle,
            routed,
            gates,
            hidden_pre,
            hidden_low,
            expert_out,
            saved,
        ) = kept
        grad_float = grad_top.astype(jnp.float32)
        grad_gate = jnp.sum(grad_float[None] * expert_out, -1).T
        grad_chosen = gates * (grad_gate - jnp.sum(gates * grad_gate, -1, keepdims=True))
        select = (expert_ids[None, :] == pair[:, None]).astype(jnp.float32)
        grad_logits = jnp.sum(grad_chosen[:, :, None] * select[None], 1)
        routed_float = routed.astype(jnp.float32)
        grad_route = jnp.dot(routed_float.T, grad_logits, precision=HIGH)
        grad_routed = jnp.dot(grad_logits, route_float.T, precision=HIGH)
        grad_eout = (gates.T[:, :, None] * grad_float[None]).astype(jnp.bfloat16)
        slot = ()
        weights_in, weights_out = joined(
            lax.all_to_all(
                lax.all_to_all(
                    shortened(slabs(need)), "gx", split_axis=1, concat_axis=1, tiled=True
                ),
                "gy",
                split_axis=2,
                concat_axis=2,
                tiled=True,
            )
        )
        grad_act = jnp.einsum(
            "kld,kfd->klf", grad_eout, weights_out, preferred_element_type=jnp.float32
        )
        unused_act, gelu_back = jax.vjp(jax.nn.gelu, hidden_pre)
        grad_pre = gelu_back(grad_act)[0].astype(jnp.bfloat16)
        grad_in = jnp.einsum("ld,klf->kdf", routed, grad_pre, preferred_element_type=jnp.float32)
        grad_out = jnp.einsum(
            "klf,kld->kfd", hidden_low, grad_eout, preferred_element_type=jnp.float32
        )
        grad_routed = grad_routed + jnp.einsum(
            "klf,kdf->ld", grad_pre, weights_in, preferred_element_type=jnp.float32
        )
        slot = (grad_in, grad_out)
        unused_two, norm_two_back = jax.vjp(layer_norm, middle, gain_two, bias_two)
        grad_mid_norm, grad_gain_two, grad_bias_two = norm_two_back(grad_routed)
        grad_middle = grad_float + grad_mid_norm
        grad_attended = grad_middle.astype(jnp.bfloat16)
        grad_attn_w = contract_rows(heads_out, grad_attended)
        grad_heads = (
            contract_cols(grad_attended, attn_full)
            .astype(jnp.bfloat16)
            .reshape(length, HEADS, head_size)
        )
        masked = attention_probs(project, segment)
        probs_float = jnp.exp(masked - log_total)
        probs_low = probs_float.astype(jnp.bfloat16)
        queries = project[:, :width].reshape(length, HEADS, head_size)
        keys_all = project[:, width : 2 * width].reshape(length, HEADS, head_size)
        values_all = project[:, 2 * width :].reshape(length, HEADS, head_size)
        grad_values = jnp.einsum(
            "hqk,qhd->khd", probs_low, grad_heads, preferred_element_type=jnp.float32
        )
        grad_probs = jnp.einsum(
            "qhd,khd->hqk", grad_heads, values_all, preferred_element_type=jnp.float32
        )
        row_dot = jnp.sum(probs_float * grad_probs, -1, keepdims=True)
        grad_scores = (probs_float * (grad_probs - row_dot)).astype(jnp.bfloat16)
        grad_queries = (
            jnp.einsum("hqk,khd->qhd", grad_scores, keys_all, preferred_element_type=jnp.float32)
            * scale
        )
        grad_keys = (
            jnp.einsum("hqk,qhd->khd", grad_scores, queries, preferred_element_type=jnp.float32)
            * scale
        )
        grad_qkv = jnp.concatenate(
            [
                grad_queries.reshape(length, width),
                grad_keys.reshape(length, width),
                grad_values.reshape(length, width),
            ],
            -1,
        ).astype(jnp.bfloat16)
        grad_qkv_w = contract_rows(normed, grad_qkv)
        grad_normed = contract_cols(grad_qkv, qkv_full)
        unused_one, norm_one_back = jax.vjp(
            layer_norm, block.astype(jnp.float32), gain_one, bias_one
        )
        grad_in_norm, grad_gain_one, grad_bias_one = norm_one_back(grad_normed)
        grad_tokens = (grad_middle + grad_in_norm).astype(jnp.bfloat16)
        terms = (
            grad_qkv_w,
            grad_attn_w,
            grad_route,
            grad_gain_one,
            grad_bias_one,
            grad_gain_two,
            grad_bias_two,
        )
        dense_acc = tuple((total + term for total, term in zip(dense_acc, terms)))
        return ((dense_acc, shard_in, shard_out, holding), (grad_tokens, slot))

    dense_zero = (
        jnp.zeros((width, 3 * width), jnp.float32),
        jnp.zeros((width, width), jnp.float32),
        jnp.zeros((width, experts), jnp.float32),
        jnp.zeros((width,), jnp.float32),
        jnp.zeros((width,), jnp.float32),
        jnp.zeros((width,), jnp.float32),
        jnp.zeros((width,), jnp.float32),
    )
    shard_zero_in = jnp.zeros((experts, slab_in, hidden), jnp.float32)
    shard_zero_out = jnp.zeros((experts, slab_out, width), jnp.float32)
    holding_zero = ()
    (dense_acc, shard_in, shard_out, holding), (grad_tokens_all, slots) = lax.scan(
        backward_step,
        (dense_zero, shard_zero_in, shard_zero_out, holding_zero),
        (tokens, cotangent, segment_ids, needs, own_pairs, kept_all),
    )
    slot_in = slots[0].reshape(micro * 2, width, hidden)
    slot_out = slots[1].reshape(micro * 2, hidden, width)
    amount = slot_in.shape[0]
    returned = lax.all_to_all(
        lax.all_to_all(
            shortened(
                (
                    slot_in.reshape(amount, outer, inner, slab_in, hidden),
                    slot_out.reshape(amount, outer, inner, slab_out, width),
                )
            ),
            "gx",
            split_axis=1,
            concat_axis=1,
            tiled=True,
        ),
        "gy",
        split_axis=2,
        concat_axis=2,
        tiled=True,
    )
    onehot = (
        needs.reshape(micro * 2, outer, inner)[None] == expert_ids[:, None, None, None]
    ).astype(jnp.float32)
    added = tuple(
        (jnp.einsum("esab,sabrc->erc", onehot, piece, precision=HIGH) for piece in returned)
    )
    shard_in = shard_in + added[0]
    shard_out = shard_out + added[1]
    dense_shards = (
        lax.psum_scatter(dense_acc[0], ("gx", "gy"), scatter_dimension=0, tiled=True),
        lax.psum_scatter(dense_acc[1], ("gx", "gy"), scatter_dimension=0, tiled=True),
        lax.psum_scatter(dense_acc[2], ("gx", "gy"), scatter_dimension=0, tiled=True),
        lax.psum_scatter(dense_acc[3], ("gx", "gy"), scatter_dimension=0, tiled=True),
        lax.psum_scatter(dense_acc[4], ("gx", "gy"), scatter_dimension=0, tiled=True),
        lax.psum_scatter(dense_acc[5], ("gx", "gy"), scatter_dimension=0, tiled=True),
        lax.psum_scatter(dense_acc[6], ("gx", "gy"), scatter_dimension=0, tiled=True),
    )
    return (
        mixed_all,
        grad_tokens_all,
        dense_shards[0],
        dense_shards[1],
        dense_shards[2],
        shard_in,
        shard_out,
        dense_shards[3],
        dense_shards[4],
        dense_shards[5],
        dense_shards[6],
    )


MESH = pl.DeviceIdType.MESH
ROWS = 224
SIDE = 128
ROOT2PI = math.sqrt(2.0 / math.pi)


(
    DOWN, DPLANE, DCORNER, DLAST, DWAIT, ATT, WIN, WO, WINWAIT, WSIBWAIT, WAVE, COWN,
    CPLANE, CCORNER, CNEAR, CMZ, RPLANE, RCORNER, GFIRST, MFIRST, GHELP, MHELP, GPLANE, MPLANE, PAIR, ADDPAIR, DENSE,
) = range(27)

SIDE_PACKS = (0, 1)

EARLY = ((0, 3), (1, 3))

FRONT_STEPS = (
    (DOWN,), (COWN, 0), (WIN, 3, 0), (WIN, 0, 2), (DPLANE, 1), (DPLANE, 2), (DPLANE, 3), (WIN, 1, 3),
    (COWN, 1), (WIN, 1, 1), (DCORNER, 2), (DCORNER, 0), (DCORNER, 3), (WIN, 3, 2), (CNEAR, 0), (CMZ, 0, 1, 0),
    (CNEAR, 1), (WIN, 0, 1), (DLAST, 3), (DCORNER, 1), (CMZ, 0, 1, 1), (WIN, 2, 2), (WIN, 2, 0), (WIN, 0, 3),
    (WO,), (CMZ, 1, 1, 0), (DLAST, 2), (CMZ, 0, 2, 0), (WIN, 1, 0), (DLAST, 0), (DLAST, 1), (WIN, 2, 1),
    (CMZ, 1, 1, 1), (CMZ, 0, 2, 1), (DWAIT,), (WIN, 1, 2), (ATT, 0), (WIN, 2, 3), (WIN, 3, 1), (ATT, 1),
    (RPLANE, 1, 0), (CMZ, 1, 2, 1), (WIN, 3, 3), (RPLANE, 1, 1), (RCORNER, 0, 0), (WINWAIT,), (RPLANE, 2, 1),
    (RPLANE, 2, 0), (CMZ, 1, 2, 0), (WSIBWAIT,), (RCORNER, 1, 1), (RCORNER, 1, 0), (WAVE, 0, 0),
    (RCORNER, 0, 1), (RCORNER, 2, 1), (RPLANE, 3, 1), (WAVE, 1, 1), (RCORNER, 2, 0), (RPLANE, 3, 0),
    (WAVE, 1, 0), (CMZ, 1, 3, 0), (WAVE, 2, 1), (CMZ, 0, 3, 0), (RCORNER, 3, 1), (WAVE, 2, 0), (CMZ, 1, 3, 1),
    (RCORNER, 3, 0), (WAVE, 0, 1), (CMZ, 0, 3, 1), (WAVE, 3, 0), (WAVE, 3, 1),
)
TAIL_STEPS = (
    (MHELP, 0, 0), (GFIRST, 0, 0), (PAIR,), (GFIRST, 2, 0), (GFIRST, 0, 1), (ADDPAIR,), (GHELP, 0, 0),
    (MHELP, 1, 0), (MHELP, 2, 0), (GHELP, 0, 1), (MHELP, 0, 1), (GFIRST, 1, 1), (GFIRST, 1, 0),
    (GPLANE, 0, 0), (WIN, 0, 1), (GHELP, 2, 0), (GPLANE, 0, 1), (MHELP, 3, 1), (GHELP, 1, 0), (GHELP, 1, 1),
    (GFIRST, 2, 1), (MFIRST, 0, 0), (GPLANE, 2, 0), (GPLANE, 1, 0), (MFIRST, 0, 1), (WIN, 0, 0),
    (GHELP, 2, 1), (GPLANE, 1, 1), (MPLANE, 0, 0), (GFIRST, 3, 1), (GFIRST, 3, 0), (MFIRST, 1, 0),
    (MFIRST, 3, 1), (MPLANE, 0, 1), (GPLANE, 2, 1), (GHELP, 3, 1), (GHELP, 3, 0), (MPLANE, 1, 0),
    (MFIRST, 1, 1), (WIN, 3, 3), (GPLANE, 3, 1), (MFIRST, 2, 0), (GPLANE, 3, 0), (WIN, 1, 0), (ATT, 0),
    (MPLANE, 2, 0), (MFIRST, 3, 0), (MFIRST, 2, 1), (MHELP, 3, 0), (MPLANE, 1, 1), (WIN, 2, 2), (WIN, 2, 1),
    (ATT, 1), (ATT, 2), (WIN, 3, 0), (WIN, 2, 3), (ATT, 3), (WIN, 1, 1), (MHELP, 1, 1), (WIN, 2, 0), (ATT, 4),
    (ATT, 5), (MPLANE, 3, 0), (MPLANE, 2, 1), (WIN, 3, 2), (WIN, 1, 3), (DENSE,), (MHELP, 2, 1), (WIN, 1, 2),
    (WIN, 0, 2), (WIN, 3, 1), (MPLANE, 3, 1),
)


def dot(left, right):
    return jnp.dot(left, right, preferred_element_type=jnp.float32)


class Place:
    def __init__(self):
        self.z = lax.axis_index("gx")
        g = lax.axis_index("gy")
        self.core = g % 2
        across_x = g + 2 - 4 * ((g // 2) % 2)
        across_y = g + 4 - 8 * (g // 4)
        across_both = across_x + 4 - 8 * (across_x // 4)
        self.at = (g, across_x, across_y, across_both)
        self.step_x, self.step_y = across_x - g, across_y - g
        self.sibling = (self.z, g + 1 - 2 * self.core)

    def plane(self, k):
        return (self.z + k) % 4

    def nearest(self, j):
        z = self.z
        return (0, 1 + 2 * (z // 2), 2 + z - 3 * (z // 2), 3 - z + z // 2)[j]

    def device(self, rel, k):
        return (self.plane(k), self.at[rel])

    def chip(self, rel, k):
        return self.plane(k) * 4 + self.at[rel] // 2

    def index(self, rel, k):
        return self.plane(k) * 8 + self.at[rel]

    def pair(self, pack_task, task_experts, rel, k, p):
        at = self.at[0] + self.step_x * (rel % 2) + self.step_y * (rel // 2)
        task = pack_task[(self.plane(k) * 8 + at) * 2 + p]
        return task_experts[task, 0], task_experts[task, 1]

    def greet(self):
        barrier = pltpu.get_barrier_semaphore()
        others = [(rel, k) for rel in range(4) for k in range(4) if (rel, k) != (0, 0)]
        for rel, k in others:
            pl.semaphore_signal(
                barrier, inc=1, device_id=self.device(rel, k), device_id_type=MESH
            )
        pl.semaphore_signal(barrier, inc=1, device_id=self.sibling, device_id_type=MESH)
        pl.semaphore_wait(barrier, len(others) + 1)


def send(started, src, dst, send_sem, recv_sem, device):
    copy = pltpu.make_async_remote_copy(
        src_ref=src,
        dst_ref=dst,
        send_sem=send_sem,
        recv_sem=recv_sem,
        device_id=device,
        device_id_type=MESH,
    )
    copy.start()
    started.append(copy)


def arrived(ref, sem):
    pltpu.make_async_copy(ref, ref, sem).wait()


def back(k):
    return (4 - k) % 4


class Spread:
    def __init__(self, place, here, there, packs, half, chained, sems):
        self.place, self.here, self.there = place, here, there
        self.packs, self.half, self.chained, self.started = packs, half, chained, []
        self.send_sem, self.recv_sem = sems

    def go(self, kind, at_send, k_there, rel, k, p, src, rel_there, device, only_if=None):
        copy = pltpu.make_async_remote_copy(
            src_ref=src,
            dst_ref=self.there(rel_there, k_there, p, rel, k),
            send_sem=self.send_sem.at[kind, at_send * self.packs + p],
            recv_sem=self.recv_sem.at[kind % 4, k_there * self.packs + p],
            device_id=device,
            device_id_type=MESH,
        )
        if only_if is None:
            copy.start()
        else:
            pl.when(only_if)(copy.start)
        self.started.append((copy, only_if))

    def wait(self, kind, rel, k, p):
        arrived(self.here(rel, k, p), self.recv_sem.at[kind, k * self.packs + p])

    def own(self, p, src):
        place = self.place
        if self.chained:
            self.go(0, 0, 3, 0, 0, p, src, 0, place.device(0, 1), place.z < 3)
            self.go(4, 0, 1, 0, 0, p, src, 0, place.device(0, 3), place.z > 0)
        else:
            for k in (1, 2, 3):
                self.go(0, k, back(k), 0, 0, p, src, 0, place.device(0, k))
        self.go(1, 0, 0, 0, 0, p, src, 1, place.device(1, 0))
        self.go(2, 0, 0, 0, 0, p, src, 2, place.device(2, 0))

    def plane(self, j, p):
        place = self.place
        k = place.nearest(j)
        self.wait(0, 0, k, p)
        src = self.here(0, k, p)
        if self.chained:
            step = 2 * ((place.z - place.plane(k) + 3) // 4) - 1
            goes = (place.z + step >= 0) & (place.z + step <= 3)
            on = (place.plane(step + 4), place.at[0])
            self.go(0, k, (k - step + 4) % 4, 0, k, p, src, 0, on, goes)
        self.go(1, k, k, 0, k, p, src, 1, place.device(1, 0))
        self.go(2, k, k, 0, k, p, src, 2, place.device(2, 0))

    def corner(self, j, p):
        k = self.place.nearest(j)
        rel = 1 + self.half(j, p)
        self.wait(rel, rel, k, p)
        self.go(3, k, k, rel, k, p, self.here(rel, k, p), 3, self.place.device(3 - rel, 0))

    def last(self, j, p):
        k = self.place.nearest(j)
        rel = 2 - self.half(j, p)
        self.wait(rel, rel, k, p)
        self.wait(3, 3, k, p)

    def finish(self):
        for copy, only_if in self.started:
            if only_if is None:
                copy.wait_send()
            else:
                pl.when(only_if)(copy.wait_send)


class SideSpread(Spread):
    def side(self, p):
        return 1 + p

    def along(self, w, rel, k, p, src, first):
        place = self.place
        if first:
            ways = ((2 + w, 3, 1, place.z < 3), (4 + w, 1, 3, place.z > 0))
        else:
            step = 2 * ((place.z - place.plane(k) + 3) // 4) - 1
            goes = (place.z + step >= 0) & (place.z + step <= 3)
            ways = ((2 + w, (k - step + 4) % 4, step + 4, goes),)
        for kind, k_there, on, goes in ways:
            self.go(kind, k, k_there, rel, k, p, src, rel, (place.plane(on), place.at[0]), goes)

    def go(self, kind, at_send, k_there, rel, k, p, src, rel_there, device, only_if=None):
        copy = pltpu.make_async_remote_copy(
            src_ref=src,
            dst_ref=self.there(rel_there, k_there, p, rel, k),
            send_sem=self.send_sem.at[kind, at_send * self.packs + p],
            recv_sem=self.recv_sem.at[rel_there, k_there * self.packs + p],
            device_id=device,
            device_id_type=MESH,
        )
        if only_if is None:
            copy.start()
        else:
            pl.when(only_if)(copy.start)
        self.started.append((copy, only_if))

    def own(self, p, src):
        side, other = self.side(p), 3 - self.side(p)
        self.go(6, 0, 0, 0, 0, p, src, side, self.place.device(side, 0))
        self.along(0, 0, 0, p, src, True)
        self.go(0, 0, 0, 0, 0, p, src, other, self.place.device(other, 0))

    def near(self, p):
        side, other = self.side(p), 3 - self.side(p)
        self.wait(side, side, 0, p)
        src = self.here(side, 0, p)
        self.along(1, side, 0, p, src, True)
        self.go(1, 0, 0, side, 0, p, src, 3, self.place.device(other, 0))

    def passed(self, w, j, p):
        side, other = self.side(p), 3 - self.side(p)
        rel, k = side * w, self.place.nearest(j)
        self.wait(rel, rel, k, p)
        src = self.here(rel, k, p)
        self.along(w, rel, k, p, src, False)
        self.go(w, k, k, rel, k, p, src, 3 if w else other, self.place.device(other, 0))

    def last(self, j, p):
        k = self.place.nearest(j)
        for rel in (3 - self.side(p), 3):
            self.wait(rel, rel, k, p)


def norm_parts(values):
    center = values - jnp.mean(values, -1, keepdims=True)
    spread = jnp.mean(center * center, -1, keepdims=True)
    rise = lax.rsqrt(spread + EPS)
    return center * rise, rise


def real_rows():
    return lax.broadcasted_iota(jnp.int32, (ROWS, 1), 0) < PACK


def head_lanes(h):
    lane = lax.broadcasted_iota(jnp.int32, (1, SIDE), 1)
    inside = (lane >= h * HEAD) & (lane < (h + 1) * HEAD)
    return inside.astype(jnp.bfloat16)


def softmax_rows(queries, keys, same):
    scores = contract_cols(queries, keys) * (1.0 / math.sqrt(HEAD))
    scores = jnp.where(same, scores, MASK_FILL)
    raised = jnp.exp(scores - jnp.max(scores, -1, keepdims=True))
    return raised * (1.0 / jnp.sum(raised, -1, keepdims=True))


def pick(logits, expert):
    lane = lax.broadcasted_iota(jnp.int32, logits.shape, 1)
    return jnp.sum(jnp.where(lane == expert, logits, 0.0), -1, keepdims=True)


def two_gates(logits, first, second):
    gap = pick(logits, second) - pick(logits, first)
    return 1.0 / (1.0 + jnp.exp(gap)), 1.0 / (1.0 + jnp.exp(-gap))


def lengthened(ref, p):
    rows = ref[p].astype(jnp.float32)
    return jnp.concatenate([rows, jnp.zeros((ROWS - PACK, rows.shape[1]), jnp.float32)], axis=0)


def same_documents(segments, flat_ids, tall_ids):
    flat_ids[...] = jnp.full(flat_ids.shape, -1.0, jnp.float32)
    flat_ids[: segments.shape[0], :PACK] = segments[...].astype(jnp.float32)
    tall_ids[...] = jnp.transpose(flat_ids[...])


def same_document(flat_ids, tall_ids, p):
    return tall_ids[:ROWS, p : p + 1] == flat_ids[p : p + 1, :ROWS]


def front_kernel(
    pack_task, task_experts, tok, segments, w_qkv_own, w_attn_own, route_own,
    gain_one_own, bias_one_own, gain_two_own, bias_two_own, cot_own, w_in, w_out,
    in_terms, out_terms, mixed_out, grad_out, dense_out, early_y, early_x, proj, heads, middle,
    dense, routed_all, cot_all, w_in_all, w_out_all, in_stage, out_stage, mixed_all, grad_all,
    turned, square, flat_ids, tall_ids, gate_row,
    cot_send, cot_recv, routed_send, routed_recv, dense_send, dense_recv,
    core_send, core_recv, in_send, in_recv, pair_send, pair_recv, local_sem, out_sem, early_sem,
):
    place = Place()
    width, experts = tok.shape[2], route_own.shape[1]
    other = 1 - place.core

    def block_here(ref):
        return lambda rel, k, p: ref.at[rel, k * 2 + p]

    def block_there(ref):
        return lambda rel_there, k_there, p, rel, k: ref.at[rel_there, k_there * 2 + p]

    own = place.index(0, 0)
    dense[own, :, : 3 * width] = w_qkv_own[...]
    dense[own, :, 3 * width : 4 * width] = w_attn_own[...]
    square[...] = jnp.zeros_like(square)
    for i, ref in enumerate((gain_one_own, bias_one_own, gain_two_own, bias_two_own)):
        square[GAIN_ONE + i : GAIN_ONE + i + 1, : ref.shape[0]] = (
            ref[...].astype(jnp.float32).reshape(1, ref.shape[0])
        )
    columns = jnp.transpose(square[...])[: gain_one_own.shape[0]]
    square[: gain_one_own.shape[0], :] = columns
    square[: gain_one_own.shape[0], :experts] = route_own[...].astype(jnp.float32)
    dense[own, :, 4 * width :] = square[: gain_one_own.shape[0], :].astype(jnp.bfloat16)
    for p in range(2):
        cot_all[0, p] = lengthened(cot_own, p).astype(jnp.bfloat16)
    place.greet()

    dense_tree = Spread(
        place,
        lambda rel, k, p: dense.at[place.index(rel, k)],
        lambda rel_there, k_there, p, rel, k: dense.at[place.index(rel, k)],
        1,
        lambda j, p: j % 2,
        False,
        (dense_send, dense_recv),
    )
    core_started, in_started, pair_started, local, outs, early = [], [], [], [], [], []

    def to_core(rel, k):
        slot = dense.at[place.index(rel, k)]
        send(
            core_started, slot, slot, core_send.at[rel, k], core_recv.at[rel, k], place.sibling
        )

    def tree(kind, ref, sems):
        return kind(place, block_here(ref), block_there(ref), 2, lambda j, p: p, True, sems)

    cot_side = tree(SideSpread, cot_all, (cot_send, cot_recv))
    cot_plain = tree(Spread, cot_all, (cot_send, cot_recv))
    cot_trees = [cot_side if p in SIDE_PACKS else cot_plain for p in range(2)]
    routed_tree = tree(Spread, routed_all, (routed_send, routed_recv))

    def local_copy(src, dst):
        copy = pltpu.make_async_copy(src, dst, local_sem.at[len(local)])
        copy.start()
        local.append(copy)

    def down():
        dense_tree.own(0, dense.at[own])
        to_core(0, 0)
        local_copy(w_in.at[:, :, pl.ds(pl.multiple_of(place.chip(0, 0) * SIDE, SIDE), SIDE)],
                   w_in_all.at[place.chip(0, 0), place.core])
        same_documents(segments, flat_ids, tall_ids)
        gate_row[...] = jnp.zeros_like(gate_row)

    def dplane(j):
        dense_tree.plane(j, 0)
        to_core(0, place.nearest(j))

    def dcorner(j):
        k = place.nearest(j)
        dense_tree.corner(j, 0)
        other_side = 2 - j % 2
        dense_tree.wait(other_side, other_side, k, 0)
        to_core(1, k)
        to_core(2, k)

    def dlast(j):
        k = place.nearest(j)
        dense_tree.wait(3, 3, k, 0)
        to_core(3, k)

    def dwait():
        for k in range(4):
            for rel in range(4):
                slot = dense.at[place.plane(k) * 8 + place.at[rel] + 1 - 2 * place.core]
                arrived(slot, core_recv.at[rel, k])
        local_copy(dense, dense_out)
        small = dense[:, :, 4 * width : 4 * width + SIDE].reshape(width, SIDE)
        turned[...] = jnp.transpose(small.astype(jnp.float32))

    def att(p):
        row = [turned[GAIN_ONE + i : GAIN_ONE + i + 1, :] for i in range(4)]
        block = lengthened(tok, p)
        unit, unused = norm_parts(block)
        normed = (unit * row[0] + row[1]).astype(jnp.bfloat16)
        w_qkv = dense[:, :, : 3 * width].reshape(width, 3 * width)
        proj[p] = dot(normed, w_qkv).astype(jnp.bfloat16)
        same = same_document(flat_ids, tall_ids, p)

        def pair_of_heads(j, carry):
            at = pl.multiple_of(j * SIDE, SIDE)
            queries = proj[p, :, pl.ds(at, SIDE)]
            keys = proj[p, :, pl.ds(at + width, SIDE)]
            values = proj[p, :, pl.ds(at + 2 * width, SIDE)]
            out = jnp.zeros((ROWS, SIDE), jnp.float32)
            for h in range(2):
                lanes = head_lanes(h)
                probs = softmax_rows(queries * lanes, keys, same).astype(jnp.bfloat16)
                out = out + dot(probs, values * lanes)
            heads[p, :, pl.ds(at, SIDE)] = out.astype(jnp.bfloat16)
            return carry

        lax.fori_loop(0, width // SIDE, pair_of_heads, 0)
        w_attn = dense[:, :, 3 * width : 4 * width].reshape(width, width)
        mid = block + dot(heads[p], w_attn)
        middle[p] = mid
        unit, unused = norm_parts(mid)
        routed_all[0, p] = jnp.where(real_rows(), unit * row[2] + row[3], 0.0).astype(jnp.bfloat16)
        routed_tree.own(p, routed_all.at[0, p])

    def win(rel, j):
        k = place.nearest(j)
        columns = pl.ds(pl.multiple_of(place.chip(rel, k) * SIDE, SIDE), SIDE)
        send(
            in_started, w_in.at[:, :, columns], w_in_all.at[place.chip(0, 0), place.core],
            in_send.at[rel, k], in_recv.at[rel, (4 - k) % 4], place.device(rel, k),
        )

    def wo():
        local_copy(w_out, w_out_all.at[place.core])
        send(
            pair_started, w_out, w_out_all.at[place.core], pair_send.at[0], pair_recv.at[0],
            place.sibling,
        )

    def winwait():
        for rel in range(4):
            for k in range(4):
                if (rel, k) != (0, 0):
                    arrived(w_in_all.at[place.chip(rel, k), place.core], in_recv.at[rel, k])
        local[0].wait()
        mine = w_in_all.at[:, place.core]
        send(pair_started, mine, mine, pair_send.at[1], pair_recv.at[1], place.sibling)

    def wsibwait():
        for copy in local[1:]:
            copy.wait()
        arrived(w_out_all.at[other], pair_recv.at[0])
        arrived(w_in_all.at[:, other], pair_recv.at[1])

    def put(src, dst):
        copy = pltpu.make_async_copy(src, dst, out_sem.at[len(outs)])
        copy.start()
        outs.append(copy)

    def wave(j, p):
        at = place.nearest(j) * 2 + p
        k = place.nearest(j)
        cot_trees[p].last(j, p)
        routed_tree.wait(2 - p, 2 - p, k, p)
        count = len(outs) // 4
        stage = count % 2
        if count >= 2:
            outs[4 * count - 8].wait()
            outs[4 * count - 7].wait()

        def one_block(rel, carry):
            pair = place.pair(pack_task, task_experts, rel, place.nearest(j), p)
            rows, cots = routed_all[rel, at], cot_all[rel, at]
            gated, grad_pre, mixed, grad = expert_block(
                pair, rows, cots, w_in_all, w_out_all, dense, gate_row
            )
            mixed_all[rel, at] = mixed
            grad_all[rel, at] = grad
            in_stage[stage, rel] = contract_rows(rows, grad_pre).astype(jnp.bfloat16)
            out_stage[stage, rel] = contract_rows(gated, cots).astype(jnp.bfloat16)
            return carry

        lax.fori_loop(0, 3, one_block, 0)
        routed_tree.wait(3, 3, k, p)
        one_block(3, 0)
        put(in_stage.at[stage], in_terms.at[:, at])
        put(out_stage.at[stage], out_terms.at[:, at])
        put(grad_all.at[:, at], grad_out.at[:, at])
        put(mixed_all.at[:, at], mixed_out.at[:, at])
        for i, (back_j, rel) in enumerate(EARLY):
            if back_j == 3 - j:
                copy = pltpu.make_async_copy(
                    grad_all.at[2 - p if rel == 1 else rel, at],
                    (early_y, early_x)[p].at[i],
                    early_sem.at[p, i],
                )
                copy.start()
                early.append(copy)

    steps = {
        DOWN: down, DPLANE: dplane, DCORNER: dcorner, DLAST: dlast, DWAIT: dwait,
        ATT: att, WIN: win, WO: wo, WINWAIT: winwait, WSIBWAIT: wsibwait, WAVE: wave,
        COWN: lambda p: cot_trees[p].own(p, cot_all.at[0, p]),
        CPLANE: cot_plain.plane, CCORNER: cot_plain.corner,
        CNEAR: cot_side.near, CMZ: cot_side.passed,
        RPLANE: routed_tree.plane, RCORNER: routed_tree.corner,
    }
    for name, *where in FRONT_STEPS:
        steps[name](*where)
    for i, copy in enumerate(outs):
        if i % 4 >= 2 or i >= len(outs) - 8:
            copy.wait()
    for copy in early:
        copy.wait()
    for each in (dense_tree, cot_side, cot_plain, routed_tree):
        each.finish()
    for copy in core_started + in_started + pair_started:
        copy.wait_send()


def expert_block(pair, rows, cots, w_in_all, w_out_all, dense, gate_row):
    width, slab = rows.shape[1], 2 * SIDE
    first, second = pair
    w_in = jnp.concatenate([w_in_all[:, :, e].reshape(width, SIDE) for e in pair], axis=1)
    w_out = jnp.concatenate([w_out_all[:, e].reshape(SIDE, width) for e in pair], axis=0)
    route = dense[:, :, 4 * width : 4 * width + SIDE].reshape(width, SIDE)
    gate_a, gate_b = two_gates(dot(rows, route), first, second)
    lane = lax.broadcasted_iota(jnp.int32, (1, slab), 1)
    gates = jnp.where(lane < SIDE, gate_a, gate_b)
    hidden = dot(rows, w_in)
    back_act = contract_cols(cots, w_out)
    square = hidden * hidden
    bend = jnp.tanh(ROOT2PI * hidden * (1.0 + 0.044715 * square))
    half = 0.5 * (1.0 + bend)
    act = (hidden * half).astype(jnp.bfloat16).astype(jnp.float32)
    slope = half + 0.5 * hidden * (1.0 - bend * bend) * (ROOT2PI * (1.0 + 0.134145 * square))
    gated = (gates * act).astype(jnp.bfloat16)
    grad_pre = (gates * back_act * slope).astype(jnp.bfloat16)
    product = (act * back_act).astype(jnp.bfloat16)
    signs = jnp.broadcast_to(jnp.where(lane < SIDE, 1.0, -1.0), (8, slab)).astype(jnp.bfloat16)
    gate_row[:, :ROWS] = contract_cols(signs, product)
    mixed = dot(gated, w_out).astype(jnp.bfloat16)
    grads = contract_cols(grad_pre, w_in)
    grad = jnp.concatenate([grads[:PACK], gate_row[...]], axis=0).astype(jnp.bfloat16)
    return gated, grad_pre, mixed, grad


def sum_kernel(
    pack_task, task_experts, where, in_terms, out_terms, d_in, d_out_own, d_out_far, heads, nexts,
    total_in, total_out,
):
    group = d_out_own.shape[0]
    experts = group * pl.num_programs(0)
    slots = in_terms.shape[0] * in_terms.shape[1]

    @pl.when(pl.program_id(0) == 0)
    def list_uses():
        def clear(e, carry):
            heads[e] = -1
            return carry

        lax.fori_loop(0, experts, clear, 0)
        g = where[1]
        step_x, step_y = 2 - 4 * ((g // 2) % 2), 4 - 8 * (g // 4)

        def one(slot, carry):
            rel, k, p = slot // 8, (slot // 2) % 4, slot % 2
            at = g + step_x * (rel % 2) + step_y * (rel // 2)
            task = pack_task[(((where[0] + k) % 4) * 8 + at) * 2 + p]
            for i in range(2):
                e = task_experts[task, i]
                nexts[slot * 2 + i] = heads[e]
                heads[e] = slot * 2 + i
            return carry

        lax.fori_loop(0, slots, one, 0)

    def terms(use):
        slot = use // 2
        rel, at, half = slot // 8, slot % 8, pl.multiple_of((use % 2) * SIDE, SIDE)
        return (
            in_terms[rel, at, :, pl.ds(half, SIDE)].astype(jnp.float32),
            out_terms[rel, at, pl.ds(half, SIDE), :].astype(jnp.float32),
        )

    def add_terms(use):
        new_in, new_out = terms(use)
        total_in[...] += new_in
        total_out[...] += new_out
        return nexts[use]

    own = pl.ds(pl.multiple_of(where[2] * HEAD, HEAD), HEAD)
    far = pl.ds(pl.multiple_of((1 - where[2]) * HEAD, HEAD), HEAD)

    def one_expert(i, carry):
        head = heads[pl.program_id(0) * group + i]

        @pl.when(head < 0)
        def unused():
            total_in[...] = jnp.zeros_like(total_in)
            total_out[...] = jnp.zeros_like(total_out)

        @pl.when(head >= 0)
        def used():
            total_in[...], total_out[...] = terms(head)
            lax.while_loop(lambda use: use >= 0, add_terms, nexts[head])

        low = total_in[...].astype(jnp.bfloat16).reshape(16, 2, 16, SIDE)
        d_in[0, :, i] = low[:, 0]
        d_in[1, :, i] = low[:, 1]
        d_out_own[i] = total_out[own, :]
        d_out_far[i] = total_out[far, :].astype(jnp.bfloat16)
        return carry

    lax.fori_loop(0, group, one_expert, 0)


class Collect:
    def __init__(self, place, part, corner, from_x, from_y, from_z, packs, half, sems):
        self.place, self.part = place, part
        self.corner, self.from_x, self.from_y, self.from_z = corner, from_x, from_y, from_z
        self.packs, self.half, self.started = packs, half, []
        self.send_sem, self.recv_sem = sems

    def go(self, kind, src, dst, at_send, at_recv, device):
        send(
            self.started, src, dst, self.send_sem.at[kind, at_send],
            self.recv_sem.at[kind, at_recv], device,
        )

    def opposite(self, k, p):
        at = k * self.packs + p
        towards = 2 if self.half(k, p) == 0 else 1
        self.go(3, self.part(3, k, p), self.corner.at[at], at, at, self.place.device(towards, 0))

    def straight(self, k, p):
        at = k * self.packs + p
        if self.half(k, p) == 0:
            self.go(2, self.part(2, k, p), self.from_y.at[at], at, at, self.place.device(2, 0))
        else:
            self.go(1, self.part(1, k, p), self.from_x.at[at], at, at, self.place.device(1, 0))

    def helped(self, k, p, mine):
        at = k * self.packs + p
        ref = self.corner.at[at]
        arrived(ref, self.recv_sem.at[3, at])
        total = ref[...].astype(jnp.float32) + mine().astype(jnp.float32)
        ref[...] = total.astype(jnp.bfloat16)
        if self.half(k, p) == 0:
            self.go(1, ref, self.from_x.at[at], at, at, self.place.device(1, 0))
        else:
            self.go(2, ref, self.from_y.at[at], at, at, self.place.device(2, 0))

    def plane(self, k, p, mine):
        at = k * self.packs + p
        arrived(self.from_x.at[at], self.recv_sem.at[1, at])
        arrived(self.from_y.at[at], self.recv_sem.at[2, at])
        total = self.from_x[at].astype(jnp.float32) + self.from_y[at].astype(jnp.float32)
        total = total + mine().astype(jnp.float32)
        if k:
            self.from_x[at] = total.astype(jnp.bfloat16)
            there = back(k) * self.packs + p
            self.go(
                0, self.from_x.at[at], self.from_z.at[there], at, there, self.place.device(0, k)
            )
            return None
        for other in (1, 2, 3):
            at = other * self.packs + p
            arrived(self.from_z.at[at], self.recv_sem.at[0, at])
            total = total + self.from_z[at].astype(jnp.float32)
        return total

    def finish(self):
        for copy in self.started:
            copy.wait_send()


class Return:
    def __init__(self, place, part, own, from_z, sems, load):
        self.place, self.part, self.own, self.from_z = place, part, own, from_z
        self.send_sem, self.recv_sem, self.z_sem = sems
        self.started, self.loads = [], {}
        for kind, j, p in self.needs:
            rel = self.beside(p) if kind else 0
            at = self.at(j, p)
            self.loads[kind, j, p] = load(part.at[rel, at], own.at[kind, at])

    needs = [(kind, j, p) for j in range(4) for p in range(2) for kind in (1, 0)]

    def at(self, j, p):
        return self.place.nearest(3 - j) * 2 + p

    def beside(self, p):
        return 1 + p

    def go(self, kind, at, src, dst, recv_sem, device):
        send(self.started, src, dst, self.send_sem.at[kind, at], recv_sem, device)

    def mine(self, kind, j, p):
        return self.own[kind, self.at(j, p)].astype(jnp.float32)

    def along(self, kind, send_kind, j, p, ref, total):
        place = self.place
        k = place.nearest(3 - j)
        step = 2 * ((place.plane(k) - place.z + 3) // 4) - 1
        behind = self.from_z.at[kind, k * 2 + p]
        more = (place.z - step >= 0) & (place.z - step <= 3)

        @pl.when(more)
        def add():
            arrived(behind, self.z_sem.at[kind, k * 2 + p])
            ref[...] = (total() + behind[...].astype(jnp.float32)).astype(jnp.bfloat16)

        @pl.when(jnp.logical_not(more))
        def first():
            ref[...] = total().astype(jnp.bfloat16)

        there = (k - step + 4) % 4
        slot = (there + (4 - there) // 4 * (2 - 2 * step)) * 2 + p
        self.go(
            send_kind, k * 2 + p, ref, self.from_z.at[kind, slot], self.z_sem.at[kind, slot],
            (place.plane(step + 4), place.at[0]),
        )

    def owned(self, kind, p, total, out):
        out[...] = total()
        for slot, comes in ((p, self.place.z > 0), (8 + p, self.place.z < 3)):

            @pl.when(comes)
            def add(slot=slot):
                ref = self.from_z.at[kind, slot]
                arrived(ref, self.z_sem.at[kind, slot])
                out[...] += ref[...].astype(jnp.float32)

    def finish(self):
        for copy in self.started:
            copy.wait_send()


class PlaneFirst(Return):
    def __init__(self, place, part, own, from_z, sems, load, corner, from_x, from_y, got):
        self.corner, self.near, self.early = corner, (None, from_x, from_y), {}
        for i, (j, rel) in enumerate(EARLY):
            for p in range(2):
                into = corner if rel == 3 else self.near[2 - p]
                at = place.nearest(3 - j) * 2 + p
                self.early[rel == 3, j, p] = load(got[p].at[i], into.at[at])
        super().__init__(place, part, own, from_z, sems, load)

    def here(self, far, j, p, ref, sem):
        if (far, j, p) in self.early:
            self.early[far, j, p].wait()
        else:
            arrived(ref, sem)

    def first(self, j, p):
        at, way = self.at(j, p), 2 - p
        if (True, j, p) not in self.early:
            self.go(
                3, at, self.part.at[3, at], self.corner.at[at], self.recv_sem.at[3, at],
                self.place.device(way, 0),
            )
        if (False, j, p) not in self.early:
            self.go(
                way, at, self.part.at[way, at], self.near[way].at[at], self.recv_sem.at[way, at],
                self.place.device(way, 0),
            )

    def helped(self, j, p):
        at, way = self.at(j, p), 1 + p
        ref = self.corner.at[at]
        self.loads[1, j, p].wait()
        self.here(True, j, p, ref, self.recv_sem.at[3, at])
        ref[...] = (ref[...].astype(jnp.float32) + self.mine(1, j, p)).astype(jnp.bfloat16)
        self.go(
            way, at, ref, self.near[way].at[at], self.recv_sem.at[way, at],
            self.place.device(way, 0),
        )

    def plane(self, j, p, out):
        at = self.at(j, p)
        self.loads[0, j, p].wait()
        self.here(False, j, p, self.near[2 - p].at[at], self.recv_sem.at[2 - p, at])
        arrived(self.near[1 + p].at[at], self.recv_sem.at[1 + p, at])

        def total():
            both = self.near[1][at].astype(jnp.float32) + self.near[2][at].astype(jnp.float32)
            return both + self.mine(0, j, p)

        if j < 3:
            self.along(0, 0, j, p, self.near[1].at[at], total)
        else:
            self.owned(0, p, total, out)


class SideFirst(Return):
    def __init__(self, place, part, own, from_z, sems, load, near, last, total):
        super().__init__(place, part, own, from_z, sems, load)
        self.near, self.last, self.total = near, last, total

    def first(self, j, p):
        at, way = self.at(j, p), 2 - p
        for kind, rel in ((1, 3), (0, way)):
            self.go(
                kind, at, self.part.at[rel, at], self.near.at[kind, at],
                self.recv_sem.at[kind, at], self.place.device(way, 0),
            )

    def plane(self, j, p, out):
        at, way = self.at(j, p), 1 + p
        for kind in (1, 0):
            ref = self.near.at[kind, at]
            self.loads[kind, j, p].wait()
            arrived(ref, self.recv_sem.at[kind, at])

            def total(kind=kind, ref=ref):
                return ref[...].astype(jnp.float32) + self.mine(kind, j, p)

            if j < 3:
                self.along(kind, 2 + kind, j, p, ref, total)
            elif kind:
                self.owned(kind, p, total, self.total)
                ref[...] = self.total[...].astype(jnp.bfloat16)
                self.go(
                    2, at, ref, self.last.at[p], self.recv_sem.at[2, p], self.place.device(way, 0)
                )
            else:
                self.owned(kind, p, total, out)
        if j == 3:
            arrived(self.last.at[p], self.recv_sem.at[2, p])
            out[...] += self.last[p].astype(jnp.float32)


def tail_kernel(
    pack_task, task_experts, tok, cot, segments, proj, heads, middle, dense, grad_part, mixed_part,
    d_in, d_out_far, got_y, got_x,
    mixed, d_tok, d_dense, d_in_all, d_out_all,
    g_own, g_corner, g_x, g_y, g_z, m_own, m_near, m_last, m_z, m_total, m_out,
    total_grad, grad_mid, grad_heads, grad_qkv, acc, small_rows, turned, flat_ids, tall_ids,
    in_far, in_mine, far_dense, got_dense, part_dense, s_corner, s_x, s_y, s_z,
    g_send, g_recv, gz_recv, m_send, m_recv, mz_recv, s_send, s_recv, in_send, in_recv,
    pair_send, pair_recv, load_sem,
):
    place = Place()
    width = tok.shape[2]
    place.greet()

    loads = []

    def load(src, dst):
        copy = pltpu.make_async_copy(src, dst, load_sem.at[len(loads)])
        copy.start()
        loads.append(copy)
        return copy

    grads = PlaneFirst(
        place, grad_part, g_own, g_z, (g_send, g_recv, gz_recv), load, g_corner, g_x, g_y,
        (got_y, got_x),
    )
    in_load = load(d_in.at[place.core], in_mine)
    mixes = SideFirst(
        place, mixed_part, m_own, m_z, (m_send, m_recv, mz_recv), load, m_near, m_last, m_total
    )
    pair_started, in_started, kept = [], [], {}
    planes = (2, 1, 3, 0)

    same_documents(segments, flat_ids, tall_ids)
    small = dense[:, :, 4 * width : 4 * width + SIDE].reshape(width, SIDE)
    turned[...] = jnp.transpose(small.astype(jnp.float32))
    small_rows[...] = jnp.zeros_like(small_rows)
    gain_one, bias_one, gain_two, bias_two = (
        turned[GAIN_ONE + i : GAIN_ONE + i + 1, :] for i in range(4)
    )

    def pair():
        send(
            pair_started, d_in.at[1 - place.core], in_far, pair_send.at[0], pair_recv.at[0],
            place.sibling,
        )
        send(
            pair_started, d_out_far, d_out_all, pair_send.at[1], pair_recv.at[1], place.sibling
        )

    def addpair():
        in_load.wait()
        arrived(in_far, pair_recv.at[0])

        def one(i, carry):
            total = in_mine[i].astype(jnp.float32) + in_far[i].astype(jnp.float32)
            in_mine[i] = total.astype(jnp.bfloat16)
            return carry

        lax.fori_loop(0, in_mine.shape[0], one, 0)
        columns = pl.ds(pl.multiple_of(place.chip(0, 0) * SIDE, SIDE), SIDE)
        kept["local"] = load(in_mine.at[place.chip(0, 0)], d_in_all.at[:, :, columns])

    def win(rel, j):
        k = planes[j]
        columns = pl.ds(pl.multiple_of(place.chip(0, 0) * SIDE, SIDE), SIDE)
        send(
            in_started, in_mine.at[place.chip(rel, k)], d_in_all.at[:, :, columns],
            in_send.at[rel, k], in_recv.at[rel, back(k)], place.device(rel, k),
        )

    def mplane(j, p):
        mixes.plane(j, p, m_out)
        if j == 3:
            mixed[p] = (middle[p] + m_out[...]).astype(jnp.bfloat16)

    def add_to(p, columns, value):
        if p == 0:
            acc[:, columns] = value
        else:
            acc[:, columns] += value

    def add_row(at, value):
        small_rows[at : at + 1, :] += jnp.sum(value, 0, keepdims=True)

    def att(part):
        p = part // 3
        (att_routed, att_heads, att_normed)[part % 3](p)

    def att_routed(p):
        first, second = place.pair(pack_task, task_experts, 0, 0, p)
        got = total_grad[p]
        tall = jnp.concatenate(
            [got[PACK:, : 2 * SIDE], jnp.zeros((SIDE - 8, 2 * SIDE), jnp.float32)], axis=0
        )
        gap_grad = jnp.transpose(tall)[:ROWS, 0:1]
        got = jnp.where(real_rows(), got, 0.0)
        mid = middle[p]
        unit, rise = norm_parts(mid)
        routed = jnp.where(real_rows(), unit * gain_two + bias_two, 0.0).astype(jnp.bfloat16)
        route = dense[:, :, 4 * width : 4 * width + SIDE].reshape(width, SIDE)
        gate_a, gate_b = two_gates(dot(routed, route), first, second)
        grad_a = gate_a * gate_b * gap_grad
        lane = lax.broadcasted_iota(jnp.int32, (ROWS, SIDE), 1)
        grad_logits = jnp.where(lane == first, grad_a, jnp.where(lane == second, -grad_a, 0.0))
        grad_logits = jnp.where(real_rows(), grad_logits, 0.0).astype(jnp.bfloat16)
        add_to(p, pl.ds(4 * width, SIDE), contract_rows(routed, grad_logits))
        got = got + contract_cols(grad_logits, route)
        add_row(2, got * unit)
        add_row(3, got)
        u = got * gain_two
        grad_middle = lengthened(cot, p) + rise * (
            u - jnp.mean(u, -1, keepdims=True) - unit * jnp.mean(u * unit, -1, keepdims=True)
        )
        grad_mid[...] = grad_middle
        attended = grad_middle.astype(jnp.bfloat16)
        add_to(p, pl.ds(3 * width, width), contract_rows(heads[p], attended))
        w_attn = dense[:, :, 3 * width : 4 * width].reshape(width, width)
        grad_heads[...] = contract_cols(attended, w_attn).astype(jnp.bfloat16)

    def att_heads(p):
        same = same_document(flat_ids, tall_ids, p)

        def pair_of_heads(j, carry):
            at = pl.multiple_of(j * SIDE, SIDE)
            queries = proj[p, :, pl.ds(at, SIDE)]
            keys = proj[p, :, pl.ds(at + width, SIDE)]
            values = proj[p, :, pl.ds(at + 2 * width, SIDE)]
            out_grad = grad_heads[:, pl.ds(at, SIDE)]
            zero = jnp.zeros((ROWS, SIDE), jnp.float32)
            grad_q, grad_k, grad_v = zero, zero, zero
            for h in range(2):
                lanes = head_lanes(h)
                probs = softmax_rows(queries * lanes, keys, same)
                mine_grad = out_grad * lanes
                grad_v = grad_v + contract_rows(probs.astype(jnp.bfloat16), mine_grad)
                grad_probs = contract_cols(mine_grad, values)
                row_dot = jnp.sum(probs * grad_probs, -1, keepdims=True)
                grad_scores = (probs * (grad_probs - row_dot)).astype(jnp.bfloat16)
                grad_q = grad_q + dot(grad_scores, keys * lanes)
                grad_k = grad_k + contract_rows(grad_scores, queries * lanes)
            scale = 1.0 / math.sqrt(HEAD)
            grad_qkv[:, pl.ds(at, SIDE)] = (grad_q * scale).astype(jnp.bfloat16)
            grad_qkv[:, pl.ds(at + width, SIDE)] = (grad_k * scale).astype(jnp.bfloat16)
            grad_qkv[:, pl.ds(at + 2 * width, SIDE)] = grad_v.astype(jnp.bfloat16)
            return carry

        lax.fori_loop(0, width // SIDE, pair_of_heads, 0)

    def att_normed(p):
        unit, rise = norm_parts(lengthened(tok, p))
        normed = (unit * gain_one + bias_one).astype(jnp.bfloat16)
        add_to(p, pl.ds(0, 3 * width), contract_rows(normed, grad_qkv[...]))
        w_qkv = dense[:, :, : 3 * width].reshape(width, 3 * width)
        grad_normed = contract_cols(grad_qkv[...], w_qkv)
        add_row(0, grad_normed * unit)
        add_row(1, grad_normed)
        u = grad_normed * gain_one
        d_tok[p] = (
            grad_mid[...]
            + rise
            * (u - jnp.mean(u, -1, keepdims=True) - unit * jnp.mean(u * unit, -1, keepdims=True))
        ).astype(jnp.bfloat16)

    def dense_part(rel, k, p):
        return got_dense.at[place.chip(rel, k)]

    sums = Collect(
        place, dense_part, s_corner, s_x, s_y, s_z, 1, lambda k, p: k % 2, (s_send, s_recv)
    )
    def dense_step():
        tall = jnp.concatenate(
            [
                jnp.zeros((GAIN_ONE, width), jnp.float32),
                small_rows[...],
                jnp.zeros((SIDE - GAIN_ONE - 8, width), jnp.float32),
            ],
            axis=0,
        )
        acc[:, 4 * width :] += jnp.transpose(tall)
        columns_all = acc.shape[1]

        def cut(i, carry):
            own_rows = pl.ds(pl.multiple_of(i * 32 + place.core * 16, 16), 16)
            far_rows = pl.ds(pl.multiple_of(i * 32 + 16 - place.core * 16, 16), 16)
            far_dense[i] = acc[far_rows, :].astype(jnp.bfloat16)
            part_dense[i] = acc[own_rows, :]
            return carry

        lax.fori_loop(0, 16, cut, 0)
        send(
            pair_started, far_dense, got_dense, pair_send.at[2], pair_recv.at[2], place.sibling
        )
        arrived(got_dense, pair_recv.at[2])

        def join(i, carry):
            far_dense_sum = part_dense[i] + got_dense[i].astype(jnp.float32)
            got_dense[i] = far_dense_sum.astype(jnp.bfloat16)
            return carry

        lax.fori_loop(0, 16, join, 0)

        for k in (2, 1, 3, 0):
            sums.opposite(k, 0)
        for k in (2, 1, 3, 0):
            sums.straight(k, 0)
        for k in (2, 1, 3, 0):
            sums.helped(k, 0, lambda k=k: got_dense[place.chip(1 + k % 2, k)])
        for k in (2, 1, 3):
            sums.plane(k, 0, lambda k=k: got_dense[place.chip(0, k)])
        d_dense[...] = sums.plane(0, 0, lambda: got_dense[place.chip(0, 0)])

    steps = {
        GFIRST: grads.first, GHELP: grads.helped,
        GPLANE: lambda j, p: grads.plane(j, p, total_grad.at[p]),
        MFIRST: mixes.first, MPLANE: mplane, MHELP: lambda j, p: None,
        PAIR: pair, ADDPAIR: addpair, WIN: win, ATT: att, DENSE: dense_step,
    }
    for name, *where in TAIL_STEPS:
        steps[name](*where)

    for rel in range(4):
        for k in range(4):
            if (rel, k) != (0, 0):
                place_columns = pl.ds(pl.multiple_of(place.chip(rel, k) * SIDE, SIDE), SIDE)
                arrived(d_in_all.at[:, :, place_columns], in_recv.at[rel, k])
    kept["local"].wait()
    arrived(d_out_all, pair_recv.at[1])
    for tree in (grads, mixes, sums):
        tree.finish()
    for copy in pair_started + in_started:
        copy.wait_send()


def last_kernel(
    mixed_tall, d_tok_tall, d_dense, d_in_low, d_out_own, d_out_far,
    mixed, d_tok, d_qkv, d_attn, d_route, d_in, d_out, gain_one, bias_one, gain_two, bias_two,
):
    width, experts = mixed.shape[2], d_route.shape[1]

    @pl.when(pl.program_id(0) == 0)
    def small():
        for p in range(mixed.shape[0]):
            mixed[p] = mixed_tall[p, :PACK]
            d_tok[p] = d_tok_tall[p, :PACK]
        d_qkv[...] = d_dense[:, : 3 * width]
        d_attn[...] = d_dense[:, 3 * width : 4 * width]
        d_route[...] = d_dense[:, 4 * width : 4 * width + experts]
        rows = jnp.transpose(d_dense[:, 4 * width :])
        for i, ref in enumerate((gain_one, bias_one, gain_two, bias_two)):
            ref[...] = rows[GAIN_ONE + i]

    d_in[...] = d_in_low[...].astype(jnp.float32)
    d_out[...] = d_out_own[...] + d_out_far[...].astype(jnp.float32)


def shards_fast(
    tokens,
    segment_ids,
    pack_task,
    task_experts,
    w_qkv,
    w_attn_out,
    w_router,
    w_expert_in,
    w_expert_out,
    norm1_gain,
    norm1_bias,
    norm2_gain,
    norm2_bias,
    cotangent,
):
    packs, length, width = tokens.shape
    experts, slab_in, hidden = w_expert_in.shape
    slab_out = w_expert_out.shape[1]
    dense_width = 4 * width + SIDE
    any_space = pl.BlockSpec(memory_space=pl.ANY)
    vmem = pl.BlockSpec(memory_space=pltpu.VMEM)
    smem = pl.BlockSpec(memory_space=pltpu.SMEM)
    low, full = jnp.bfloat16, jnp.float32
    flat = jax.ShapeDtypeStruct
    dma = pltpu.SemaphoreType.DMA

    z, g = lax.axis_index("gx"), lax.axis_index("gy")
    where = jnp.stack([z, g, g % 2])

    blocks = flat((4, 4 * packs, ROWS, width), low)
    in_sums = flat((4, 4 * packs, width, 2 * SIDE), low)
    out_sums = flat((4, 4 * packs, 2 * SIDE, width), low)

    def held(shape):
        return pltpu.VMEM(shape.shape, shape.dtype)

    early_blocks = flat((len(EARLY), ROWS, width), low)
    (
        in_terms, out_terms, mixed_part, grad_part, dense, early_y, early_x, proj, heads, middle,
    ) = pl.pallas_call(
        front_kernel,
        out_shape=(
            in_sums, out_sums, blocks, blocks,
            flat((32, slab_in, dense_width), low),
            early_blocks, early_blocks,
            flat((packs, ROWS, 3 * width), low),
            flat((packs, ROWS, width), low),
            flat((packs, ROWS, width), full),
        ),
        in_specs=[smem] * 2 + [vmem] * 10 + [any_space] * 2,
        out_specs=(any_space,) * 7 + (vmem,) * 3,
        scratch_shapes=[
            pltpu.VMEM((32, slab_in, dense_width), low),
            held(blocks), held(blocks),
            pltpu.VMEM((16, 2, experts, slab_in, SIDE), low),
            pltpu.VMEM((2, experts, slab_out, width), low),
            pltpu.VMEM((2, 4, width, 2 * SIDE), low),
            pltpu.VMEM((2, 4, 2 * SIDE, width), low),
            held(blocks), held(blocks),
            pltpu.VMEM((SIDE, width), full),
            pltpu.VMEM((SIDE, SIDE), full),
            pltpu.VMEM((8, 2 * SIDE), full),
            pltpu.VMEM((2 * SIDE, 8), full),
            pltpu.VMEM((8, width), full),
            dma((7, 8)), dma((4, 8)), dma((5, 8)), dma((4, 8)), dma((5, 4)), dma((4, 4)),
            dma((4, 4)), dma((4, 4)), dma((4, 4)), dma((4, 4)), dma((2,)), dma((2,)), dma((3,)),
            dma((32,)), dma((2, len(EARLY))),
        ],
        compiler_params=pltpu.CompilerParams(
            collective_id=0, has_side_effects=True, vmem_limit_bytes=60 << 20
        ),
        name="front",
    )(
        pack_task, task_experts, tokens, segment_ids, w_qkv, w_attn_out, w_router,
        norm1_gain, norm1_bias, norm2_gain, norm2_bias, cotangent, w_expert_in, w_expert_out,
    )

    across = lax.axis_size("gy")
    got_y = lax.ppermute(early_y, "gy", [(i, i ^ 4) for i in range(across)])
    got_x = lax.ppermute(early_x, "gy", [(i, i ^ 2) for i in range(across)])

    def by_expert(rows):
        return pl.BlockSpec((experts // 8, rows, width), lambda e, *unused: (e, 0, 0))

    d_in, d_out_own, d_out_far = pl.pallas_call(
        sum_kernel,
        grid_spec=pltpu.PrefetchScalarGridSpec(
            num_scalar_prefetch=3,
            grid=(8,),
            in_specs=[vmem] * 2,
            out_specs=[
                pl.BlockSpec((2, 16, experts // 8, slab_in, SIDE), lambda e, *unused: (0, 0, e, 0, 0)),
                by_expert(slab_out), by_expert(slab_out),
            ],
            scratch_shapes=[
                pltpu.SMEM((experts,), jnp.int32),
                pltpu.SMEM((32 * packs,), jnp.int32),
                pltpu.VMEM((width, SIDE), full),
                pltpu.VMEM((SIDE, width), full),
            ],
        ),
        out_shape=(
            flat((2, 16, experts, slab_in, SIDE), low),
            flat((experts, slab_out, width), full),
            flat((experts, slab_out, width), low),
        ),
        compiler_params=pltpu.CompilerParams(vmem_limit_bytes=60 << 20),
        cost_estimate=pl.CostEstimate(
            flops=10**10, bytes_accessed=40 * 10**6, transcendentals=0
        ),
        name="sums",
    )(pack_task, task_experts, where, in_terms, out_terms)

    parts = pltpu.VMEM((4 * packs, ROWS, width), low)
    slices = pltpu.VMEM((4, slab_in, dense_width), low)
    sliced = pltpu.VMEM((16, slab_in, dense_width), low)
    mixed_tall, d_tok_tall, d_dense, d_in_all, d_out_all = pl.pallas_call(
        tail_kernel,
        out_shape=(
            flat((packs, ROWS, width), low),
            flat((packs, ROWS, width), low),
            flat((slab_in, dense_width), full),
            flat((experts, slab_in, hidden), low),
            flat((experts, slab_out, width), low),
        ),
        in_specs=[smem] * 2 + [vmem] * 7 + [any_space] * 6,
        out_specs=(vmem,) * 3 + (any_space,) * 2,
        scratch_shapes=[
            pltpu.VMEM((2, 4 * packs, ROWS, width), low), parts, parts, parts,
            pltpu.VMEM((1, 5 * packs, ROWS, width), low),
            pltpu.VMEM((2, 4 * packs, ROWS, width), low),
            pltpu.VMEM((2, 4 * packs, ROWS, width), low),
            pltpu.VMEM((packs, ROWS, width), low),
            pltpu.VMEM((2, 5 * packs, ROWS, width), low),
            pltpu.VMEM((ROWS, width), full),
            pltpu.VMEM((ROWS, width), full),
            pltpu.VMEM((packs, ROWS, width), full),
            pltpu.VMEM((ROWS, width), full),
            pltpu.VMEM((ROWS, width), low),
            pltpu.VMEM((ROWS, 3 * width), low),
            pltpu.VMEM((width, dense_width), full),
            pltpu.VMEM((8, width), full),
            pltpu.VMEM((SIDE, width), full),
            pltpu.VMEM((8, 2 * SIDE), full),
            pltpu.VMEM((2 * SIDE, 8), full),
            pltpu.VMEM((16, experts, slab_in, SIDE), low),
            pltpu.VMEM((16, experts, slab_in, SIDE), low),
            sliced, sliced,
            pltpu.VMEM((16, slab_in, dense_width), full),
            slices, slices, slices, slices,
            dma((4, 8)), dma((4, 8)), dma((1, 10)), dma((4, 8)), dma((4, 8)), dma((2, 10)),
            dma((4, 4)), dma((4, 4)), dma((4, 4)), dma((4, 4)), dma((3,)), dma((3,)), dma((48,)),
        ],
        compiler_params=pltpu.CompilerParams(
            collective_id=1, has_side_effects=True, vmem_limit_bytes=60 << 20
        ),
        name="tail",
    )(
        pack_task, task_experts, tokens, cotangent, segment_ids, proj, heads, middle, dense,
        grad_part, mixed_part, d_in, d_out_far, got_y, got_x,
    )

    group = experts // 2

    def some(rows, columns):
        return pl.BlockSpec((group, rows, columns), lambda i: (i, 0, 0))

    def whole(*shape):
        return pl.BlockSpec(shape, lambda i: (0,) * len(shape))

    return pl.pallas_call(
        last_kernel,
        grid=(2,),
        in_specs=[
            whole(packs, ROWS, width), whole(packs, ROWS, width), whole(slab_in, dense_width),
            some(slab_in, hidden), some(slab_out, width), some(slab_out, width),
        ],
        out_specs=(
            whole(packs, length, width), whole(packs, length, width),
            whole(slab_in, 3 * width), whole(slab_in, width), whole(slab_in, experts),
            some(slab_in, hidden), some(slab_out, width),
        ) + (whole(slab_in),) * 4,
        out_shape=(
            flat((packs, length, width), low), flat((packs, length, width), low),
            flat((slab_in, 3 * width), full), flat((slab_in, width), full),
            flat((slab_in, experts), full),
            flat((experts, slab_in, hidden), full), flat((experts, slab_out, width), full),
        ) + (flat((slab_in,), full),) * 4,
        compiler_params=pltpu.CompilerParams(vmem_limit_bytes=60 << 20),
        name="last",
    )(mixed_tall, d_tok_tall, d_dense, d_in_all, d_out_own, d_out_all)


def solution(mesh):
    outer, inner = mesh.shape["gx"], mesh.shape["gy"]

    def shards(*arrays):
        packs, length, width = arrays[0].shape
        experts, slab_in, hidden = arrays[7].shape
        fits = (
            (outer, inner) == (4, 8)
            and packs == 2
            and length == PACK
            and experts == GAIN_ONE
            and width == HEADS * HEAD
            and slab_in == 16
            and hidden == 16 * SIDE
        )
        return (shards_fast if fits else shards_any)(*arrays)

    placed = (
        P(("gx", "gy"), None, None),
        P(("gx", "gy"), None),
        P(),
        P(),
        P(("gx", "gy"), None),
        P(("gx", "gy"), None),
        P(("gx", "gy"), None),
        P(None, ("gx", "gy"), None),
        P(None, ("gx", "gy"), None),
        P(("gx", "gy")),
        P(("gx", "gy")),
        P(("gx", "gy")),
        P(("gx", "gy")),
        P(("gx", "gy"), None, None),
    )
    return jax.shard_map(
        shards,
        mesh=mesh,
        in_specs=placed,
        out_specs=(
            P(("gx", "gy"), None, None),
            P(("gx", "gy"), None, None),
            P(("gx", "gy"), None),
            P(("gx", "gy"), None),
            P(("gx", "gy"), None),
            P(None, ("gx", "gy"), None),
            P(None, ("gx", "gy"), None),
            P(("gx", "gy")),
            P(("gx", "gy")),
            P(("gx", "gy")),
            P(("gx", "gy")),
        ),
        check_vma=False,
    )
```

```python
import functools
import math

import jax
import jax.numpy as jnp
from jax import lax
from jax.experimental import pallas as pl
from jax.experimental.pallas import tpu as pltpu
from jax.sharding import PartitionSpec as P

HEADS = 8
HEAD = 64
PACK = 216
GAIN_ONE = 32


EPS = 1e-05
MASK_FILL = -1e30
HIGH = lax.Precision.HIGHEST


def shortened(value):

    def short(part):
        return part.astype(jnp.bfloat16) if part.dtype == jnp.float32 else part

    return jax.tree.map(short, value)


def layer_norm(values, gain, bias):
    center = values - jnp.mean(values, -1, keepdims=True)
    spread = jnp.mean(center * center, -1, keepdims=True)
    return center * lax.rsqrt(spread + EPS) * gain + bias


def contract_rows(left, right):
    return lax.dot_general(
        left, right, (((0,), (0,)), ((), ())), preferred_element_type=jnp.float32
    )


def contract_cols(left, right):
    return lax.dot_general(
        left, right, (((1,), (1,)), ((), ())), preferred_element_type=jnp.float32
    )


def shards_any(
    tokens,
    segment_ids,
    pack_task,
    task_experts,
    w_qkv,
    w_attn_out,
    w_router,
    w_expert_in,
    w_expert_out,
    norm1_gain,
    norm1_bias,
    norm2_gain,
    norm2_bias,
    cotangent,
):
    outer = lax.axis_size("gx")
    inner = lax.axis_size("gy")
    devices = outer * inner
    micro, length, width = tokens.shape
    experts, slab_in, hidden = w_expert_in.shape
    slab_out = w_expert_out.shape[1]
    head_size = width // HEADS
    scale = 1.0 / math.sqrt(head_size)
    device = lax.axis_index("gx") * inner + lax.axis_index("gy")
    gathered = (
        lax.all_gather(w_qkv, ("gx", "gy"), axis=0, tiled=True),
        lax.all_gather(w_attn_out, ("gx", "gy"), axis=0, tiled=True),
        lax.all_gather(w_router, ("gx", "gy"), axis=0, tiled=True),
        lax.all_gather(norm1_gain, ("gx", "gy"), axis=0, tiled=True),
        lax.all_gather(norm1_bias, ("gx", "gy"), axis=0, tiled=True),
        lax.all_gather(norm2_gain, ("gx", "gy"), axis=0, tiled=True),
        lax.all_gather(norm2_bias, ("gx", "gy"), axis=0, tiled=True),
    )
    qkv_full, attn_full, route_full = (gathered[0], gathered[1], gathered[2])
    gain_one, bias_one, gain_two, bias_two = tuple(
        (piece.astype(jnp.float32) for piece in gathered[3:])
    )
    route_float = route_full.astype(jnp.float32)
    pack_pairs = task_experts[pack_task]
    needs = jnp.transpose(pack_pairs.reshape(outer, inner, micro, 2), (2, 3, 0, 1))
    route_pairs = jnp.transpose(pack_pairs.reshape(devices, micro, 2), (1, 0, 2))
    own_pairs = lax.dynamic_slice_in_dim(pack_pairs, device * micro, micro, 0)
    expert_ids = jnp.arange(experts, dtype=jnp.int32)

    def slabs(need):
        return (w_expert_in[need], w_expert_out[need])

    def joined(pieces):
        return (
            pieces[0].reshape(pieces[0].shape[0], width, hidden),
            pieces[1].reshape(pieces[1].shape[0], hidden, width),
        )

    def attention_probs(project, segment):
        queries = project[:, :width].reshape(length, HEADS, head_size)
        keys_all = project[:, width : 2 * width].reshape(length, HEADS, head_size)
        scores = (
            jnp.einsum("qhd,khd->hqk", queries, keys_all, preferred_element_type=jnp.float32)
            * scale
        )
        same_doc = segment[:, None] == segment[None, :]
        return jnp.where(same_doc[None], scores, MASK_FILL)

    def forward_step(carry, inputs):
        block, segment, need, pair, senders = inputs
        block_float = block.astype(jnp.float32)
        normed = layer_norm(block_float, gain_one, bias_one).astype(jnp.bfloat16)
        project = jnp.dot(normed, qkv_full, preferred_element_type=jnp.float32).astype(jnp.bfloat16)
        masked = attention_probs(project, segment)
        peak = jnp.max(masked, -1, keepdims=True)
        raised = jnp.exp(masked - peak)
        totals = jnp.sum(raised, -1, keepdims=True)
        log_total = peak + jnp.log(totals)
        attn_low = (raised / totals).astype(jnp.bfloat16)
        values_all = project[:, 2 * width :].reshape(length, HEADS, head_size)
        heads_out = (
            jnp.einsum("hqk,khd->qhd", attn_low, values_all, preferred_element_type=jnp.float32)
            .reshape(length, width)
            .astype(jnp.bfloat16)
        )
        middle = block_float + jnp.dot(heads_out, attn_full, preferred_element_type=jnp.float32)
        routed = layer_norm(middle, gain_two, bias_two).astype(jnp.bfloat16)
        logits = jnp.dot(routed, route_full, preferred_element_type=jnp.float32)
        select = (expert_ids[None, :] == pair[:, None]).astype(jnp.float32)
        chosen = jnp.sum(logits[:, None, :] * select[None], -1)
        raised_gate = jnp.exp(chosen - jnp.max(chosen, -1, keepdims=True))
        gates = raised_gate / jnp.sum(raised_gate, -1, keepdims=True)
        weights_in, weights_out = joined(
            lax.all_to_all(
                lax.all_to_all(
                    shortened(slabs(need)), "gx", split_axis=1, concat_axis=1, tiled=True
                ),
                "gy",
                split_axis=2,
                concat_axis=2,
                tiled=True,
            )
        )
        hidden_pre = jnp.einsum(
            "ld,kdf->klf", routed, weights_in, preferred_element_type=jnp.float32
        )
        hidden_low = jax.nn.gelu(hidden_pre).astype(jnp.bfloat16)
        expert_out = jnp.einsum(
            "klf,kfd->kld", hidden_low, weights_out, preferred_element_type=jnp.float32
        )
        saved = ()
        mixed = middle + gates[:, 0:1] * expert_out[0] + gates[:, 1:2] * expert_out[1]
        kept = (
            normed,
            project,
            log_total,
            heads_out,
            middle,
            routed,
            gates,
            hidden_pre,
            hidden_low,
            expert_out,
            saved,
        )
        return (carry, (mixed.astype(jnp.bfloat16), kept))

    start = jnp.zeros((), jnp.float32)
    unused, (mixed_all, kept_all) = lax.scan(
        forward_step, start, (tokens, segment_ids, needs, own_pairs, route_pairs)
    )

    def backward_step(carry, inputs):
        dense_acc, shard_in, shard_out, holding = carry
        block, grad_top, segment, need, pair, kept = inputs
        (
            normed,
            project,
            log_total,
            heads_out,
            middle,
            routed,
            gates,
            hidden_pre,
            hidden_low,
            expert_out,
            saved,
        ) = kept
        grad_float = grad_top.astype(jnp.float32)
        grad_gate = jnp.sum(grad_float[None] * expert_out, -1).T
        grad_chosen = gates * (grad_gate - jnp.sum(gates * grad_gate, -1, keepdims=True))
        select = (expert_ids[None, :] == pair[:, None]).astype(jnp.float32)
        grad_logits = jnp.sum(grad_chosen[:, :, None] * select[None], 1)
        routed_float = routed.astype(jnp.float32)
        grad_route = jnp.dot(routed_float.T, grad_logits, precision=HIGH)
        grad_routed = jnp.dot(grad_logits, route_float.T, precision=HIGH)
        grad_eout = (gates.T[:, :, None] * grad_float[None]).astype(jnp.bfloat16)
        slot = ()
        weights_in, weights_out = joined(
            lax.all_to_all(
                lax.all_to_all(
                    shortened(slabs(need)), "gx", split_axis=1, concat_axis=1, tiled=True
                ),
                "gy",
                split_axis=2,
                concat_axis=2,
                tiled=True,
            )
        )
        grad_act = jnp.einsum(
            "kld,kfd->klf", grad_eout, weights_out, preferred_element_type=jnp.float32
        )
        unused_act, gelu_back = jax.vjp(jax.nn.gelu, hidden_pre)
        grad_pre = gelu_back(grad_act)[0].astype(jnp.bfloat16)
        grad_in = jnp.einsum("ld,klf->kdf", routed, grad_pre, preferred_element_type=jnp.float32)
        grad_out = jnp.einsum(
            "klf,kld->kfd", hidden_low, grad_eout, preferred_element_type=jnp.float32
        )
        grad_routed = grad_routed + jnp.einsum(
            "klf,kdf->ld", grad_pre, weights_in, preferred_element_type=jnp.float32
        )
        slot = (grad_in, grad_out)
        unused_two, norm_two_back = jax.vjp(layer_norm, middle, gain_two, bias_two)
        grad_mid_norm, grad_gain_two, grad_bias_two = norm_two_back(grad_routed)
        grad_middle = grad_float + grad_mid_norm
        grad_attended = grad_middle.astype(jnp.bfloat16)
        grad_attn_w = contract_rows(heads_out, grad_attended)
        grad_heads = (
            contract_cols(grad_attended, attn_full)
            .astype(jnp.bfloat16)
            .reshape(length, HEADS, head_size)
        )
        masked = attention_probs(project, segment)
        probs_float = jnp.exp(masked - log_total)
        probs_low = probs_float.astype(jnp.bfloat16)
        queries = project[:, :width].reshape(length, HEADS, head_size)
        keys_all = project[:, width : 2 * width].reshape(length, HEADS, head_size)
        values_all = project[:, 2 * width :].reshape(length, HEADS, head_size)
        grad_values = jnp.einsum(
            "hqk,qhd->khd", probs_low, grad_heads, preferred_element_type=jnp.float32
        )
        grad_probs = jnp.einsum(
            "qhd,khd->hqk", grad_heads, values_all, preferred_element_type=jnp.float32
        )
        row_dot = jnp.sum(probs_float * grad_probs, -1, keepdims=True)
        grad_scores = (probs_float * (grad_probs - row_dot)).astype(jnp.bfloat16)
        grad_queries = (
            jnp.einsum("hqk,khd->qhd", grad_scores, keys_all, preferred_element_type=jnp.float32)
            * scale
        )
        grad_keys = (
            jnp.einsum("hqk,qhd->khd", grad_scores, queries, preferred_element_type=jnp.float32)
            * scale
        )
        grad_qkv = jnp.concatenate(
            [
                grad_queries.reshape(length, width),
                grad_keys.reshape(length, width),
                grad_values.reshape(length, width),
            ],
            -1,
        ).astype(jnp.bfloat16)
        grad_qkv_w = contract_rows(normed, grad_qkv)
        grad_normed = contract_cols(grad_qkv, qkv_full)
        unused_one, norm_one_back = jax.vjp(
            layer_norm, block.astype(jnp.float32), gain_one, bias_one
        )
        grad_in_norm, grad_gain_one, grad_bias_one = norm_one_back(grad_normed)
        grad_tokens = (grad_middle + grad_in_norm).astype(jnp.bfloat16)
        terms = (
            grad_qkv_w,
            grad_attn_w,
            grad_route,
            grad_gain_one,
            grad_bias_one,
            grad_gain_two,
            grad_bias_two,
        )
        dense_acc = tuple((total + term for total, term in zip(dense_acc, terms)))
        return ((dense_acc, shard_in, shard_out, holding), (grad_tokens, slot))

    dense_zero = (
        jnp.zeros((width, 3 * width), jnp.float32),
        jnp.zeros((width, width), jnp.float32),
        jnp.zeros((width, experts), jnp.float32),
        jnp.zeros((width,), jnp.float32),
        jnp.zeros((width,), jnp.float32),
        jnp.zeros((width,), jnp.float32),
        jnp.zeros((width,), jnp.float32),
    )
    shard_zero_in = jnp.zeros((experts, slab_in, hidden), jnp.float32)
    shard_zero_out = jnp.zeros((experts, slab_out, width), jnp.float32)
    holding_zero = ()
    (dense_acc, shard_in, shard_out, holding), (grad_tokens_all, slots) = lax.scan(
        backward_step,
        (dense_zero, shard_zero_in, shard_zero_out, holding_zero),
        (tokens, cotangent, segment_ids, needs, own_pairs, kept_all),
    )
    slot_in = slots[0].reshape(micro * 2, width, hidden)
    slot_out = slots[1].reshape(micro * 2, hidden, width)
    amount = slot_in.shape[0]
    returned = lax.all_to_all(
        lax.all_to_all(
            shortened(
                (
                    slot_in.reshape(amount, outer, inner, slab_in, hidden),
                    slot_out.reshape(amount, outer, inner, slab_out, width),
                )
            ),
            "gx",
            split_axis=1,
            concat_axis=1,
            tiled=True,
        ),
        "gy",
        split_axis=2,
        concat_axis=2,
        tiled=True,
    )
    onehot = (
        needs.reshape(micro * 2, outer, inner)[None] == expert_ids[:, None, None, None]
    ).astype(jnp.float32)
    added = tuple(
        (jnp.einsum("esab,sabrc->erc", onehot, piece, precision=HIGH) for piece in returned)
    )
    shard_in = shard_in + added[0]
    shard_out = shard_out + added[1]
    dense_shards = (
        lax.psum_scatter(dense_acc[0], ("gx", "gy"), scatter_dimension=0, tiled=True),
        lax.psum_scatter(dense_acc[1], ("gx", "gy"), scatter_dimension=0, tiled=True),
        lax.psum_scatter(dense_acc[2], ("gx", "gy"), scatter_dimension=0, tiled=True),
        lax.psum_scatter(dense_acc[3], ("gx", "gy"), scatter_dimension=0, tiled=True),
        lax.psum_scatter(dense_acc[4], ("gx", "gy"), scatter_dimension=0, tiled=True),
        lax.psum_scatter(dense_acc[5], ("gx", "gy"), scatter_dimension=0, tiled=True),
        lax.psum_scatter(dense_acc[6], ("gx", "gy"), scatter_dimension=0, tiled=True),
    )
    return (
        mixed_all,
        grad_tokens_all,
        dense_shards[0],
        dense_shards[1],
        dense_shards[2],
        shard_in,
        shard_out,
        dense_shards[3],
        dense_shards[4],
        dense_shards[5],
        dense_shards[6],
    )


MESH = pl.DeviceIdType.MESH
ROWS = 224
SIDE = 128
ROOT2PI = math.sqrt(2.0 / math.pi)


(
    DOWN, DPLANE, DCORNER, DLAST, DWAIT, ATT, WIN, WO, WINWAIT, WSIBWAIT, WAVE, COWN,
    CPLANE, CCORNER, CNEAR, CMZ, RPLANE, RCORNER, GFIRST, MFIRST, GHELP, MHELP, GPLANE, MPLANE, PAIR, ADDPAIR, DENSE,
) = range(27)

SIDE_PACKS = (0, 1)

EARLY = ((0, 3), (1, 3))

FRONT_STEPS = (
    (DOWN,), (WIN, 3, 2), (WIN, 2, 0), (COWN, 1), (COWN, 0), (DPLANE, 1), (CMZ, 0, 1, 1), (WIN, 0, 2),
    (DPLANE, 2), (DPLANE, 3), (CNEAR, 1), (CNEAR, 0), (WIN, 0, 1), (WIN, 1, 1), (CMZ, 0, 1, 0), (WIN, 1, 3),
    (WIN, 1, 0), (WO,), (DCORNER, 0), (DCORNER, 1), (DCORNER, 3), (DCORNER, 2), (WIN, 3, 0), (DLAST, 0),
    (CMZ, 1, 1, 1), (WIN, 2, 1), (CMZ, 1, 1, 0), (WIN, 2, 2), (DLAST, 3), (CMZ, 0, 2, 0), (WIN, 2, 3),
    (WIN, 3, 1), (CMZ, 0, 2, 1), (DLAST, 1), (DLAST, 2), (DWAIT,), (WIN, 1, 2), (ATT, 0), (RCORNER, 0, 0),
    (ATT, 1), (RPLANE, 1, 0), (CMZ, 1, 2, 1), (WIN, 3, 3), (RPLANE, 1, 1), (WIN, 0, 3), (RCORNER, 0, 1),
    (RCORNER, 1, 0), (WINWAIT,), (RPLANE, 2, 1), (RPLANE, 2, 0), (RCORNER, 1, 1), (CMZ, 1, 2, 0), (WSIBWAIT,),
    (WAVE, 0, 0), (CMZ, 0, 3, 0), (WAVE, 1, 0), (RCORNER, 2, 1), (RPLANE, 3, 1), (WAVE, 1, 1),
    (RCORNER, 2, 0), (RPLANE, 3, 0), (WAVE, 0, 1), (CMZ, 1, 3, 0), (CMZ, 0, 3, 1), (RCORNER, 3, 1),
    (WAVE, 2, 1), (CMZ, 1, 3, 1), (RCORNER, 3, 0), (WAVE, 2, 0), (WAVE, 3, 0), (WAVE, 3, 1),
)
TAIL_STEPS = (
    (GFIRST, 0, 0), (MHELP, 2, 0), (GFIRST, 1, 0), (MHELP, 3, 0), (PAIR,), (GHELP, 0, 0), (GFIRST, 0, 1),
    (GHELP, 1, 0), (GHELP, 0, 1), (GFIRST, 2, 0), (ADDPAIR,), (WIN, 0, 1), (GFIRST, 1, 1), (GFIRST, 2, 1),
    (GPLANE, 0, 0), (MFIRST, 0, 1), (GHELP, 1, 1), (MFIRST, 0, 0), (GPLANE, 0, 1), (GPLANE, 1, 0),
    (WIN, 0, 0), (MHELP, 2, 1), (GFIRST, 3, 1), (GHELP, 2, 1), (GHELP, 2, 0), (GPLANE, 1, 1), (GFIRST, 3, 0),
    (MFIRST, 1, 1), (MHELP, 3, 1), (MPLANE, 0, 0), (GPLANE, 2, 1), (MFIRST, 1, 0), (GHELP, 3, 0),
    (MPLANE, 0, 1), (MHELP, 0, 1), (GPLANE, 2, 0), (MFIRST, 2, 0), (MPLANE, 1, 0), (MFIRST, 2, 1),
    (MFIRST, 3, 1), (GHELP, 3, 1), (MPLANE, 1, 1), (WIN, 3, 1), (MPLANE, 2, 0), (GPLANE, 3, 0), (WIN, 1, 0),
    (GPLANE, 3, 1), (MFIRST, 3, 0), (ATT, 0), (WIN, 3, 3), (ATT, 1), (MPLANE, 2, 1), (ATT, 2), (MHELP, 0, 0),
    (MHELP, 1, 0), (MHELP, 1, 1), (ATT, 3), (WIN, 2, 3), (WIN, 1, 2), (WIN, 3, 2), (WIN, 2, 1), (WIN, 2, 2),
    (ATT, 4), (ATT, 5), (MPLANE, 3, 0), (WIN, 1, 1), (WIN, 3, 0), (WIN, 1, 3), (WIN, 2, 0), (WIN, 0, 2),
    (MPLANE, 3, 1), (DENSE,),
)


def dot(left, right):
    return jnp.dot(left, right, preferred_element_type=jnp.float32)


class Place:
    def __init__(self):
        self.z = lax.axis_index("gx")
        g = lax.axis_index("gy")
        self.core = g % 2
        across_x = g + 2 - 4 * ((g // 2) % 2)
        across_y = g + 4 - 8 * (g // 4)
        across_both = across_x + 4 - 8 * (across_x // 4)
        self.at = (g, across_x, across_y, across_both)
        self.step_x, self.step_y = across_x - g, across_y - g
        self.sibling = (self.z, g + 1 - 2 * self.core)

    def plane(self, k):
        return (self.z + k) % 4

    def nearest(self, j):
        z = self.z
        return (0, 1 + 2 * (z // 2), 2 + z - 3 * (z // 2), 3 - z + z // 2)[j]

    def device(self, rel, k):
        return (self.plane(k), self.at[rel])

    def chip(self, rel, k):
        return self.plane(k) * 4 + self.at[rel] // 2

    def index(self, rel, k):
        return self.plane(k) * 8 + self.at[rel]

    def pair(self, pack_task, task_experts, rel, k, p):
        at = self.at[0] + self.step_x * (rel % 2) + self.step_y * (rel // 2)
        task = pack_task[(self.plane(k) * 8 + at) * 2 + p]
        return task_experts[task, 0], task_experts[task, 1]

    def greet(self):
        barrier = pltpu.get_barrier_semaphore()
        others = [(rel, k) for rel in range(4) for k in range(4) if (rel, k) != (0, 0)]
        for rel, k in others:
            pl.semaphore_signal(
                barrier, inc=1, device_id=self.device(rel, k), device_id_type=MESH
            )
        pl.semaphore_signal(barrier, inc=1, device_id=self.sibling, device_id_type=MESH)
        pl.semaphore_wait(barrier, len(others) + 1)


def send(started, src, dst, send_sem, recv_sem, device):
    copy = pltpu.make_async_remote_copy(
        src_ref=src,
        dst_ref=dst,
        send_sem=send_sem,
        recv_sem=recv_sem,
        device_id=device,
        device_id_type=MESH,
    )
    copy.start()
    started.append(copy)


def arrived(ref, sem):
    pltpu.make_async_copy(ref, ref, sem).wait()


def back(k):
    return (4 - k) % 4


class Spread:
    def __init__(self, place, here, there, packs, half, chained, sems):
        self.place, self.here, self.there = place, here, there
        self.packs, self.half, self.chained, self.started = packs, half, chained, []
        self.send_sem, self.recv_sem = sems

    def go(self, kind, at_send, k_there, rel, k, p, src, rel_there, device, only_if=None):
        copy = pltpu.make_async_remote_copy(
            src_ref=src,
            dst_ref=self.there(rel_there, k_there, p, rel, k),
            send_sem=self.send_sem.at[kind, at_send * self.packs + p],
            recv_sem=self.recv_sem.at[kind % 4, k_there * self.packs + p],
            device_id=device,
            device_id_type=MESH,
        )
        if only_if is None:
            copy.start()
        else:
            pl.when(only_if)(copy.start)
        self.started.append((copy, only_if))

    def wait(self, kind, rel, k, p):
        arrived(self.here(rel, k, p), self.recv_sem.at[kind, k * self.packs + p])

    def own(self, p, src):
        place = self.place
        if self.chained:
            self.go(0, 0, 3, 0, 0, p, src, 0, place.device(0, 1), place.z < 3)
            self.go(4, 0, 1, 0, 0, p, src, 0, place.device(0, 3), place.z > 0)
        else:
            for k in (1, 2, 3):
                self.go(0, k, back(k), 0, 0, p, src, 0, place.device(0, k))
        self.go(1, 0, 0, 0, 0, p, src, 1, place.device(1, 0))
        self.go(2, 0, 0, 0, 0, p, src, 2, place.device(2, 0))

    def plane(self, j, p):
        place = self.place
        k = place.nearest(j)
        self.wait(0, 0, k, p)
        src = self.here(0, k, p)
        if self.chained:
            step = 2 * ((place.z - place.plane(k) + 3) // 4) - 1
            goes = (place.z + step >= 0) & (place.z + step <= 3)
            on = (place.plane(step + 4), place.at[0])
            self.go(0, k, (k - step + 4) % 4, 0, k, p, src, 0, on, goes)
        self.go(1, k, k, 0, k, p, src, 1, place.device(1, 0))
        self.go(2, k, k, 0, k, p, src, 2, place.device(2, 0))

    def corner(self, j, p):
        k = self.place.nearest(j)
        rel = 1 + self.half(j, p)
        self.wait(rel, rel, k, p)
        self.go(3, k, k, rel, k, p, self.here(rel, k, p), 3, self.place.device(3 - rel, 0))

    def last(self, j, p):
        k = self.place.nearest(j)
        rel = 2 - self.half(j, p)
        self.wait(rel, rel, k, p)
        self.wait(3, 3, k, p)

    def finish(self):
        for copy, only_if in self.started:
            if only_if is None:
                copy.wait_send()
            else:
                pl.when(only_if)(copy.wait_send)


class SideSpread(Spread):
    def side(self, p):
        return 1 + p

    def along(self, w, rel, k, p, src, first):
        place = self.place
        if first:
            ways = ((2 + w, 3, 1, place.z < 3), (4 + w, 1, 3, place.z > 0))
        else:
            step = 2 * ((place.z - place.plane(k) + 3) // 4) - 1
            goes = (place.z + step >= 0) & (place.z + step <= 3)
            ways = ((2 + w, (k - step + 4) % 4, step + 4, goes),)
        for kind, k_there, on, goes in ways:
            self.go(kind, k, k_there, rel, k, p, src, rel, (place.plane(on), place.at[0]), goes)

    def go(self, kind, at_send, k_there, rel, k, p, src, rel_there, device, only_if=None):
        copy = pltpu.make_async_remote_copy(
            src_ref=src,
            dst_ref=self.there(rel_there, k_there, p, rel, k),
            send_sem=self.send_sem.at[kind, at_send * self.packs + p],
            recv_sem=self.recv_sem.at[rel_there, k_there * self.packs + p],
            device_id=device,
            device_id_type=MESH,
        )
        if only_if is None:
            copy.start()
        else:
            pl.when(only_if)(copy.start)
        self.started.append((copy, only_if))

    def own(self, p, src):
        side, other = self.side(p), 3 - self.side(p)
        self.go(6, 0, 0, 0, 0, p, src, side, self.place.device(side, 0))
        self.along(0, 0, 0, p, src, True)
        self.go(0, 0, 0, 0, 0, p, src, other, self.place.device(other, 0))

    def near(self, p):
        side, other = self.side(p), 3 - self.side(p)
        self.wait(side, side, 0, p)
        src = self.here(side, 0, p)
        self.along(1, side, 0, p, src, True)
        self.go(1, 0, 0, side, 0, p, src, 3, self.place.device(other, 0))

    def passed(self, w, j, p):
        side, other = self.side(p), 3 - self.side(p)
        rel, k = side * w, self.place.nearest(j)
        self.wait(rel, rel, k, p)
        src = self.here(rel, k, p)
        self.along(w, rel, k, p, src, False)
        self.go(w, k, k, rel, k, p, src, 3 if w else other, self.place.device(other, 0))

    def last(self, j, p):
        k = self.place.nearest(j)
        for rel in (3 - self.side(p), 3):
            self.wait(rel, rel, k, p)


def norm_parts(values):
    center = values - jnp.mean(values, -1, keepdims=True)
    spread = jnp.mean(center * center, -1, keepdims=True)
    rise = lax.rsqrt(spread + EPS)
    return center * rise, rise


def real_rows():
    return lax.broadcasted_iota(jnp.int32, (ROWS, 1), 0) < PACK


def head_lanes(h):
    lane = lax.broadcasted_iota(jnp.int32, (1, SIDE), 1)
    inside = (lane >= h * HEAD) & (lane < (h + 1) * HEAD)
    return inside.astype(jnp.bfloat16)


def softmax_rows(queries, keys, same):
    scores = contract_cols(queries, keys) * (1.0 / math.sqrt(HEAD))
    scores = jnp.where(same, scores, MASK_FILL)
    raised = jnp.exp(scores - jnp.max(scores, -1, keepdims=True))
    return raised * (1.0 / jnp.sum(raised, -1, keepdims=True))


def pick(logits, expert):
    lane = lax.broadcasted_iota(jnp.int32, logits.shape, 1)
    return jnp.sum(jnp.where(lane == expert, logits, 0.0), -1, keepdims=True)


def two_gates(logits, first, second):
    gap = pick(logits, second) - pick(logits, first)
    return 1.0 / (1.0 + jnp.exp(gap)), 1.0 / (1.0 + jnp.exp(-gap))


def lengthened(ref, p):
    rows = ref[p].astype(jnp.float32)
    return jnp.concatenate([rows, jnp.zeros((ROWS - PACK, rows.shape[1]), jnp.float32)], axis=0)


def same_documents(segments, flat_ids, tall_ids):
    flat_ids[...] = jnp.full(flat_ids.shape, -1.0, jnp.float32)
    flat_ids[: segments.shape[0], :PACK] = segments[...].astype(jnp.float32)
    tall_ids[...] = jnp.transpose(flat_ids[...])


def same_document(flat_ids, tall_ids, p):
    return tall_ids[:ROWS, p : p + 1] == flat_ids[p : p + 1, :ROWS]


def front_kernel(
    pack_task, task_experts, tok, segments, w_qkv_own, w_attn_own, route_own,
    gain_one_own, bias_one_own, gain_two_own, bias_two_own, cot_own, w_in, w_out,
    in_terms, out_terms, mixed_out, grad_out, dense_out, early_y, early_x, proj, heads, middle,
    dense, routed_all, cot_all, w_in_all, w_out_all, in_stage, out_stage, mixed_all, grad_all,
    turned, square, flat_ids, tall_ids, gate_row,
    cot_send, cot_recv, routed_send, routed_recv, dense_send, dense_recv,
    core_send, core_recv, in_send, in_recv, pair_send, pair_recv, local_sem, out_sem, early_sem,
):
    place = Place()
    width, experts = tok.shape[2], route_own.shape[1]
    other = 1 - place.core

    def block_here(ref):
        return lambda rel, k, p: ref.at[rel, k * 2 + p]

    def block_there(ref):
        return lambda rel_there, k_there, p, rel, k: ref.at[rel_there, k_there * 2 + p]

    own = place.index(0, 0)
    dense[own, :, : 3 * width] = w_qkv_own[...]
    dense[own, :, 3 * width : 4 * width] = w_attn_own[...]
    square[...] = jnp.zeros_like(square)
    for i, ref in enumerate((gain_one_own, bias_one_own, gain_two_own, bias_two_own)):
        square[GAIN_ONE + i : GAIN_ONE + i + 1, : ref.shape[0]] = (
            ref[...].astype(jnp.float32).reshape(1, ref.shape[0])
        )
    columns = jnp.transpose(square[...])[: gain_one_own.shape[0]]
    square[: gain_one_own.shape[0], :] = columns
    square[: gain_one_own.shape[0], :experts] = route_own[...].astype(jnp.float32)
    dense[own, :, 4 * width :] = square[: gain_one_own.shape[0], :].astype(jnp.bfloat16)
    for p in range(2):
        cot_all[0, p] = lengthened(cot_own, p).astype(jnp.bfloat16)
    place.greet()

    dense_tree = Spread(
        place,
        lambda rel, k, p: dense.at[place.index(rel, k)],
        lambda rel_there, k_there, p, rel, k: dense.at[place.index(rel, k)],
        1,
        lambda j, p: j % 2,
        False,
        (dense_send, dense_recv),
    )
    core_started, in_started, pair_started, local, outs, early = [], [], [], [], [], []

    def to_core(rel, k):
        slot = dense.at[place.index(rel, k)]
        send(
            core_started, slot, slot, core_send.at[rel, k], core_recv.at[rel, k], place.sibling
        )

    def tree(kind, ref, sems):
        return kind(place, block_here(ref), block_there(ref), 2, lambda j, p: p, True, sems)

    cot_side = tree(SideSpread, cot_all, (cot_send, cot_recv))
    cot_plain = tree(Spread, cot_all, (cot_send, cot_recv))
    cot_trees = [cot_side if p in SIDE_PACKS else cot_plain for p in range(2)]
    routed_tree = tree(Spread, routed_all, (routed_send, routed_recv))

    def local_copy(src, dst):
        copy = pltpu.make_async_copy(src, dst, local_sem.at[len(local)])
        copy.start()
        local.append(copy)

    def down():
        dense_tree.own(0, dense.at[own])
        to_core(0, 0)
        local_copy(w_in.at[:, :, pl.ds(pl.multiple_of(place.chip(0, 0) * SIDE, SIDE), SIDE)],
                   w_in_all.at[place.chip(0, 0), place.core])
        same_documents(segments, flat_ids, tall_ids)
        gate_row[...] = jnp.zeros_like(gate_row)

    def dplane(j):
        dense_tree.plane(j, 0)
        to_core(0, place.nearest(j))

    def dcorner(j):
        k = place.nearest(j)
        dense_tree.corner(j, 0)
        other_side = 2 - j % 2
        dense_tree.wait(other_side, other_side, k, 0)
        to_core(1, k)
        to_core(2, k)

    def dlast(j):
        k = place.nearest(j)
        dense_tree.wait(3, 3, k, 0)
        to_core(3, k)

    def dwait():
        for k in range(4):
            for rel in range(4):
                slot = dense.at[place.plane(k) * 8 + place.at[rel] + 1 - 2 * place.core]
                arrived(slot, core_recv.at[rel, k])
        local_copy(dense, dense_out)
        small = dense[:, :, 4 * width : 4 * width + SIDE].reshape(width, SIDE)
        turned[...] = jnp.transpose(small.astype(jnp.float32))

    def att(p):
        row = [turned[GAIN_ONE + i : GAIN_ONE + i + 1, :] for i in range(4)]
        block = lengthened(tok, p)
        unit, unused = norm_parts(block)
        normed = (unit * row[0] + row[1]).astype(jnp.bfloat16)
        w_qkv = dense[:, :, : 3 * width].reshape(width, 3 * width)
        proj[p] = dot(normed, w_qkv).astype(jnp.bfloat16)
        same = same_document(flat_ids, tall_ids, p)

        def pair_of_heads(j, carry):
            at = pl.multiple_of(j * SIDE, SIDE)
            queries = proj[p, :, pl.ds(at, SIDE)]
            keys = proj[p, :, pl.ds(at + width, SIDE)]
            values = proj[p, :, pl.ds(at + 2 * width, SIDE)]
            out = jnp.zeros((ROWS, SIDE), jnp.float32)
            for h in range(2):
                lanes = head_lanes(h)
                probs = softmax_rows(queries * lanes, keys, same).astype(jnp.bfloat16)
                out = out + dot(probs, values * lanes)
            heads[p, :, pl.ds(at, SIDE)] = out.astype(jnp.bfloat16)
            return carry

        lax.fori_loop(0, width // SIDE, pair_of_heads, 0)
        w_attn = dense[:, :, 3 * width : 4 * width].reshape(width, width)
        mid = block + dot(heads[p], w_attn)
        middle[p] = mid
        unit, unused = norm_parts(mid)
        routed_all[0, p] = jnp.where(real_rows(), unit * row[2] + row[3], 0.0).astype(jnp.bfloat16)
        routed_tree.own(p, routed_all.at[0, p])

    def win(rel, j):
        k = place.nearest(j)
        columns = pl.ds(pl.multiple_of(place.chip(rel, k) * SIDE, SIDE), SIDE)
        send(
            in_started, w_in.at[:, :, columns], w_in_all.at[place.chip(0, 0), place.core],
            in_send.at[rel, k], in_recv.at[rel, (4 - k) % 4], place.device(rel, k),
        )

    def wo():
        local_copy(w_out, w_out_all.at[place.core])
        send(
            pair_started, w_out, w_out_all.at[place.core], pair_send.at[0], pair_recv.at[0],
            place.sibling,
        )

    def winwait():
        for rel in range(4):
            for k in range(4):
                if (rel, k) != (0, 0):
                    arrived(w_in_all.at[place.chip(rel, k), place.core], in_recv.at[rel, k])
        local[0].wait()
        mine = w_in_all.at[:, place.core]
        send(pair_started, mine, mine, pair_send.at[1], pair_recv.at[1], place.sibling)

    def wsibwait():
        for copy in local[1:]:
            copy.wait()
        arrived(w_out_all.at[other], pair_recv.at[0])
        arrived(w_in_all.at[:, other], pair_recv.at[1])

    def put(src, dst):
        copy = pltpu.make_async_copy(src, dst, out_sem.at[len(outs)])
        copy.start()
        outs.append(copy)

    def wave(j, p):
        at = place.nearest(j) * 2 + p
        k = place.nearest(j)
        cot_trees[p].last(j, p)
        routed_tree.wait(2 - p, 2 - p, k, p)
        count = len(outs) // 4
        stage = count % 2
        if count >= 2:
            outs[4 * count - 8].wait()
            outs[4 * count - 7].wait()

        def one_block(rel, carry):
            pair = place.pair(pack_task, task_experts, rel, place.nearest(j), p)
            rows, cots = routed_all[rel, at], cot_all[rel, at]
            gated, grad_pre, mixed, grad = expert_block(
                pair, rows, cots, w_in_all, w_out_all, dense, gate_row
            )
            mixed_all[rel, at] = mixed
            grad_all[rel, at] = grad
            in_stage[stage, rel] = contract_rows(rows, grad_pre).astype(jnp.bfloat16)
            out_stage[stage, rel] = contract_rows(gated, cots).astype(jnp.bfloat16)
            return carry

        lax.fori_loop(0, 3, one_block, 0)
        routed_tree.wait(3, 3, k, p)
        one_block(3, 0)
        put(in_stage.at[stage], in_terms.at[:, at])
        put(out_stage.at[stage], out_terms.at[:, at])
        put(grad_all.at[:, at], grad_out.at[:, at])
        put(mixed_all.at[:, at], mixed_out.at[:, at])
        for i, (back_j, rel) in enumerate(EARLY):
            if back_j == 3 - j:
                copy = pltpu.make_async_copy(
                    grad_all.at[2 - p if rel == 1 else rel, at],
                    (early_y, early_x)[p].at[i],
                    early_sem.at[p, i],
                )
                copy.start()
                early.append(copy)

    steps = {
        DOWN: down, DPLANE: dplane, DCORNER: dcorner, DLAST: dlast, DWAIT: dwait,
        ATT: att, WIN: win, WO: wo, WINWAIT: winwait, WSIBWAIT: wsibwait, WAVE: wave,
        COWN: lambda p: cot_trees[p].own(p, cot_all.at[0, p]),
        CPLANE: cot_plain.plane, CCORNER: cot_plain.corner,
        CNEAR: cot_side.near, CMZ: cot_side.passed,
        RPLANE: routed_tree.plane, RCORNER: routed_tree.corner,
    }
    for name, *where in FRONT_STEPS:
        steps[name](*where)
    for i, copy in enumerate(outs):
        if i % 4 >= 2 or i >= len(outs) - 8:
            copy.wait()
    for copy in early:
        copy.wait()
    for each in (dense_tree, cot_side, cot_plain, routed_tree):
        each.finish()
    for copy in core_started + in_started + pair_started:
        copy.wait_send()


def expert_block(pair, rows, cots, w_in_all, w_out_all, dense, gate_row):
    width, slab = rows.shape[1], 2 * SIDE
    first, second = pair
    w_in = jnp.concatenate([w_in_all[:, :, e].reshape(width, SIDE) for e in pair], axis=1)
    w_out = jnp.concatenate([w_out_all[:, e].reshape(SIDE, width) for e in pair], axis=0)
    route = dense[:, :, 4 * width : 4 * width + SIDE].reshape(width, SIDE)
    gate_a, gate_b = two_gates(dot(rows, route), first, second)
    lane = lax.broadcasted_iota(jnp.int32, (1, slab), 1)
    gates = jnp.where(lane < SIDE, gate_a, gate_b)
    hidden = dot(rows, w_in)
    back_act = contract_cols(cots, w_out)
    square = hidden * hidden
    bend = jnp.tanh(ROOT2PI * hidden * (1.0 + 0.044715 * square))
    half = 0.5 * (1.0 + bend)
    act = (hidden * half).astype(jnp.bfloat16).astype(jnp.float32)
    slope = half + 0.5 * hidden * (1.0 - bend * bend) * (ROOT2PI * (1.0 + 0.134145 * square))
    gated = (gates * act).astype(jnp.bfloat16)
    grad_pre = (gates * back_act * slope).astype(jnp.bfloat16)
    product = (act * back_act).astype(jnp.bfloat16)
    signs = jnp.broadcast_to(jnp.where(lane < SIDE, 1.0, -1.0), (8, slab)).astype(jnp.bfloat16)
    gate_row[:, :ROWS] = contract_cols(signs, product)
    mixed = dot(gated, w_out).astype(jnp.bfloat16)
    grads = contract_cols(grad_pre, w_in)
    grad = jnp.concatenate([grads[:PACK], gate_row[...]], axis=0).astype(jnp.bfloat16)
    return gated, grad_pre, mixed, grad


def sum_kernel(
    pack_task, task_experts, in_terms, out_terms, d_in, d_out_own, d_out_far, heads, nexts,
    total_in, total_out,
):
    z, g = lax.axis_index("gx"), lax.axis_index("gy")
    experts = d_out_own.shape[0]
    slots = in_terms.shape[0] * in_terms.shape[1]

    @pl.when(pl.program_id(0) == 0)
    def list_uses():
        def clear(e, carry):
            heads[e] = -1
            return carry

        lax.fori_loop(0, experts, clear, 0)
        step_x, step_y = 2 - 4 * ((g // 2) % 2), 4 - 8 * (g // 4)

        def one(slot, carry):
            rel, k, p = slot // 8, (slot // 2) % 4, slot % 2
            at = g + step_x * (rel % 2) + step_y * (rel // 2)
            task = pack_task[(((z + k) % 4) * 8 + at) * 2 + p]
            for i in range(2):
                e = task_experts[task, i]
                nexts[slot * 2 + i] = heads[e]
                heads[e] = slot * 2 + i
            return carry

        lax.fori_loop(0, slots, one, 0)

    def terms(use):
        slot = use // 2
        rel, at, half = slot // 8, slot % 8, pl.multiple_of((use % 2) * SIDE, SIDE)
        return (
            in_terms[rel, at, :, pl.ds(half, SIDE)].astype(jnp.float32),
            out_terms[rel, at, pl.ds(half, SIDE), :].astype(jnp.float32),
        )

    def add_terms(use):
        new_in, new_out = terms(use)
        total_in[...] += new_in
        total_out[...] += new_out
        return nexts[use]

    own = pl.ds(pl.multiple_of((g % 2) * HEAD, HEAD), HEAD)
    far = pl.ds(pl.multiple_of((1 - g % 2) * HEAD, HEAD), HEAD)

    def one_expert(i, carry):
        head = heads[i]

        @pl.when(head < 0)
        def unused():
            total_in[...] = jnp.zeros_like(total_in)
            total_out[...] = jnp.zeros_like(total_out)

        @pl.when(head >= 0)
        def used():
            total_in[...], total_out[...] = terms(head)
            lax.while_loop(lambda use: use >= 0, add_terms, nexts[head])

        low = total_in[...].astype(jnp.bfloat16).reshape(-1, 2, 16, SIDE)
        d_in[0, :, i] = low[:, 0]
        d_in[1, :, i] = low[:, 1]
        d_out_own[i] = total_out[own, :].astype(jnp.bfloat16)
        d_out_far[i] = total_out[far, :].astype(jnp.bfloat16)
        return carry

    lax.fori_loop(0, experts, one_expert, 0)


class Collect:
    def __init__(self, place, part, corner, from_x, from_y, from_z, packs, half, sems):
        self.place, self.part = place, part
        self.corner, self.from_x, self.from_y, self.from_z = corner, from_x, from_y, from_z
        self.packs, self.half, self.started = packs, half, []
        self.send_sem, self.recv_sem = sems

    def go(self, kind, src, dst, at_send, at_recv, device):
        send(
            self.started, src, dst, self.send_sem.at[kind, at_send],
            self.recv_sem.at[kind, at_recv], device,
        )

    def opposite(self, k, p):
        at = k * self.packs + p
        towards = 2 if self.half(k, p) == 0 else 1
        self.go(3, self.part(3, k, p), self.corner.at[at], at, at, self.place.device(towards, 0))

    def straight(self, k, p):
        at = k * self.packs + p
        if self.half(k, p) == 0:
            self.go(2, self.part(2, k, p), self.from_y.at[at], at, at, self.place.device(2, 0))
        else:
            self.go(1, self.part(1, k, p), self.from_x.at[at], at, at, self.place.device(1, 0))

    def helped(self, k, p, mine):
        at = k * self.packs + p
        ref = self.corner.at[at]
        arrived(ref, self.recv_sem.at[3, at])
        total = ref[...].astype(jnp.float32) + mine().astype(jnp.float32)
        ref[...] = total.astype(jnp.bfloat16)
        if self.half(k, p) == 0:
            self.go(1, ref, self.from_x.at[at], at, at, self.place.device(1, 0))
        else:
            self.go(2, ref, self.from_y.at[at], at, at, self.place.device(2, 0))

    def plane(self, k, p, mine):
        at = k * self.packs + p
        arrived(self.from_x.at[at], self.recv_sem.at[1, at])
        arrived(self.from_y.at[at], self.recv_sem.at[2, at])
        total = self.from_x[at].astype(jnp.float32) + self.from_y[at].astype(jnp.float32)
        total = total + mine().astype(jnp.float32)
        if k:
            self.from_x[at] = total.astype(jnp.bfloat16)
            there = back(k) * self.packs + p
            self.go(
                0, self.from_x.at[at], self.from_z.at[there], at, there, self.place.device(0, k)
            )
            return None
        for other in (1, 2, 3):
            at = other * self.packs + p
            arrived(self.from_z.at[at], self.recv_sem.at[0, at])
            total = total + self.from_z[at].astype(jnp.float32)
        return total

    def finish(self):
        for copy in self.started:
            copy.wait_send()


class Return:
    def __init__(self, place, part, own, from_z, sems, load):
        self.place, self.part, self.own, self.from_z = place, part, own, from_z
        self.send_sem, self.recv_sem, self.z_sem = sems
        self.started, self.loads = [], {}
        for kind, j, p in self.needs:
            rel = self.beside(p) if kind else 0
            at = self.at(j, p)
            self.loads[kind, j, p] = load(part.at[rel, at], own.at[kind, at])

    needs = [(kind, j, p) for j in range(4) for p in range(2) for kind in (1, 0)]

    def at(self, j, p):
        return self.place.nearest(3 - j) * 2 + p

    def beside(self, p):
        return 1 + p

    def go(self, kind, at, src, dst, recv_sem, device):
        send(self.started, src, dst, self.send_sem.at[kind, at], recv_sem, device)

    def mine(self, kind, j, p):
        return self.own[kind, self.at(j, p)].astype(jnp.float32)

    def along(self, kind, send_kind, j, p, ref, total):
        place = self.place
        k = place.nearest(3 - j)
        step = 2 * ((place.plane(k) - place.z + 3) // 4) - 1
        behind = self.from_z.at[kind, k * 2 + p]
        more = (place.z - step >= 0) & (place.z - step <= 3)

        @pl.when(more)
        def add():
            arrived(behind, self.z_sem.at[kind, k * 2 + p])
            ref[...] = (total() + behind[...].astype(jnp.float32)).astype(jnp.bfloat16)

        @pl.when(jnp.logical_not(more))
        def first():
            ref[...] = total().astype(jnp.bfloat16)

        there = (k - step + 4) % 4
        slot = (there + (4 - there) // 4 * (2 - 2 * step)) * 2 + p
        self.go(
            send_kind, k * 2 + p, ref, self.from_z.at[kind, slot], self.z_sem.at[kind, slot],
            (place.plane(step + 4), place.at[0]),
        )

    def owned(self, kind, p, total, out):
        out[...] = total()
        for slot, comes in ((p, self.place.z > 0), (8 + p, self.place.z < 3)):

            @pl.when(comes)
            def add(slot=slot):
                ref = self.from_z.at[kind, slot]
                arrived(ref, self.z_sem.at[kind, slot])
                out[...] += ref[...].astype(jnp.float32)

    def finish(self):
        for copy in self.started:
            copy.wait_send()


class PlaneFirst(Return):
    def __init__(self, place, part, own, from_z, sems, load, corner, from_x, from_y, got):
        self.corner, self.near, self.early = corner, (None, from_x, from_y), {}
        for i, (j, rel) in enumerate(EARLY):
            for p in range(2):
                into = corner if rel == 3 else self.near[2 - p]
                at = place.nearest(3 - j) * 2 + p
                self.early[rel == 3, j, p] = load(got[p].at[i], into.at[at])
        super().__init__(place, part, own, from_z, sems, load)

    def here(self, far, j, p, ref, sem):
        if (far, j, p) in self.early:
            self.early[far, j, p].wait()
        else:
            arrived(ref, sem)

    def first(self, j, p):
        at, way = self.at(j, p), 2 - p
        if (True, j, p) not in self.early:
            self.go(
                3, at, self.part.at[3, at], self.corner.at[at], self.recv_sem.at[3, at],
                self.place.device(way, 0),
            )
        if (False, j, p) not in self.early:
            self.go(
                way, at, self.part.at[way, at], self.near[way].at[at], self.recv_sem.at[way, at],
                self.place.device(way, 0),
            )

    def helped(self, j, p):
        at, way = self.at(j, p), 1 + p
        ref = self.corner.at[at]
        self.loads[1, j, p].wait()
        self.here(True, j, p, ref, self.recv_sem.at[3, at])
        ref[...] = (ref[...].astype(jnp.float32) + self.mine(1, j, p)).astype(jnp.bfloat16)
        self.go(
            way, at, ref, self.near[way].at[at], self.recv_sem.at[way, at],
            self.place.device(way, 0),
        )

    def plane(self, j, p, out):
        at = self.at(j, p)
        self.loads[0, j, p].wait()
        self.here(False, j, p, self.near[2 - p].at[at], self.recv_sem.at[2 - p, at])
        arrived(self.near[1 + p].at[at], self.recv_sem.at[1 + p, at])

        def total():
            both = self.near[1][at].astype(jnp.float32) + self.near[2][at].astype(jnp.float32)
            return both + self.mine(0, j, p)

        if j < 3:
            self.along(0, 0, j, p, self.near[1].at[at], total)
        else:
            self.owned(0, p, total, out)


class SideFirst(Return):
    def __init__(self, place, part, own, from_z, sems, load, near, last, total):
        super().__init__(place, part, own, from_z, sems, load)
        self.near, self.last, self.total = near, last, total

    def first(self, j, p):
        at, way = self.at(j, p), 2 - p
        for kind, rel in ((1, 3), (0, way)):
            self.go(
                kind, at, self.part.at[rel, at], self.near.at[kind, at],
                self.recv_sem.at[kind, at], self.place.device(way, 0),
            )

    def plane(self, j, p, out):
        at, way = self.at(j, p), 1 + p
        for kind in (1, 0):
            ref = self.near.at[kind, at]
            self.loads[kind, j, p].wait()
            arrived(ref, self.recv_sem.at[kind, at])

            def total(kind=kind, ref=ref):
                return ref[...].astype(jnp.float32) + self.mine(kind, j, p)

            if j < 3:
                self.along(kind, 2 + kind, j, p, ref, total)
            elif kind:
                self.owned(kind, p, total, self.total)
                ref[...] = self.total[...].astype(jnp.bfloat16)
                self.go(
                    2, at, ref, self.last.at[p], self.recv_sem.at[2, p], self.place.device(way, 0)
                )
            else:
                self.owned(kind, p, total, out)
        if j == 3:
            arrived(self.last.at[p], self.recv_sem.at[2, p])
            out[...] += self.last[p].astype(jnp.float32)


def tail_kernel(
    pack_task, task_experts, tok, cot, segments, proj, heads, middle, dense, grad_part, mixed_part,
    d_in, d_out_far, got_y, got_x,
    mixed, d_tok, d_dense, d_in_all, d_out_all,
    g_own, g_corner, g_x, g_y, g_z, m_own, m_near, m_last, m_z, m_total, m_out,
    total_grad, grad_mid, grad_heads, grad_qkv, acc, small_rows, turned, flat_ids, tall_ids,
    in_far, in_mine, far_dense, got_dense, part_dense, s_corner, s_x, s_y, s_z,
    g_send, g_recv, gz_recv, m_send, m_recv, mz_recv, s_send, s_recv, in_send, in_recv,
    pair_send, pair_recv, load_sem,
):
    place = Place()
    width = tok.shape[2]
    place.greet()

    loads = []

    def load(src, dst):
        copy = pltpu.make_async_copy(src, dst, load_sem.at[len(loads)])
        copy.start()
        loads.append(copy)
        return copy

    grads = PlaneFirst(
        place, grad_part, g_own, g_z, (g_send, g_recv, gz_recv), load, g_corner, g_x, g_y,
        (got_y, got_x),
    )
    in_load = load(d_in.at[place.core], in_mine)
    mixes = SideFirst(
        place, mixed_part, m_own, m_z, (m_send, m_recv, mz_recv), load, m_near, m_last, m_total
    )
    pair_started, in_started, kept = [], [], {}
    planes = (2, 1, 3, 0)

    same_documents(segments, flat_ids, tall_ids)
    small = dense[:, :, 4 * width : 4 * width + SIDE].reshape(width, SIDE)
    turned[...] = jnp.transpose(small.astype(jnp.float32))
    small_rows[...] = jnp.zeros_like(small_rows)
    gain_one, bias_one, gain_two, bias_two = (
        turned[GAIN_ONE + i : GAIN_ONE + i + 1, :] for i in range(4)
    )

    def pair():
        send(
            pair_started, d_in.at[1 - place.core], in_far, pair_send.at[0], pair_recv.at[0],
            place.sibling,
        )
        send(
            pair_started, d_out_far, d_out_all, pair_send.at[1], pair_recv.at[1], place.sibling
        )

    def addpair():
        in_load.wait()
        arrived(in_far, pair_recv.at[0])

        def one(i, carry):
            total = in_mine[i].astype(jnp.float32) + in_far[i].astype(jnp.float32)
            in_mine[i] = total.astype(jnp.bfloat16)
            return carry

        lax.fori_loop(0, in_mine.shape[0], one, 0)
        columns = pl.ds(pl.multiple_of(place.chip(0, 0) * SIDE, SIDE), SIDE)
        kept["local"] = load(in_mine.at[place.chip(0, 0)], d_in_all.at[:, :, columns])

    def win(rel, j):
        k = planes[j]
        columns = pl.ds(pl.multiple_of(place.chip(0, 0) * SIDE, SIDE), SIDE)
        send(
            in_started, in_mine.at[place.chip(rel, k)], d_in_all.at[:, :, columns],
            in_send.at[rel, k], in_recv.at[rel, back(k)], place.device(rel, k),
        )

    def mplane(j, p):
        mixes.plane(j, p, m_out)
        if j == 3:
            mixed[p] = (middle[p] + m_out[...]).astype(jnp.bfloat16)

    def add_to(p, columns, value):
        if p == 0:
            acc[:, columns] = value
        else:
            acc[:, columns] += value

    def add_row(at, value):
        small_rows[at : at + 1, :] += jnp.sum(value, 0, keepdims=True)

    def att(part):
        p = part // 3
        (att_routed, att_heads, att_normed)[part % 3](p)

    def att_routed(p):
        first, second = place.pair(pack_task, task_experts, 0, 0, p)
        got = total_grad[p]
        tall = jnp.concatenate(
            [got[PACK:, : 2 * SIDE], jnp.zeros((SIDE - 8, 2 * SIDE), jnp.float32)], axis=0
        )
        gap_grad = jnp.transpose(tall)[:ROWS, 0:1]
        got = jnp.where(real_rows(), got, 0.0)
        mid = middle[p]
        unit, rise = norm_parts(mid)
        routed = jnp.where(real_rows(), unit * gain_two + bias_two, 0.0).astype(jnp.bfloat16)
        route = dense[:, :, 4 * width : 4 * width + SIDE].reshape(width, SIDE)
        gate_a, gate_b = two_gates(dot(routed, route), first, second)
        grad_a = gate_a * gate_b * gap_grad
        lane = lax.broadcasted_iota(jnp.int32, (ROWS, SIDE), 1)
        grad_logits = jnp.where(lane == first, grad_a, jnp.where(lane == second, -grad_a, 0.0))
        grad_logits = jnp.where(real_rows(), grad_logits, 0.0).astype(jnp.bfloat16)
        add_to(p, pl.ds(4 * width, SIDE), contract_rows(routed, grad_logits))
        got = got + contract_cols(grad_logits, route)
        add_row(2, got * unit)
        add_row(3, got)
        u = got * gain_two
        grad_middle = lengthened(cot, p) + rise * (
            u - jnp.mean(u, -1, keepdims=True) - unit * jnp.mean(u * unit, -1, keepdims=True)
        )
        grad_mid[...] = grad_middle
        attended = grad_middle.astype(jnp.bfloat16)
        add_to(p, pl.ds(3 * width, width), contract_rows(heads[p], attended))
        w_attn = dense[:, :, 3 * width : 4 * width].reshape(width, width)
        grad_heads[...] = contract_cols(attended, w_attn).astype(jnp.bfloat16)

    def att_heads(p):
        same = same_document(flat_ids, tall_ids, p)

        def pair_of_heads(j, carry):
            at = pl.multiple_of(j * SIDE, SIDE)
            queries = proj[p, :, pl.ds(at, SIDE)]
            keys = proj[p, :, pl.ds(at + width, SIDE)]
            values = proj[p, :, pl.ds(at + 2 * width, SIDE)]
            out_grad = grad_heads[:, pl.ds(at, SIDE)]
            zero = jnp.zeros((ROWS, SIDE), jnp.float32)
            grad_q, grad_k, grad_v = zero, zero, zero
            for h in range(2):
                lanes = head_lanes(h)
                probs = softmax_rows(queries * lanes, keys, same)
                mine_grad = out_grad * lanes
                grad_v = grad_v + contract_rows(probs.astype(jnp.bfloat16), mine_grad)
                grad_probs = contract_cols(mine_grad, values)
                row_dot = jnp.sum(probs * grad_probs, -1, keepdims=True)
                grad_scores = (probs * (grad_probs - row_dot)).astype(jnp.bfloat16)
                grad_q = grad_q + dot(grad_scores, keys * lanes)
                grad_k = grad_k + contract_rows(grad_scores, queries * lanes)
            scale = 1.0 / math.sqrt(HEAD)
            grad_qkv[:, pl.ds(at, SIDE)] = (grad_q * scale).astype(jnp.bfloat16)
            grad_qkv[:, pl.ds(at + width, SIDE)] = (grad_k * scale).astype(jnp.bfloat16)
            grad_qkv[:, pl.ds(at + 2 * width, SIDE)] = grad_v.astype(jnp.bfloat16)
            return carry

        lax.fori_loop(0, width // SIDE, pair_of_heads, 0)

    def att_normed(p):
        unit, rise = norm_parts(lengthened(tok, p))
        normed = (unit * gain_one + bias_one).astype(jnp.bfloat16)
        add_to(p, pl.ds(0, 3 * width), contract_rows(normed, grad_qkv[...]))
        w_qkv = dense[:, :, : 3 * width].reshape(width, 3 * width)
        grad_normed = contract_cols(grad_qkv[...], w_qkv)
        add_row(0, grad_normed * unit)
        add_row(1, grad_normed)
        u = grad_normed * gain_one
        d_tok[p] = (
            grad_mid[...]
            + rise
            * (u - jnp.mean(u, -1, keepdims=True) - unit * jnp.mean(u * unit, -1, keepdims=True))
        ).astype(jnp.bfloat16)

    def dense_part(rel, k, p):
        return got_dense.at[place.chip(rel, k)]

    sums = Collect(
        place, dense_part, s_corner, s_x, s_y, s_z, 1, lambda k, p: k % 2, (s_send, s_recv)
    )
    def dense_step():
        tall = jnp.concatenate(
            [
                jnp.zeros((GAIN_ONE, width), jnp.float32),
                small_rows[...],
                jnp.zeros((SIDE - GAIN_ONE - 8, width), jnp.float32),
            ],
            axis=0,
        )
        acc[:, 4 * width :] += jnp.transpose(tall)
        columns_all = acc.shape[1]

        def cut(i, carry):
            own_rows = pl.ds(pl.multiple_of(i * 32 + place.core * 16, 16), 16)
            far_rows = pl.ds(pl.multiple_of(i * 32 + 16 - place.core * 16, 16), 16)
            far_dense[i] = acc[far_rows, :].astype(jnp.bfloat16)
            part_dense[i] = acc[own_rows, :]
            return carry

        lax.fori_loop(0, 16, cut, 0)
        send(
            pair_started, far_dense, got_dense, pair_send.at[2], pair_recv.at[2], place.sibling
        )
        arrived(got_dense, pair_recv.at[2])

        def join(i, carry):
            far_dense_sum = part_dense[i] + got_dense[i].astype(jnp.float32)
            got_dense[i] = far_dense_sum.astype(jnp.bfloat16)
            return carry

        lax.fori_loop(0, 16, join, 0)

        for k in (2, 1, 3, 0):
            sums.opposite(k, 0)
        for k in (2, 1, 3, 0):
            sums.straight(k, 0)
        for k in (2, 1, 3, 0):
            sums.helped(k, 0, lambda k=k: got_dense[place.chip(1 + k % 2, k)])
        for k in (2, 1, 3):
            sums.plane(k, 0, lambda k=k: got_dense[place.chip(0, k)])
        d_dense[...] = sums.plane(0, 0, lambda: got_dense[place.chip(0, 0)])

    steps = {
        GFIRST: grads.first, GHELP: grads.helped,
        GPLANE: lambda j, p: grads.plane(j, p, total_grad.at[p]),
        MFIRST: mixes.first, MPLANE: mplane, MHELP: lambda j, p: None,
        PAIR: pair, ADDPAIR: addpair, WIN: win, ATT: att, DENSE: dense_step,
    }
    for name, *where in TAIL_STEPS:
        steps[name](*where)

    for rel in range(4):
        for k in range(4):
            if (rel, k) != (0, 0):
                place_columns = pl.ds(pl.multiple_of(place.chip(rel, k) * SIDE, SIDE), SIDE)
                arrived(d_in_all.at[:, :, place_columns], in_recv.at[rel, k])
    kept["local"].wait()
    arrived(d_out_all, pair_recv.at[1])
    for tree in (grads, mixes, sums):
        tree.finish()
    for copy in pair_started + in_started:
        copy.wait_send()


def last_kernel(
    mixed_tall, d_tok_tall, d_dense, d_in_low, d_out_own, d_out_far,
    mixed, d_tok, d_qkv, d_attn, d_route, d_in, d_out, gain_one, bias_one, gain_two, bias_two,
):
    width, experts = mixed.shape[2], d_route.shape[1]

    @pl.when(pl.program_id(0) == 0)
    def small():
        for p in range(mixed.shape[0]):
            mixed[p] = mixed_tall[p, :PACK]
            d_tok[p] = d_tok_tall[p, :PACK]
        d_qkv[...] = d_dense[:, : 3 * width]
        d_attn[...] = d_dense[:, 3 * width : 4 * width]
        d_route[...] = d_dense[:, 4 * width : 4 * width + experts]
        rows = jnp.transpose(d_dense[:, 4 * width :])
        for i, ref in enumerate((gain_one, bias_one, gain_two, bias_two)):
            ref[...] = rows[GAIN_ONE + i]

    d_in[...] = d_in_low[...].astype(jnp.float32)
    d_out[...] = d_out_own[...].astype(jnp.float32) + d_out_far[...].astype(jnp.float32)


def shards_fast(
    tokens,
    segment_ids,
    pack_task,
    task_experts,
    w_qkv,
    w_attn_out,
    w_router,
    w_expert_in,
    w_expert_out,
    norm1_gain,
    norm1_bias,
    norm2_gain,
    norm2_bias,
    cotangent,
):
    packs, length, width = tokens.shape
    experts, slab_in, hidden = w_expert_in.shape
    slab_out = w_expert_out.shape[1]
    dense_width = 4 * width + SIDE
    any_space = pl.BlockSpec(memory_space=pl.ANY)
    vmem = pl.BlockSpec(memory_space=pltpu.VMEM)
    smem = pl.BlockSpec(memory_space=pltpu.SMEM)
    low, full = jnp.bfloat16, jnp.float32
    flat = jax.ShapeDtypeStruct
    dma = pltpu.SemaphoreType.DMA

    blocks = flat((4, 4 * packs, ROWS, width), low)
    in_sums = flat((4, 4 * packs, width, 2 * SIDE), low)
    out_sums = flat((4, 4 * packs, 2 * SIDE, width), low)

    def held(shape):
        return pltpu.VMEM(shape.shape, shape.dtype)

    early_blocks = flat((len(EARLY), ROWS, width), low)
    (
        in_terms, out_terms, mixed_part, grad_part, dense, early_y, early_x, proj, heads, middle,
    ) = pl.pallas_call(
        front_kernel,
        out_shape=(
            in_sums, out_sums, blocks, blocks,
            flat((32, slab_in, dense_width), low),
            early_blocks, early_blocks,
            flat((packs, ROWS, 3 * width), low),
            flat((packs, ROWS, width), low),
            flat((packs, ROWS, width), full),
        ),
        in_specs=[smem] * 2 + [vmem] * 10 + [any_space] * 2,
        out_specs=(any_space,) * 7 + (vmem,) * 3,
        scratch_shapes=[
            pltpu.VMEM((32, slab_in, dense_width), low),
            held(blocks), held(blocks),
            pltpu.VMEM((16, 2, experts, slab_in, SIDE), low),
            pltpu.VMEM((2, experts, slab_out, width), low),
            pltpu.VMEM((2, 4, width, 2 * SIDE), low),
            pltpu.VMEM((2, 4, 2 * SIDE, width), low),
            held(blocks), held(blocks),
            pltpu.VMEM((SIDE, width), full),
            pltpu.VMEM((SIDE, SIDE), full),
            pltpu.VMEM((8, 2 * SIDE), full),
            pltpu.VMEM((2 * SIDE, 8), full),
            pltpu.VMEM((8, width), full),
            dma((7, 8)), dma((4, 8)), dma((5, 8)), dma((4, 8)), dma((5, 4)), dma((4, 4)),
            dma((4, 4)), dma((4, 4)), dma((4, 4)), dma((4, 4)), dma((2,)), dma((2,)), dma((3,)),
            dma((32,)), dma((2, len(EARLY))),
        ],
        compiler_params=pltpu.CompilerParams(
            collective_id=0, has_side_effects=True, vmem_limit_bytes=60 << 20
        ),
        name="front",
    )(
        pack_task, task_experts, tokens, segment_ids, w_qkv, w_attn_out, w_router,
        norm1_gain, norm1_bias, norm2_gain, norm2_bias, cotangent, w_expert_in, w_expert_out,
    )

    across = lax.axis_size("gy")
    got_y = lax.ppermute(early_y, "gy", [(i, i ^ 4) for i in range(across)])
    got_x = lax.ppermute(early_x, "gy", [(i, i ^ 2) for i in range(across)])

    part = width // 2

    by_columns = pl.BlockSpec((experts, slab_out, part), lambda i, *unused: (0, 0, i))
    d_in, d_out_own, d_out_far = pl.pallas_call(
        sum_kernel,
        grid_spec=pltpu.PrefetchScalarGridSpec(
            num_scalar_prefetch=2,
            grid=(2,),
            in_specs=[
                pl.BlockSpec((4, 4 * packs, part, 2 * SIDE), lambda i, *unused: (0, 0, i, 0)),
                pl.BlockSpec((4, 4 * packs, 2 * SIDE, part), lambda i, *unused: (0, 0, 0, i)),
            ],
            out_specs=[
                pl.BlockSpec((2, 8, experts, slab_in, SIDE), lambda i, *unused: (0, i, 0, 0, 0)),
                by_columns, by_columns,
            ],
            scratch_shapes=[
                pltpu.SMEM((experts,), jnp.int32),
                pltpu.SMEM((32 * packs,), jnp.int32),
                pltpu.VMEM((part, SIDE), full),
                pltpu.VMEM((SIDE, part), full),
            ],
        ),
        out_shape=(
            flat((2, 16, experts, slab_in, SIDE), low),
            flat((experts, slab_out, width), low),
            flat((experts, slab_out, width), low),
        ),
        compiler_params=pltpu.CompilerParams(vmem_limit_bytes=60 << 20),
        cost_estimate=pl.CostEstimate(
            flops=10**10, bytes_accessed=40 * 10**6, transcendentals=0
        ),
        name="sums",
    )(pack_task, task_experts, in_terms, out_terms)

    parts = pltpu.VMEM((4 * packs, ROWS, width), low)
    slices = pltpu.VMEM((4, slab_in, dense_width), low)
    sliced = pltpu.VMEM((16, slab_in, dense_width), low)
    mixed_tall, d_tok_tall, d_dense, d_in_all, d_out_all = pl.pallas_call(
        tail_kernel,
        out_shape=(
            flat((packs, ROWS, width), low),
            flat((packs, ROWS, width), low),
            flat((slab_in, dense_width), full),
            flat((experts, slab_in, hidden), low),
            flat((experts, slab_out, width), low),
        ),
        in_specs=[smem] * 2 + [vmem] * 7 + [any_space] * 6,
        out_specs=(vmem,) * 3 + (any_space,) * 2,
        scratch_shapes=[
            pltpu.VMEM((2, 4 * packs, ROWS, width), low), parts, parts, parts,
            pltpu.VMEM((1, 5 * packs, ROWS, width), low),
            pltpu.VMEM((2, 4 * packs, ROWS, width), low),
            pltpu.VMEM((2, 4 * packs, ROWS, width), low),
            pltpu.VMEM((packs, ROWS, width), low),
            pltpu.VMEM((2, 5 * packs, ROWS, width), low),
            pltpu.VMEM((ROWS, width), full),
            pltpu.VMEM((ROWS, width), full),
            pltpu.VMEM((packs, ROWS, width), full),
            pltpu.VMEM((ROWS, width), full),
            pltpu.VMEM((ROWS, width), low),
            pltpu.VMEM((ROWS, 3 * width), low),
            pltpu.VMEM((width, dense_width), full),
            pltpu.VMEM((8, width), full),
            pltpu.VMEM((SIDE, width), full),
            pltpu.VMEM((8, 2 * SIDE), full),
            pltpu.VMEM((2 * SIDE, 8), full),
            pltpu.VMEM((16, experts, slab_in, SIDE), low),
            pltpu.VMEM((16, experts, slab_in, SIDE), low),
            sliced, sliced,
            pltpu.VMEM((16, slab_in, dense_width), full),
            slices, slices, slices, slices,
            dma((4, 8)), dma((4, 8)), dma((1, 10)), dma((4, 8)), dma((4, 8)), dma((2, 10)),
            dma((4, 4)), dma((4, 4)), dma((4, 4)), dma((4, 4)), dma((3,)), dma((3,)), dma((48,)),
        ],
        compiler_params=pltpu.CompilerParams(
            collective_id=1, has_side_effects=True, vmem_limit_bytes=60 << 20
        ),
        name="tail",
    )(
        pack_task, task_experts, tokens, cotangent, segment_ids, proj, heads, middle, dense,
        grad_part, mixed_part, d_in, d_out_far, got_y, got_x,
    )

    group = experts // 2

    def some(rows, columns):
        return pl.BlockSpec((group, rows, columns), lambda i: (i, 0, 0))

    def whole(*shape):
        return pl.BlockSpec(shape, lambda i: (0,) * len(shape))

    return pl.pallas_call(
        last_kernel,
        grid=(2,),
        in_specs=[
            whole(packs, ROWS, width), whole(packs, ROWS, width), whole(slab_in, dense_width),
            some(slab_in, hidden), some(slab_out, width), some(slab_out, width),
        ],
        out_specs=(
            whole(packs, length, width), whole(packs, length, width),
            whole(slab_in, 3 * width), whole(slab_in, width), whole(slab_in, experts),
            some(slab_in, hidden), some(slab_out, width),
        ) + (whole(slab_in),) * 4,
        out_shape=(
            flat((packs, length, width), low), flat((packs, length, width), low),
            flat((slab_in, 3 * width), full), flat((slab_in, width), full),
            flat((slab_in, experts), full),
            flat((experts, slab_in, hidden), full), flat((experts, slab_out, width), full),
        ) + (flat((slab_in,), full),) * 4,
        compiler_params=pltpu.CompilerParams(vmem_limit_bytes=60 << 20),
        name="last",
    )(mixed_tall, d_tok_tall, d_dense, d_in_all, d_out_own, d_out_all)


def solution(mesh):
    outer, inner = mesh.shape["gx"], mesh.shape["gy"]

    def shards(*arrays):
        packs, length, width = arrays[0].shape
        experts, slab_in, hidden = arrays[7].shape
        fits = (
            (outer, inner) == (4, 8)
            and packs == 2
            and length == PACK
            and experts == GAIN_ONE
            and width == HEADS * HEAD
            and slab_in == 16
            and hidden == 16 * SIDE
        )
        return (shards_fast if fits else shards_any)(*arrays)

    placed = (
        P(("gx", "gy"), None, None),
        P(("gx", "gy"), None),
        P(),
        P(),
        P(("gx", "gy"), None),
        P(("gx", "gy"), None),
        P(("gx", "gy"), None),
        P(None, ("gx", "gy"), None),
        P(None, ("gx", "gy"), None),
        P(("gx", "gy")),
        P(("gx", "gy")),
        P(("gx", "gy")),
        P(("gx", "gy")),
        P(("gx", "gy"), None, None),
    )
    return jax.shard_map(
        shards,
        mesh=mesh,
        in_specs=placed,
        out_specs=(
            P(("gx", "gy"), None, None),
            P(("gx", "gy"), None, None),
            P(("gx", "gy"), None),
            P(("gx", "gy"), None),
            P(("gx", "gy"), None),
            P(None, ("gx", "gy"), None),
            P(None, ("gx", "gy"), None),
            P(("gx", "gy")),
            P(("gx", "gy")),
            P(("gx", "gy")),
            P(("gx", "gy")),
        ),
        check_vma=False,
    )
```

```python
import functools
import math

import jax
import jax.numpy as jnp
from jax import lax
from jax.experimental import pallas as pl
from jax.experimental.pallas import tpu as pltpu
from jax.sharding import PartitionSpec as P

HEADS = 8
HEAD = 64
PACK = 216
GAIN_ONE = 32


EPS = 1e-05
MASK_FILL = -1e30
HIGH = lax.Precision.HIGHEST


def shortened(value):

    def short(part):
        return part.astype(jnp.bfloat16) if part.dtype == jnp.float32 else part

    return jax.tree.map(short, value)


def layer_norm(values, gain, bias):
    center = values - jnp.mean(values, -1, keepdims=True)
    spread = jnp.mean(center * center, -1, keepdims=True)
    return center * lax.rsqrt(spread + EPS) * gain + bias


def contract_rows(left, right):
    return lax.dot_general(
        left, right, (((0,), (0,)), ((), ())), preferred_element_type=jnp.float32
    )


def contract_cols(left, right):
    return lax.dot_general(
        left, right, (((1,), (1,)), ((), ())), preferred_element_type=jnp.float32
    )


def shards_any(
    tokens,
    segment_ids,
    pack_task,
    task_experts,
    w_qkv,
    w_attn_out,
    w_router,
    w_expert_in,
    w_expert_out,
    norm1_gain,
    norm1_bias,
    norm2_gain,
    norm2_bias,
    cotangent,
):
    outer = lax.axis_size("gx")
    inner = lax.axis_size("gy")
    devices = outer * inner
    micro, length, width = tokens.shape
    experts, slab_in, hidden = w_expert_in.shape
    slab_out = w_expert_out.shape[1]
    head_size = width // HEADS
    scale = 1.0 / math.sqrt(head_size)
    device = lax.axis_index("gx") * inner + lax.axis_index("gy")
    gathered = (
        lax.all_gather(w_qkv, ("gx", "gy"), axis=0, tiled=True),
        lax.all_gather(w_attn_out, ("gx", "gy"), axis=0, tiled=True),
        lax.all_gather(w_router, ("gx", "gy"), axis=0, tiled=True),
        lax.all_gather(norm1_gain, ("gx", "gy"), axis=0, tiled=True),
        lax.all_gather(norm1_bias, ("gx", "gy"), axis=0, tiled=True),
        lax.all_gather(norm2_gain, ("gx", "gy"), axis=0, tiled=True),
        lax.all_gather(norm2_bias, ("gx", "gy"), axis=0, tiled=True),
    )
    qkv_full, attn_full, route_full = (gathered[0], gathered[1], gathered[2])
    gain_one, bias_one, gain_two, bias_two = tuple(
        (piece.astype(jnp.float32) for piece in gathered[3:])
    )
    route_float = route_full.astype(jnp.float32)
    pack_pairs = task_experts[pack_task]
    needs = jnp.transpose(pack_pairs.reshape(outer, inner, micro, 2), (2, 3, 0, 1))
    route_pairs = jnp.transpose(pack_pairs.reshape(devices, micro, 2), (1, 0, 2))
    own_pairs = lax.dynamic_slice_in_dim(pack_pairs, device * micro, micro, 0)
    expert_ids = jnp.arange(experts, dtype=jnp.int32)

    def slabs(need):
        return (w_expert_in[need], w_expert_out[need])

    def joined(pieces):
        return (
            pieces[0].reshape(pieces[0].shape[0], width, hidden),
            pieces[1].reshape(pieces[1].shape[0], hidden, width),
        )

    def attention_probs(project, segment):
        queries = project[:, :width].reshape(length, HEADS, head_size)
        keys_all = project[:, width : 2 * width].reshape(length, HEADS, head_size)
        scores = (
            jnp.einsum("qhd,khd->hqk", queries, keys_all, preferred_element_type=jnp.float32)
            * scale
        )
        same_doc = segment[:, None] == segment[None, :]
        return jnp.where(same_doc[None], scores, MASK_FILL)

    def forward_step(carry, inputs):
        block, segment, need, pair, senders = inputs
        block_float = block.astype(jnp.float32)
        normed = layer_norm(block_float, gain_one, bias_one).astype(jnp.bfloat16)
        project = jnp.dot(normed, qkv_full, preferred_element_type=jnp.float32).astype(jnp.bfloat16)
        masked = attention_probs(project, segment)
        peak = jnp.max(masked, -1, keepdims=True)
        raised = jnp.exp(masked - peak)
        totals = jnp.sum(raised, -1, keepdims=True)
        log_total = peak + jnp.log(totals)
        attn_low = (raised / totals).astype(jnp.bfloat16)
        values_all = project[:, 2 * width :].reshape(length, HEADS, head_size)
        heads_out = (
            jnp.einsum("hqk,khd->qhd", attn_low, values_all, preferred_element_type=jnp.float32)
            .reshape(length, width)
            .astype(jnp.bfloat16)
        )
        middle = block_float + jnp.dot(heads_out, attn_full, preferred_element_type=jnp.float32)
        routed = layer_norm(middle, gain_two, bias_two).astype(jnp.bfloat16)
        logits = jnp.dot(routed, route_full, preferred_element_type=jnp.float32)
        select = (expert_ids[None, :] == pair[:, None]).astype(jnp.float32)
        chosen = jnp.sum(logits[:, None, :] * select[None], -1)
        raised_gate = jnp.exp(chosen - jnp.max(chosen, -1, keepdims=True))
        gates = raised_gate / jnp.sum(raised_gate, -1, keepdims=True)
        weights_in, weights_out = joined(
            lax.all_to_all(
                lax.all_to_all(
                    shortened(slabs(need)), "gx", split_axis=1, concat_axis=1, tiled=True
                ),
                "gy",
                split_axis=2,
                concat_axis=2,
                tiled=True,
            )
        )
        hidden_pre = jnp.einsum(
            "ld,kdf->klf", routed, weights_in, preferred_element_type=jnp.float32
        )
        hidden_low = jax.nn.gelu(hidden_pre).astype(jnp.bfloat16)
        expert_out = jnp.einsum(
            "klf,kfd->kld", hidden_low, weights_out, preferred_element_type=jnp.float32
        )
        saved = ()
        mixed = middle + gates[:, 0:1] * expert_out[0] + gates[:, 1:2] * expert_out[1]
        kept = (
            normed,
            project,
            log_total,
            heads_out,
            middle,
            routed,
            gates,
            hidden_pre,
            hidden_low,
            expert_out,
            saved,
        )
        return (carry, (mixed.astype(jnp.bfloat16), kept))

    start = jnp.zeros((), jnp.float32)
    unused, (mixed_all, kept_all) = lax.scan(
        forward_step, start, (tokens, segment_ids, needs, own_pairs, route_pairs)
    )

    def backward_step(carry, inputs):
        dense_acc, shard_in, shard_out, holding = carry
        block, grad_top, segment, need, pair, kept = inputs
        (
            normed,
            project,
            log_total,
            heads_out,
            middle,
            routed,
            gates,
            hidden_pre,
            hidden_low,
            expert_out,
            saved,
        ) = kept
        grad_float = grad_top.astype(jnp.float32)
        grad_gate = jnp.sum(grad_float[None] * expert_out, -1).T
        grad_chosen = gates * (grad_gate - jnp.sum(gates * grad_gate, -1, keepdims=True))
        select = (expert_ids[None, :] == pair[:, None]).astype(jnp.float32)
        grad_logits = jnp.sum(grad_chosen[:, :, None] * select[None], 1)
        routed_float = routed.astype(jnp.float32)
        grad_route = jnp.dot(routed_float.T, grad_logits, precision=HIGH)
        grad_routed = jnp.dot(grad_logits, route_float.T, precision=HIGH)
        grad_eout = (gates.T[:, :, None] * grad_float[None]).astype(jnp.bfloat16)
        slot = ()
        weights_in, weights_out = joined(
            lax.all_to_all(
                lax.all_to_all(
                    shortened(slabs(need)), "gx", split_axis=1, concat_axis=1, tiled=True
                ),
                "gy",
                split_axis=2,
                concat_axis=2,
                tiled=True,
            )
        )
        grad_act = jnp.einsum(
            "kld,kfd->klf", grad_eout, weights_out, preferred_element_type=jnp.float32
        )
        unused_act, gelu_back = jax.vjp(jax.nn.gelu, hidden_pre)
        grad_pre = gelu_back(grad_act)[0].astype(jnp.bfloat16)
        grad_in = jnp.einsum("ld,klf->kdf", routed, grad_pre, preferred_element_type=jnp.float32)
        grad_out = jnp.einsum(
            "klf,kld->kfd", hidden_low, grad_eout, preferred_element_type=jnp.float32
        )
        grad_routed = grad_routed + jnp.einsum(
            "klf,kdf->ld", grad_pre, weights_in, preferred_element_type=jnp.float32
        )
        slot = (grad_in, grad_out)
        unused_two, norm_two_back = jax.vjp(layer_norm, middle, gain_two, bias_two)
        grad_mid_norm, grad_gain_two, grad_bias_two = norm_two_back(grad_routed)
        grad_middle = grad_float + grad_mid_norm
        grad_attended = grad_middle.astype(jnp.bfloat16)
        grad_attn_w = contract_rows(heads_out, grad_attended)
        grad_heads = (
            contract_cols(grad_attended, attn_full)
            .astype(jnp.bfloat16)
            .reshape(length, HEADS, head_size)
        )
        masked = attention_probs(project, segment)
        probs_float = jnp.exp(masked - log_total)
        probs_low = probs_float.astype(jnp.bfloat16)
        queries = project[:, :width].reshape(length, HEADS, head_size)
        keys_all = project[:, width : 2 * width].reshape(length, HEADS, head_size)
        values_all = project[:, 2 * width :].reshape(length, HEADS, head_size)
        grad_values = jnp.einsum(
            "hqk,qhd->khd", probs_low, grad_heads, preferred_element_type=jnp.float32
        )
        grad_probs = jnp.einsum(
            "qhd,khd->hqk", grad_heads, values_all, preferred_element_type=jnp.float32
        )
        row_dot = jnp.sum(probs_float * grad_probs, -1, keepdims=True)
        grad_scores = (probs_float * (grad_probs - row_dot)).astype(jnp.bfloat16)
        grad_queries = (
            jnp.einsum("hqk,khd->qhd", grad_scores, keys_all, preferred_element_type=jnp.float32)
            * scale
        )
        grad_keys = (
            jnp.einsum("hqk,qhd->khd", grad_scores, queries, preferred_element_type=jnp.float32)
            * scale
        )
        grad_qkv = jnp.concatenate(
            [
                grad_queries.reshape(length, width),
                grad_keys.reshape(length, width),
                grad_values.reshape(length, width),
            ],
            -1,
        ).astype(jnp.bfloat16)
        grad_qkv_w = contract_rows(normed, grad_qkv)
        grad_normed = contract_cols(grad_qkv, qkv_full)
        unused_one, norm_one_back = jax.vjp(
            layer_norm, block.astype(jnp.float32), gain_one, bias_one
        )
        grad_in_norm, grad_gain_one, grad_bias_one = norm_one_back(grad_normed)
        grad_tokens = (grad_middle + grad_in_norm).astype(jnp.bfloat16)
        terms = (
            grad_qkv_w,
            grad_attn_w,
            grad_route,
            grad_gain_one,
            grad_bias_one,
            grad_gain_two,
            grad_bias_two,
        )
        dense_acc = tuple((total + term for total, term in zip(dense_acc, terms)))
        return ((dense_acc, shard_in, shard_out, holding), (grad_tokens, slot))

    dense_zero = (
        jnp.zeros((width, 3 * width), jnp.float32),
        jnp.zeros((width, width), jnp.float32),
        jnp.zeros((width, experts), jnp.float32),
        jnp.zeros((width,), jnp.float32),
        jnp.zeros((width,), jnp.float32),
        jnp.zeros((width,), jnp.float32),
        jnp.zeros((width,), jnp.float32),
    )
    shard_zero_in = jnp.zeros((experts, slab_in, hidden), jnp.float32)
    shard_zero_out = jnp.zeros((experts, slab_out, width), jnp.float32)
    holding_zero = ()
    (dense_acc, shard_in, shard_out, holding), (grad_tokens_all, slots) = lax.scan(
        backward_step,
        (dense_zero, shard_zero_in, shard_zero_out, holding_zero),
        (tokens, cotangent, segment_ids, needs, own_pairs, kept_all),
    )
    slot_in = slots[0].reshape(micro * 2, width, hidden)
    slot_out = slots[1].reshape(micro * 2, hidden, width)
    amount = slot_in.shape[0]
    returned = lax.all_to_all(
        lax.all_to_all(
            shortened(
                (
                    slot_in.reshape(amount, outer, inner, slab_in, hidden),
                    slot_out.reshape(amount, outer, inner, slab_out, width),
                )
            ),
            "gx",
            split_axis=1,
            concat_axis=1,
            tiled=True,
        ),
        "gy",
        split_axis=2,
        concat_axis=2,
        tiled=True,
    )
    onehot = (
        needs.reshape(micro * 2, outer, inner)[None] == expert_ids[:, None, None, None]
    ).astype(jnp.float32)
    added = tuple(
        (jnp.einsum("esab,sabrc->erc", onehot, piece, precision=HIGH) for piece in returned)
    )
    shard_in = shard_in + added[0]
    shard_out = shard_out + added[1]
    dense_shards = (
        lax.psum_scatter(dense_acc[0], ("gx", "gy"), scatter_dimension=0, tiled=True),
        lax.psum_scatter(dense_acc[1], ("gx", "gy"), scatter_dimension=0, tiled=True),
        lax.psum_scatter(dense_acc[2], ("gx", "gy"), scatter_dimension=0, tiled=True),
        lax.psum_scatter(dense_acc[3], ("gx", "gy"), scatter_dimension=0, tiled=True),
        lax.psum_scatter(dense_acc[4], ("gx", "gy"), scatter_dimension=0, tiled=True),
        lax.psum_scatter(dense_acc[5], ("gx", "gy"), scatter_dimension=0, tiled=True),
        lax.psum_scatter(dense_acc[6], ("gx", "gy"), scatter_dimension=0, tiled=True),
    )
    return (
        mixed_all,
        grad_tokens_all,
        dense_shards[0],
        dense_shards[1],
        dense_shards[2],
        shard_in,
        shard_out,
        dense_shards[3],
        dense_shards[4],
        dense_shards[5],
        dense_shards[6],
    )


MESH = pl.DeviceIdType.MESH
ROWS = 224
SIDE = 128
ROOT2PI = math.sqrt(2.0 / math.pi)


(
    DOWN, DPLANE, DCORNER, DLAST, DWAIT, ATT, WIN, WO, WINWAIT, WSIBWAIT, WAVE, COWN,
    CPLANE, CCORNER, CNEAR, CMZ, RPLANE, RCORNER, GFIRST, MFIRST, GHELP, MHELP, GPLANE, MPLANE, PAIR, ADDPAIR, DENSE,
) = range(27)

SIDE_PACKS = (0, 1)

EARLY = ((0, 3), (1, 3))

FRONT_STEPS = (
    (DOWN,), (COWN, 1), (COWN, 0), (WIN, 3, 2), (WIN, 2, 0), (DPLANE, 1), (CMZ, 0, 1, 1), (WIN, 0, 2),
    (DPLANE, 2), (DPLANE, 3), (CNEAR, 1), (CNEAR, 0), (WIN, 0, 1), (WIN, 1, 1), (CMZ, 0, 1, 0), (WIN, 1, 3),
    (WIN, 1, 0), (WO,), (DCORNER, 0), (DCORNER, 1), (DCORNER, 3), (DCORNER, 2), (WIN, 3, 0), (DLAST, 0),
    (CMZ, 1, 1, 1), (WIN, 2, 1), (CMZ, 1, 1, 0), (WIN, 2, 2), (DLAST, 3), (CMZ, 0, 2, 0), (WIN, 2, 3),
    (WIN, 3, 1), (CMZ, 0, 2, 1), (DLAST, 1), (DLAST, 2), (DWAIT,), (WIN, 1, 2), (ATT, 0), (RCORNER, 0, 0),
    (ATT, 1), (RPLANE, 1, 0), (CMZ, 1, 2, 1), (WIN, 3, 3), (RPLANE, 1, 1), (WIN, 0, 3), (RCORNER, 0, 1),
    (RCORNER, 1, 0), (WINWAIT,), (RPLANE, 2, 1), (RPLANE, 2, 0), (RCORNER, 1, 1), (CMZ, 1, 2, 0), (WSIBWAIT,),
    (WAVE, 0, 0), (CMZ, 0, 3, 0), (WAVE, 1, 0), (RCORNER, 2, 1), (RPLANE, 3, 1), (WAVE, 1, 1),
    (RCORNER, 2, 0), (RPLANE, 3, 0), (WAVE, 0, 1), (CMZ, 1, 3, 0), (CMZ, 0, 3, 1), (RCORNER, 3, 1),
    (WAVE, 2, 1), (CMZ, 1, 3, 1), (RCORNER, 3, 0), (WAVE, 2, 0), (WAVE, 3, 0), (WAVE, 3, 1),
)
TAIL_STEPS = (
    (GFIRST, 0, 0), (MHELP, 2, 0), (GFIRST, 1, 0), (MHELP, 3, 0), (PAIR,), (GHELP, 0, 0), (GFIRST, 0, 1),
    (GHELP, 1, 0), (GHELP, 0, 1), (GFIRST, 2, 0), (ADDPAIR,), (WIN, 0, 1), (GFIRST, 1, 1), (GFIRST, 2, 1),
    (GPLANE, 0, 0), (MFIRST, 0, 1), (GHELP, 1, 1), (MFIRST, 0, 0), (GPLANE, 0, 1), (GPLANE, 1, 0),
    (WIN, 0, 0), (MHELP, 2, 1), (GFIRST, 3, 1), (GHELP, 2, 1), (GHELP, 2, 0), (GPLANE, 1, 1), (GFIRST, 3, 0),
    (MFIRST, 1, 1), (MHELP, 3, 1), (MPLANE, 0, 0), (GPLANE, 2, 1), (MFIRST, 1, 0), (GHELP, 3, 0),
    (MPLANE, 0, 1), (MHELP, 0, 1), (GPLANE, 2, 0), (MFIRST, 2, 0), (MPLANE, 1, 0), (MFIRST, 2, 1),
    (MFIRST, 3, 1), (GHELP, 3, 1), (MPLANE, 1, 1), (WIN, 3, 1), (MPLANE, 2, 0), (GPLANE, 3, 0), (WIN, 1, 0),
    (GPLANE, 3, 1), (MFIRST, 3, 0), (ATT, 0), (WIN, 3, 3), (ATT, 1), (MPLANE, 2, 1), (ATT, 2), (MHELP, 0, 0),
    (MHELP, 1, 0), (MHELP, 1, 1), (ATT, 3), (WIN, 2, 3), (WIN, 1, 2), (WIN, 3, 2), (WIN, 2, 1), (WIN, 2, 2),
    (ATT, 4), (ATT, 5), (MPLANE, 3, 0), (WIN, 1, 1), (WIN, 3, 0), (WIN, 1, 3), (WIN, 2, 0), (WIN, 0, 2),
    (MPLANE, 3, 1), (DENSE,),
)


def dot(left, right):
    return jnp.dot(left, right, preferred_element_type=jnp.float32)


class Place:
    def __init__(self):
        self.z = lax.axis_index("gx")
        g = lax.axis_index("gy")
        self.core = g % 2
        across_x = g + 2 - 4 * ((g // 2) % 2)
        across_y = g + 4 - 8 * (g // 4)
        across_both = across_x + 4 - 8 * (across_x // 4)
        self.at = (g, across_x, across_y, across_both)
        self.step_x, self.step_y = across_x - g, across_y - g
        self.sibling = (self.z, g + 1 - 2 * self.core)

    def plane(self, k):
        return (self.z + k) % 4

    def nearest(self, j):
        z = self.z
        return (0, 1 + 2 * (z // 2), 2 + z - 3 * (z // 2), 3 - z + z // 2)[j]

    def device(self, rel, k):
        return (self.plane(k), self.at[rel])

    def chip(self, rel, k):
        return self.plane(k) * 4 + self.at[rel] // 2

    def index(self, rel, k):
        return self.plane(k) * 8 + self.at[rel]

    def pair(self, pack_task, task_experts, rel, k, p):
        at = self.at[0] + self.step_x * (rel % 2) + self.step_y * (rel // 2)
        task = pack_task[(self.plane(k) * 8 + at) * 2 + p]
        return task_experts[0, task], task_experts[1, task]

    def greet(self):
        barrier = pltpu.get_barrier_semaphore()
        others = [(rel, k) for rel in range(4) for k in range(4) if (rel, k) != (0, 0)]
        for rel, k in others:
            pl.semaphore_signal(
                barrier, inc=1, device_id=self.device(rel, k), device_id_type=MESH
            )
        pl.semaphore_signal(barrier, inc=1, device_id=self.sibling, device_id_type=MESH)

    def meet(self):
        pl.semaphore_wait(pltpu.get_barrier_semaphore(), 16)


def send(started, src, dst, send_sem, recv_sem, device):
    copy = pltpu.make_async_remote_copy(
        src_ref=src,
        dst_ref=dst,
        send_sem=send_sem,
        recv_sem=recv_sem,
        device_id=device,
        device_id_type=MESH,
    )
    copy.start()
    started.append(copy)


def arrived(ref, sem):
    pltpu.make_async_copy(ref, ref, sem).wait()


def back(k):
    return (4 - k) % 4


class Spread:
    def __init__(self, place, here, there, packs, half, chained, sems):
        self.place, self.here, self.there = place, here, there
        self.packs, self.half, self.chained, self.started = packs, half, chained, []
        self.send_sem, self.recv_sem = sems

    def go(self, kind, at_send, k_there, rel, k, p, src, rel_there, device, only_if=None):
        copy = pltpu.make_async_remote_copy(
            src_ref=src,
            dst_ref=self.there(rel_there, k_there, p, rel, k),
            send_sem=self.send_sem.at[kind, at_send * self.packs + p],
            recv_sem=self.recv_sem.at[kind % 4, k_there * self.packs + p],
            device_id=device,
            device_id_type=MESH,
        )
        if only_if is None:
            copy.start()
        else:
            pl.when(only_if)(copy.start)
        self.started.append((copy, only_if))

    def wait(self, kind, rel, k, p):
        arrived(self.here(rel, k, p), self.recv_sem.at[kind, k * self.packs + p])

    def own(self, p, src):
        place = self.place
        if self.chained:
            self.go(0, 0, 3, 0, 0, p, src, 0, place.device(0, 1), place.z < 3)
            self.go(4, 0, 1, 0, 0, p, src, 0, place.device(0, 3), place.z > 0)
        else:
            for k in (1, 2, 3):
                self.go(0, k, back(k), 0, 0, p, src, 0, place.device(0, k))
        self.go(1, 0, 0, 0, 0, p, src, 1, place.device(1, 0))
        self.go(2, 0, 0, 0, 0, p, src, 2, place.device(2, 0))

    def plane(self, j, p):
        place = self.place
        k = place.nearest(j)
        self.wait(0, 0, k, p)
        src = self.here(0, k, p)
        if self.chained:
            step = 2 * ((place.z - place.plane(k) + 3) // 4) - 1
            goes = (place.z + step >= 0) & (place.z + step <= 3)
            on = (place.plane(step + 4), place.at[0])
            self.go(0, k, (k - step + 4) % 4, 0, k, p, src, 0, on, goes)
        self.go(1, k, k, 0, k, p, src, 1, place.device(1, 0))
        self.go(2, k, k, 0, k, p, src, 2, place.device(2, 0))

    def corner(self, j, p):
        k = self.place.nearest(j)
        rel = 1 + self.half(j, p)
        self.wait(rel, rel, k, p)
        self.go(3, k, k, rel, k, p, self.here(rel, k, p), 3, self.place.device(3 - rel, 0))

    def last(self, j, p):
        k = self.place.nearest(j)
        rel = 2 - self.half(j, p)
        self.wait(rel, rel, k, p)
        self.wait(3, 3, k, p)

    def finish(self):
        for copy, only_if in self.started:
            if only_if is None:
                copy.wait_send()
            else:
                pl.when(only_if)(copy.wait_send)


class SideSpread(Spread):
    def side(self, p):
        return 1 + p

    def along(self, w, rel, k, p, src, first):
        place = self.place
        if first:
            ways = ((2 + w, 3, 1, place.z < 3), (4 + w, 1, 3, place.z > 0))
        else:
            step = 2 * ((place.z - place.plane(k) + 3) // 4) - 1
            goes = (place.z + step >= 0) & (place.z + step <= 3)
            ways = ((2 + w, (k - step + 4) % 4, step + 4, goes),)
        for kind, k_there, on, goes in ways:
            self.go(kind, k, k_there, rel, k, p, src, rel, (place.plane(on), place.at[0]), goes)

    def go(self, kind, at_send, k_there, rel, k, p, src, rel_there, device, only_if=None):
        copy = pltpu.make_async_remote_copy(
            src_ref=src,
            dst_ref=self.there(rel_there, k_there, p, rel, k),
            send_sem=self.send_sem.at[kind, at_send * self.packs + p],
            recv_sem=self.recv_sem.at[rel_there, k_there * self.packs + p],
            device_id=device,
            device_id_type=MESH,
        )
        if only_if is None:
            copy.start()
        else:
            pl.when(only_if)(copy.start)
        self.started.append((copy, only_if))

    def own(self, p, src):
        side, other = self.side(p), 3 - self.side(p)
        self.go(6, 0, 0, 0, 0, p, src, side, self.place.device(side, 0))
        self.along(0, 0, 0, p, src, True)
        self.go(0, 0, 0, 0, 0, p, src, other, self.place.device(other, 0))

    def near(self, p):
        side, other = self.side(p), 3 - self.side(p)
        self.wait(side, side, 0, p)
        src = self.here(side, 0, p)
        self.along(1, side, 0, p, src, True)
        self.go(1, 0, 0, side, 0, p, src, 3, self.place.device(other, 0))

    def passed(self, w, j, p):
        side, other = self.side(p), 3 - self.side(p)
        rel, k = side * w, self.place.nearest(j)
        self.wait(rel, rel, k, p)
        src = self.here(rel, k, p)
        self.along(w, rel, k, p, src, False)
        self.go(w, k, k, rel, k, p, src, 3 if w else other, self.place.device(other, 0))

    def last(self, j, p):
        k = self.place.nearest(j)
        for rel in (3 - self.side(p), 3):
            self.wait(rel, rel, k, p)


def norm_parts(values):
    center = values - jnp.mean(values, -1, keepdims=True)
    spread = jnp.mean(center * center, -1, keepdims=True)
    rise = lax.rsqrt(spread + EPS)
    return center * rise, rise


def real_rows():
    return lax.broadcasted_iota(jnp.int32, (ROWS, 1), 0) < PACK


def head_lanes(h):
    lane = lax.broadcasted_iota(jnp.int32, (1, SIDE), 1)
    inside = (lane >= h * HEAD) & (lane < (h + 1) * HEAD)
    return inside.astype(jnp.bfloat16)


def softmax_rows(queries, keys, same):
    scores = contract_cols(queries, keys) * (1.0 / math.sqrt(HEAD))
    scores = jnp.where(same, scores, MASK_FILL)
    raised = jnp.exp(scores - jnp.max(scores, -1, keepdims=True))
    return raised * (1.0 / jnp.sum(raised, -1, keepdims=True))


def pick(logits, expert):
    lane = lax.broadcasted_iota(jnp.int32, logits.shape, 1)
    return jnp.sum(jnp.where(lane == expert, logits, 0.0), -1, keepdims=True)


def two_gates(logits, first, second):
    gap = pick(logits, second) - pick(logits, first)
    return 1.0 / (1.0 + jnp.exp(gap)), 1.0 / (1.0 + jnp.exp(-gap))


def lengthened(ref, p):
    rows = ref[p].astype(jnp.float32)
    return jnp.concatenate([rows, jnp.zeros((ROWS - PACK, rows.shape[1]), jnp.float32)], axis=0)


def same_documents(segments, flat_ids, tall_ids):
    flat_ids[...] = jnp.full(flat_ids.shape, -1.0, jnp.float32)
    flat_ids[: segments.shape[0], :PACK] = segments[...].astype(jnp.float32)
    tall_ids[...] = jnp.transpose(flat_ids[...])


def same_document(flat_ids, tall_ids, p):
    return tall_ids[:ROWS, p : p + 1] == flat_ids[p : p + 1, :ROWS]


def front_kernel(
    pack_task, task_experts, tok, segments, w_qkv_own, w_attn_own, route_own,
    gain_one_own, bias_one_own, gain_two_own, bias_two_own, cot_own, w_in, w_out,
    in_terms, out_terms, mixed_out, grad_out, dense_out, early_y, early_x, proj, heads, middle,
    dense, routed_all, cot_all, w_in_all, w_out_all, in_stage, out_stage, mixed_all, grad_all,
    turned, square, flat_ids, tall_ids, gate_row,
    cot_send, cot_recv, routed_send, routed_recv, dense_send, dense_recv,
    core_send, core_recv, in_send, in_recv, pair_send, pair_recv, local_sem, out_sem, early_sem,
):
    place = Place()
    place.greet()
    width, experts = tok.shape[2], route_own.shape[1]
    other = 1 - place.core

    def block_here(ref):
        return lambda rel, k, p: ref.at[rel, k * 2 + p]

    def block_there(ref):
        return lambda rel_there, k_there, p, rel, k: ref.at[rel_there, k_there * 2 + p]

    own = place.index(0, 0)
    dense[own, :, : 3 * width] = w_qkv_own[...]
    dense[own, :, 3 * width : 4 * width] = w_attn_own[...]
    square[...] = jnp.zeros_like(square)
    for i, ref in enumerate((gain_one_own, bias_one_own, gain_two_own, bias_two_own)):
        square[GAIN_ONE + i : GAIN_ONE + i + 1, : ref.shape[0]] = (
            ref[...].astype(jnp.float32).reshape(1, ref.shape[0])
        )
    columns = jnp.transpose(square[...])[: gain_one_own.shape[0]]
    square[: gain_one_own.shape[0], :] = columns
    square[: gain_one_own.shape[0], :experts] = route_own[...].astype(jnp.float32)
    dense[own, :, 4 * width :] = square[: gain_one_own.shape[0], :].astype(jnp.bfloat16)
    for p in range(2):
        cot_all[0, p] = cot_own[p]
    same_documents(segments, flat_ids, tall_ids)
    gate_row[...] = jnp.zeros_like(gate_row)
    place.meet()

    dense_tree = Spread(
        place,
        lambda rel, k, p: dense.at[place.index(rel, k)],
        lambda rel_there, k_there, p, rel, k: dense.at[place.index(rel, k)],
        1,
        lambda j, p: j % 2,
        False,
        (dense_send, dense_recv),
    )
    core_started, in_started, pair_started, local, outs, early = [], [], [], [], [], []

    def to_core(rel, k):
        slot = dense.at[place.index(rel, k)]
        send(
            core_started, slot, slot, core_send.at[rel, k], core_recv.at[rel, k], place.sibling
        )

    def tree(kind, ref, sems):
        return kind(place, block_here(ref), block_there(ref), 2, lambda j, p: p, True, sems)

    cot_side = tree(SideSpread, cot_all, (cot_send, cot_recv))
    cot_plain = tree(Spread, cot_all, (cot_send, cot_recv))
    cot_trees = [cot_side if p in SIDE_PACKS else cot_plain for p in range(2)]
    routed_tree = tree(Spread, routed_all, (routed_send, routed_recv))

    def local_copy(src, dst):
        copy = pltpu.make_async_copy(src, dst, local_sem.at[len(local)])
        copy.start()
        local.append(copy)

    def down():
        dense_tree.own(0, dense.at[own])
        to_core(0, 0)
        local_copy(w_in.at[:, :, pl.ds(pl.multiple_of(place.chip(0, 0) * SIDE, SIDE), SIDE)],
                   w_in_all.at[place.chip(0, 0), place.core])

    def dplane(j):
        dense_tree.plane(j, 0)
        to_core(0, place.nearest(j))

    def dcorner(j):
        k = place.nearest(j)
        dense_tree.corner(j, 0)
        other_side = 2 - j % 2
        dense_tree.wait(other_side, other_side, k, 0)
        to_core(1, k)
        to_core(2, k)

    def dlast(j):
        k = place.nearest(j)
        dense_tree.wait(3, 3, k, 0)
        to_core(3, k)

    def dwait():
        for k in range(4):
            for rel in range(4):
                slot = dense.at[place.plane(k) * 8 + place.at[rel] + 1 - 2 * place.core]
                arrived(slot, core_recv.at[rel, k])
        local_copy(dense, dense_out)
        small = dense[:, :, 4 * width : 4 * width + SIDE].reshape(width, SIDE)
        turned[...] = jnp.transpose(small.astype(jnp.float32))

    def att(p):
        row = [turned[GAIN_ONE + i : GAIN_ONE + i + 1, :] for i in range(4)]
        block = lengthened(tok, p)
        unit, unused = norm_parts(block)
        normed = (unit * row[0] + row[1]).astype(jnp.bfloat16)
        w_qkv = dense[:, :, : 3 * width].reshape(width, 3 * width)
        proj[p] = dot(normed, w_qkv).astype(jnp.bfloat16)
        same = same_document(flat_ids, tall_ids, p)

        def pair_of_heads(j, carry):
            at = pl.multiple_of(j * SIDE, SIDE)
            queries = proj[p, :, pl.ds(at, SIDE)]
            keys = proj[p, :, pl.ds(at + width, SIDE)]
            values = proj[p, :, pl.ds(at + 2 * width, SIDE)]
            out = jnp.zeros((ROWS, SIDE), jnp.float32)
            for h in range(2):
                lanes = head_lanes(h)
                probs = softmax_rows(queries * lanes, keys, same).astype(jnp.bfloat16)
                out = out + dot(probs, values * lanes)
            heads[p, :, pl.ds(at, SIDE)] = out.astype(jnp.bfloat16)
            return carry

        lax.fori_loop(0, width // SIDE, pair_of_heads, 0)
        w_attn = dense[:, :, 3 * width : 4 * width].reshape(width, width)
        mid = block + dot(heads[p], w_attn)
        middle[p] = mid
        unit, unused = norm_parts(mid)
        routed_all[0, p] = (unit * row[2] + row[3])[:PACK].astype(jnp.bfloat16)
        routed_tree.own(p, routed_all.at[0, p])

    def win(rel, j):
        k = place.nearest(j)
        columns = pl.ds(pl.multiple_of(place.chip(rel, k) * SIDE, SIDE), SIDE)
        send(
            in_started, w_in.at[:, :, columns], w_in_all.at[place.chip(0, 0), place.core],
            in_send.at[rel, k], in_recv.at[rel, (4 - k) % 4], place.device(rel, k),
        )

    def wo():
        local_copy(w_out, w_out_all.at[place.core])
        send(
            pair_started, w_out, w_out_all.at[place.core], pair_send.at[0], pair_recv.at[0],
            place.sibling,
        )

    def winwait():
        for rel in range(4):
            for k in range(4):
                if (rel, k) != (0, 0):
                    arrived(w_in_all.at[place.chip(rel, k), place.core], in_recv.at[rel, k])
        local[0].wait()
        mine = w_in_all.at[:, place.core]
        send(pair_started, mine, mine, pair_send.at[1], pair_recv.at[1], place.sibling)

    def wsibwait():
        for copy in local[1:]:
            copy.wait()
        arrived(w_out_all.at[other], pair_recv.at[0])
        arrived(w_in_all.at[:, other], pair_recv.at[1])

    def put(src, dst):
        copy = pltpu.make_async_copy(src, dst, out_sem.at[len(outs)])
        copy.start()
        outs.append(copy)

    def wave(j, p):
        at = place.nearest(j) * 2 + p
        k = place.nearest(j)
        cot_trees[p].last(j, p)
        routed_tree.wait(2 - p, 2 - p, k, p)
        count = len(outs) // 4
        stage = count % 2
        if count >= 2:
            outs[4 * count - 8].wait()
            outs[4 * count - 7].wait()

        def one_block(rel, carry):
            pair = place.pair(pack_task, task_experts, rel, place.nearest(j), p)
            rows, cots = routed_all[rel, at], cot_all[rel, at]
            gated, grad_pre, mixed, grad = expert_block(
                pair, rows, cots, w_in_all, w_out_all, dense, gate_row.at[rel]
            )
            mixed_all[rel, at] = mixed
            grad_all[rel, at] = grad
            in_stage[stage, rel] = contract_rows(rows, grad_pre).astype(jnp.bfloat16)
            out_stage[stage, rel] = contract_rows(gated, cots).astype(jnp.bfloat16)
            return carry

        lax.fori_loop(0, 3, one_block, 0)
        routed_tree.wait(3, 3, k, p)
        one_block(3, 0)
        put(in_stage.at[stage], in_terms.at[:, at])
        put(out_stage.at[stage], out_terms.at[:, at])
        put(grad_all.at[:, at], grad_out.at[:, at])
        put(mixed_all.at[:, at], mixed_out.at[:, at])
        for i, (back_j, rel) in enumerate(EARLY):
            if back_j == 3 - j:
                copy = pltpu.make_async_copy(
                    grad_all.at[2 - p if rel == 1 else rel, at],
                    (early_y, early_x)[p].at[i],
                    early_sem.at[p, i],
                )
                copy.start()
                early.append(copy)

    steps = {
        DOWN: down, DPLANE: dplane, DCORNER: dcorner, DLAST: dlast, DWAIT: dwait,
        ATT: att, WIN: win, WO: wo, WINWAIT: winwait, WSIBWAIT: wsibwait, WAVE: wave,
        COWN: lambda p: cot_trees[p].own(p, cot_all.at[0, p]),
        CPLANE: cot_plain.plane, CCORNER: cot_plain.corner,
        CNEAR: cot_side.near, CMZ: cot_side.passed,
        RPLANE: routed_tree.plane, RCORNER: routed_tree.corner,
    }
    for name, *where in FRONT_STEPS:
        steps[name](*where)
    for i, copy in enumerate(outs):
        if i % 4 >= 2 or i >= len(outs) - 8:
            copy.wait()
    for copy in early:
        copy.wait()
    for each in (dense_tree, cot_side, cot_plain, routed_tree):
        each.finish()
    for copy in core_started + in_started + pair_started:
        copy.wait_send()


def expert_block(pair, rows, cots, w_in_all, w_out_all, dense, gate_row):
    width, slab = rows.shape[1], 2 * SIDE
    first, second = pair
    w_in = jnp.concatenate([w_in_all[:, :, e].reshape(width, SIDE) for e in pair], axis=1)
    w_out = jnp.concatenate([w_out_all[:, e].reshape(SIDE, width) for e in pair], axis=0)
    route = dense[:, :, 4 * width : 4 * width + SIDE].reshape(width, SIDE)
    gate_a, gate_b = two_gates(dot(rows, route), first, second)
    lane = lax.broadcasted_iota(jnp.int32, (1, slab), 1)
    gates = jnp.where(lane < SIDE, gate_a, gate_b)
    hidden = dot(rows, w_in)
    back_act = contract_cols(cots, w_out)
    square = hidden * hidden
    bend = jnp.tanh(ROOT2PI * hidden * (1.0 + 0.044715 * square))
    half = 0.5 * (1.0 + bend)
    act = (hidden * half).astype(jnp.bfloat16).astype(jnp.float32)
    slope = half + 0.5 * hidden * (1.0 - bend * bend) * (ROOT2PI * (1.0 + 0.134145 * square))
    gated = (gates * act).astype(jnp.bfloat16)
    grad_pre = (gates * back_act * slope).astype(jnp.bfloat16)
    product = (act * back_act).astype(jnp.bfloat16)
    signs = jnp.broadcast_to(jnp.where(lane < SIDE, 1.0, -1.0), (8, slab)).astype(jnp.bfloat16)
    gate_row[:, :PACK] = contract_cols(signs, product)
    mixed = dot(gated, w_out).astype(jnp.bfloat16)
    grads = contract_cols(grad_pre, w_in)
    grad = jnp.concatenate([grads, gate_row[...]], axis=0).astype(jnp.bfloat16)
    return gated, grad_pre, mixed, grad


def sum_kernel(
    pack_task, task_experts, in_terms, out_terms, d_in, d_out_own, d_out_far, heads, nexts,
    total_in, total_out,
):
    z, g = lax.axis_index("gx"), lax.axis_index("gy")
    experts = d_out_own.shape[0]
    slots = in_terms.shape[0] * in_terms.shape[1]

    @pl.when(pl.program_id(0) == 0)
    def list_uses():
        def clear(e, carry):
            heads[e] = -1
            return carry

        lax.fori_loop(0, experts, clear, 0)
        step_x, step_y = 2 - 4 * ((g // 2) % 2), 4 - 8 * (g // 4)

        def one(slot, carry):
            rel, k, p = slot // 8, (slot // 2) % 4, slot % 2
            at = g + step_x * (rel % 2) + step_y * (rel // 2)
            task = pack_task[(((z + k) % 4) * 8 + at) * 2 + p]
            for i in range(2):
                e = task_experts[i, task]
                nexts[slot * 2 + i] = heads[e]
                heads[e] = slot * 2 + i
            return carry

        lax.fori_loop(0, slots, one, 0)

    def terms(use):
        slot = use // 2
        rel, at, half = slot // 8, slot % 8, pl.multiple_of((use % 2) * SIDE, SIDE)
        return (
            in_terms[rel, at, :, pl.ds(half, SIDE)].astype(jnp.float32),
            out_terms[rel, at, pl.ds(half, SIDE), :].astype(jnp.float32),
        )

    def add_terms(use):
        new_in, new_out = terms(use)
        total_in[...] += new_in
        total_out[...] += new_out
        return nexts[use]

    own = pl.ds(pl.multiple_of((g % 2) * HEAD, HEAD), HEAD)
    far = pl.ds(pl.multiple_of((1 - g % 2) * HEAD, HEAD), HEAD)

    def one_expert(i, carry):
        head = heads[i]

        @pl.when(head < 0)
        def unused():
            total_in[...] = jnp.zeros_like(total_in)
            total_out[...] = jnp.zeros_like(total_out)

        @pl.when(head >= 0)
        def used():
            total_in[...], total_out[...] = terms(head)
            lax.while_loop(lambda use: use >= 0, add_terms, nexts[head])

        low = total_in[...].astype(jnp.bfloat16).reshape(-1, 2, 16, SIDE)
        d_in[0, :, i] = low[:, 0]
        d_in[1, :, i] = low[:, 1]
        d_out_own[i] = total_out[own, :].astype(jnp.bfloat16)
        d_out_far[i] = total_out[far, :].astype(jnp.bfloat16)
        return carry

    lax.fori_loop(0, experts, one_expert, 0)


class Collect:
    def __init__(self, place, part, corner, from_x, from_y, from_z, packs, half, sems):
        self.place, self.part = place, part
        self.corner, self.from_x, self.from_y, self.from_z = corner, from_x, from_y, from_z
        self.packs, self.half, self.started = packs, half, []
        self.send_sem, self.recv_sem = sems

    def go(self, kind, src, dst, at_send, at_recv, device):
        send(
            self.started, src, dst, self.send_sem.at[kind, at_send],
            self.recv_sem.at[kind, at_recv], device,
        )

    def opposite(self, k, p):
        at = k * self.packs + p
        towards = 2 if self.half(k, p) == 0 else 1
        self.go(3, self.part(3, k, p), self.corner.at[at], at, at, self.place.device(towards, 0))

    def straight(self, k, p):
        at = k * self.packs + p
        if self.half(k, p) == 0:
            self.go(2, self.part(2, k, p), self.from_y.at[at], at, at, self.place.device(2, 0))
        else:
            self.go(1, self.part(1, k, p), self.from_x.at[at], at, at, self.place.device(1, 0))

    def helped(self, k, p, mine):
        at = k * self.packs + p
        ref = self.corner.at[at]
        arrived(ref, self.recv_sem.at[3, at])
        total = ref[...].astype(jnp.float32) + mine().astype(jnp.float32)
        ref[...] = total.astype(jnp.bfloat16)
        if self.half(k, p) == 0:
            self.go(1, ref, self.from_x.at[at], at, at, self.place.device(1, 0))
        else:
            self.go(2, ref, self.from_y.at[at], at, at, self.place.device(2, 0))

    def plane(self, k, p, mine):
        at = k * self.packs + p
        arrived(self.from_x.at[at], self.recv_sem.at[1, at])
        arrived(self.from_y.at[at], self.recv_sem.at[2, at])
        total = self.from_x[at].astype(jnp.float32) + self.from_y[at].astype(jnp.float32)
        total = total + mine().astype(jnp.float32)
        if k:
            self.from_x[at] = total.astype(jnp.bfloat16)
            there = back(k) * self.packs + p
            self.go(
                0, self.from_x.at[at], self.from_z.at[there], at, there, self.place.device(0, k)
            )
            return None
        for other in (1, 2, 3):
            at = other * self.packs + p
            arrived(self.from_z.at[at], self.recv_sem.at[0, at])
            total = total + self.from_z[at].astype(jnp.float32)
        return total

    def finish(self):
        for copy in self.started:
            copy.wait_send()


class Return:
    def __init__(self, place, part, own, from_z, sems, load):
        self.place, self.part, self.own, self.from_z = place, part, own, from_z
        self.send_sem, self.recv_sem, self.z_sem = sems
        self.started, self.loads = [], {}
        for kind, j, p in self.needs:
            rel = self.beside(p) if kind else 0
            at = self.at(j, p)
            self.loads[kind, j, p] = load(part.at[rel, at], own.at[kind, at])

    needs = [(kind, j, p) for j in range(4) for p in range(2) for kind in (1, 0)]

    def at(self, j, p):
        return self.place.nearest(3 - j) * 2 + p

    def beside(self, p):
        return 1 + p

    def go(self, kind, at, src, dst, recv_sem, device):
        send(self.started, src, dst, self.send_sem.at[kind, at], recv_sem, device)

    def mine(self, kind, j, p):
        return self.own[kind, self.at(j, p)].astype(jnp.float32)

    def along(self, kind, send_kind, j, p, ref, total):
        place = self.place
        k = place.nearest(3 - j)
        step = 2 * ((place.plane(k) - place.z + 3) // 4) - 1
        behind = self.from_z.at[kind, k * 2 + p]
        more = (place.z - step >= 0) & (place.z - step <= 3)

        @pl.when(more)
        def add():
            arrived(behind, self.z_sem.at[kind, k * 2 + p])
            ref[...] = (total() + behind[...].astype(jnp.float32)).astype(jnp.bfloat16)

        @pl.when(jnp.logical_not(more))
        def first():
            ref[...] = total().astype(jnp.bfloat16)

        there = (k - step + 4) % 4
        slot = (there + (4 - there) // 4 * (2 - 2 * step)) * 2 + p
        self.go(
            send_kind, k * 2 + p, ref, self.from_z.at[kind, slot], self.z_sem.at[kind, slot],
            (place.plane(step + 4), place.at[0]),
        )

    def owned(self, kind, p, total, out):
        out[...] = total()
        for slot, comes in ((p, self.place.z > 0), (8 + p, self.place.z < 3)):

            @pl.when(comes)
            def add(slot=slot):
                ref = self.from_z.at[kind, slot]
                arrived(ref, self.z_sem.at[kind, slot])
                out[...] += ref[...].astype(jnp.float32)

    def finish(self):
        for copy in self.started:
            copy.wait_send()


class PlaneFirst(Return):
    def __init__(self, place, part, own, from_z, sems, load, corner, from_x, from_y, got):
        self.corner, self.near, self.early = corner, (None, from_x, from_y), {}
        for i, (j, rel) in enumerate(EARLY):
            for p in range(2):
                into = corner if rel == 3 else self.near[2 - p]
                at = place.nearest(3 - j) * 2 + p
                self.early[rel == 3, j, p] = load(got[p].at[i], into.at[at])
        super().__init__(place, part, own, from_z, sems, load)

    def here(self, far, j, p, ref, sem):
        if (far, j, p) in self.early:
            self.early[far, j, p].wait()
        else:
            arrived(ref, sem)

    def first(self, j, p):
        at, way = self.at(j, p), 2 - p
        if (True, j, p) not in self.early:
            self.go(
                3, at, self.part.at[3, at], self.corner.at[at], self.recv_sem.at[3, at],
                self.place.device(way, 0),
            )
        if (False, j, p) not in self.early:
            self.go(
                way, at, self.part.at[way, at], self.near[way].at[at], self.recv_sem.at[way, at],
                self.place.device(way, 0),
            )

    def helped(self, j, p):
        at, way = self.at(j, p), 1 + p
        ref = self.corner.at[at]
        self.loads[1, j, p].wait()
        self.here(True, j, p, ref, self.recv_sem.at[3, at])
        ref[...] = (ref[...].astype(jnp.float32) + self.mine(1, j, p)).astype(jnp.bfloat16)
        self.go(
            way, at, ref, self.near[way].at[at], self.recv_sem.at[way, at],
            self.place.device(way, 0),
        )

    def plane(self, j, p, out):
        at = self.at(j, p)
        self.loads[0, j, p].wait()
        self.here(False, j, p, self.near[2 - p].at[at], self.recv_sem.at[2 - p, at])
        arrived(self.near[1 + p].at[at], self.recv_sem.at[1 + p, at])

        def total():
            both = self.near[1][at].astype(jnp.float32) + self.near[2][at].astype(jnp.float32)
            return both + self.mine(0, j, p)

        if j < 3:
            self.along(0, 0, j, p, self.near[1].at[at], total)
        else:
            self.owned(0, p, total, out)


class SideFirst(Return):
    def __init__(self, place, part, own, from_z, sems, load, near, last, total):
        super().__init__(place, part, own, from_z, sems, load)
        self.near, self.last, self.total = near, last, total

    def first(self, j, p):
        at, way = self.at(j, p), 2 - p
        for kind, rel in ((1, 3), (0, way)):
            self.go(
                kind, at, self.part.at[rel, at], self.near.at[kind, at],
                self.recv_sem.at[kind, at], self.place.device(way, 0),
            )

    def plane(self, j, p, out):
        at, way = self.at(j, p), 1 + p
        for kind in (1, 0):
            ref = self.near.at[kind, at]
            self.loads[kind, j, p].wait()
            arrived(ref, self.recv_sem.at[kind, at])

            def total(kind=kind, ref=ref):
                return ref[...].astype(jnp.float32) + self.mine(kind, j, p)

            if j < 3:
                self.along(kind, 2 + kind, j, p, ref, total)
            elif kind:
                self.owned(kind, p, total, self.total)
                ref[...] = self.total[...].astype(jnp.bfloat16)
                self.go(
                    2, at, ref, self.last.at[p], self.recv_sem.at[2, p], self.place.device(way, 0)
                )
            else:
                self.owned(kind, p, total, out)
        if j == 3:
            arrived(self.last.at[p], self.recv_sem.at[2, p])
            out[...] += self.last[p].astype(jnp.float32)


def tail_kernel(
    pack_task, task_experts, tok, cot, segments, proj, heads, middle, dense, grad_part, mixed_part,
    d_in, d_out_far, got_y, got_x,
    mixed, d_tok, d_dense, d_in_all, d_out_all,
    g_own, g_corner, g_x, g_y, g_z, m_own, m_near, m_last, m_z, m_total, m_out,
    total_grad, grad_mid, grad_heads, grad_qkv, acc, small_rows, turned, flat_ids, tall_ids,
    in_far, in_mine, far_dense, got_dense, part_dense, s_corner, s_x, s_y, s_z,
    g_send, g_recv, gz_recv, m_send, m_recv, mz_recv, s_send, s_recv, in_send, in_recv,
    pair_send, pair_recv, load_sem,
):
    place = Place()
    width = tok.shape[2]
    place.greet()

    loads = []

    def load(src, dst):
        copy = pltpu.make_async_copy(src, dst, load_sem.at[len(loads)])
        copy.start()
        loads.append(copy)
        return copy

    grads = PlaneFirst(
        place, grad_part, g_own, g_z, (g_send, g_recv, gz_recv), load, g_corner, g_x, g_y,
        (got_y, got_x),
    )
    in_load = load(d_in.at[place.core], in_mine)
    mixes = SideFirst(
        place, mixed_part, m_own, m_z, (m_send, m_recv, mz_recv), load, m_near, m_last, m_total
    )
    pair_started, in_started, kept = [], [], {}
    planes = (2, 1, 3, 0)

    same_documents(segments, flat_ids, tall_ids)
    small = dense[:, :, 4 * width : 4 * width + SIDE].reshape(width, SIDE)
    turned[...] = jnp.transpose(small.astype(jnp.float32))
    small_rows[...] = jnp.zeros_like(small_rows)
    gain_one, bias_one, gain_two, bias_two = (
        turned[GAIN_ONE + i : GAIN_ONE + i + 1, :] for i in range(4)
    )

    place.meet()

    def pair():
        send(
            pair_started, d_in.at[1 - place.core], in_far, pair_send.at[0], pair_recv.at[0],
            place.sibling,
        )
        send(
            pair_started, d_out_far, d_out_all, pair_send.at[1], pair_recv.at[1], place.sibling
        )

    def addpair():
        in_load.wait()
        arrived(in_far, pair_recv.at[0])

        def one(i, carry):
            total = in_mine[i].astype(jnp.float32) + in_far[i].astype(jnp.float32)
            in_mine[i] = total.astype(jnp.bfloat16)
            return carry

        lax.fori_loop(0, in_mine.shape[0], one, 0)
        columns = pl.ds(pl.multiple_of(place.chip(0, 0) * SIDE, SIDE), SIDE)
        kept["local"] = load(in_mine.at[place.chip(0, 0)], d_in_all.at[:, :, columns])

    def win(rel, j):
        k = planes[j]
        columns = pl.ds(pl.multiple_of(place.chip(0, 0) * SIDE, SIDE), SIDE)
        send(
            in_started, in_mine.at[place.chip(rel, k)], d_in_all.at[:, :, columns],
            in_send.at[rel, k], in_recv.at[rel, back(k)], place.device(rel, k),
        )

    def mplane(j, p):
        mixes.plane(j, p, m_out)
        if j == 3:
            mixed[p] = (middle[p, :PACK] + m_out[...]).astype(jnp.bfloat16)

    def add_to(p, columns, value):
        if p == 0:
            acc[:, columns] = value
        else:
            acc[:, columns] += value

    def add_row(at, value):
        small_rows[at : at + 1, :] += jnp.sum(value, 0, keepdims=True)

    def att(part):
        p = part // 3
        (att_routed, att_heads, att_normed)[part % 3](p)

    def att_routed(p):
        first, second = place.pair(pack_task, task_experts, 0, 0, p)
        got = total_grad[p]
        tall = jnp.concatenate(
            [got[PACK:, : 2 * SIDE], jnp.zeros((SIDE - 8, 2 * SIDE), jnp.float32)], axis=0
        )
        gap_grad = jnp.transpose(tall)[:ROWS, 0:1]
        got = jnp.where(real_rows(), got, 0.0)
        mid = middle[p]
        unit, rise = norm_parts(mid)
        routed = jnp.where(real_rows(), unit * gain_two + bias_two, 0.0).astype(jnp.bfloat16)
        route = dense[:, :, 4 * width : 4 * width + SIDE].reshape(width, SIDE)
        gate_a, gate_b = two_gates(dot(routed, route), first, second)
        grad_a = gate_a * gate_b * gap_grad
        lane = lax.broadcasted_iota(jnp.int32, (ROWS, SIDE), 1)
        grad_logits = jnp.where(lane == first, grad_a, jnp.where(lane == second, -grad_a, 0.0))
        grad_logits = jnp.where(real_rows(), grad_logits, 0.0).astype(jnp.bfloat16)
        add_to(p, pl.ds(4 * width, SIDE), contract_rows(routed, grad_logits))
        got = got + contract_cols(grad_logits, route)
        add_row(2, got * unit)
        add_row(3, got)
        u = got * gain_two
        grad_middle = lengthened(cot, p) + rise * (
            u - jnp.mean(u, -1, keepdims=True) - unit * jnp.mean(u * unit, -1, keepdims=True)
        )
        grad_mid[...] = grad_middle
        attended = grad_middle.astype(jnp.bfloat16)
        add_to(p, pl.ds(3 * width, width), contract_rows(heads[p], attended))
        w_attn = dense[:, :, 3 * width : 4 * width].reshape(width, width)
        grad_heads[...] = contract_cols(attended, w_attn).astype(jnp.bfloat16)

    def att_heads(p):
        same = same_document(flat_ids, tall_ids, p)

        def pair_of_heads(j, carry):
            at = pl.multiple_of(j * SIDE, SIDE)
            queries = proj[p, :, pl.ds(at, SIDE)]
            keys = proj[p, :, pl.ds(at + width, SIDE)]
            values = proj[p, :, pl.ds(at + 2 * width, SIDE)]
            out_grad = grad_heads[:, pl.ds(at, SIDE)]
            zero = jnp.zeros((ROWS, SIDE), jnp.float32)
            grad_q, grad_k, grad_v = zero, zero, zero
            for h in range(2):
                lanes = head_lanes(h)
                probs = softmax_rows(queries * lanes, keys, same)
                mine_grad = out_grad * lanes
                grad_v = grad_v + contract_rows(probs.astype(jnp.bfloat16), mine_grad)
                grad_probs = contract_cols(mine_grad, values)
                row_dot = jnp.sum(probs * grad_probs, -1, keepdims=True)
                grad_scores = (probs * (grad_probs - row_dot)).astype(jnp.bfloat16)
                grad_q = grad_q + dot(grad_scores, keys * lanes)
                grad_k = grad_k + contract_rows(grad_scores, queries * lanes)
            scale = 1.0 / math.sqrt(HEAD)
            grad_qkv[:, pl.ds(at, SIDE)] = (grad_q * scale).astype(jnp.bfloat16)
            grad_qkv[:, pl.ds(at + width, SIDE)] = (grad_k * scale).astype(jnp.bfloat16)
            grad_qkv[:, pl.ds(at + 2 * width, SIDE)] = grad_v.astype(jnp.bfloat16)
            return carry

        lax.fori_loop(0, width // SIDE, pair_of_heads, 0)

    def att_normed(p):
        unit, rise = norm_parts(lengthened(tok, p))
        normed = (unit * gain_one + bias_one).astype(jnp.bfloat16)
        add_to(p, pl.ds(0, 3 * width), contract_rows(normed, grad_qkv[...]))
        w_qkv = dense[:, :, : 3 * width].reshape(width, 3 * width)
        grad_normed = contract_cols(grad_qkv[...], w_qkv)
        add_row(0, grad_normed * unit)
        add_row(1, grad_normed)
        u = grad_normed * gain_one
        d_tok[p] = (
            grad_mid[...]
            + rise
            * (u - jnp.mean(u, -1, keepdims=True) - unit * jnp.mean(u * unit, -1, keepdims=True))
        ).astype(jnp.bfloat16)

    def dense_part(rel, k, p):
        return got_dense.at[place.chip(rel, k)]

    sums = Collect(
        place, dense_part, s_corner, s_x, s_y, s_z, 1, lambda k, p: k % 2, (s_send, s_recv)
    )
    def dense_step():
        tall = jnp.concatenate(
            [
                jnp.zeros((GAIN_ONE, width), jnp.float32),
                small_rows[...],
                jnp.zeros((SIDE - GAIN_ONE - 8, width), jnp.float32),
            ],
            axis=0,
        )
        acc[:, 4 * width :] += jnp.transpose(tall)
        columns_all = acc.shape[1]

        def cut(i, carry):
            own_rows = pl.ds(pl.multiple_of(i * 32 + place.core * 16, 16), 16)
            far_rows = pl.ds(pl.multiple_of(i * 32 + 16 - place.core * 16, 16), 16)
            far_dense[i] = acc[far_rows, :].astype(jnp.bfloat16)
            part_dense[i] = acc[own_rows, :]
            return carry

        lax.fori_loop(0, 16, cut, 0)
        send(
            pair_started, far_dense, got_dense, pair_send.at[2], pair_recv.at[2], place.sibling
        )
        arrived(got_dense, pair_recv.at[2])

        def join(i, carry):
            far_dense_sum = part_dense[i] + got_dense[i].astype(jnp.float32)
            got_dense[i] = far_dense_sum.astype(jnp.bfloat16)
            return carry

        lax.fori_loop(0, 16, join, 0)

        for k in (2, 1, 3, 0):
            sums.opposite(k, 0)
        for k in (2, 1, 3, 0):
            sums.straight(k, 0)
        for k in (2, 1, 3, 0):
            sums.helped(k, 0, lambda k=k: got_dense[place.chip(1 + k % 2, k)])
        for k in (2, 1, 3):
            sums.plane(k, 0, lambda k=k: got_dense[place.chip(0, k)])
        d_dense[...] = sums.plane(0, 0, lambda: got_dense[place.chip(0, 0)])

    steps = {
        GFIRST: grads.first, GHELP: grads.helped,
        GPLANE: lambda j, p: grads.plane(j, p, total_grad.at[p]),
        MFIRST: mixes.first, MPLANE: mplane, MHELP: lambda j, p: None,
        PAIR: pair, ADDPAIR: addpair, WIN: win, ATT: att, DENSE: dense_step,
    }
    for name, *where in TAIL_STEPS:
        steps[name](*where)

    for rel in range(4):
        for k in range(4):
            if (rel, k) != (0, 0):
                place_columns = pl.ds(pl.multiple_of(place.chip(rel, k) * SIDE, SIDE), SIDE)
                arrived(d_in_all.at[:, :, place_columns], in_recv.at[rel, k])
    kept["local"].wait()
    arrived(d_out_all, pair_recv.at[1])
    for tree in (grads, mixes, sums):
        tree.finish()
    for copy in pair_started + in_started:
        copy.wait_send()


def last_kernel(
    mixed_own, d_tok_tall, d_dense, d_in_low, d_out_own, d_out_far,
    mixed, d_tok, d_qkv, d_attn, d_route, d_in, d_out, gain_one, bias_one, gain_two, bias_two,
):
    width, experts = mixed.shape[2], d_route.shape[1]

    @pl.when(pl.program_id(0) == 0)
    def small():
        for p in range(mixed.shape[0]):
            mixed[p] = mixed_own[p]
            d_tok[p] = d_tok_tall[p, :PACK]
        d_qkv[...] = d_dense[:, : 3 * width]
        d_attn[...] = d_dense[:, 3 * width : 4 * width]
        d_route[...] = d_dense[:, 4 * width : 4 * width + experts]
        rows = jnp.transpose(d_dense[:, 4 * width :])
        for i, ref in enumerate((gain_one, bias_one, gain_two, bias_two)):
            ref[...] = rows[GAIN_ONE + i]

    d_in[...] = d_in_low[...].astype(jnp.float32)
    d_out[...] = d_out_own[...].astype(jnp.float32) + d_out_far[...].astype(jnp.float32)


def shards_fast(
    tokens,
    segment_ids,
    pack_task,
    task_experts,
    w_qkv,
    w_attn_out,
    w_router,
    w_expert_in,
    w_expert_out,
    norm1_gain,
    norm1_bias,
    norm2_gain,
    norm2_bias,
    cotangent,
):
    packs, length, width = tokens.shape
    experts, slab_in, hidden = w_expert_in.shape
    slab_out = w_expert_out.shape[1]
    dense_width = 4 * width + SIDE
    any_space = pl.BlockSpec(memory_space=pl.ANY)
    vmem = pl.BlockSpec(memory_space=pltpu.VMEM)
    smem = pl.BlockSpec(memory_space=pltpu.SMEM)
    low, full = jnp.bfloat16, jnp.float32
    flat = jax.ShapeDtypeStruct
    dma = pltpu.SemaphoreType.DMA
    by_rank = task_experts.T

    blocks = flat((4, 4 * packs, length, width), low)
    tall_blocks = flat((4, 4 * packs, ROWS, width), low)
    in_sums = flat((4, 4 * packs, width, 2 * SIDE), low)
    out_sums = flat((4, 4 * packs, 2 * SIDE, width), low)

    def held(shape):
        return pltpu.VMEM(shape.shape, shape.dtype)

    early_blocks = flat((len(EARLY), ROWS, width), low)
    (
        in_terms, out_terms, mixed_part, grad_part, dense, early_y, early_x, proj, heads, middle,
    ) = pl.pallas_call(
        front_kernel,
        out_shape=(
            in_sums, out_sums, blocks, tall_blocks,
            flat((32, slab_in, dense_width), low),
            early_blocks, early_blocks,
            flat((packs, ROWS, 3 * width), low),
            flat((packs, ROWS, width), low),
            flat((packs, ROWS, width), full),
        ),
        in_specs=[smem] * 2 + [vmem] * 10 + [any_space] * 2,
        out_specs=(any_space,) * 7 + (vmem,) * 3,
        scratch_shapes=[
            pltpu.VMEM((32, slab_in, dense_width), low),
            held(blocks), held(blocks),
            pltpu.VMEM((16, 2, experts, slab_in, SIDE), low),
            pltpu.VMEM((2, experts, slab_out, width), low),
            pltpu.VMEM((2, 4, width, 2 * SIDE), low),
            pltpu.VMEM((2, 4, 2 * SIDE, width), low),
            held(blocks), held(tall_blocks),
            pltpu.VMEM((SIDE, width), full),
            pltpu.VMEM((SIDE, SIDE), full),
            pltpu.VMEM((8, 2 * SIDE), full),
            pltpu.VMEM((2 * SIDE, 8), full),
            pltpu.VMEM((4, 8, width), full),
            dma((7, 8)), dma((4, 8)), dma((5, 8)), dma((4, 8)), dma((5, 4)), dma((4, 4)),
            dma((4, 4)), dma((4, 4)), dma((4, 4)), dma((4, 4)), dma((2,)), dma((2,)), dma((3,)),
            dma((32,)), dma((2, len(EARLY))),
        ],
        compiler_params=pltpu.CompilerParams(
            collective_id=0, has_side_effects=True, vmem_limit_bytes=60 << 20
        ),
        name="front",
    )(
        pack_task, by_rank, tokens, segment_ids, w_qkv, w_attn_out, w_router,
        norm1_gain, norm1_bias, norm2_gain, norm2_bias, cotangent, w_expert_in, w_expert_out,
    )

    across = lax.axis_size("gy")
    got_y = lax.ppermute(early_y, "gy", [(i, i ^ 4) for i in range(across)])
    got_x = lax.ppermute(early_x, "gy", [(i, i ^ 2) for i in range(across)])

    part = width // 2

    by_columns = pl.BlockSpec((experts, slab_out, part), lambda i, *unused: (0, 0, i))
    d_in, d_out_own, d_out_far = pl.pallas_call(
        sum_kernel,
        grid_spec=pltpu.PrefetchScalarGridSpec(
            num_scalar_prefetch=2,
            grid=(2,),
            in_specs=[
                pl.BlockSpec((4, 4 * packs, part, 2 * SIDE), lambda i, *unused: (0, 0, i, 0)),
                pl.BlockSpec((4, 4 * packs, 2 * SIDE, part), lambda i, *unused: (0, 0, 0, i)),
            ],
            out_specs=[
                pl.BlockSpec((2, 8, experts, slab_in, SIDE), lambda i, *unused: (0, i, 0, 0, 0)),
                by_columns, by_columns,
            ],
            scratch_shapes=[
                pltpu.SMEM((experts,), jnp.int32),
                pltpu.SMEM((32 * packs,), jnp.int32),
                pltpu.VMEM((part, SIDE), full),
                pltpu.VMEM((SIDE, part), full),
            ],
        ),
        out_shape=(
            flat((2, 16, experts, slab_in, SIDE), low),
            flat((experts, slab_out, width), low),
            flat((experts, slab_out, width), low),
        ),
        compiler_params=pltpu.CompilerParams(vmem_limit_bytes=60 << 20),
        cost_estimate=pl.CostEstimate(
            flops=10**10, bytes_accessed=40 * 10**6, transcendentals=0
        ),
        name="sums",
    )(pack_task, by_rank, in_terms, out_terms)

    parts = pltpu.VMEM((4 * packs, ROWS, width), low)
    slices = pltpu.VMEM((4, slab_in, dense_width), low)
    sliced = pltpu.VMEM((16, slab_in, dense_width), low)
    mixed_own, d_tok_tall, d_dense, d_in_all, d_out_all = pl.pallas_call(
        tail_kernel,
        out_shape=(
            flat((packs, length, width), low),
            flat((packs, ROWS, width), low),
            flat((slab_in, dense_width), full),
            flat((experts, slab_in, hidden), low),
            flat((experts, slab_out, width), low),
        ),
        in_specs=[smem] * 2 + [vmem] * 7 + [any_space] * 6,
        out_specs=(vmem,) * 3 + (any_space,) * 2,
        scratch_shapes=[
            pltpu.VMEM((2, 4 * packs, ROWS, width), low), parts, parts, parts,
            pltpu.VMEM((1, 5 * packs, ROWS, width), low),
            pltpu.VMEM((2, 4 * packs, length, width), low),
            pltpu.VMEM((2, 4 * packs, length, width), low),
            pltpu.VMEM((packs, length, width), low),
            pltpu.VMEM((2, 5 * packs, length, width), low),
            pltpu.VMEM((length, width), full),
            pltpu.VMEM((length, width), full),
            pltpu.VMEM((packs, ROWS, width), full),
            pltpu.VMEM((ROWS, width), full),
            pltpu.VMEM((ROWS, width), low),
            pltpu.VMEM((ROWS, 3 * width), low),
            pltpu.VMEM((width, dense_width), full),
            pltpu.VMEM((8, width), full),
            pltpu.VMEM((SIDE, width), full),
            pltpu.VMEM((8, 2 * SIDE), full),
            pltpu.VMEM((2 * SIDE, 8), full),
            pltpu.VMEM((16, experts, slab_in, SIDE), low),
            pltpu.VMEM((16, experts, slab_in, SIDE), low),
            sliced, sliced,
            pltpu.VMEM((16, slab_in, dense_width), full),
            slices, slices, slices, slices,
            dma((4, 8)), dma((4, 8)), dma((1, 10)), dma((4, 8)), dma((4, 8)), dma((2, 10)),
            dma((4, 4)), dma((4, 4)), dma((4, 4)), dma((4, 4)), dma((3,)), dma((3,)), dma((48,)),
        ],
        compiler_params=pltpu.CompilerParams(
            collective_id=1, has_side_effects=True, vmem_limit_bytes=60 << 20
        ),
        name="tail",
    )(
        pack_task, by_rank, tokens, cotangent, segment_ids, proj, heads, middle, dense,
        grad_part, mixed_part, d_in, d_out_far, got_y, got_x,
    )

    group = experts // 2

    def some(rows, columns):
        return pl.BlockSpec((group, rows, columns), lambda i: (i, 0, 0))

    def whole(*shape):
        return pl.BlockSpec(shape, lambda i: (0,) * len(shape))

    return pl.pallas_call(
        last_kernel,
        grid=(2,),
        in_specs=[
            whole(packs, length, width), whole(packs, ROWS, width), whole(slab_in, dense_width),
            some(slab_in, hidden), some(slab_out, width), some(slab_out, width),
        ],
        out_specs=(
            whole(packs, length, width), whole(packs, length, width),
            whole(slab_in, 3 * width), whole(slab_in, width), whole(slab_in, experts),
            some(slab_in, hidden), some(slab_out, width),
        ) + (whole(slab_in),) * 4,
        out_shape=(
            flat((packs, length, width), low), flat((packs, length, width), low),
            flat((slab_in, 3 * width), full), flat((slab_in, width), full),
            flat((slab_in, experts), full),
            flat((experts, slab_in, hidden), full), flat((experts, slab_out, width), full),
        ) + (flat((slab_in,), full),) * 4,
        compiler_params=pltpu.CompilerParams(vmem_limit_bytes=60 << 20),
        name="last",
    )(mixed_own, d_tok_tall, d_dense, d_in_all, d_out_own, d_out_all)


def solution(mesh):
    outer, inner = mesh.shape["gx"], mesh.shape["gy"]

    def shards(*arrays):
        packs, length, width = arrays[0].shape
        experts, slab_in, hidden = arrays[7].shape
        fits = (
            (outer, inner) == (4, 8)
            and packs == 2
            and length == PACK
            and experts == GAIN_ONE
            and width == HEADS * HEAD
            and slab_in == 16
            and hidden == 16 * SIDE
        )
        return (shards_fast if fits else shards_any)(*arrays)

    placed = (
        P(("gx", "gy"), None, None),
        P(("gx", "gy"), None),
        P(),
        P(),
        P(("gx", "gy"), None),
        P(("gx", "gy"), None),
        P(("gx", "gy"), None),
        P(None, ("gx", "gy"), None),
        P(None, ("gx", "gy"), None),
        P(("gx", "gy")),
        P(("gx", "gy")),
        P(("gx", "gy")),
        P(("gx", "gy")),
        P(("gx", "gy"), None, None),
    )
    return jax.shard_map(
        shards,
        mesh=mesh,
        in_specs=placed,
        out_specs=(
            P(("gx", "gy"), None, None),
            P(("gx", "gy"), None, None),
            P(("gx", "gy"), None),
            P(("gx", "gy"), None),
            P(("gx", "gy"), None),
            P(None, ("gx", "gy"), None),
            P(None, ("gx", "gy"), None),
            P(("gx", "gy")),
            P(("gx", "gy")),
            P(("gx", "gy")),
            P(("gx", "gy")),
        ),
        check_vma=False,
    )
```

```python
import functools
import math

import jax
import jax.numpy as jnp
from jax import lax
from jax.experimental import pallas as pl
from jax.experimental.pallas import tpu as pltpu
from jax.sharding import PartitionSpec as P

HEADS = 8
HEAD = 64
PACK = 216
GAIN_ONE = 32


EPS = 1e-05
MASK_FILL = -1e30
HIGH = lax.Precision.HIGHEST


def shortened(value):

    def short(part):
        return part.astype(jnp.bfloat16) if part.dtype == jnp.float32 else part

    return jax.tree.map(short, value)


def layer_norm(values, gain, bias):
    center = values - jnp.mean(values, -1, keepdims=True)
    spread = jnp.mean(center * center, -1, keepdims=True)
    return center * lax.rsqrt(spread + EPS) * gain + bias


def contract_rows(left, right):
    return lax.dot_general(
        left, right, (((0,), (0,)), ((), ())), preferred_element_type=jnp.float32
    )


def contract_cols(left, right):
    return lax.dot_general(
        left, right, (((1,), (1,)), ((), ())), preferred_element_type=jnp.float32
    )


def shards_any(
    tokens,
    segment_ids,
    pack_task,
    task_experts,
    w_qkv,
    w_attn_out,
    w_router,
    w_expert_in,
    w_expert_out,
    norm1_gain,
    norm1_bias,
    norm2_gain,
    norm2_bias,
    cotangent,
):
    outer = lax.axis_size("gx")
    inner = lax.axis_size("gy")
    devices = outer * inner
    micro, length, width = tokens.shape
    experts, slab_in, hidden = w_expert_in.shape
    slab_out = w_expert_out.shape[1]
    head_size = width // HEADS
    scale = 1.0 / math.sqrt(head_size)
    device = lax.axis_index("gx") * inner + lax.axis_index("gy")
    gathered = (
        lax.all_gather(w_qkv, ("gx", "gy"), axis=0, tiled=True),
        lax.all_gather(w_attn_out, ("gx", "gy"), axis=0, tiled=True),
        lax.all_gather(w_router, ("gx", "gy"), axis=0, tiled=True),
        lax.all_gather(norm1_gain, ("gx", "gy"), axis=0, tiled=True),
        lax.all_gather(norm1_bias, ("gx", "gy"), axis=0, tiled=True),
        lax.all_gather(norm2_gain, ("gx", "gy"), axis=0, tiled=True),
        lax.all_gather(norm2_bias, ("gx", "gy"), axis=0, tiled=True),
    )
    qkv_full, attn_full, route_full = (gathered[0], gathered[1], gathered[2])
    gain_one, bias_one, gain_two, bias_two = tuple(
        (piece.astype(jnp.float32) for piece in gathered[3:])
    )
    route_float = route_full.astype(jnp.float32)
    pack_pairs = task_experts[pack_task]
    needs = jnp.transpose(pack_pairs.reshape(outer, inner, micro, 2), (2, 3, 0, 1))
    route_pairs = jnp.transpose(pack_pairs.reshape(devices, micro, 2), (1, 0, 2))
    own_pairs = lax.dynamic_slice_in_dim(pack_pairs, device * micro, micro, 0)
    expert_ids = jnp.arange(experts, dtype=jnp.int32)

    def slabs(need):
        return (w_expert_in[need], w_expert_out[need])

    def joined(pieces):
        return (
            pieces[0].reshape(pieces[0].shape[0], width, hidden),
            pieces[1].reshape(pieces[1].shape[0], hidden, width),
        )

    def attention_probs(project, segment):
        queries = project[:, :width].reshape(length, HEADS, head_size)
        keys_all = project[:, width : 2 * width].reshape(length, HEADS, head_size)
        scores = (
            jnp.einsum("qhd,khd->hqk", queries, keys_all, preferred_element_type=jnp.float32)
            * scale
        )
        same_doc = segment[:, None] == segment[None, :]
        return jnp.where(same_doc[None], scores, MASK_FILL)

    def forward_step(carry, inputs):
        block, segment, need, pair, senders = inputs
        block_float = block.astype(jnp.float32)
        normed = layer_norm(block_float, gain_one, bias_one).astype(jnp.bfloat16)
        project = jnp.dot(normed, qkv_full, preferred_element_type=jnp.float32).astype(jnp.bfloat16)
        masked = attention_probs(project, segment)
        peak = jnp.max(masked, -1, keepdims=True)
        raised = jnp.exp(masked - peak)
        totals = jnp.sum(raised, -1, keepdims=True)
        log_total = peak + jnp.log(totals)
        attn_low = (raised / totals).astype(jnp.bfloat16)
        values_all = project[:, 2 * width :].reshape(length, HEADS, head_size)
        heads_out = (
            jnp.einsum("hqk,khd->qhd", attn_low, values_all, preferred_element_type=jnp.float32)
            .reshape(length, width)
            .astype(jnp.bfloat16)
        )
        middle = block_float + jnp.dot(heads_out, attn_full, preferred_element_type=jnp.float32)
        routed = layer_norm(middle, gain_two, bias_two).astype(jnp.bfloat16)
        logits = jnp.dot(routed, route_full, preferred_element_type=jnp.float32)
        select = (expert_ids[None, :] == pair[:, None]).astype(jnp.float32)
        chosen = jnp.sum(logits[:, None, :] * select[None], -1)
        raised_gate = jnp.exp(chosen - jnp.max(chosen, -1, keepdims=True))
        gates = raised_gate / jnp.sum(raised_gate, -1, keepdims=True)
        weights_in, weights_out = joined(
            lax.all_to_all(
                lax.all_to_all(
                    shortened(slabs(need)), "gx", split_axis=1, concat_axis=1, tiled=True
                ),
                "gy",
                split_axis=2,
                concat_axis=2,
                tiled=True,
            )
        )
        hidden_pre = jnp.einsum(
            "ld,kdf->klf", routed, weights_in, preferred_element_type=jnp.float32
        )
        hidden_low = jax.nn.gelu(hidden_pre).astype(jnp.bfloat16)
        expert_out = jnp.einsum(
            "klf,kfd->kld", hidden_low, weights_out, preferred_element_type=jnp.float32
        )
        saved = ()
        mixed = middle + gates[:, 0:1] * expert_out[0] + gates[:, 1:2] * expert_out[1]
        kept = (
            normed,
            project,
            log_total,
            heads_out,
            middle,
            routed,
            gates,
            hidden_pre,
            hidden_low,
            expert_out,
            saved,
        )
        return (carry, (mixed.astype(jnp.bfloat16), kept))

    start = jnp.zeros((), jnp.float32)
    unused, (mixed_all, kept_all) = lax.scan(
        forward_step, start, (tokens, segment_ids, needs, own_pairs, route_pairs)
    )

    def backward_step(carry, inputs):
        dense_acc, shard_in, shard_out, holding = carry
        block, grad_top, segment, need, pair, kept = inputs
        (
            normed,
            project,
            log_total,
            heads_out,
            middle,
            routed,
            gates,
            hidden_pre,
            hidden_low,
            expert_out,
            saved,
        ) = kept
        grad_float = grad_top.astype(jnp.float32)
        grad_gate = jnp.sum(grad_float[None] * expert_out, -1).T
        grad_chosen = gates * (grad_gate - jnp.sum(gates * grad_gate, -1, keepdims=True))
        select = (expert_ids[None, :] == pair[:, None]).astype(jnp.float32)
        grad_logits = jnp.sum(grad_chosen[:, :, None] * select[None], 1)
        routed_float = routed.astype(jnp.float32)
        grad_route = jnp.dot(routed_float.T, grad_logits, precision=HIGH)
        grad_routed = jnp.dot(grad_logits, route_float.T, precision=HIGH)
        grad_eout = (gates.T[:, :, None] * grad_float[None]).astype(jnp.bfloat16)
        slot = ()
        weights_in, weights_out = joined(
            lax.all_to_all(
                lax.all_to_all(
                    shortened(slabs(need)), "gx", split_axis=1, concat_axis=1, tiled=True
                ),
                "gy",
                split_axis=2,
                concat_axis=2,
                tiled=True,
            )
        )
        grad_act = jnp.einsum(
            "kld,kfd->klf", grad_eout, weights_out, preferred_element_type=jnp.float32
        )
        unused_act, gelu_back = jax.vjp(jax.nn.gelu, hidden_pre)
        grad_pre = gelu_back(grad_act)[0].astype(jnp.bfloat16)
        grad_in = jnp.einsum("ld,klf->kdf", routed, grad_pre, preferred_element_type=jnp.float32)
        grad_out = jnp.einsum(
            "klf,kld->kfd", hidden_low, grad_eout, preferred_element_type=jnp.float32
        )
        grad_routed = grad_routed + jnp.einsum(
            "klf,kdf->ld", grad_pre, weights_in, preferred_element_type=jnp.float32
        )
        slot = (grad_in, grad_out)
        unused_two, norm_two_back = jax.vjp(layer_norm, middle, gain_two, bias_two)
        grad_mid_norm, grad_gain_two, grad_bias_two = norm_two_back(grad_routed)
        grad_middle = grad_float + grad_mid_norm
        grad_attended = grad_middle.astype(jnp.bfloat16)
        grad_attn_w = contract_rows(heads_out, grad_attended)
        grad_heads = (
            contract_cols(grad_attended, attn_full)
            .astype(jnp.bfloat16)
            .reshape(length, HEADS, head_size)
        )
        masked = attention_probs(project, segment)
        probs_float = jnp.exp(masked - log_total)
        probs_low = probs_float.astype(jnp.bfloat16)
        queries = project[:, :width].reshape(length, HEADS, head_size)
        keys_all = project[:, width : 2 * width].reshape(length, HEADS, head_size)
        values_all = project[:, 2 * width :].reshape(length, HEADS, head_size)
        grad_values = jnp.einsum(
            "hqk,qhd->khd", probs_low, grad_heads, preferred_element_type=jnp.float32
        )
        grad_probs = jnp.einsum(
            "qhd,khd->hqk", grad_heads, values_all, preferred_element_type=jnp.float32
        )
        row_dot = jnp.sum(probs_float * grad_probs, -1, keepdims=True)
        grad_scores = (probs_float * (grad_probs - row_dot)).astype(jnp.bfloat16)
        grad_queries = (
            jnp.einsum("hqk,khd->qhd", grad_scores, keys_all, preferred_element_type=jnp.float32)
            * scale
        )
        grad_keys = (
            jnp.einsum("hqk,qhd->khd", grad_scores, queries, preferred_element_type=jnp.float32)
            * scale
        )
        grad_qkv = jnp.concatenate(
            [
                grad_queries.reshape(length, width),
                grad_keys.reshape(length, width),
                grad_values.reshape(length, width),
            ],
            -1,
        ).astype(jnp.bfloat16)
        grad_qkv_w = contract_rows(normed, grad_qkv)
        grad_normed = contract_cols(grad_qkv, qkv_full)
        unused_one, norm_one_back = jax.vjp(
            layer_norm, block.astype(jnp.float32), gain_one, bias_one
        )
        grad_in_norm, grad_gain_one, grad_bias_one = norm_one_back(grad_normed)
        grad_tokens = (grad_middle + grad_in_norm).astype(jnp.bfloat16)
        terms = (
            grad_qkv_w,
            grad_attn_w,
            grad_route,
            grad_gain_one,
            grad_bias_one,
            grad_gain_two,
            grad_bias_two,
        )
        dense_acc = tuple((total + term for total, term in zip(dense_acc, terms)))
        return ((dense_acc, shard_in, shard_out, holding), (grad_tokens, slot))

    dense_zero = (
        jnp.zeros((width, 3 * width), jnp.float32),
        jnp.zeros((width, width), jnp.float32),
        jnp.zeros((width, experts), jnp.float32),
        jnp.zeros((width,), jnp.float32),
        jnp.zeros((width,), jnp.float32),
        jnp.zeros((width,), jnp.float32),
        jnp.zeros((width,), jnp.float32),
    )
    shard_zero_in = jnp.zeros((experts, slab_in, hidden), jnp.float32)
    shard_zero_out = jnp.zeros((experts, slab_out, width), jnp.float32)
    holding_zero = ()
    (dense_acc, shard_in, shard_out, holding), (grad_tokens_all, slots) = lax.scan(
        backward_step,
        (dense_zero, shard_zero_in, shard_zero_out, holding_zero),
        (tokens, cotangent, segment_ids, needs, own_pairs, kept_all),
    )
    slot_in = slots[0].reshape(micro * 2, width, hidden)
    slot_out = slots[1].reshape(micro * 2, hidden, width)
    amount = slot_in.shape[0]
    returned = lax.all_to_all(
        lax.all_to_all(
            shortened(
                (
                    slot_in.reshape(amount, outer, inner, slab_in, hidden),
                    slot_out.reshape(amount, outer, inner, slab_out, width),
                )
            ),
            "gx",
            split_axis=1,
            concat_axis=1,
            tiled=True,
        ),
        "gy",
        split_axis=2,
        concat_axis=2,
        tiled=True,
    )
    onehot = (
        needs.reshape(micro * 2, outer, inner)[None] == expert_ids[:, None, None, None]
    ).astype(jnp.float32)
    added = tuple(
        (jnp.einsum("esab,sabrc->erc", onehot, piece, precision=HIGH) for piece in returned)
    )
    shard_in = shard_in + added[0]
    shard_out = shard_out + added[1]
    dense_shards = (
        lax.psum_scatter(dense_acc[0], ("gx", "gy"), scatter_dimension=0, tiled=True),
        lax.psum_scatter(dense_acc[1], ("gx", "gy"), scatter_dimension=0, tiled=True),
        lax.psum_scatter(dense_acc[2], ("gx", "gy"), scatter_dimension=0, tiled=True),
        lax.psum_scatter(dense_acc[3], ("gx", "gy"), scatter_dimension=0, tiled=True),
        lax.psum_scatter(dense_acc[4], ("gx", "gy"), scatter_dimension=0, tiled=True),
        lax.psum_scatter(dense_acc[5], ("gx", "gy"), scatter_dimension=0, tiled=True),
        lax.psum_scatter(dense_acc[6], ("gx", "gy"), scatter_dimension=0, tiled=True),
    )
    return (
        mixed_all,
        grad_tokens_all,
        dense_shards[0],
        dense_shards[1],
        dense_shards[2],
        shard_in,
        shard_out,
        dense_shards[3],
        dense_shards[4],
        dense_shards[5],
        dense_shards[6],
    )


MESH = pl.DeviceIdType.MESH
ROWS = 224
SIDE = 128
ROOT2PI = math.sqrt(2.0 / math.pi)


(
    DOWN, DPLANE, DCORNER, DLAST, DWAIT, ATT, WIN, WO, WINWAIT, WSIBWAIT, WAVE, COWN,
    CPLANE, CCORNER, CNEAR, CMZ, RPLANE, RCORNER, GFIRST, MFIRST, GHELP, MHELP, GPLANE, MPLANE, PAIR, ADDPAIR, DENSE,
) = range(27)

SIDE_PACKS = (0, 1)

EARLY = ((0, 3), (1, 3))

FRONT_STEPS = (
    (DOWN,), (WIN, 2, 0), (COWN, 0), (COWN, 1), (CMZ, 0, 1, 1), (DPLANE, 1), (WIN, 2, 2), (DPLANE, 3),
    (DPLANE, 2), (CNEAR, 0), (DCORNER, 0), (CNEAR, 1), (WIN, 1, 2), (DCORNER, 2), (WIN, 1, 3), (WIN, 0, 2),
    (WIN, 1, 1), (CMZ, 0, 1, 0), (DCORNER, 3), (DCORNER, 1), (WIN, 3, 0), (DLAST, 0), (CMZ, 1, 1, 1),
    (WIN, 3, 2), (DLAST, 3), (WIN, 2, 1), (DLAST, 1), (DLAST, 2), (WIN, 0, 1), (WIN, 3, 3), (WIN, 1, 0),
    (CMZ, 1, 1, 0), (DWAIT,), (WO,), (CMZ, 0, 2, 0), (WIN, 2, 3), (WIN, 3, 1), (CMZ, 0, 2, 1), (ATT, 0),
    (RCORNER, 0, 0), (ATT, 1), (RPLANE, 1, 0), (CMZ, 1, 2, 1), (RCORNER, 1, 0), (RCORNER, 0, 1),
    (RPLANE, 1, 1), (WIN, 0, 3), (RPLANE, 2, 0), (WINWAIT,), (RPLANE, 2, 1), (WSIBWAIT,), (RCORNER, 1, 1),
    (CMZ, 1, 2, 0), (WAVE, 0, 0), (CMZ, 0, 3, 1), (CMZ, 0, 3, 0), (WAVE, 1, 0), (RCORNER, 2, 0),
    (RCORNER, 2, 1), (RPLANE, 3, 1), (WAVE, 0, 1), (RPLANE, 3, 0), (WAVE, 1, 1), (CMZ, 1, 3, 0), (WAVE, 2, 1),
    (CMZ, 1, 3, 1), (RCORNER, 3, 0), (WAVE, 2, 0), (RCORNER, 3, 1), (WAVE, 3, 0), (WAVE, 3, 1),
)
TAIL_STEPS = (
    (GFIRST, 0, 0), (PAIR,), (GFIRST, 1, 0), (GFIRST, 0, 1), (MHELP, 0, 1), (GHELP, 0, 0), (GHELP, 1, 0),
    (GHELP, 0, 1), (GFIRST, 2, 0), (ADDPAIR,), (WIN, 0, 1), (GFIRST, 1, 1), (GFIRST, 2, 1), (GHELP, 1, 1),
    (GPLANE, 0, 0), (MFIRST, 0, 1), (MFIRST, 0, 0), (WIN, 0, 0), (GPLANE, 0, 1), (MHELP, 2, 1),
    (GPLANE, 1, 0), (GFIRST, 3, 1), (GHELP, 2, 0), (GHELP, 2, 1), (GFIRST, 3, 0), (GPLANE, 1, 1),
    (MFIRST, 1, 1), (MFIRST, 1, 0), (MHELP, 3, 0), (MPLANE, 0, 0), (MPLANE, 0, 1), (GPLANE, 2, 1),
    (MHELP, 2, 0), (MHELP, 3, 1), (GHELP, 3, 0), (MFIRST, 2, 0), (GPLANE, 2, 0), (MHELP, 1, 0),
    (MPLANE, 1, 0), (MFIRST, 2, 1), (MPLANE, 1, 1), (GHELP, 3, 1), (MFIRST, 3, 1), (WIN, 3, 1),
    (MPLANE, 2, 0), (GPLANE, 3, 0), (GPLANE, 3, 1), (ATT, 0), (WIN, 3, 3), (WIN, 1, 0), (MFIRST, 3, 0),
    (ATT, 1), (MPLANE, 2, 1), (WIN, 2, 3), (WIN, 2, 1), (ATT, 2), (ATT, 3), (WIN, 3, 2), (MHELP, 0, 0),
    (WIN, 1, 2), (ATT, 4), (MPLANE, 3, 0), (MHELP, 1, 1), (ATT, 5), (WIN, 1, 3), (WIN, 1, 1), (WIN, 2, 0),
    (WIN, 2, 2), (WIN, 3, 0), (MPLANE, 3, 1), (WIN, 0, 2), (DENSE,),
)


def dot(left, right):
    return jnp.dot(left, right, preferred_element_type=jnp.float32)


class Place:
    def __init__(self):
        self.z = lax.axis_index("gx")
        g = lax.axis_index("gy")
        self.core = g % 2
        across_x = g + 2 - 4 * ((g // 2) % 2)
        across_y = g + 4 - 8 * (g // 4)
        across_both = across_x + 4 - 8 * (across_x // 4)
        self.at = (g, across_x, across_y, across_both)
        self.step_x, self.step_y = across_x - g, across_y - g
        self.sibling = (self.z, g + 1 - 2 * self.core)

    def plane(self, k):
        return (self.z + k) % 4

    def nearest(self, j):
        z = self.z
        return (0, 1 + 2 * (z // 2), 2 + z - 3 * (z // 2), 3 - z + z // 2)[j]

    def device(self, rel, k):
        return (self.plane(k), self.at[rel])

    def chip(self, rel, k):
        return self.plane(k) * 4 + self.at[rel] // 2

    def index(self, rel, k):
        return self.plane(k) * 8 + self.at[rel]

    def pair(self, pack_task, task_experts, rel, k, p):
        at = self.at[0] + self.step_x * (rel % 2) + self.step_y * (rel // 2)
        task = pack_task[(self.plane(k) * 8 + at) * 2 + p]
        return task_experts[0, task], task_experts[1, task]

    def greet(self):
        barrier = pltpu.get_barrier_semaphore()
        others = [(rel, k) for rel in range(4) for k in range(4) if (rel, k) != (0, 0)]
        for rel, k in others:
            pl.semaphore_signal(
                barrier, inc=1, device_id=self.device(rel, k), device_id_type=MESH
            )
        pl.semaphore_signal(barrier, inc=1, device_id=self.sibling, device_id_type=MESH)

    def meet(self):
        pl.semaphore_wait(pltpu.get_barrier_semaphore(), 16)


def send(started, src, dst, send_sem, recv_sem, device):
    copy = pltpu.make_async_remote_copy(
        src_ref=src,
        dst_ref=dst,
        send_sem=send_sem,
        recv_sem=recv_sem,
        device_id=device,
        device_id_type=MESH,
    )
    copy.start()
    started.append(copy)


def arrived(ref, sem):
    pltpu.make_async_copy(ref, ref, sem).wait()


def back(k):
    return (4 - k) % 4


class Spread:
    def __init__(self, place, here, there, packs, half, chained, sems):
        self.place, self.here, self.there = place, here, there
        self.packs, self.half, self.chained, self.started = packs, half, chained, []
        self.send_sem, self.recv_sem = sems

    def go(self, kind, at_send, k_there, rel, k, p, src, rel_there, device, only_if=None):
        copy = pltpu.make_async_remote_copy(
            src_ref=src,
            dst_ref=self.there(rel_there, k_there, p, rel, k),
            send_sem=self.send_sem.at[kind, at_send * self.packs + p],
            recv_sem=self.recv_sem.at[kind % 4, k_there * self.packs + p],
            device_id=device,
            device_id_type=MESH,
        )
        if only_if is None:
            copy.start()
        else:
            pl.when(only_if)(copy.start)
        self.started.append((copy, only_if))

    def wait(self, kind, rel, k, p):
        arrived(self.here(rel, k, p), self.recv_sem.at[kind, k * self.packs + p])

    def own(self, p, src):
        place = self.place
        if self.chained:
            self.go(0, 0, 3, 0, 0, p, src, 0, place.device(0, 1), place.z < 3)
            self.go(4, 0, 1, 0, 0, p, src, 0, place.device(0, 3), place.z > 0)
        else:
            for k in (1, 2, 3):
                self.go(0, k, back(k), 0, 0, p, src, 0, place.device(0, k))
        self.go(1, 0, 0, 0, 0, p, src, 1, place.device(1, 0))
        self.go(2, 0, 0, 0, 0, p, src, 2, place.device(2, 0))

    def plane(self, j, p):
        place = self.place
        k = place.nearest(j)
        self.wait(0, 0, k, p)
        src = self.here(0, k, p)
        if self.chained:
            step = 2 * ((place.z - place.plane(k) + 3) // 4) - 1
            goes = (place.z + step >= 0) & (place.z + step <= 3)
            on = (place.plane(step + 4), place.at[0])
            self.go(0, k, (k - step + 4) % 4, 0, k, p, src, 0, on, goes)
        self.go(1, k, k, 0, k, p, src, 1, place.device(1, 0))
        self.go(2, k, k, 0, k, p, src, 2, place.device(2, 0))

    def corner(self, j, p):
        k = self.place.nearest(j)
        rel = 1 + self.half(j, p)
        self.wait(rel, rel, k, p)
        self.go(3, k, k, rel, k, p, self.here(rel, k, p), 3, self.place.device(3 - rel, 0))

    def last(self, j, p):
        k = self.place.nearest(j)
        rel = 2 - self.half(j, p)
        self.wait(rel, rel, k, p)
        self.wait(3, 3, k, p)

    def finish(self):
        for copy, only_if in self.started:
            if only_if is None:
                copy.wait_send()
            else:
                pl.when(only_if)(copy.wait_send)


class SideSpread(Spread):
    def side(self, p):
        return 1 + p

    def along(self, w, rel, k, p, src, first):
        place = self.place
        if first:
            ways = ((2 + w, 3, 1, place.z < 3), (4 + w, 1, 3, place.z > 0))
        else:
            step = 2 * ((place.z - place.plane(k) + 3) // 4) - 1
            goes = (place.z + step >= 0) & (place.z + step <= 3)
            ways = ((2 + w, (k - step + 4) % 4, step + 4, goes),)
        for kind, k_there, on, goes in ways:
            self.go(kind, k, k_there, rel, k, p, src, rel, (place.plane(on), place.at[0]), goes)

    def go(self, kind, at_send, k_there, rel, k, p, src, rel_there, device, only_if=None):
        copy = pltpu.make_async_remote_copy(
            src_ref=src,
            dst_ref=self.there(rel_there, k_there, p, rel, k),
            send_sem=self.send_sem.at[kind, at_send * self.packs + p],
            recv_sem=self.recv_sem.at[rel_there, k_there * self.packs + p],
            device_id=device,
            device_id_type=MESH,
        )
        if only_if is None:
            copy.start()
        else:
            pl.when(only_if)(copy.start)
        self.started.append((copy, only_if))

    def own(self, p, src):
        side, other = self.side(p), 3 - self.side(p)
        self.go(6, 0, 0, 0, 0, p, src, side, self.place.device(side, 0))
        self.along(0, 0, 0, p, src, True)
        self.go(0, 0, 0, 0, 0, p, src, other, self.place.device(other, 0))

    def near(self, p):
        side, other = self.side(p), 3 - self.side(p)
        self.wait(side, side, 0, p)
        src = self.here(side, 0, p)
        self.along(1, side, 0, p, src, True)
        self.go(1, 0, 0, side, 0, p, src, 3, self.place.device(other, 0))

    def passed(self, w, j, p):
        side, other = self.side(p), 3 - self.side(p)
        rel, k = side * w, self.place.nearest(j)
        self.wait(rel, rel, k, p)
        src = self.here(rel, k, p)
        self.along(w, rel, k, p, src, False)
        self.go(w, k, k, rel, k, p, src, 3 if w else other, self.place.device(other, 0))

    def last(self, j, p):
        k = self.place.nearest(j)
        for rel in (3 - self.side(p), 3):
            self.wait(rel, rel, k, p)


def norm_parts(values):
    center = values - jnp.mean(values, -1, keepdims=True)
    spread = jnp.mean(center * center, -1, keepdims=True)
    rise = lax.rsqrt(spread + EPS)
    return center * rise, rise


def real_rows():
    return lax.broadcasted_iota(jnp.int32, (ROWS, 1), 0) < PACK


def head_lanes(h):
    lane = lax.broadcasted_iota(jnp.int32, (1, SIDE), 1)
    inside = (lane >= h * HEAD) & (lane < (h + 1) * HEAD)
    return inside.astype(jnp.bfloat16)


def softmax_rows(queries, keys, same):
    scores = contract_cols(queries, keys) * (1.0 / math.sqrt(HEAD))
    scores = jnp.where(same, scores, MASK_FILL)
    raised = jnp.exp(scores - jnp.max(scores, -1, keepdims=True))
    return raised * (1.0 / jnp.sum(raised, -1, keepdims=True))


def pick(logits, expert):
    lane = lax.broadcasted_iota(jnp.int32, logits.shape, 1)
    return jnp.sum(jnp.where(lane == expert, logits, 0.0), -1, keepdims=True)


def two_gates(logits, first, second):
    gap = pick(logits, second) - pick(logits, first)
    return 1.0 / (1.0 + jnp.exp(gap)), 1.0 / (1.0 + jnp.exp(-gap))


def lengthened(ref, p):
    rows = ref[p].astype(jnp.float32)
    return jnp.concatenate([rows, jnp.zeros((ROWS - PACK, rows.shape[1]), jnp.float32)], axis=0)


def same_documents(segments, flat_ids, tall_ids):
    flat_ids[...] = jnp.full(flat_ids.shape, -1.0, jnp.float32)
    flat_ids[: segments.shape[0], :PACK] = segments[...].astype(jnp.float32)
    tall_ids[...] = jnp.transpose(flat_ids[...])


def same_document(flat_ids, tall_ids, p):
    return tall_ids[:ROWS, p : p + 1] == flat_ids[p : p + 1, :ROWS]


def front_kernel(
    pack_task, task_experts, tok, segments, w_qkv_own, w_attn_own, route_own,
    gain_one_own, bias_one_own, gain_two_own, bias_two_own, cot_own, w_in, w_out,
    in_terms, out_terms, mixed_out, grad_out, dense_out, early_y, early_x, proj, heads, middle,
    dense, routed_all, cot_all, w_in_all, w_out_all, in_stage, out_stage, mixed_all, grad_all,
    turned, square, flat_ids, tall_ids, gate_row,
    cot_send, cot_recv, routed_send, routed_recv, dense_send, dense_recv,
    core_send, core_recv, in_send, in_recv, pair_send, pair_recv, local_sem, out_sem, early_sem,
):
    place = Place()
    place.greet()
    width, experts = tok.shape[2], route_own.shape[1]
    other = 1 - place.core

    def block_here(ref):
        return lambda rel, k, p: ref.at[rel, k * 2 + p]

    def block_there(ref):
        return lambda rel_there, k_there, p, rel, k: ref.at[rel_there, k_there * 2 + p]

    own = place.index(0, 0)
    dense[own, :, : 3 * width] = w_qkv_own[...]
    dense[own, :, 3 * width : 4 * width] = w_attn_own[...]
    square[...] = jnp.zeros_like(square)
    for i, ref in enumerate((gain_one_own, bias_one_own, gain_two_own, bias_two_own)):
        square[GAIN_ONE + i : GAIN_ONE + i + 1, : ref.shape[0]] = (
            ref[...].astype(jnp.float32).reshape(1, ref.shape[0])
        )
    columns = jnp.transpose(square[...])[: gain_one_own.shape[0]]
    square[: gain_one_own.shape[0], :] = columns
    square[: gain_one_own.shape[0], :experts] = route_own[...].astype(jnp.float32)
    dense[own, :, 4 * width :] = square[: gain_one_own.shape[0], :].astype(jnp.bfloat16)
    for p in range(2):
        cot_all[0, p] = cot_own[p]
    same_documents(segments, flat_ids, tall_ids)
    gate_row[...] = jnp.zeros_like(gate_row)
    place.meet()

    dense_tree = Spread(
        place,
        lambda rel, k, p: dense.at[place.index(rel, k)],
        lambda rel_there, k_there, p, rel, k: dense.at[place.index(rel, k)],
        1,
        lambda j, p: j % 2,
        False,
        (dense_send, dense_recv),
    )
    core_started, in_started, pair_started, local, outs, early = [], [], [], [], [], []

    def to_core(rel, k):
        slot = dense.at[place.index(rel, k)]
        send(
            core_started, slot, slot, core_send.at[rel, k], core_recv.at[rel, k], place.sibling
        )

    def tree(kind, ref, sems):
        return kind(place, block_here(ref), block_there(ref), 2, lambda j, p: p, True, sems)

    cot_side = tree(SideSpread, cot_all, (cot_send, cot_recv))
    cot_plain = tree(Spread, cot_all, (cot_send, cot_recv))
    cot_trees = [cot_side if p in SIDE_PACKS else cot_plain for p in range(2)]
    routed_tree = tree(Spread, routed_all, (routed_send, routed_recv))

    def local_copy(src, dst):
        copy = pltpu.make_async_copy(src, dst, local_sem.at[len(local)])
        copy.start()
        local.append(copy)

    def down():
        dense_tree.own(0, dense.at[own])
        to_core(0, 0)
        local_copy(w_in.at[:, :, pl.ds(pl.multiple_of(place.chip(0, 0) * SIDE, SIDE), SIDE)],
                   w_in_all.at[place.chip(0, 0), place.core])

    def dplane(j):
        dense_tree.plane(j, 0)
        to_core(0, place.nearest(j))

    def dcorner(j):
        k = place.nearest(j)
        dense_tree.corner(j, 0)
        other_side = 2 - j % 2
        dense_tree.wait(other_side, other_side, k, 0)
        to_core(1, k)
        to_core(2, k)

    def dlast(j):
        k = place.nearest(j)
        dense_tree.wait(3, 3, k, 0)
        to_core(3, k)

    def dwait():
        for k in range(4):
            for rel in range(4):
                slot = dense.at[place.plane(k) * 8 + place.at[rel] + 1 - 2 * place.core]
                arrived(slot, core_recv.at[rel, k])
        local_copy(dense, dense_out)
        small = dense[:, :, 4 * width : 4 * width + SIDE].reshape(width, SIDE)
        turned[...] = jnp.transpose(small.astype(jnp.float32))

    def att(p):
        row = [turned[GAIN_ONE + i : GAIN_ONE + i + 1, :] for i in range(4)]
        block = lengthened(tok, p)
        unit, unused = norm_parts(block)
        normed = (unit * row[0] + row[1]).astype(jnp.bfloat16)
        w_qkv = dense[:, :, : 3 * width].reshape(width, 3 * width)
        proj[p] = dot(normed, w_qkv).astype(jnp.bfloat16)
        same = same_document(flat_ids, tall_ids, p)

        def pair_of_heads(j, carry):
            at = pl.multiple_of(j * SIDE, SIDE)
            queries = proj[p, :, pl.ds(at, SIDE)]
            keys = proj[p, :, pl.ds(at + width, SIDE)]
            values = proj[p, :, pl.ds(at + 2 * width, SIDE)]
            out = jnp.zeros((ROWS, SIDE), jnp.float32)
            for h in range(2):
                lanes = head_lanes(h)
                probs = softmax_rows(queries * lanes, keys, same).astype(jnp.bfloat16)
                out = out + dot(probs, values * lanes)
            heads[p, :, pl.ds(at, SIDE)] = out.astype(jnp.bfloat16)
            return carry

        lax.fori_loop(0, width // SIDE, pair_of_heads, 0)
        w_attn = dense[:, :, 3 * width : 4 * width].reshape(width, width)
        mid = block + dot(heads[p], w_attn)
        middle[p] = mid
        unit, unused = norm_parts(mid)
        routed_all[0, p] = (unit * row[2] + row[3])[:PACK].astype(jnp.bfloat16)
        routed_tree.own(p, routed_all.at[0, p])

    def win(rel, j):
        k = place.nearest(j)
        columns = pl.ds(pl.multiple_of(place.chip(rel, k) * SIDE, SIDE), SIDE)
        send(
            in_started, w_in.at[:, :, columns], w_in_all.at[place.chip(0, 0), place.core],
            in_send.at[rel, k], in_recv.at[rel, (4 - k) % 4], place.device(rel, k),
        )

    def wo():
        local_copy(w_out, w_out_all.at[place.core])
        send(
            pair_started, w_out, w_out_all.at[place.core], pair_send.at[0], pair_recv.at[0],
            place.sibling,
        )

    def winwait():
        for rel in range(4):
            for k in range(4):
                if (rel, k) != (0, 0):
                    arrived(w_in_all.at[place.chip(rel, k), place.core], in_recv.at[rel, k])
        local[0].wait()
        mine = w_in_all.at[:, place.core]
        send(pair_started, mine, mine, pair_send.at[1], pair_recv.at[1], place.sibling)

    def wsibwait():
        for copy in local[1:]:
            copy.wait()
        arrived(w_out_all.at[other], pair_recv.at[0])
        arrived(w_in_all.at[:, other], pair_recv.at[1])

    def put(src, dst):
        copy = pltpu.make_async_copy(src, dst, out_sem.at[len(outs)])
        copy.start()
        outs.append(copy)

    def wave(j, p):
        at = place.nearest(j) * 2 + p
        k = place.nearest(j)
        cot_trees[p].last(j, p)
        routed_tree.wait(2 - p, 2 - p, k, p)
        count = len(outs) // 4
        stage = count % 2
        if count >= 2:
            outs[4 * count - 8].wait()
            outs[4 * count - 7].wait()

        def one_block(rel, carry):
            pair = place.pair(pack_task, task_experts, rel, place.nearest(j), p)
            rows, cots = routed_all[rel, at], cot_all[rel, at]
            gated, grad_pre, mixed, grad = expert_block(
                pair, rows, cots, w_in_all, w_out_all, dense, gate_row.at[rel]
            )
            mixed_all[rel, at] = mixed
            grad_all[rel, at] = grad
            in_stage[stage, rel] = contract_rows(rows, grad_pre).astype(jnp.bfloat16)
            out_stage[stage, rel] = contract_rows(gated, cots).astype(jnp.bfloat16)
            return carry

        lax.fori_loop(0, 3, one_block, 0)
        routed_tree.wait(3, 3, k, p)
        one_block(3, 0)
        put(in_stage.at[stage], in_terms.at[:, at])
        put(out_stage.at[stage], out_terms.at[:, at])
        put(grad_all.at[:, at], grad_out.at[:, at])
        put(mixed_all.at[:, at], mixed_out.at[:, at])
        for i, (back_j, rel) in enumerate(EARLY):
            if back_j == 3 - j:
                copy = pltpu.make_async_copy(
                    grad_all.at[2 - p if rel == 1 else rel, at],
                    (early_y, early_x)[p].at[i],
                    early_sem.at[p, i],
                )
                copy.start()
                early.append(copy)

    steps = {
        DOWN: down, DPLANE: dplane, DCORNER: dcorner, DLAST: dlast, DWAIT: dwait,
        ATT: att, WIN: win, WO: wo, WINWAIT: winwait, WSIBWAIT: wsibwait, WAVE: wave,
        COWN: lambda p: cot_trees[p].own(p, cot_all.at[0, p]),
        CPLANE: cot_plain.plane, CCORNER: cot_plain.corner,
        CNEAR: cot_side.near, CMZ: cot_side.passed,
        RPLANE: routed_tree.plane, RCORNER: routed_tree.corner,
    }
    for name, *where in FRONT_STEPS:
        steps[name](*where)
    for i, copy in enumerate(outs):
        if i % 4 >= 2 or i >= len(outs) - 8:
            copy.wait()
    for copy in early:
        copy.wait()
    for each in (dense_tree, cot_side, cot_plain, routed_tree):
        each.finish()
    for copy in core_started + in_started + pair_started:
        copy.wait_send()


def expert_block(pair, rows, cots, w_in_all, w_out_all, dense, gate_row):
    width, slab = rows.shape[1], 2 * SIDE
    first, second = pair
    w_in = jnp.concatenate([w_in_all[:, :, e].reshape(width, SIDE) for e in pair], axis=1)
    w_out = jnp.concatenate([w_out_all[:, e].reshape(SIDE, width) for e in pair], axis=0)
    route = dense[:, :, 4 * width : 4 * width + SIDE].reshape(width, SIDE)
    gate_a, gate_b = two_gates(dot(rows, route), first, second)
    lane = lax.broadcasted_iota(jnp.int32, (1, slab), 1)
    gates = jnp.where(lane < SIDE, gate_a, gate_b)
    hidden = dot(rows, w_in)
    back_act = contract_cols(cots, w_out)
    square = hidden * hidden
    bend = jnp.tanh(ROOT2PI * hidden * (1.0 + 0.044715 * square))
    half = 0.5 * (1.0 + bend)
    act = (hidden * half).astype(jnp.bfloat16).astype(jnp.float32)
    slope = half + 0.5 * hidden * (1.0 - bend * bend) * (ROOT2PI * (1.0 + 0.134145 * square))
    gated = (gates * act).astype(jnp.bfloat16)
    grad_pre = (gates * back_act * slope).astype(jnp.bfloat16)
    product = (act * back_act).astype(jnp.bfloat16)
    signs = jnp.broadcast_to(jnp.where(lane < SIDE, 1.0, -1.0), (8, slab)).astype(jnp.bfloat16)
    gate_row[:, :PACK] = contract_cols(signs, product)
    mixed = dot(gated, w_out).astype(jnp.bfloat16)
    grads = contract_cols(grad_pre, w_in)
    grad = jnp.concatenate([grads, gate_row[...]], axis=0).astype(jnp.bfloat16)
    return gated, grad_pre, mixed, grad


def sum_kernel(
    pack_task, task_experts, in_terms, out_terms, d_in, d_out_own, d_out_far, heads, nexts,
    total_in, total_out,
):
    z, g = lax.axis_index("gx"), lax.axis_index("gy")
    experts = d_out_own.shape[0]
    slots = in_terms.shape[0] * in_terms.shape[1]

    @pl.when(pl.program_id(0) == 0)
    def list_uses():
        def clear(e, carry):
            heads[e] = -1
            return carry

        lax.fori_loop(0, experts, clear, 0)
        step_x, step_y = 2 - 4 * ((g // 2) % 2), 4 - 8 * (g // 4)

        def one(slot, carry):
            rel, k, p = slot // 8, (slot // 2) % 4, slot % 2
            at = g + step_x * (rel % 2) + step_y * (rel // 2)
            task = pack_task[(((z + k) % 4) * 8 + at) * 2 + p]
            for i in range(2):
                e = task_experts[i, task]
                nexts[slot * 2 + i] = heads[e]
                heads[e] = slot * 2 + i
            return carry

        lax.fori_loop(0, slots, one, 0)

    def terms(use):
        slot = use // 2
        rel, at, half = slot // 8, slot % 8, pl.multiple_of((use % 2) * SIDE, SIDE)
        return (
            in_terms[rel, at, :, pl.ds(half, SIDE)].astype(jnp.float32),
            out_terms[rel, at, pl.ds(half, SIDE), :].astype(jnp.float32),
        )

    def add_terms(use):
        new_in, new_out = terms(use)
        total_in[...] += new_in
        total_out[...] += new_out
        return nexts[use]

    own = pl.ds(pl.multiple_of((g % 2) * HEAD, HEAD), HEAD)
    far = pl.ds(pl.multiple_of((1 - g % 2) * HEAD, HEAD), HEAD)

    def one_expert(i, carry):
        head = heads[i]

        @pl.when(head < 0)
        def unused():
            total_in[...] = jnp.zeros_like(total_in)
            total_out[...] = jnp.zeros_like(total_out)

        @pl.when(head >= 0)
        def used():
            total_in[...], total_out[...] = terms(head)
            lax.while_loop(lambda use: use >= 0, add_terms, nexts[head])

        low = total_in[...].astype(jnp.bfloat16).reshape(-1, 2, 16, SIDE)
        d_in[0, :, i] = low[:, 0]
        d_in[1, :, i] = low[:, 1]
        d_out_own[i] = total_out[own, :].astype(jnp.bfloat16)
        d_out_far[i] = total_out[far, :].astype(jnp.bfloat16)
        return carry

    lax.fori_loop(0, experts, one_expert, 0)


class Collect:
    def __init__(self, place, part, corner, from_x, from_y, from_z, packs, half, sems):
        self.place, self.part = place, part
        self.corner, self.from_x, self.from_y, self.from_z = corner, from_x, from_y, from_z
        self.packs, self.half, self.started = packs, half, []
        self.send_sem, self.recv_sem = sems

    def go(self, kind, src, dst, at_send, at_recv, device):
        send(
            self.started, src, dst, self.send_sem.at[kind, at_send],
            self.recv_sem.at[kind, at_recv], device,
        )

    def opposite(self, k, p):
        at = k * self.packs + p
        towards = 2 if self.half(k, p) == 0 else 1
        self.go(3, self.part(3, k, p), self.corner.at[at], at, at, self.place.device(towards, 0))

    def straight(self, k, p):
        at = k * self.packs + p
        if self.half(k, p) == 0:
            self.go(2, self.part(2, k, p), self.from_y.at[at], at, at, self.place.device(2, 0))
        else:
            self.go(1, self.part(1, k, p), self.from_x.at[at], at, at, self.place.device(1, 0))

    def helped(self, k, p, mine):
        at = k * self.packs + p
        ref = self.corner.at[at]
        arrived(ref, self.recv_sem.at[3, at])
        total = ref[...].astype(jnp.float32) + mine().astype(jnp.float32)
        ref[...] = total.astype(jnp.bfloat16)
        if self.half(k, p) == 0:
            self.go(1, ref, self.from_x.at[at], at, at, self.place.device(1, 0))
        else:
            self.go(2, ref, self.from_y.at[at], at, at, self.place.device(2, 0))

    def plane(self, k, p, mine):
        at = k * self.packs + p
        arrived(self.from_x.at[at], self.recv_sem.at[1, at])
        arrived(self.from_y.at[at], self.recv_sem.at[2, at])
        total = self.from_x[at].astype(jnp.float32) + self.from_y[at].astype(jnp.float32)
        total = total + mine().astype(jnp.float32)
        if k:
            self.from_x[at] = total.astype(jnp.bfloat16)
            there = back(k) * self.packs + p
            self.go(
                0, self.from_x.at[at], self.from_z.at[there], at, there, self.place.device(0, k)
            )
            return None
        for other in (1, 2, 3):
            at = other * self.packs + p
            arrived(self.from_z.at[at], self.recv_sem.at[0, at])
            total = total + self.from_z[at].astype(jnp.float32)
        return total

    def finish(self):
        for copy in self.started:
            copy.wait_send()


class Return:
    def __init__(self, place, part, own, from_z, sems, load):
        self.place, self.part, self.own, self.from_z = place, part, own, from_z
        self.send_sem, self.recv_sem, self.z_sem = sems
        self.started, self.loads = [], {}
        for kind, j, p in self.needs:
            rel = self.beside(p) if kind else 0
            at = self.at(j, p)
            self.loads[kind, j, p] = load(part.at[rel, at], own.at[kind, at])

    needs = [(kind, j, p) for j in range(4) for p in range(2) for kind in (1, 0)]

    def at(self, j, p):
        return self.place.nearest(3 - j) * 2 + p

    def beside(self, p):
        return 1 + p

    def go(self, kind, at, src, dst, recv_sem, device):
        send(self.started, src, dst, self.send_sem.at[kind, at], recv_sem, device)

    def mine(self, kind, j, p):
        return self.own[kind, self.at(j, p)].astype(jnp.float32)

    def along(self, kind, send_kind, j, p, ref, total):
        place = self.place
        k = place.nearest(3 - j)
        step = 2 * ((place.plane(k) - place.z + 3) // 4) - 1
        behind = self.from_z.at[kind, k * 2 + p]
        more = (place.z - step >= 0) & (place.z - step <= 3)

        @pl.when(more)
        def add():
            arrived(behind, self.z_sem.at[kind, k * 2 + p])
            ref[...] = (total() + behind[...].astype(jnp.float32)).astype(jnp.bfloat16)

        @pl.when(jnp.logical_not(more))
        def first():
            ref[...] = total().astype(jnp.bfloat16)

        there = (k - step + 4) % 4
        slot = (there + (4 - there) // 4 * (2 - 2 * step)) * 2 + p
        self.go(
            send_kind, k * 2 + p, ref, self.from_z.at[kind, slot], self.z_sem.at[kind, slot],
            (place.plane(step + 4), place.at[0]),
        )

    def owned(self, kind, p, total, out):
        out[...] = total()
        for slot, comes in ((p, self.place.z > 0), (8 + p, self.place.z < 3)):

            @pl.when(comes)
            def add(slot=slot):
                ref = self.from_z.at[kind, slot]
                arrived(ref, self.z_sem.at[kind, slot])
                out[...] += ref[...].astype(jnp.float32)

    def finish(self):
        for copy in self.started:
            copy.wait_send()


class PlaneFirst(Return):
    def __init__(self, place, part, own, from_z, sems, load, corner, from_x, from_y, got):
        self.corner, self.near, self.early = corner, (None, from_x, from_y), {}
        for i, (j, rel) in enumerate(EARLY):
            for p in range(2):
                into = corner if rel == 3 else self.near[2 - p]
                at = place.nearest(3 - j) * 2 + p
                self.early[rel == 3, j, p] = load(got[p].at[i], into.at[at])
        super().__init__(place, part, own, from_z, sems, load)

    def here(self, far, j, p, ref, sem):
        if (far, j, p) in self.early:
            self.early[far, j, p].wait()
        else:
            arrived(ref, sem)

    def first(self, j, p):
        at, way = self.at(j, p), 2 - p
        if (True, j, p) not in self.early:
            self.go(
                3, at, self.part.at[3, at], self.corner.at[at], self.recv_sem.at[3, at],
                self.place.device(way, 0),
            )
        if (False, j, p) not in self.early:
            self.go(
                way, at, self.part.at[way, at], self.near[way].at[at], self.recv_sem.at[way, at],
                self.place.device(way, 0),
            )

    def helped(self, j, p):
        at, way = self.at(j, p), 1 + p
        ref = self.corner.at[at]
        self.loads[1, j, p].wait()
        self.here(True, j, p, ref, self.recv_sem.at[3, at])
        ref[...] = (ref[...].astype(jnp.float32) + self.mine(1, j, p)).astype(jnp.bfloat16)
        self.go(
            way, at, ref, self.near[way].at[at], self.recv_sem.at[way, at],
            self.place.device(way, 0),
        )

    def plane(self, j, p, out):
        at = self.at(j, p)
        self.loads[0, j, p].wait()
        self.here(False, j, p, self.near[2 - p].at[at], self.recv_sem.at[2 - p, at])
        arrived(self.near[1 + p].at[at], self.recv_sem.at[1 + p, at])

        def total():
            both = self.near[1][at].astype(jnp.float32) + self.near[2][at].astype(jnp.float32)
            return both + self.mine(0, j, p)

        if j < 3:
            self.along(0, 0, j, p, self.near[1].at[at], total)
        else:
            self.owned(0, p, total, out)


class SideFirst(Return):
    def __init__(self, place, part, own, from_z, sems, load, near, last, total):
        super().__init__(place, part, own, from_z, sems, load)
        self.near, self.last, self.total = near, last, total

    def first(self, j, p):
        at, way = self.at(j, p), 2 - p
        for kind, rel in ((1, 3), (0, way)):
            self.go(
                kind, at, self.part.at[rel, at], self.near.at[kind, at],
                self.recv_sem.at[kind, at], self.place.device(way, 0),
            )

    def plane(self, j, p, out):
        at, way = self.at(j, p), 1 + p
        for kind in (1, 0):
            ref = self.near.at[kind, at]
            self.loads[kind, j, p].wait()
            arrived(ref, self.recv_sem.at[kind, at])

            def total(kind=kind, ref=ref):
                return ref[...].astype(jnp.float32) + self.mine(kind, j, p)

            if j < 3:
                self.along(kind, 2 + kind, j, p, ref, total)
            elif kind:
                self.owned(kind, p, total, self.total)
                ref[...] = self.total[...].astype(jnp.bfloat16)
                self.go(
                    2, at, ref, self.last.at[p], self.recv_sem.at[2, p], self.place.device(way, 0)
                )
            else:
                self.owned(kind, p, total, out)
        if j == 3:
            arrived(self.last.at[p], self.recv_sem.at[2, p])
            out[...] += self.last[p].astype(jnp.float32)


def tail_kernel(
    pack_task, task_experts, tok, cot, segments, proj, heads, middle, dense, grad_part, mixed_part,
    d_in, d_out_far, got_y, got_x,
    mixed, d_tok, d_dense, d_in_all, d_out_all,
    g_own, g_corner, g_x, g_y, g_z, m_own, m_near, m_last, m_z, m_total, m_out,
    total_grad, grad_mid, grad_heads, grad_qkv, acc, small_rows, turned, flat_ids, tall_ids,
    in_far, in_mine, far_dense, got_dense, part_dense, s_corner, s_x, s_y, s_z,
    g_send, g_recv, gz_recv, m_send, m_recv, mz_recv, s_send, s_recv, in_send, in_recv,
    pair_send, pair_recv, load_sem,
):
    place = Place()
    width = tok.shape[2]
    place.greet()

    loads = []

    def load(src, dst):
        copy = pltpu.make_async_copy(src, dst, load_sem.at[len(loads)])
        copy.start()
        loads.append(copy)
        return copy

    grads = PlaneFirst(
        place, grad_part, g_own, g_z, (g_send, g_recv, gz_recv), load, g_corner, g_x, g_y,
        (got_y, got_x),
    )
    in_load = load(d_in.at[place.core], in_mine)
    mixes = SideFirst(
        place, mixed_part, m_own, m_z, (m_send, m_recv, mz_recv), load, m_near, m_last, m_total
    )
    pair_started, in_started, kept = [], [], {}
    planes = (2, 1, 3, 0)

    same_documents(segments, flat_ids, tall_ids)
    small = dense[:, :, 4 * width : 4 * width + SIDE].reshape(width, SIDE)
    turned[...] = jnp.transpose(small.astype(jnp.float32))
    small_rows[...] = jnp.zeros_like(small_rows)
    gain_one, bias_one, gain_two, bias_two = (
        turned[GAIN_ONE + i : GAIN_ONE + i + 1, :] for i in range(4)
    )

    place.meet()

    def pair():
        send(
            pair_started, d_in.at[1 - place.core], in_far, pair_send.at[0], pair_recv.at[0],
            place.sibling,
        )
        send(
            pair_started, d_out_far, d_out_all, pair_send.at[1], pair_recv.at[1], place.sibling
        )

    def addpair():
        in_load.wait()
        arrived(in_far, pair_recv.at[0])

        def one(i, carry):
            total = in_mine[i].astype(jnp.float32) + in_far[i].astype(jnp.float32)
            in_mine[i] = total.astype(jnp.bfloat16)
            return carry

        lax.fori_loop(0, in_mine.shape[0], one, 0)
        columns = pl.ds(pl.multiple_of(place.chip(0, 0) * SIDE, SIDE), SIDE)
        kept["local"] = load(in_mine.at[place.chip(0, 0)], d_in_all.at[:, :, columns])

    def win(rel, j):
        k = planes[j]
        columns = pl.ds(pl.multiple_of(place.chip(0, 0) * SIDE, SIDE), SIDE)
        send(
            in_started, in_mine.at[place.chip(rel, k)], d_in_all.at[:, :, columns],
            in_send.at[rel, k], in_recv.at[rel, back(k)], place.device(rel, k),
        )

    def mplane(j, p):
        mixes.plane(j, p, m_out)
        if j == 3:
            mixed[p] = (middle[p, :PACK] + m_out[...]).astype(jnp.bfloat16)

    def add_to(p, columns, value):
        if p == 0:
            acc[:, columns] = value
        else:
            acc[:, columns] += value

    def add_row(at, value):
        small_rows[at : at + 1, :] += jnp.sum(value, 0, keepdims=True)

    def att(part):
        p = part // 3
        (att_routed, att_heads, att_normed)[part % 3](p)

    def att_routed(p):
        first, second = place.pair(pack_task, task_experts, 0, 0, p)
        got = total_grad[p]
        tall = jnp.concatenate(
            [got[PACK:, : 2 * SIDE], jnp.zeros((SIDE - 8, 2 * SIDE), jnp.float32)], axis=0
        )
        gap_grad = jnp.transpose(tall)[:ROWS, 0:1]
        got = jnp.where(real_rows(), got, 0.0)
        mid = middle[p]
        unit, rise = norm_parts(mid)
        routed = jnp.where(real_rows(), unit * gain_two + bias_two, 0.0).astype(jnp.bfloat16)
        route = dense[:, :, 4 * width : 4 * width + SIDE].reshape(width, SIDE)
        gate_a, gate_b = two_gates(dot(routed, route), first, second)
        grad_a = gate_a * gate_b * gap_grad
        lane = lax.broadcasted_iota(jnp.int32, (ROWS, SIDE), 1)
        grad_logits = jnp.where(lane == first, grad_a, jnp.where(lane == second, -grad_a, 0.0))
        grad_logits = jnp.where(real_rows(), grad_logits, 0.0).astype(jnp.bfloat16)
        add_to(p, pl.ds(4 * width, SIDE), contract_rows(routed, grad_logits))
        got = got + contract_cols(grad_logits, route)
        add_row(2, got * unit)
        add_row(3, got)
        u = got * gain_two
        grad_middle = lengthened(cot, p) + rise * (
            u - jnp.mean(u, -1, keepdims=True) - unit * jnp.mean(u * unit, -1, keepdims=True)
        )
        grad_mid[...] = grad_middle
        attended = grad_middle.astype(jnp.bfloat16)
        add_to(p, pl.ds(3 * width, width), contract_rows(heads[p], attended))
        w_attn = dense[:, :, 3 * width : 4 * width].reshape(width, width)
        grad_heads[...] = contract_cols(attended, w_attn).astype(jnp.bfloat16)

    def att_heads(p):
        same = same_document(flat_ids, tall_ids, p)

        def pair_of_heads(j, carry):
            at = pl.multiple_of(j * SIDE, SIDE)
            queries = proj[p, :, pl.ds(at, SIDE)]
            keys = proj[p, :, pl.ds(at + width, SIDE)]
            values = proj[p, :, pl.ds(at + 2 * width, SIDE)]
            out_grad = grad_heads[:, pl.ds(at, SIDE)]
            zero = jnp.zeros((ROWS, SIDE), jnp.float32)
            grad_q, grad_k, grad_v = zero, zero, zero
            for h in range(2):
                lanes = head_lanes(h)
                probs = softmax_rows(queries * lanes, keys, same)
                mine_grad = out_grad * lanes
                grad_v = grad_v + contract_rows(probs.astype(jnp.bfloat16), mine_grad)
                grad_probs = contract_cols(mine_grad, values)
                row_dot = jnp.sum(probs * grad_probs, -1, keepdims=True)
                grad_scores = (probs * (grad_probs - row_dot)).astype(jnp.bfloat16)
                grad_q = grad_q + dot(grad_scores, keys * lanes)
                grad_k = grad_k + contract_rows(grad_scores, queries * lanes)
            scale = 1.0 / math.sqrt(HEAD)
            grad_qkv[:, pl.ds(at, SIDE)] = (grad_q * scale).astype(jnp.bfloat16)
            grad_qkv[:, pl.ds(at + width, SIDE)] = (grad_k * scale).astype(jnp.bfloat16)
            grad_qkv[:, pl.ds(at + 2 * width, SIDE)] = grad_v.astype(jnp.bfloat16)
            return carry

        lax.fori_loop(0, width // SIDE, pair_of_heads, 0)

    def att_normed(p):
        unit, rise = norm_parts(lengthened(tok, p))
        normed = (unit * gain_one + bias_one).astype(jnp.bfloat16)
        add_to(p, pl.ds(0, 3 * width), contract_rows(normed, grad_qkv[...]))
        w_qkv = dense[:, :, : 3 * width].reshape(width, 3 * width)
        grad_normed = contract_cols(grad_qkv[...], w_qkv)
        add_row(0, grad_normed * unit)
        add_row(1, grad_normed)
        u = grad_normed * gain_one
        d_tok[p] = (
            grad_mid[...]
            + rise
            * (u - jnp.mean(u, -1, keepdims=True) - unit * jnp.mean(u * unit, -1, keepdims=True))
        ).astype(jnp.bfloat16)

    def dense_part(rel, k, p):
        return got_dense.at[place.chip(rel, k)]

    sums = Collect(
        place, dense_part, s_corner, s_x, s_y, s_z, 1, lambda k, p: k % 2, (s_send, s_recv)
    )
    def dense_step():
        tall = jnp.concatenate(
            [
                jnp.zeros((GAIN_ONE, width), jnp.float32),
                small_rows[...],
                jnp.zeros((SIDE - GAIN_ONE - 8, width), jnp.float32),
            ],
            axis=0,
        )
        acc[:, 4 * width :] += jnp.transpose(tall)
        columns_all = acc.shape[1]

        def cut(i, carry):
            own_rows = pl.ds(pl.multiple_of(i * 32 + place.core * 16, 16), 16)
            far_rows = pl.ds(pl.multiple_of(i * 32 + 16 - place.core * 16, 16), 16)
            far_dense[i] = acc[far_rows, :].astype(jnp.bfloat16)
            part_dense[i] = acc[own_rows, :]
            return carry

        lax.fori_loop(0, 16, cut, 0)
        send(
            pair_started, far_dense, got_dense, pair_send.at[2], pair_recv.at[2], place.sibling
        )
        arrived(got_dense, pair_recv.at[2])

        def join(i, carry):
            far_dense_sum = part_dense[i] + got_dense[i].astype(jnp.float32)
            got_dense[i] = far_dense_sum.astype(jnp.bfloat16)
            return carry

        lax.fori_loop(0, 16, join, 0)

        for k in (2, 1, 3, 0):
            sums.opposite(k, 0)
        for k in (2, 1, 3, 0):
            sums.straight(k, 0)
        for k in (2, 1, 3, 0):
            sums.helped(k, 0, lambda k=k: got_dense[place.chip(1 + k % 2, k)])
        for k in (2, 1, 3):
            sums.plane(k, 0, lambda k=k: got_dense[place.chip(0, k)])
        d_dense[...] = sums.plane(0, 0, lambda: got_dense[place.chip(0, 0)])

    steps = {
        GFIRST: grads.first, GHELP: grads.helped,
        GPLANE: lambda j, p: grads.plane(j, p, total_grad.at[p]),
        MFIRST: mixes.first, MPLANE: mplane, MHELP: lambda j, p: None,
        PAIR: pair, ADDPAIR: addpair, WIN: win, ATT: att, DENSE: dense_step,
    }
    for name, *where in TAIL_STEPS:
        steps[name](*where)

    for rel in range(4):
        for k in range(4):
            if (rel, k) != (0, 0):
                place_columns = pl.ds(pl.multiple_of(place.chip(rel, k) * SIDE, SIDE), SIDE)
                arrived(d_in_all.at[:, :, place_columns], in_recv.at[rel, k])
    kept["local"].wait()
    arrived(d_out_all, pair_recv.at[1])
    for tree in (grads, mixes, sums):
        tree.finish()
    for copy in pair_started + in_started:
        copy.wait_send()


def last_kernel(
    mixed_own, d_tok_tall, d_dense, d_in_low, d_out_own, d_out_far,
    mixed, d_tok, d_qkv, d_attn, d_route, d_in, d_out, gain_one, bias_one, gain_two, bias_two,
):
    width, experts = mixed.shape[2], d_route.shape[1]

    @pl.when(pl.program_id(0) == 0)
    def small():
        for p in range(mixed.shape[0]):
            mixed[p] = mixed_own[p]
            d_tok[p] = d_tok_tall[p, :PACK]
        d_qkv[...] = d_dense[:, : 3 * width]
        d_attn[...] = d_dense[:, 3 * width : 4 * width]
        d_route[...] = d_dense[:, 4 * width : 4 * width + experts]
        rows = jnp.transpose(d_dense[:, 4 * width :])
        for i, ref in enumerate((gain_one, bias_one, gain_two, bias_two)):
            ref[...] = rows[GAIN_ONE + i]

    d_in[...] = d_in_low[...].astype(jnp.float32)
    d_out[...] = d_out_own[...].astype(jnp.float32) + d_out_far[...].astype(jnp.float32)


def shards_fast(
    tokens,
    segment_ids,
    pack_task,
    task_experts,
    w_qkv,
    w_attn_out,
    w_router,
    w_expert_in,
    w_expert_out,
    norm1_gain,
    norm1_bias,
    norm2_gain,
    norm2_bias,
    cotangent,
):
    packs, length, width = tokens.shape
    experts, slab_in, hidden = w_expert_in.shape
    slab_out = w_expert_out.shape[1]
    dense_width = 4 * width + SIDE
    any_space = pl.BlockSpec(memory_space=pl.ANY)
    vmem = pl.BlockSpec(memory_space=pltpu.VMEM)
    smem = pl.BlockSpec(memory_space=pltpu.SMEM)
    low, full = jnp.bfloat16, jnp.float32
    flat = jax.ShapeDtypeStruct
    dma = pltpu.SemaphoreType.DMA
    by_rank = task_experts.T

    blocks = flat((4, 4 * packs, length, width), low)
    tall_blocks = flat((4, 4 * packs, ROWS, width), low)
    in_sums = flat((4, 4 * packs, width, 2 * SIDE), low)
    out_sums = flat((4, 4 * packs, 2 * SIDE, width), low)

    def held(shape):
        return pltpu.VMEM(shape.shape, shape.dtype)

    early_blocks = flat((len(EARLY), ROWS, width), low)
    (
        in_terms, out_terms, mixed_part, grad_part, dense, early_y, early_x, proj, heads, middle,
    ) = pl.pallas_call(
        front_kernel,
        out_shape=(
            in_sums, out_sums, blocks, tall_blocks,
            flat((32, slab_in, dense_width), low),
            early_blocks, early_blocks,
            flat((packs, ROWS, 3 * width), low),
            flat((packs, ROWS, width), low),
            flat((packs, ROWS, width), full),
        ),
        in_specs=[smem] * 2 + [vmem] * 10 + [any_space] * 2,
        out_specs=(any_space,) * 7 + (vmem,) * 3,
        scratch_shapes=[
            pltpu.VMEM((32, slab_in, dense_width), low),
            held(blocks), held(blocks),
            pltpu.VMEM((16, 2, experts, slab_in, SIDE), low),
            pltpu.VMEM((2, experts, slab_out, width), low),
            pltpu.VMEM((2, 4, width, 2 * SIDE), low),
            pltpu.VMEM((2, 4, 2 * SIDE, width), low),
            held(blocks), held(tall_blocks),
            pltpu.VMEM((SIDE, width), full),
            pltpu.VMEM((SIDE, SIDE), full),
            pltpu.VMEM((8, 2 * SIDE), full),
            pltpu.VMEM((2 * SIDE, 8), full),
            pltpu.VMEM((4, 8, width), full),
            dma((7, 8)), dma((4, 8)), dma((5, 8)), dma((4, 8)), dma((5, 4)), dma((4, 4)),
            dma((4, 4)), dma((4, 4)), dma((4, 4)), dma((4, 4)), dma((2,)), dma((2,)), dma((3,)),
            dma((32,)), dma((2, len(EARLY))),
        ],
        compiler_params=pltpu.CompilerParams(
            collective_id=0, has_side_effects=True, vmem_limit_bytes=60 << 20
        ),
        name="front",
    )(
        pack_task, by_rank, tokens, segment_ids, w_qkv, w_attn_out, w_router,
        norm1_gain, norm1_bias, norm2_gain, norm2_bias, cotangent, w_expert_in, w_expert_out,
    )

    across = lax.axis_size("gy")
    got_y = lax.ppermute(early_y, "gy", [(i, i ^ 4) for i in range(across)])
    got_x = lax.ppermute(early_x, "gy", [(i, i ^ 2) for i in range(across)])

    part = width // 2

    by_columns = pl.BlockSpec((experts, slab_out, part), lambda i, *unused: (0, 0, i))
    d_in, d_out_own, d_out_far = pl.pallas_call(
        sum_kernel,
        grid_spec=pltpu.PrefetchScalarGridSpec(
            num_scalar_prefetch=2,
            grid=(2,),
            in_specs=[
                pl.BlockSpec((4, 4 * packs, part, 2 * SIDE), lambda i, *unused: (0, 0, i, 0)),
                pl.BlockSpec((4, 4 * packs, 2 * SIDE, part), lambda i, *unused: (0, 0, 0, i)),
            ],
            out_specs=[
                pl.BlockSpec((2, 8, experts, slab_in, SIDE), lambda i, *unused: (0, i, 0, 0, 0)),
                by_columns, by_columns,
            ],
            scratch_shapes=[
                pltpu.SMEM((experts,), jnp.int32),
                pltpu.SMEM((32 * packs,), jnp.int32),
                pltpu.VMEM((part, SIDE), full),
                pltpu.VMEM((SIDE, part), full),
            ],
        ),
        out_shape=(
            flat((2, 16, experts, slab_in, SIDE), low),
            flat((experts, slab_out, width), low),
            flat((experts, slab_out, width), low),
        ),
        compiler_params=pltpu.CompilerParams(vmem_limit_bytes=60 << 20),
        cost_estimate=pl.CostEstimate(
            flops=10**10, bytes_accessed=40 * 10**6, transcendentals=0
        ),
        name="sums",
    )(pack_task, by_rank, in_terms, out_terms)

    parts = pltpu.VMEM((4 * packs, ROWS, width), low)
    slices = pltpu.VMEM((4, slab_in, dense_width), low)
    sliced = pltpu.VMEM((16, slab_in, dense_width), low)
    mixed_own, d_tok_tall, d_dense, d_in_all, d_out_all = pl.pallas_call(
        tail_kernel,
        out_shape=(
            flat((packs, length, width), low),
            flat((packs, ROWS, width), low),
            flat((slab_in, dense_width), full),
            flat((experts, slab_in, hidden), low),
            flat((experts, slab_out, width), low),
        ),
        in_specs=[smem] * 2 + [vmem] * 7 + [any_space] * 6,
        out_specs=(vmem,) * 3 + (any_space,) * 2,
        scratch_shapes=[
            pltpu.VMEM((2, 4 * packs, ROWS, width), low), parts, parts, parts,
            pltpu.VMEM((1, 5 * packs, ROWS, width), low),
            pltpu.VMEM((2, 4 * packs, length, width), low),
            pltpu.VMEM((2, 4 * packs, length, width), low),
            pltpu.VMEM((packs, length, width), low),
            pltpu.VMEM((2, 5 * packs, length, width), low),
            pltpu.VMEM((length, width), full),
            pltpu.VMEM((length, width), full),
            pltpu.VMEM((packs, ROWS, width), full),
            pltpu.VMEM((ROWS, width), full),
            pltpu.VMEM((ROWS, width), low),
            pltpu.VMEM((ROWS, 3 * width), low),
            pltpu.VMEM((width, dense_width), full),
            pltpu.VMEM((8, width), full),
            pltpu.VMEM((SIDE, width), full),
            pltpu.VMEM((8, 2 * SIDE), full),
            pltpu.VMEM((2 * SIDE, 8), full),
            pltpu.VMEM((16, experts, slab_in, SIDE), low),
            pltpu.VMEM((16, experts, slab_in, SIDE), low),
            sliced, sliced,
            pltpu.VMEM((16, slab_in, dense_width), full),
            slices, slices, slices, slices,
            dma((4, 8)), dma((4, 8)), dma((1, 10)), dma((4, 8)), dma((4, 8)), dma((2, 10)),
            dma((4, 4)), dma((4, 4)), dma((4, 4)), dma((4, 4)), dma((3,)), dma((3,)), dma((48,)),
        ],
        compiler_params=pltpu.CompilerParams(
            collective_id=1, has_side_effects=True, vmem_limit_bytes=60 << 20
        ),
        name="tail",
    )(
        pack_task, by_rank, tokens, cotangent, segment_ids, proj, heads, middle, dense,
        grad_part, mixed_part, d_in, d_out_far, got_y, got_x,
    )

    group = experts // 2

    def some(rows, columns):
        return pl.BlockSpec((group, rows, columns), lambda i: (i, 0, 0))

    def whole(*shape):
        return pl.BlockSpec(shape, lambda i: (0,) * len(shape))

    return pl.pallas_call(
        last_kernel,
        grid=(2,),
        in_specs=[
            whole(packs, length, width), whole(packs, ROWS, width), whole(slab_in, dense_width),
            some(slab_in, hidden), some(slab_out, width), some(slab_out, width),
        ],
        out_specs=(
            whole(packs, length, width), whole(packs, length, width),
            whole(slab_in, 3 * width), whole(slab_in, width), whole(slab_in, experts),
            some(slab_in, hidden), some(slab_out, width),
        ) + (whole(slab_in),) * 4,
        out_shape=(
            flat((packs, length, width), low), flat((packs, length, width), low),
            flat((slab_in, 3 * width), full), flat((slab_in, width), full),
            flat((slab_in, experts), full),
            flat((experts, slab_in, hidden), full), flat((experts, slab_out, width), full),
        ) + (flat((slab_in,), full),) * 4,
        compiler_params=pltpu.CompilerParams(vmem_limit_bytes=60 << 20),
        name="last",
    )(mixed_own, d_tok_tall, d_dense, d_in_all, d_out_own, d_out_all)


def solution(mesh):
    outer, inner = mesh.shape["gx"], mesh.shape["gy"]

    def shards(*arrays):
        packs, length, width = arrays[0].shape
        experts, slab_in, hidden = arrays[7].shape
        fits = (
            (outer, inner) == (4, 8)
            and packs == 2
            and length == PACK
            and experts == GAIN_ONE
            and width == HEADS * HEAD
            and slab_in == 16
            and hidden == 16 * SIDE
        )
        return (shards_fast if fits else shards_any)(*arrays)

    placed = (
        P(("gx", "gy"), None, None),
        P(("gx", "gy"), None),
        P(),
        P(),
        P(("gx", "gy"), None),
        P(("gx", "gy"), None),
        P(("gx", "gy"), None),
        P(None, ("gx", "gy"), None),
        P(None, ("gx", "gy"), None),
        P(("gx", "gy")),
        P(("gx", "gy")),
        P(("gx", "gy")),
        P(("gx", "gy")),
        P(("gx", "gy"), None, None),
    )
    return jax.shard_map(
        shards,
        mesh=mesh,
        in_specs=placed,
        out_specs=(
            P(("gx", "gy"), None, None),
            P(("gx", "gy"), None, None),
            P(("gx", "gy"), None),
            P(("gx", "gy"), None),
            P(("gx", "gy"), None),
            P(None, ("gx", "gy"), None),
            P(None, ("gx", "gy"), None),
            P(("gx", "gy")),
            P(("gx", "gy")),
            P(("gx", "gy")),
            P(("gx", "gy")),
        ),
        check_vma=False,
    )
```

```python
import functools
import math

import jax
import jax.numpy as jnp
from jax import lax
from jax.experimental import pallas as pl
from jax.experimental.pallas import tpu as pltpu
from jax.sharding import PartitionSpec as P

HEADS = 8
HEAD = 64
PACK = 216
GAIN_ONE = 32


EPS = 1e-05
MASK_FILL = -1e30
HIGH = lax.Precision.HIGHEST


def shortened(value):

    def short(part):
        return part.astype(jnp.bfloat16) if part.dtype == jnp.float32 else part

    return jax.tree.map(short, value)


def layer_norm(values, gain, bias):
    center = values - jnp.mean(values, -1, keepdims=True)
    spread = jnp.mean(center * center, -1, keepdims=True)
    return center * lax.rsqrt(spread + EPS) * gain + bias


def contract_rows(left, right):
    return lax.dot_general(
        left, right, (((0,), (0,)), ((), ())), preferred_element_type=jnp.float32
    )


def contract_cols(left, right):
    return lax.dot_general(
        left, right, (((1,), (1,)), ((), ())), preferred_element_type=jnp.float32
    )


def shards_any(
    tokens,
    segment_ids,
    pack_task,
    task_experts,
    w_qkv,
    w_attn_out,
    w_router,
    w_expert_in,
    w_expert_out,
    norm1_gain,
    norm1_bias,
    norm2_gain,
    norm2_bias,
    cotangent,
):
    outer = lax.axis_size("gx")
    inner = lax.axis_size("gy")
    devices = outer * inner
    micro, length, width = tokens.shape
    experts, slab_in, hidden = w_expert_in.shape
    slab_out = w_expert_out.shape[1]
    head_size = width // HEADS
    scale = 1.0 / math.sqrt(head_size)
    device = lax.axis_index("gx") * inner + lax.axis_index("gy")
    gathered = (
        lax.all_gather(w_qkv, ("gx", "gy"), axis=0, tiled=True),
        lax.all_gather(w_attn_out, ("gx", "gy"), axis=0, tiled=True),
        lax.all_gather(w_router, ("gx", "gy"), axis=0, tiled=True),
        lax.all_gather(norm1_gain, ("gx", "gy"), axis=0, tiled=True),
        lax.all_gather(norm1_bias, ("gx", "gy"), axis=0, tiled=True),
        lax.all_gather(norm2_gain, ("gx", "gy"), axis=0, tiled=True),
        lax.all_gather(norm2_bias, ("gx", "gy"), axis=0, tiled=True),
    )
    qkv_full, attn_full, route_full = (gathered[0], gathered[1], gathered[2])
    gain_one, bias_one, gain_two, bias_two = tuple(
        (piece.astype(jnp.float32) for piece in gathered[3:])
    )
    route_float = route_full.astype(jnp.float32)
    pack_pairs = task_experts[pack_task]
    needs = jnp.transpose(pack_pairs.reshape(outer, inner, micro, 2), (2, 3, 0, 1))
    route_pairs = jnp.transpose(pack_pairs.reshape(devices, micro, 2), (1, 0, 2))
    own_pairs = lax.dynamic_slice_in_dim(pack_pairs, device * micro, micro, 0)
    expert_ids = jnp.arange(experts, dtype=jnp.int32)

    def slabs(need):
        return (w_expert_in[need], w_expert_out[need])

    def joined(pieces):
        return (
            pieces[0].reshape(pieces[0].shape[0], width, hidden),
            pieces[1].reshape(pieces[1].shape[0], hidden, width),
        )

    def attention_probs(project, segment):
        queries = project[:, :width].reshape(length, HEADS, head_size)
        keys_all = project[:, width : 2 * width].reshape(length, HEADS, head_size)
        scores = (
            jnp.einsum("qhd,khd->hqk", queries, keys_all, preferred_element_type=jnp.float32)
            * scale
        )
        same_doc = segment[:, None] == segment[None, :]
        return jnp.where(same_doc[None], scores, MASK_FILL)

    def forward_step(carry, inputs):
        block, segment, need, pair, senders = inputs
        block_float = block.astype(jnp.float32)
        normed = layer_norm(block_float, gain_one, bias_one).astype(jnp.bfloat16)
        project = jnp.dot(normed, qkv_full, preferred_element_type=jnp.float32).astype(jnp.bfloat16)
        masked = attention_probs(project, segment)
        peak = jnp.max(masked, -1, keepdims=True)
        raised = jnp.exp(masked - peak)
        totals = jnp.sum(raised, -1, keepdims=True)
        log_total = peak + jnp.log(totals)
        attn_low = (raised / totals).astype(jnp.bfloat16)
        values_all = project[:, 2 * width :].reshape(length, HEADS, head_size)
        heads_out = (
            jnp.einsum("hqk,khd->qhd", attn_low, values_all, preferred_element_type=jnp.float32)
            .reshape(length, width)
            .astype(jnp.bfloat16)
        )
        middle = block_float + jnp.dot(heads_out, attn_full, preferred_element_type=jnp.float32)
        routed = layer_norm(middle, gain_two, bias_two).astype(jnp.bfloat16)
        logits = jnp.dot(routed, route_full, preferred_element_type=jnp.float32)
        select = (expert_ids[None, :] == pair[:, None]).astype(jnp.float32)
        chosen = jnp.sum(logits[:, None, :] * select[None], -1)
        raised_gate = jnp.exp(chosen - jnp.max(chosen, -1, keepdims=True))
        gates = raised_gate / jnp.sum(raised_gate, -1, keepdims=True)
        weights_in, weights_out = joined(
            lax.all_to_all(
                lax.all_to_all(
                    shortened(slabs(need)), "gx", split_axis=1, concat_axis=1, tiled=True
                ),
                "gy",
                split_axis=2,
                concat_axis=2,
                tiled=True,
            )
        )
        hidden_pre = jnp.einsum(
            "ld,kdf->klf", routed, weights_in, preferred_element_type=jnp.float32
        )
        hidden_low = jax.nn.gelu(hidden_pre).astype(jnp.bfloat16)
        expert_out = jnp.einsum(
            "klf,kfd->kld", hidden_low, weights_out, preferred_element_type=jnp.float32
        )
        saved = ()
        mixed = middle + gates[:, 0:1] * expert_out[0] + gates[:, 1:2] * expert_out[1]
        kept = (
            normed,
            project,
            log_total,
            heads_out,
            middle,
            routed,
            gates,
            hidden_pre,
            hidden_low,
            expert_out,
            saved,
        )
        return (carry, (mixed.astype(jnp.bfloat16), kept))

    start = jnp.zeros((), jnp.float32)
    unused, (mixed_all, kept_all) = lax.scan(
        forward_step, start, (tokens, segment_ids, needs, own_pairs, route_pairs)
    )

    def backward_step(carry, inputs):
        dense_acc, shard_in, shard_out, holding = carry
        block, grad_top, segment, need, pair, kept = inputs
        (
            normed,
            project,
            log_total,
            heads_out,
            middle,
            routed,
            gates,
            hidden_pre,
            hidden_low,
            expert_out,
            saved,
        ) = kept
        grad_float = grad_top.astype(jnp.float32)
        grad_gate = jnp.sum(grad_float[None] * expert_out, -1).T
        grad_chosen = gates * (grad_gate - jnp.sum(gates * grad_gate, -1, keepdims=True))
        select = (expert_ids[None, :] == pair[:, None]).astype(jnp.float32)
        grad_logits = jnp.sum(grad_chosen[:, :, None] * select[None], 1)
        routed_float = routed.astype(jnp.float32)
        grad_route = jnp.dot(routed_float.T, grad_logits, precision=HIGH)
        grad_routed = jnp.dot(grad_logits, route_float.T, precision=HIGH)
        grad_eout = (gates.T[:, :, None] * grad_float[None]).astype(jnp.bfloat16)
        slot = ()
        weights_in, weights_out = joined(
            lax.all_to_all(
                lax.all_to_all(
                    shortened(slabs(need)), "gx", split_axis=1, concat_axis=1, tiled=True
                ),
                "gy",
                split_axis=2,
                concat_axis=2,
                tiled=True,
            )
        )
        grad_act = jnp.einsum(
            "kld,kfd->klf", grad_eout, weights_out, preferred_element_type=jnp.float32
        )
        unused_act, gelu_back = jax.vjp(jax.nn.gelu, hidden_pre)
        grad_pre = gelu_back(grad_act)[0].astype(jnp.bfloat16)
        grad_in = jnp.einsum("ld,klf->kdf", routed, grad_pre, preferred_element_type=jnp.float32)
        grad_out = jnp.einsum(
            "klf,kld->kfd", hidden_low, grad_eout, preferred_element_type=jnp.float32
        )
        grad_routed = grad_routed + jnp.einsum(
            "klf,kdf->ld", grad_pre, weights_in, preferred_element_type=jnp.float32
        )
        slot = (grad_in, grad_out)
        unused_two, norm_two_back = jax.vjp(layer_norm, middle, gain_two, bias_two)
        grad_mid_norm, grad_gain_two, grad_bias_two = norm_two_back(grad_routed)
        grad_middle = grad_float + grad_mid_norm
        grad_attended = grad_middle.astype(jnp.bfloat16)
        grad_attn_w = contract_rows(heads_out, grad_attended)
        grad_heads = (
            contract_cols(grad_attended, attn_full)
            .astype(jnp.bfloat16)
            .reshape(length, HEADS, head_size)
        )
        masked = attention_probs(project, segment)
        probs_float = jnp.exp(masked - log_total)
        probs_low = probs_float.astype(jnp.bfloat16)
        queries = project[:, :width].reshape(length, HEADS, head_size)
        keys_all = project[:, width : 2 * width].reshape(length, HEADS, head_size)
        values_all = project[:, 2 * width :].reshape(length, HEADS, head_size)
        grad_values = jnp.einsum(
            "hqk,qhd->khd", probs_low, grad_heads, preferred_element_type=jnp.float32
        )
        grad_probs = jnp.einsum(
            "qhd,khd->hqk", grad_heads, values_all, preferred_element_type=jnp.float32
        )
        row_dot = jnp.sum(probs_float * grad_probs, -1, keepdims=True)
        grad_scores = (probs_float * (grad_probs - row_dot)).astype(jnp.bfloat16)
        grad_queries = (
            jnp.einsum("hqk,khd->qhd", grad_scores, keys_all, preferred_element_type=jnp.float32)
            * scale
        )
        grad_keys = (
            jnp.einsum("hqk,qhd->khd", grad_scores, queries, preferred_element_type=jnp.float32)
            * scale
        )
        grad_qkv = jnp.concatenate(
            [
                grad_queries.reshape(length, width),
                grad_keys.reshape(length, width),
                grad_values.reshape(length, width),
            ],
            -1,
        ).astype(jnp.bfloat16)
        grad_qkv_w = contract_rows(normed, grad_qkv)
        grad_normed = contract_cols(grad_qkv, qkv_full)
        unused_one, norm_one_back = jax.vjp(
            layer_norm, block.astype(jnp.float32), gain_one, bias_one
        )
        grad_in_norm, grad_gain_one, grad_bias_one = norm_one_back(grad_normed)
        grad_tokens = (grad_middle + grad_in_norm).astype(jnp.bfloat16)
        terms = (
            grad_qkv_w,
            grad_attn_w,
            grad_route,
            grad_gain_one,
            grad_bias_one,
            grad_gain_two,
            grad_bias_two,
        )
        dense_acc = tuple((total + term for total, term in zip(dense_acc, terms)))
        return ((dense_acc, shard_in, shard_out, holding), (grad_tokens, slot))

    dense_zero = (
        jnp.zeros((width, 3 * width), jnp.float32),
        jnp.zeros((width, width), jnp.float32),
        jnp.zeros((width, experts), jnp.float32),
        jnp.zeros((width,), jnp.float32),
        jnp.zeros((width,), jnp.float32),
        jnp.zeros((width,), jnp.float32),
        jnp.zeros((width,), jnp.float32),
    )
    shard_zero_in = jnp.zeros((experts, slab_in, hidden), jnp.float32)
    shard_zero_out = jnp.zeros((experts, slab_out, width), jnp.float32)
    holding_zero = ()
    (dense_acc, shard_in, shard_out, holding), (grad_tokens_all, slots) = lax.scan(
        backward_step,
        (dense_zero, shard_zero_in, shard_zero_out, holding_zero),
        (tokens, cotangent, segment_ids, needs, own_pairs, kept_all),
    )
    slot_in = slots[0].reshape(micro * 2, width, hidden)
    slot_out = slots[1].reshape(micro * 2, hidden, width)
    amount = slot_in.shape[0]
    returned = lax.all_to_all(
        lax.all_to_all(
            shortened(
                (
                    slot_in.reshape(amount, outer, inner, slab_in, hidden),
                    slot_out.reshape(amount, outer, inner, slab_out, width),
                )
            ),
            "gx",
            split_axis=1,
            concat_axis=1,
            tiled=True,
        ),
        "gy",
        split_axis=2,
        concat_axis=2,
        tiled=True,
    )
    onehot = (
        needs.reshape(micro * 2, outer, inner)[None] == expert_ids[:, None, None, None]
    ).astype(jnp.float32)
    added = tuple(
        (jnp.einsum("esab,sabrc->erc", onehot, piece, precision=HIGH) for piece in returned)
    )
    shard_in = shard_in + added[0]
    shard_out = shard_out + added[1]
    dense_shards = (
        lax.psum_scatter(dense_acc[0], ("gx", "gy"), scatter_dimension=0, tiled=True),
        lax.psum_scatter(dense_acc[1], ("gx", "gy"), scatter_dimension=0, tiled=True),
        lax.psum_scatter(dense_acc[2], ("gx", "gy"), scatter_dimension=0, tiled=True),
        lax.psum_scatter(dense_acc[3], ("gx", "gy"), scatter_dimension=0, tiled=True),
        lax.psum_scatter(dense_acc[4], ("gx", "gy"), scatter_dimension=0, tiled=True),
        lax.psum_scatter(dense_acc[5], ("gx", "gy"), scatter_dimension=0, tiled=True),
        lax.psum_scatter(dense_acc[6], ("gx", "gy"), scatter_dimension=0, tiled=True),
    )
    return (
        mixed_all,
        grad_tokens_all,
        dense_shards[0],
        dense_shards[1],
        dense_shards[2],
        shard_in,
        shard_out,
        dense_shards[3],
        dense_shards[4],
        dense_shards[5],
        dense_shards[6],
    )


MESH = pl.DeviceIdType.MESH
ROWS = 224
SIDE = 128
ROOT2PI = math.sqrt(2.0 / math.pi)


(
    DOWN, DPLANE, DCORNER, DLAST, DWAIT, ATT, WIN, WO, WINWAIT, WSIBWAIT, WAVE, COWN,
    CPLANE, CCORNER, CNEAR, CMZ, RPLANE, RCORNER, GFIRST, MFIRST, GHELP, MHELP, GPLANE, MPLANE, PAIR, ADDPAIR, DENSE,
) = range(27)

SIDE_PACKS = (0, 1)

EARLY = ((0, 3), (1, 3))

FRONT_STEPS = (
    (DOWN,), (WIN, 2, 0), (COWN, 0), (COWN, 1), (CMZ, 0, 1, 1), (DPLANE, 1), (WIN, 2, 2), (DPLANE, 3),
    (DPLANE, 2), (CNEAR, 0), (DCORNER, 0), (CNEAR, 1), (WIN, 1, 2), (DCORNER, 2), (WIN, 1, 3), (WIN, 0, 2),
    (WIN, 1, 1), (CMZ, 0, 1, 0), (DCORNER, 3), (DCORNER, 1), (WIN, 3, 0), (DLAST, 0), (CMZ, 1, 1, 1),
    (WIN, 3, 2), (DLAST, 3), (WIN, 2, 1), (DLAST, 1), (DLAST, 2), (WIN, 0, 1), (WIN, 3, 3), (WIN, 1, 0),
    (CMZ, 1, 1, 0), (DWAIT,), (WO,), (CMZ, 0, 2, 0), (WIN, 2, 3), (WIN, 3, 1), (CMZ, 0, 2, 1), (ATT, 0),
    (RCORNER, 0, 0), (ATT, 1), (RPLANE, 1, 0), (CMZ, 1, 2, 1), (RCORNER, 1, 0), (RCORNER, 0, 1),
    (RPLANE, 1, 1), (WIN, 0, 3), (RPLANE, 2, 0), (WINWAIT,), (RPLANE, 2, 1), (WSIBWAIT,), (RCORNER, 1, 1),
    (CMZ, 1, 2, 0), (WAVE, 0, 0), (CMZ, 0, 3, 1), (CMZ, 0, 3, 0), (WAVE, 1, 0), (RCORNER, 2, 0),
    (RCORNER, 2, 1), (RPLANE, 3, 1), (WAVE, 0, 1), (RPLANE, 3, 0), (WAVE, 1, 1), (CMZ, 1, 3, 0), (WAVE, 2, 1),
    (CMZ, 1, 3, 1), (RCORNER, 3, 0), (WAVE, 2, 0), (RCORNER, 3, 1), (WAVE, 3, 0), (WAVE, 3, 1),
)
TAIL_STEPS = (
    (GFIRST, 0, 0), (PAIR,), (GFIRST, 1, 0), (GFIRST, 0, 1), (MHELP, 0, 1), (GHELP, 0, 0), (GHELP, 1, 0),
    (GHELP, 0, 1), (GFIRST, 2, 0), (ADDPAIR,), (WIN, 0, 1), (GFIRST, 1, 1), (GFIRST, 2, 1), (GHELP, 1, 1),
    (GPLANE, 0, 0), (MFIRST, 0, 1), (MFIRST, 0, 0), (WIN, 0, 0), (GPLANE, 0, 1), (MHELP, 2, 1),
    (GPLANE, 1, 0), (GFIRST, 3, 1), (GHELP, 2, 0), (GHELP, 2, 1), (GFIRST, 3, 0), (GPLANE, 1, 1),
    (MFIRST, 1, 1), (MFIRST, 1, 0), (MHELP, 3, 0), (MPLANE, 0, 0), (MPLANE, 0, 1), (GPLANE, 2, 1),
    (MHELP, 2, 0), (MHELP, 3, 1), (GHELP, 3, 0), (MFIRST, 2, 0), (GPLANE, 2, 0), (MHELP, 1, 0),
    (MPLANE, 1, 0), (MFIRST, 2, 1), (MPLANE, 1, 1), (GHELP, 3, 1), (MFIRST, 3, 1), (WIN, 3, 1),
    (MPLANE, 2, 0), (GPLANE, 3, 0), (GPLANE, 3, 1), (ATT, 0), (WIN, 3, 3), (WIN, 1, 0), (MFIRST, 3, 0),
    (ATT, 1), (MPLANE, 2, 1), (WIN, 2, 3), (WIN, 2, 1), (ATT, 2), (ATT, 3), (WIN, 3, 2), (MHELP, 0, 0),
    (WIN, 1, 2), (ATT, 4), (MPLANE, 3, 0), (MHELP, 1, 1), (ATT, 5), (WIN, 1, 3), (WIN, 1, 1), (WIN, 2, 0),
    (WIN, 2, 2), (WIN, 3, 0), (MPLANE, 3, 1), (WIN, 0, 2), (DENSE,),
)


def dot(left, right):
    return jnp.dot(left, right, preferred_element_type=jnp.float32)


class Place:
    def __init__(self):
        self.z = lax.axis_index("gx")
        g = lax.axis_index("gy")
        self.core = g % 2
        across_x = g + 2 - 4 * ((g // 2) % 2)
        across_y = g + 4 - 8 * (g // 4)
        across_both = across_x + 4 - 8 * (across_x // 4)
        self.at = (g, across_x, across_y, across_both)
        self.step_x, self.step_y = across_x - g, across_y - g
        self.sibling = (self.z, g + 1 - 2 * self.core)

    def plane(self, k):
        return (self.z + k) % 4

    def nearest(self, j):
        z = self.z
        return (0, 1 + 2 * (z // 2), 2 + z - 3 * (z // 2), 3 - z + z // 2)[j]

    def device(self, rel, k):
        return (self.plane(k), self.at[rel])

    def chip(self, rel, k):
        return self.plane(k) * 4 + self.at[rel] // 2

    def index(self, rel, k):
        return self.plane(k) * 8 + self.at[rel]

    def pair(self, pack_task, task_experts, rel, k, p):
        at = self.at[0] + self.step_x * (rel % 2) + self.step_y * (rel // 2)
        task = pack_task[(self.plane(k) * 8 + at) * 2 + p]
        return task_experts[0, task], task_experts[1, task]

    def greet(self):
        barrier = pltpu.get_barrier_semaphore()
        others = [(rel, k) for rel in range(4) for k in range(4) if (rel, k) != (0, 0)]
        for rel, k in others:
            pl.semaphore_signal(
                barrier, inc=1, device_id=self.device(rel, k), device_id_type=MESH
            )
        pl.semaphore_signal(barrier, inc=1, device_id=self.sibling, device_id_type=MESH)

    def meet(self):
        pl.semaphore_wait(pltpu.get_barrier_semaphore(), 16)


def send(started, src, dst, send_sem, recv_sem, device):
    copy = pltpu.make_async_remote_copy(
        src_ref=src,
        dst_ref=dst,
        send_sem=send_sem,
        recv_sem=recv_sem,
        device_id=device,
        device_id_type=MESH,
    )
    copy.start()
    started.append(copy)


def arrived(ref, sem):
    pltpu.make_async_copy(ref, ref, sem).wait()


def back(k):
    return (4 - k) % 4


class Spread:
    def __init__(self, place, here, there, packs, half, chained, sems):
        self.place, self.here, self.there = place, here, there
        self.packs, self.half, self.chained, self.started = packs, half, chained, []
        self.send_sem, self.recv_sem = sems

    def go(self, kind, at_send, k_there, rel, k, p, src, rel_there, device, only_if=None):
        copy = pltpu.make_async_remote_copy(
            src_ref=src,
            dst_ref=self.there(rel_there, k_there, p, rel, k),
            send_sem=self.send_sem.at[kind, at_send * self.packs + p],
            recv_sem=self.recv_sem.at[kind % 4, k_there * self.packs + p],
            device_id=device,
            device_id_type=MESH,
        )
        if only_if is None:
            copy.start()
        else:
            pl.when(only_if)(copy.start)
        self.started.append((copy, only_if))

    def wait(self, kind, rel, k, p):
        arrived(self.here(rel, k, p), self.recv_sem.at[kind, k * self.packs + p])

    def own(self, p, src):
        place = self.place
        if self.chained:
            self.go(0, 0, 3, 0, 0, p, src, 0, place.device(0, 1), place.z < 3)
            self.go(4, 0, 1, 0, 0, p, src, 0, place.device(0, 3), place.z > 0)
        else:
            for k in (1, 2, 3):
                self.go(0, k, back(k), 0, 0, p, src, 0, place.device(0, k))
        self.go(1, 0, 0, 0, 0, p, src, 1, place.device(1, 0))
        self.go(2, 0, 0, 0, 0, p, src, 2, place.device(2, 0))

    def plane(self, j, p):
        place = self.place
        k = place.nearest(j)
        self.wait(0, 0, k, p)
        src = self.here(0, k, p)
        if self.chained:
            step = 2 * ((place.z - place.plane(k) + 3) // 4) - 1
            goes = (place.z + step >= 0) & (place.z + step <= 3)
            on = (place.plane(step + 4), place.at[0])
            self.go(0, k, (k - step + 4) % 4, 0, k, p, src, 0, on, goes)
        self.go(1, k, k, 0, k, p, src, 1, place.device(1, 0))
        self.go(2, k, k, 0, k, p, src, 2, place.device(2, 0))

    def corner(self, j, p):
        k = self.place.nearest(j)
        rel = 1 + self.half(j, p)
        self.wait(rel, rel, k, p)
        self.go(3, k, k, rel, k, p, self.here(rel, k, p), 3, self.place.device(3 - rel, 0))

    def last(self, j, p):
        k = self.place.nearest(j)
        rel = 2 - self.half(j, p)
        self.wait(rel, rel, k, p)
        self.wait(3, 3, k, p)

    def finish(self):
        for copy, only_if in self.started:
            if only_if is None:
                copy.wait_send()
            else:
                pl.when(only_if)(copy.wait_send)


class SideSpread(Spread):
    def side(self, p):
        return 1 + p

    def along(self, w, rel, k, p, src, first):
        place = self.place
        if first:
            ways = ((2 + w, 3, 1, place.z < 3), (4 + w, 1, 3, place.z > 0))
        else:
            step = 2 * ((place.z - place.plane(k) + 3) // 4) - 1
            goes = (place.z + step >= 0) & (place.z + step <= 3)
            ways = ((2 + w, (k - step + 4) % 4, step + 4, goes),)
        for kind, k_there, on, goes in ways:
            self.go(kind, k, k_there, rel, k, p, src, rel, (place.plane(on), place.at[0]), goes)

    def go(self, kind, at_send, k_there, rel, k, p, src, rel_there, device, only_if=None):
        copy = pltpu.make_async_remote_copy(
            src_ref=src,
            dst_ref=self.there(rel_there, k_there, p, rel, k),
            send_sem=self.send_sem.at[kind, at_send * self.packs + p],
            recv_sem=self.recv_sem.at[rel_there, k_there * self.packs + p],
            device_id=device,
            device_id_type=MESH,
        )
        if only_if is None:
            copy.start()
        else:
            pl.when(only_if)(copy.start)
        self.started.append((copy, only_if))

    def own(self, p, src):
        side, other = self.side(p), 3 - self.side(p)
        self.go(6, 0, 0, 0, 0, p, src, side, self.place.device(side, 0))
        self.along(0, 0, 0, p, src, True)
        self.go(0, 0, 0, 0, 0, p, src, other, self.place.device(other, 0))

    def near(self, p):
        side, other = self.side(p), 3 - self.side(p)
        self.wait(side, side, 0, p)
        src = self.here(side, 0, p)
        self.along(1, side, 0, p, src, True)
        self.go(1, 0, 0, side, 0, p, src, 3, self.place.device(other, 0))

    def passed(self, w, j, p):
        side, other = self.side(p), 3 - self.side(p)
        rel, k = side * w, self.place.nearest(j)
        self.wait(rel, rel, k, p)
        src = self.here(rel, k, p)
        self.along(w, rel, k, p, src, False)
        self.go(w, k, k, rel, k, p, src, 3 if w else other, self.place.device(other, 0))

    def last(self, j, p):
        k = self.place.nearest(j)
        for rel in (3 - self.side(p), 3):
            self.wait(rel, rel, k, p)


def norm_parts(values):
    center = values - jnp.mean(values, -1, keepdims=True)
    spread = jnp.mean(center * center, -1, keepdims=True)
    rise = lax.rsqrt(spread + EPS)
    return center * rise, rise


def real_rows():
    return lax.broadcasted_iota(jnp.int32, (ROWS, 1), 0) < PACK


def head_lanes(h):
    lane = lax.broadcasted_iota(jnp.int32, (1, SIDE), 1)
    inside = (lane >= h * HEAD) & (lane < (h + 1) * HEAD)
    return inside.astype(jnp.bfloat16)


def softmax_rows(queries, keys, same):
    scores = contract_cols(queries, keys) * (1.0 / math.sqrt(HEAD))
    scores = jnp.where(same, scores, MASK_FILL)
    raised = jnp.exp(scores - jnp.max(scores, -1, keepdims=True))
    return raised * (1.0 / jnp.sum(raised, -1, keepdims=True))


def pick(logits, expert):
    lane = lax.broadcasted_iota(jnp.int32, logits.shape, 1)
    return jnp.sum(jnp.where(lane == expert, logits, 0.0), -1, keepdims=True)


def two_gates(logits, first, second):
    gap = pick(logits, second) - pick(logits, first)
    return 1.0 / (1.0 + jnp.exp(gap)), 1.0 / (1.0 + jnp.exp(-gap))


def lengthened(ref, p):
    rows = ref[p].astype(jnp.float32)
    return jnp.concatenate([rows, jnp.zeros((ROWS - PACK, rows.shape[1]), jnp.float32)], axis=0)


def same_documents(segments, flat_ids, tall_ids):
    flat_ids[...] = jnp.full(flat_ids.shape, -1.0, jnp.float32)
    flat_ids[: segments.shape[0], :PACK] = segments[...].astype(jnp.float32)
    tall_ids[...] = jnp.transpose(flat_ids[...])


def same_document(flat_ids, tall_ids, p):
    return tall_ids[:ROWS, p : p + 1] == flat_ids[p : p + 1, :ROWS]


def front_kernel(
    pack_task, task_experts, tok, segments, w_qkv_own, w_attn_own, route_own,
    gain_one_own, bias_one_own, gain_two_own, bias_two_own, cot_own, w_in, w_out,
    in_terms, out_terms, mixed_out, grad_out, dense_out, early_y, early_x, proj, heads, middle,
    dense, routed_all, cot_all, w_in_all, w_out_all, in_stage, out_stage, mixed_all, grad_all,
    turned, square, flat_ids, tall_ids, gate_row,
    cot_send, cot_recv, routed_send, routed_recv, dense_send, dense_recv,
    core_send, core_recv, in_send, in_recv, pair_send, pair_recv, local_sem, out_sem, early_sem,
):
    place = Place()
    place.greet()
    width, experts = tok.shape[2], route_own.shape[1]
    other = 1 - place.core

    def block_here(ref):
        return lambda rel, k, p: ref.at[rel, k * 2 + p]

    def block_there(ref):
        return lambda rel_there, k_there, p, rel, k: ref.at[rel_there, k_there * 2 + p]

    own = place.index(0, 0)
    dense[own, :, : 3 * width] = w_qkv_own[...]
    dense[own, :, 3 * width : 4 * width] = w_attn_own[...]
    square[...] = jnp.zeros_like(square)
    for i, ref in enumerate((gain_one_own, bias_one_own, gain_two_own, bias_two_own)):
        square[GAIN_ONE + i : GAIN_ONE + i + 1, : ref.shape[0]] = (
            ref[...].astype(jnp.float32).reshape(1, ref.shape[0])
        )
    columns = jnp.transpose(square[...])[: gain_one_own.shape[0]]
    square[: gain_one_own.shape[0], :] = columns
    square[: gain_one_own.shape[0], :experts] = route_own[...].astype(jnp.float32)
    dense[own, :, 4 * width :] = square[: gain_one_own.shape[0], :].astype(jnp.bfloat16)
    for p in range(2):
        cot_all[0, p] = cot_own[p]
    same_documents(segments, flat_ids, tall_ids)
    gate_row[...] = jnp.zeros_like(gate_row)
    place.meet()

    dense_tree = Spread(
        place,
        lambda rel, k, p: dense.at[place.index(rel, k)],
        lambda rel_there, k_there, p, rel, k: dense.at[place.index(rel, k)],
        1,
        lambda j, p: j % 2,
        False,
        (dense_send, dense_recv),
    )
    core_started, in_started, pair_started, local, outs, early = [], [], [], [], [], []

    def to_core(rel, k):
        slot = dense.at[place.index(rel, k)]
        send(
            core_started, slot, slot, core_send.at[rel, k], core_recv.at[rel, k], place.sibling
        )

    def tree(kind, ref, sems):
        return kind(place, block_here(ref), block_there(ref), 2, lambda j, p: p, True, sems)

    cot_side = tree(SideSpread, cot_all, (cot_send, cot_recv))
    cot_plain = tree(Spread, cot_all, (cot_send, cot_recv))
    cot_trees = [cot_side if p in SIDE_PACKS else cot_plain for p in range(2)]
    routed_tree = tree(Spread, routed_all, (routed_send, routed_recv))

    def local_copy(src, dst):
        copy = pltpu.make_async_copy(src, dst, local_sem.at[len(local)])
        copy.start()
        local.append(copy)

    def down():
        dense_tree.own(0, dense.at[own])
        to_core(0, 0)
        local_copy(w_in.at[:, :, pl.ds(pl.multiple_of(place.chip(0, 0) * SIDE, SIDE), SIDE)],
                   w_in_all.at[place.chip(0, 0), place.core])

    def dplane(j):
        dense_tree.plane(j, 0)
        to_core(0, place.nearest(j))

    def dcorner(j):
        k = place.nearest(j)
        dense_tree.corner(j, 0)
        other_side = 2 - j % 2
        dense_tree.wait(other_side, other_side, k, 0)
        to_core(1, k)
        to_core(2, k)

    def dlast(j):
        k = place.nearest(j)
        dense_tree.wait(3, 3, k, 0)
        to_core(3, k)

    def dwait():
        for k in range(4):
            for rel in range(4):
                slot = dense.at[place.plane(k) * 8 + place.at[rel] + 1 - 2 * place.core]
                arrived(slot, core_recv.at[rel, k])
        local_copy(dense, dense_out)
        small = dense[:, :, 4 * width : 4 * width + SIDE].reshape(width, SIDE)
        turned[...] = jnp.transpose(small.astype(jnp.float32))

    def att(p):
        row = [turned[GAIN_ONE + i : GAIN_ONE + i + 1, :] for i in range(4)]
        block = lengthened(tok, p)
        unit, unused = norm_parts(block)
        normed = (unit * row[0] + row[1]).astype(jnp.bfloat16)
        w_qkv = dense[:, :, : 3 * width].reshape(width, 3 * width)
        proj[p] = dot(normed, w_qkv).astype(jnp.bfloat16)
        same = same_document(flat_ids, tall_ids, p)

        def pair_of_heads(j, carry):
            at = pl.multiple_of(j * SIDE, SIDE)
            queries = proj[p, :, pl.ds(at, SIDE)]
            keys = proj[p, :, pl.ds(at + width, SIDE)]
            values = proj[p, :, pl.ds(at + 2 * width, SIDE)]
            out = jnp.zeros((ROWS, SIDE), jnp.float32)
            for h in range(2):
                lanes = head_lanes(h)
                probs = softmax_rows(queries * lanes, keys, same).astype(jnp.bfloat16)
                out = out + dot(probs, values * lanes)
            heads[p, :, pl.ds(at, SIDE)] = out.astype(jnp.bfloat16)
            return carry

        lax.fori_loop(0, width // SIDE, pair_of_heads, 0)
        w_attn = dense[:, :, 3 * width : 4 * width].reshape(width, width)
        mid = block + dot(heads[p], w_attn)
        middle[p] = mid
        unit, unused = norm_parts(mid)
        routed_all[0, p] = (unit * row[2] + row[3])[:PACK].astype(jnp.bfloat16)
        routed_tree.own(p, routed_all.at[0, p])

    def win(rel, j):
        k = place.nearest(j)
        columns = pl.ds(pl.multiple_of(place.chip(rel, k) * SIDE, SIDE), SIDE)
        send(
            in_started, w_in.at[:, :, columns], w_in_all.at[place.chip(0, 0), place.core],
            in_send.at[rel, k], in_recv.at[rel, (4 - k) % 4], place.device(rel, k),
        )

    def wo():
        local_copy(w_out, w_out_all.at[place.core])
        send(
            pair_started, w_out, w_out_all.at[place.core], pair_send.at[0], pair_recv.at[0],
            place.sibling,
        )

    def winwait():
        for rel in range(4):
            for k in range(4):
                if (rel, k) != (0, 0):
                    arrived(w_in_all.at[place.chip(rel, k), place.core], in_recv.at[rel, k])
        local[0].wait()
        mine = w_in_all.at[:, place.core]
        send(pair_started, mine, mine, pair_send.at[1], pair_recv.at[1], place.sibling)

    def wsibwait():
        for copy in local[1:]:
            copy.wait()
        arrived(w_out_all.at[other], pair_recv.at[0])
        arrived(w_in_all.at[:, other], pair_recv.at[1])

    def put(src, dst):
        copy = pltpu.make_async_copy(src, dst, out_sem.at[len(outs)])
        copy.start()
        outs.append(copy)

    def wave(j, p):
        at = place.nearest(j) * 2 + p
        k = place.nearest(j)
        cot_trees[p].last(j, p)
        routed_tree.wait(2 - p, 2 - p, k, p)
        count = len(outs) // 4
        stage = count % 2
        if count >= 2:
            outs[4 * count - 8].wait()
            outs[4 * count - 7].wait()

        def one_block(rel, carry):
            pair = place.pair(pack_task, task_experts, rel, place.nearest(j), p)
            rows, cots = routed_all[rel, at], cot_all[rel, at]
            gated, grad_pre, mixed, grad = expert_block(
                pair, rows, cots, w_in_all, w_out_all, dense, gate_row.at[rel]
            )
            mixed_all[rel, at] = mixed
            grad_all[rel, at] = grad
            in_stage[stage, rel] = contract_rows(rows, grad_pre).astype(jnp.bfloat16)
            out_stage[stage, rel] = contract_rows(gated, cots).astype(jnp.bfloat16)
            return carry

        lax.fori_loop(0, 3, one_block, 0)
        routed_tree.wait(3, 3, k, p)
        one_block(3, 0)
        put(in_stage.at[stage], in_terms.at[:, at])
        put(out_stage.at[stage], out_terms.at[:, at])
        put(grad_all.at[:, at], grad_out.at[:, at])
        put(mixed_all.at[:, at], mixed_out.at[:, at])
        for i, (back_j, rel) in enumerate(EARLY):
            if back_j == 3 - j:
                copy = pltpu.make_async_copy(
                    grad_all.at[2 - p if rel == 1 else rel, at],
                    (early_y, early_x)[p].at[i],
                    early_sem.at[p, i],
                )
                copy.start()
                early.append(copy)

    steps = {
        DOWN: down, DPLANE: dplane, DCORNER: dcorner, DLAST: dlast, DWAIT: dwait,
        ATT: att, WIN: win, WO: wo, WINWAIT: winwait, WSIBWAIT: wsibwait, WAVE: wave,
        COWN: lambda p: cot_trees[p].own(p, cot_all.at[0, p]),
        CPLANE: cot_plain.plane, CCORNER: cot_plain.corner,
        CNEAR: cot_side.near, CMZ: cot_side.passed,
        RPLANE: routed_tree.plane, RCORNER: routed_tree.corner,
    }
    for name, *where in FRONT_STEPS:
        steps[name](*where)
    for i, copy in enumerate(outs):
        if i % 4 >= 2 or i >= len(outs) - 8:
            copy.wait()
    for copy in early:
        copy.wait()
    for each in (dense_tree, cot_side, cot_plain, routed_tree):
        each.finish()
    for copy in core_started + in_started + pair_started:
        copy.wait_send()


def expert_block(pair, rows, cots, w_in_all, w_out_all, dense, gate_row):
    width, slab = rows.shape[1], 2 * SIDE
    first, second = pair
    w_in = jnp.concatenate([w_in_all[:, :, e].reshape(width, SIDE) for e in pair], axis=1)
    w_out = jnp.concatenate([w_out_all[:, e].reshape(SIDE, width) for e in pair], axis=0)
    route = dense[:, :, 4 * width : 4 * width + SIDE].reshape(width, SIDE)
    gate_a, gate_b = two_gates(dot(rows, route), first, second)
    lane = lax.broadcasted_iota(jnp.int32, (1, slab), 1)
    gates = jnp.where(lane < SIDE, gate_a, gate_b)
    hidden = dot(rows, w_in)
    back_act = contract_cols(cots, w_out)
    square = hidden * hidden
    bend = jnp.tanh(ROOT2PI * hidden * (1.0 + 0.044715 * square))
    half = 0.5 * (1.0 + bend)
    act = (hidden * half).astype(jnp.bfloat16).astype(jnp.float32)
    slope = half + 0.5 * hidden * (1.0 - bend * bend) * (ROOT2PI * (1.0 + 0.134145 * square))
    gated = (gates * act).astype(jnp.bfloat16)
    grad_pre = (gates * back_act * slope).astype(jnp.bfloat16)
    product = (act * back_act).astype(jnp.bfloat16)
    signs = jnp.broadcast_to(jnp.where(lane < SIDE, 1.0, -1.0), (8, slab)).astype(jnp.bfloat16)
    gate_row[:, :PACK] = contract_cols(signs, product)
    mixed = dot(gated, w_out).astype(jnp.bfloat16)
    grads = contract_cols(grad_pre, w_in)
    grad = jnp.concatenate([grads, gate_row[...]], axis=0).astype(jnp.bfloat16)
    return gated, grad_pre, mixed, grad


def sum_kernel(
    pack_task, task_experts, in_terms, out_terms, d_in, d_out_own, d_out_far, heads, nexts,
    total_in, total_out,
):
    z, g = lax.axis_index("gx"), lax.axis_index("gy")
    experts = d_out_own.shape[0]
    slots = in_terms.shape[0] * in_terms.shape[1]

    @pl.when(pl.program_id(0) == 0)
    def list_uses():
        def clear(e, carry):
            heads[e] = -1
            return carry

        lax.fori_loop(0, experts, clear, 0)
        step_x, step_y = 2 - 4 * ((g // 2) % 2), 4 - 8 * (g // 4)

        def one(slot, carry):
            rel, k, p = slot // 8, (slot // 2) % 4, slot % 2
            at = g + step_x * (rel % 2) + step_y * (rel // 2)
            task = pack_task[(((z + k) % 4) * 8 + at) * 2 + p]
            for i in range(2):
                e = task_experts[i, task]
                nexts[slot * 2 + i] = heads[e]
                heads[e] = slot * 2 + i
            return carry

        lax.fori_loop(0, slots, one, 0, unroll=4)

    def terms(use):
        slot = use // 2
        rel, at, half = slot // 8, slot % 8, pl.multiple_of((use % 2) * SIDE, SIDE)
        return (
            in_terms[rel, at, :, pl.ds(half, SIDE)].astype(jnp.float32),
            out_terms[rel, at, pl.ds(half, SIDE), :].astype(jnp.float32),
        )

    def add_terms(use):
        new_in, new_out = terms(use)
        total_in[...] += new_in
        total_out[...] += new_out
        return nexts[use]

    own = pl.ds(pl.multiple_of((g % 2) * HEAD, HEAD), HEAD)
    far = pl.ds(pl.multiple_of((1 - g % 2) * HEAD, HEAD), HEAD)

    def one_expert(i, carry):
        head = heads[i]

        @pl.when(head < 0)
        def unused():
            total_in[...] = jnp.zeros_like(total_in)
            total_out[...] = jnp.zeros_like(total_out)

        @pl.when(head >= 0)
        def used():
            total_in[...], total_out[...] = terms(head)
            lax.while_loop(lambda use: use >= 0, add_terms, nexts[head])

        low = total_in[...].astype(jnp.bfloat16).reshape(-1, 2, 16, SIDE)
        d_in[0, :, i] = low[:, 0]
        d_in[1, :, i] = low[:, 1]
        d_out_own[i] = total_out[own, :].astype(jnp.bfloat16)
        d_out_far[i] = total_out[far, :].astype(jnp.bfloat16)
        return carry

    lax.fori_loop(0, experts, one_expert, 0)


class Collect:
    def __init__(self, place, part, corner, from_x, from_y, from_z, packs, half, sems):
        self.place, self.part = place, part
        self.corner, self.from_x, self.from_y, self.from_z = corner, from_x, from_y, from_z
        self.packs, self.half, self.started = packs, half, []
        self.send_sem, self.recv_sem = sems

    def go(self, kind, src, dst, at_send, at_recv, device):
        send(
            self.started, src, dst, self.send_sem.at[kind, at_send],
            self.recv_sem.at[kind, at_recv], device,
        )

    def opposite(self, k, p):
        at = k * self.packs + p
        towards = 2 if self.half(k, p) == 0 else 1
        self.go(3, self.part(3, k, p), self.corner.at[at], at, at, self.place.device(towards, 0))

    def straight(self, k, p):
        at = k * self.packs + p
        if self.half(k, p) == 0:
            self.go(2, self.part(2, k, p), self.from_y.at[at], at, at, self.place.device(2, 0))
        else:
            self.go(1, self.part(1, k, p), self.from_x.at[at], at, at, self.place.device(1, 0))

    def helped(self, k, p, mine):
        at = k * self.packs + p
        ref = self.corner.at[at]
        arrived(ref, self.recv_sem.at[3, at])
        total = ref[...].astype(jnp.float32) + mine().astype(jnp.float32)
        ref[...] = total.astype(jnp.bfloat16)
        if self.half(k, p) == 0:
            self.go(1, ref, self.from_x.at[at], at, at, self.place.device(1, 0))
        else:
            self.go(2, ref, self.from_y.at[at], at, at, self.place.device(2, 0))

    def plane(self, k, p, mine):
        at = k * self.packs + p
        arrived(self.from_x.at[at], self.recv_sem.at[1, at])
        arrived(self.from_y.at[at], self.recv_sem.at[2, at])
        total = self.from_x[at].astype(jnp.float32) + self.from_y[at].astype(jnp.float32)
        total = total + mine().astype(jnp.float32)
        if k:
            self.from_x[at] = total.astype(jnp.bfloat16)
            there = back(k) * self.packs + p
            self.go(
                0, self.from_x.at[at], self.from_z.at[there], at, there, self.place.device(0, k)
            )
            return None
        for other in (1, 2, 3):
            at = other * self.packs + p
            arrived(self.from_z.at[at], self.recv_sem.at[0, at])
            total = total + self.from_z[at].astype(jnp.float32)
        return total

    def finish(self):
        for copy in self.started:
            copy.wait_send()


class Return:
    def __init__(self, place, part, own, from_z, sems, load):
        self.place, self.part, self.own, self.from_z = place, part, own, from_z
        self.send_sem, self.recv_sem, self.z_sem = sems
        self.started, self.loads = [], {}
        for kind, j, p in self.needs:
            rel = self.beside(p) if kind else 0
            at = self.at(j, p)
            self.loads[kind, j, p] = load(part.at[rel, at], own.at[kind, at])

    needs = [(kind, j, p) for j in range(4) for p in range(2) for kind in (1, 0)]

    def at(self, j, p):
        return self.place.nearest(3 - j) * 2 + p

    def beside(self, p):
        return 1 + p

    def go(self, kind, at, src, dst, recv_sem, device):
        send(self.started, src, dst, self.send_sem.at[kind, at], recv_sem, device)

    def mine(self, kind, j, p):
        return self.own[kind, self.at(j, p)].astype(jnp.float32)

    def along(self, kind, send_kind, j, p, ref, total):
        place = self.place
        k = place.nearest(3 - j)
        step = 2 * ((place.plane(k) - place.z + 3) // 4) - 1
        behind = self.from_z.at[kind, k * 2 + p]
        more = (place.z - step >= 0) & (place.z - step <= 3)

        @pl.when(more)
        def add():
            arrived(behind, self.z_sem.at[kind, k * 2 + p])
            ref[...] = (total() + behind[...].astype(jnp.float32)).astype(jnp.bfloat16)

        @pl.when(jnp.logical_not(more))
        def first():
            ref[...] = total().astype(jnp.bfloat16)

        there = (k - step + 4) % 4
        slot = (there + (4 - there) // 4 * (2 - 2 * step)) * 2 + p
        self.go(
            send_kind, k * 2 + p, ref, self.from_z.at[kind, slot], self.z_sem.at[kind, slot],
            (place.plane(step + 4), place.at[0]),
        )

    def owned(self, kind, p, total, out):
        out[...] = total()
        for slot, comes in ((p, self.place.z > 0), (8 + p, self.place.z < 3)):

            @pl.when(comes)
            def add(slot=slot):
                ref = self.from_z.at[kind, slot]
                arrived(ref, self.z_sem.at[kind, slot])
                out[...] += ref[...].astype(jnp.float32)

    def finish(self):
        for copy in self.started:
            copy.wait_send()


class PlaneFirst(Return):
    def __init__(self, place, part, own, from_z, sems, load, corner, from_x, from_y, got):
        self.corner, self.near, self.early = corner, (None, from_x, from_y), {}
        for i, (j, rel) in enumerate(EARLY):
            for p in range(2):
                into = corner if rel == 3 else self.near[2 - p]
                at = place.nearest(3 - j) * 2 + p
                self.early[rel == 3, j, p] = load(got[p].at[i], into.at[at])
        super().__init__(place, part, own, from_z, sems, load)

    def here(self, far, j, p, ref, sem):
        if (far, j, p) in self.early:
            self.early[far, j, p].wait()
        else:
            arrived(ref, sem)

    def first(self, j, p):
        at, way = self.at(j, p), 2 - p
        if (True, j, p) not in self.early:
            self.go(
                3, at, self.part.at[3, at], self.corner.at[at], self.recv_sem.at[3, at],
                self.place.device(way, 0),
            )
        if (False, j, p) not in self.early:
            self.go(
                way, at, self.part.at[way, at], self.near[way].at[at], self.recv_sem.at[way, at],
                self.place.device(way, 0),
            )

    def helped(self, j, p):
        at, way = self.at(j, p), 1 + p
        ref = self.corner.at[at]
        self.loads[1, j, p].wait()
        self.here(True, j, p, ref, self.recv_sem.at[3, at])
        ref[...] = (ref[...].astype(jnp.float32) + self.mine(1, j, p)).astype(jnp.bfloat16)
        self.go(
            way, at, ref, self.near[way].at[at], self.recv_sem.at[way, at],
            self.place.device(way, 0),
        )

    def plane(self, j, p, out):
        at = self.at(j, p)
        self.loads[0, j, p].wait()
        self.here(False, j, p, self.near[2 - p].at[at], self.recv_sem.at[2 - p, at])
        arrived(self.near[1 + p].at[at], self.recv_sem.at[1 + p, at])

        def total():
            both = self.near[1][at].astype(jnp.float32) + self.near[2][at].astype(jnp.float32)
            return both + self.mine(0, j, p)

        if j < 3:
            self.along(0, 0, j, p, self.near[1].at[at], total)
        else:
            self.owned(0, p, total, out)


class SideFirst(Return):
    def __init__(self, place, part, own, from_z, sems, load, near, last, total):
        super().__init__(place, part, own, from_z, sems, load)
        self.near, self.last, self.total = near, last, total

    def first(self, j, p):
        at, way = self.at(j, p), 2 - p
        for kind, rel in ((1, 3), (0, way)):
            self.go(
                kind, at, self.part.at[rel, at], self.near.at[kind, at],
                self.recv_sem.at[kind, at], self.place.device(way, 0),
            )

    def plane(self, j, p, out):
        at, way = self.at(j, p), 1 + p
        for kind in (1, 0):
            ref = self.near.at[kind, at]
            self.loads[kind, j, p].wait()
            arrived(ref, self.recv_sem.at[kind, at])

            def total(kind=kind, ref=ref):
                return ref[...].astype(jnp.float32) + self.mine(kind, j, p)

            if j < 3:
                self.along(kind, 2 + kind, j, p, ref, total)
            elif kind:
                self.owned(kind, p, total, self.total)
                ref[...] = self.total[...].astype(jnp.bfloat16)
                self.go(
                    2, at, ref, self.last.at[p], self.recv_sem.at[2, p], self.place.device(way, 0)
                )
            else:
                self.owned(kind, p, total, out)
        if j == 3:
            arrived(self.last.at[p], self.recv_sem.at[2, p])
            out[...] += self.last[p].astype(jnp.float32)


def tail_kernel(
    pack_task, task_experts, tok, cot, segments, proj, heads, middle, dense, grad_part, mixed_part,
    d_in, d_out_far, got_y, got_x,
    mixed, d_tok, d_dense, d_in_all, d_out_all,
    g_own, g_corner, g_x, g_y, g_z, m_own, m_near, m_last, m_z, m_total, m_out,
    total_grad, grad_mid, grad_heads, grad_qkv, acc, small_rows, turned, flat_ids, tall_ids,
    in_far, in_mine, far_dense, got_dense, part_dense, s_corner, s_x, s_y, s_z,
    g_send, g_recv, gz_recv, m_send, m_recv, mz_recv, s_send, s_recv, in_send, in_recv,
    pair_send, pair_recv, load_sem,
):
    place = Place()
    width = tok.shape[2]
    place.greet()

    loads = []

    def load(src, dst):
        copy = pltpu.make_async_copy(src, dst, load_sem.at[len(loads)])
        copy.start()
        loads.append(copy)
        return copy

    grads = PlaneFirst(
        place, grad_part, g_own, g_z, (g_send, g_recv, gz_recv), load, g_corner, g_x, g_y,
        (got_y, got_x),
    )
    in_load = load(d_in.at[place.core], in_mine)
    mixes = SideFirst(
        place, mixed_part, m_own, m_z, (m_send, m_recv, mz_recv), load, m_near, m_last, m_total
    )
    pair_started, in_started, kept = [], [], {}
    planes = (2, 1, 3, 0)

    same_documents(segments, flat_ids, tall_ids)
    small = dense[:, :, 4 * width : 4 * width + SIDE].reshape(width, SIDE)
    turned[...] = jnp.transpose(small.astype(jnp.float32))
    small_rows[...] = jnp.zeros_like(small_rows)
    gain_one, bias_one, gain_two, bias_two = (
        turned[GAIN_ONE + i : GAIN_ONE + i + 1, :] for i in range(4)
    )

    place.meet()

    def pair():
        send(
            pair_started, d_in.at[1 - place.core], in_far, pair_send.at[0], pair_recv.at[0],
            place.sibling,
        )
        send(
            pair_started, d_out_far, d_out_all, pair_send.at[1], pair_recv.at[1], place.sibling
        )

    def addpair():
        in_load.wait()
        arrived(in_far, pair_recv.at[0])

        def one(i, carry):
            total = in_mine[i].astype(jnp.float32) + in_far[i].astype(jnp.float32)
            in_mine[i] = total.astype(jnp.bfloat16)
            return carry

        lax.fori_loop(0, in_mine.shape[0], one, 0)
        columns = pl.ds(pl.multiple_of(place.chip(0, 0) * SIDE, SIDE), SIDE)
        kept["local"] = load(in_mine.at[place.chip(0, 0)], d_in_all.at[:, :, columns])

    def win(rel, j):
        k = planes[j]
        columns = pl.ds(pl.multiple_of(place.chip(0, 0) * SIDE, SIDE), SIDE)
        send(
            in_started, in_mine.at[place.chip(rel, k)], d_in_all.at[:, :, columns],
            in_send.at[rel, k], in_recv.at[rel, back(k)], place.device(rel, k),
        )

    def mplane(j, p):
        mixes.plane(j, p, m_out)
        if j == 3:
            mixed[p] = (middle[p, :PACK] + m_out[...]).astype(jnp.bfloat16)

    def add_to(p, columns, value):
        if p == 0:
            acc[:, columns] = value
        else:
            acc[:, columns] += value

    def add_row(at, value):
        small_rows[at : at + 1, :] += jnp.sum(value, 0, keepdims=True)

    def att(part):
        p = part // 3
        (att_routed, att_heads, att_normed)[part % 3](p)

    def att_routed(p):
        first, second = place.pair(pack_task, task_experts, 0, 0, p)
        got = total_grad[p]
        tall = jnp.concatenate(
            [got[PACK:, : 2 * SIDE], jnp.zeros((SIDE - 8, 2 * SIDE), jnp.float32)], axis=0
        )
        gap_grad = jnp.transpose(tall)[:ROWS, 0:1]
        got = jnp.where(real_rows(), got, 0.0)
        mid = middle[p]
        unit, rise = norm_parts(mid)
        routed = jnp.where(real_rows(), unit * gain_two + bias_two, 0.0).astype(jnp.bfloat16)
        route = dense[:, :, 4 * width : 4 * width + SIDE].reshape(width, SIDE)
        gate_a, gate_b = two_gates(dot(routed, route), first, second)
        grad_a = gate_a * gate_b * gap_grad
        lane = lax.broadcasted_iota(jnp.int32, (ROWS, SIDE), 1)
        grad_logits = jnp.where(lane == first, grad_a, jnp.where(lane == second, -grad_a, 0.0))
        grad_logits = jnp.where(real_rows(), grad_logits, 0.0).astype(jnp.bfloat16)
        add_to(p, pl.ds(4 * width, SIDE), contract_rows(routed, grad_logits))
        got = got + contract_cols(grad_logits, route)
        add_row(2, got * unit)
        add_row(3, got)
        u = got * gain_two
        grad_middle = lengthened(cot, p) + rise * (
            u - jnp.mean(u, -1, keepdims=True) - unit * jnp.mean(u * unit, -1, keepdims=True)
        )
        grad_mid[...] = grad_middle
        attended = grad_middle.astype(jnp.bfloat16)
        add_to(p, pl.ds(3 * width, width), contract_rows(heads[p], attended))
        w_attn = dense[:, :, 3 * width : 4 * width].reshape(width, width)
        grad_heads[...] = contract_cols(attended, w_attn).astype(jnp.bfloat16)

    def att_heads(p):
        same = same_document(flat_ids, tall_ids, p)

        def pair_of_heads(j, carry):
            at = pl.multiple_of(j * SIDE, SIDE)
            queries = proj[p, :, pl.ds(at, SIDE)]
            keys = proj[p, :, pl.ds(at + width, SIDE)]
            values = proj[p, :, pl.ds(at + 2 * width, SIDE)]
            out_grad = grad_heads[:, pl.ds(at, SIDE)]
            zero = jnp.zeros((ROWS, SIDE), jnp.float32)
            grad_q, grad_k, grad_v = zero, zero, zero
            for h in range(2):
                lanes = head_lanes(h)
                probs = softmax_rows(queries * lanes, keys, same)
                mine_grad = out_grad * lanes
                grad_v = grad_v + contract_rows(probs.astype(jnp.bfloat16), mine_grad)
                grad_probs = contract_cols(mine_grad, values)
                row_dot = jnp.sum(probs * grad_probs, -1, keepdims=True)
                grad_scores = (probs * (grad_probs - row_dot)).astype(jnp.bfloat16)
                grad_q = grad_q + dot(grad_scores, keys * lanes)
                grad_k = grad_k + contract_rows(grad_scores, queries * lanes)
            scale = 1.0 / math.sqrt(HEAD)
            grad_qkv[:, pl.ds(at, SIDE)] = (grad_q * scale).astype(jnp.bfloat16)
            grad_qkv[:, pl.ds(at + width, SIDE)] = (grad_k * scale).astype(jnp.bfloat16)
            grad_qkv[:, pl.ds(at + 2 * width, SIDE)] = grad_v.astype(jnp.bfloat16)
            return carry

        lax.fori_loop(0, width // SIDE, pair_of_heads, 0)

    def att_normed(p):
        unit, rise = norm_parts(lengthened(tok, p))
        normed = (unit * gain_one + bias_one).astype(jnp.bfloat16)
        add_to(p, pl.ds(0, 3 * width), contract_rows(normed, grad_qkv[...]))
        w_qkv = dense[:, :, : 3 * width].reshape(width, 3 * width)
        grad_normed = contract_cols(grad_qkv[...], w_qkv)
        add_row(0, grad_normed * unit)
        add_row(1, grad_normed)
        u = grad_normed * gain_one
        d_tok[p] = (
            grad_mid[...]
            + rise
            * (u - jnp.mean(u, -1, keepdims=True) - unit * jnp.mean(u * unit, -1, keepdims=True))
        ).astype(jnp.bfloat16)

    def dense_part(rel, k, p):
        return got_dense.at[place.chip(rel, k)]

    sums = Collect(
        place, dense_part, s_corner, s_x, s_y, s_z, 1, lambda k, p: k % 2, (s_send, s_recv)
    )
    def dense_step():
        tall = jnp.concatenate(
            [
                jnp.zeros((GAIN_ONE, width), jnp.float32),
                small_rows[...],
                jnp.zeros((SIDE - GAIN_ONE - 8, width), jnp.float32),
            ],
            axis=0,
        )
        acc[:, 4 * width :] += jnp.transpose(tall)
        columns_all = acc.shape[1]

        def cut(i, carry):
            own_rows = pl.ds(pl.multiple_of(i * 32 + place.core * 16, 16), 16)
            far_rows = pl.ds(pl.multiple_of(i * 32 + 16 - place.core * 16, 16), 16)
            far_dense[i] = acc[far_rows, :].astype(jnp.bfloat16)
            part_dense[i] = acc[own_rows, :]
            return carry

        lax.fori_loop(0, 16, cut, 0)
        send(
            pair_started, far_dense, got_dense, pair_send.at[2], pair_recv.at[2], place.sibling
        )
        arrived(got_dense, pair_recv.at[2])

        def join(i, carry):
            far_dense_sum = part_dense[i] + got_dense[i].astype(jnp.float32)
            got_dense[i] = far_dense_sum.astype(jnp.bfloat16)
            return carry

        lax.fori_loop(0, 16, join, 0)

        for k in (2, 1, 3, 0):
            sums.opposite(k, 0)
        for k in (2, 1, 3, 0):
            sums.straight(k, 0)
        for k in (2, 1, 3, 0):
            sums.helped(k, 0, lambda k=k: got_dense[place.chip(1 + k % 2, k)])
        for k in (2, 1, 3):
            sums.plane(k, 0, lambda k=k: got_dense[place.chip(0, k)])
        d_dense[...] = sums.plane(0, 0, lambda: got_dense[place.chip(0, 0)])

    steps = {
        GFIRST: grads.first, GHELP: grads.helped,
        GPLANE: lambda j, p: grads.plane(j, p, total_grad.at[p]),
        MFIRST: mixes.first, MPLANE: mplane, MHELP: lambda j, p: None,
        PAIR: pair, ADDPAIR: addpair, WIN: win, ATT: att, DENSE: dense_step,
    }
    for name, *where in TAIL_STEPS:
        steps[name](*where)

    for rel in range(4):
        for k in range(4):
            if (rel, k) != (0, 0):
                place_columns = pl.ds(pl.multiple_of(place.chip(rel, k) * SIDE, SIDE), SIDE)
                arrived(d_in_all.at[:, :, place_columns], in_recv.at[rel, k])
    kept["local"].wait()
    arrived(d_out_all, pair_recv.at[1])
    for tree in (grads, mixes, sums):
        tree.finish()
    for copy in pair_started + in_started:
        copy.wait_send()


def last_kernel(
    mixed_own, d_tok_tall, d_dense, d_in_low, d_out_own, d_out_far,
    mixed, d_tok, d_qkv, d_attn, d_route, d_in, d_out, gain_one, bias_one, gain_two, bias_two,
):
    width, experts = mixed.shape[2], d_route.shape[1]

    @pl.when(pl.program_id(0) == 0)
    def small():
        for p in range(mixed.shape[0]):
            mixed[p] = mixed_own[p]
            d_tok[p] = d_tok_tall[p, :PACK]
        d_qkv[...] = d_dense[:, : 3 * width]
        d_attn[...] = d_dense[:, 3 * width : 4 * width]
        d_route[...] = d_dense[:, 4 * width : 4 * width + experts]
        rows = jnp.transpose(d_dense[:, 4 * width :])
        for i, ref in enumerate((gain_one, bias_one, gain_two, bias_two)):
            ref[...] = rows[GAIN_ONE + i]

    d_in[...] = d_in_low[...].astype(jnp.float32)
    d_out[...] = d_out_own[...].astype(jnp.float32) + d_out_far[...].astype(jnp.float32)


def shards_fast(
    tokens,
    segment_ids,
    pack_task,
    task_experts,
    w_qkv,
    w_attn_out,
    w_router,
    w_expert_in,
    w_expert_out,
    norm1_gain,
    norm1_bias,
    norm2_gain,
    norm2_bias,
    cotangent,
):
    packs, length, width = tokens.shape
    experts, slab_in, hidden = w_expert_in.shape
    slab_out = w_expert_out.shape[1]
    dense_width = 4 * width + SIDE
    any_space = pl.BlockSpec(memory_space=pl.ANY)
    vmem = pl.BlockSpec(memory_space=pltpu.VMEM)
    smem = pl.BlockSpec(memory_space=pltpu.SMEM)
    low, full = jnp.bfloat16, jnp.float32
    flat = jax.ShapeDtypeStruct
    dma = pltpu.SemaphoreType.DMA
    by_rank = task_experts.T

    blocks = flat((4, 4 * packs, length, width), low)
    tall_blocks = flat((4, 4 * packs, ROWS, width), low)
    in_sums = flat((4, 4 * packs, width, 2 * SIDE), low)
    out_sums = flat((4, 4 * packs, 2 * SIDE, width), low)

    def held(shape):
        return pltpu.VMEM(shape.shape, shape.dtype)

    early_blocks = flat((len(EARLY), ROWS, width), low)
    (
        in_terms, out_terms, mixed_part, grad_part, dense, early_y, early_x, proj, heads, middle,
    ) = pl.pallas_call(
        front_kernel,
        out_shape=(
            in_sums, out_sums, blocks, tall_blocks,
            flat((32, slab_in, dense_width), low),
            early_blocks, early_blocks,
            flat((packs, ROWS, 3 * width), low),
            flat((packs, ROWS, width), low),
            flat((packs, ROWS, width), full),
        ),
        in_specs=[smem] * 2 + [vmem] * 10 + [any_space] * 2,
        out_specs=(any_space,) * 7 + (vmem,) * 3,
        scratch_shapes=[
            pltpu.VMEM((32, slab_in, dense_width), low),
            held(blocks), held(blocks),
            pltpu.VMEM((16, 2, experts, slab_in, SIDE), low),
            pltpu.VMEM((2, experts, slab_out, width), low),
            pltpu.VMEM((2, 4, width, 2 * SIDE), low),
            pltpu.VMEM((2, 4, 2 * SIDE, width), low),
            held(blocks), held(tall_blocks),
            pltpu.VMEM((SIDE, width), full),
            pltpu.VMEM((SIDE, SIDE), full),
            pltpu.VMEM((8, 2 * SIDE), full),
            pltpu.VMEM((2 * SIDE, 8), full),
            pltpu.VMEM((4, 8, width), full),
            dma((7, 8)), dma((4, 8)), dma((5, 8)), dma((4, 8)), dma((5, 4)), dma((4, 4)),
            dma((4, 4)), dma((4, 4)), dma((4, 4)), dma((4, 4)), dma((2,)), dma((2,)), dma((3,)),
            dma((32,)), dma((2, len(EARLY))),
        ],
        compiler_params=pltpu.CompilerParams(
            collective_id=0, has_side_effects=True, vmem_limit_bytes=60 << 20
        ),
        name="front",
    )(
        pack_task, by_rank, tokens, segment_ids, w_qkv, w_attn_out, w_router,
        norm1_gain, norm1_bias, norm2_gain, norm2_bias, cotangent, w_expert_in, w_expert_out,
    )

    across = lax.axis_size("gy")
    got_y = lax.ppermute(early_y, "gy", [(i, i ^ 4) for i in range(across)])
    got_x = lax.ppermute(early_x, "gy", [(i, i ^ 2) for i in range(across)])

    part = width // 2

    by_columns = pl.BlockSpec((experts, slab_out, part), lambda i, *unused: (0, 0, i))
    d_in, d_out_own, d_out_far = pl.pallas_call(
        sum_kernel,
        grid_spec=pltpu.PrefetchScalarGridSpec(
            num_scalar_prefetch=2,
            grid=(2,),
            in_specs=[
                pl.BlockSpec((4, 4 * packs, part, 2 * SIDE), lambda i, *unused: (0, 0, i, 0)),
                pl.BlockSpec((4, 4 * packs, 2 * SIDE, part), lambda i, *unused: (0, 0, 0, i)),
            ],
            out_specs=[
                pl.BlockSpec((2, 8, experts, slab_in, SIDE), lambda i, *unused: (0, i, 0, 0, 0)),
                by_columns, by_columns,
            ],
            scratch_shapes=[
                pltpu.SMEM((experts,), jnp.int32),
                pltpu.SMEM((32 * packs,), jnp.int32),
                pltpu.VMEM((part, SIDE), full),
                pltpu.VMEM((SIDE, part), full),
            ],
        ),
        out_shape=(
            flat((2, 16, experts, slab_in, SIDE), low),
            flat((experts, slab_out, width), low),
            flat((experts, slab_out, width), low),
        ),
        compiler_params=pltpu.CompilerParams(vmem_limit_bytes=60 << 20),
        cost_estimate=pl.CostEstimate(
            flops=10**10, bytes_accessed=40 * 10**6, transcendentals=0
        ),
        name="sums",
    )(pack_task, by_rank, in_terms, out_terms)

    parts = pltpu.VMEM((4 * packs, ROWS, width), low)
    slices = pltpu.VMEM((4, slab_in, dense_width), low)
    sliced = pltpu.VMEM((16, slab_in, dense_width), low)
    mixed_own, d_tok_tall, d_dense, d_in_all, d_out_all = pl.pallas_call(
        tail_kernel,
        out_shape=(
            flat((packs, length, width), low),
            flat((packs, ROWS, width), low),
            flat((slab_in, dense_width), full),
            flat((experts, slab_in, hidden), low),
            flat((experts, slab_out, width), low),
        ),
        in_specs=[smem] * 2 + [vmem] * 7 + [any_space] * 6,
        out_specs=(vmem,) * 3 + (any_space,) * 2,
        scratch_shapes=[
            pltpu.VMEM((2, 4 * packs, ROWS, width), low), parts, parts, parts,
            pltpu.VMEM((1, 5 * packs, ROWS, width), low),
            pltpu.VMEM((2, 4 * packs, length, width), low),
            pltpu.VMEM((2, 4 * packs, length, width), low),
            pltpu.VMEM((packs, length, width), low),
            pltpu.VMEM((2, 5 * packs, length, width), low),
            pltpu.VMEM((length, width), full),
            pltpu.VMEM((length, width), full),
            pltpu.VMEM((packs, ROWS, width), full),
            pltpu.VMEM((ROWS, width), full),
            pltpu.VMEM((ROWS, width), low),
            pltpu.VMEM((ROWS, 3 * width), low),
            pltpu.VMEM((width, dense_width), full),
            pltpu.VMEM((8, width), full),
            pltpu.VMEM((SIDE, width), full),
            pltpu.VMEM((8, 2 * SIDE), full),
            pltpu.VMEM((2 * SIDE, 8), full),
            pltpu.VMEM((16, experts, slab_in, SIDE), low),
            pltpu.VMEM((16, experts, slab_in, SIDE), low),
            sliced, sliced,
            pltpu.VMEM((16, slab_in, dense_width), full),
            slices, slices, slices, slices,
            dma((4, 8)), dma((4, 8)), dma((1, 10)), dma((4, 8)), dma((4, 8)), dma((2, 10)),
            dma((4, 4)), dma((4, 4)), dma((4, 4)), dma((4, 4)), dma((3,)), dma((3,)), dma((48,)),
        ],
        compiler_params=pltpu.CompilerParams(
            collective_id=1, has_side_effects=True, vmem_limit_bytes=60 << 20
        ),
        name="tail",
    )(
        pack_task, by_rank, tokens, cotangent, segment_ids, proj, heads, middle, dense,
        grad_part, mixed_part, d_in, d_out_far, got_y, got_x,
    )

    group = experts // 2

    def some(rows, columns):
        return pl.BlockSpec((group, rows, columns), lambda i: (i, 0, 0))

    def whole(*shape):
        return pl.BlockSpec(shape, lambda i: (0,) * len(shape))

    return pl.pallas_call(
        last_kernel,
        grid=(2,),
        in_specs=[
            whole(packs, length, width), whole(packs, ROWS, width), whole(slab_in, dense_width),
            some(slab_in, hidden), some(slab_out, width), some(slab_out, width),
        ],
        out_specs=(
            whole(packs, length, width), whole(packs, length, width),
            whole(slab_in, 3 * width), whole(slab_in, width), whole(slab_in, experts),
            some(slab_in, hidden), some(slab_out, width),
        ) + (whole(slab_in),) * 4,
        out_shape=(
            flat((packs, length, width), low), flat((packs, length, width), low),
            flat((slab_in, 3 * width), full), flat((slab_in, width), full),
            flat((slab_in, experts), full),
            flat((experts, slab_in, hidden), full), flat((experts, slab_out, width), full),
        ) + (flat((slab_in,), full),) * 4,
        compiler_params=pltpu.CompilerParams(vmem_limit_bytes=60 << 20),
        name="last",
    )(mixed_own, d_tok_tall, d_dense, d_in_all, d_out_own, d_out_all)


def solution(mesh):
    outer, inner = mesh.shape["gx"], mesh.shape["gy"]

    def shards(*arrays):
        packs, length, width = arrays[0].shape
        experts, slab_in, hidden = arrays[7].shape
        fits = (
            (outer, inner) == (4, 8)
            and packs == 2
            and length == PACK
            and experts == GAIN_ONE
            and width == HEADS * HEAD
            and slab_in == 16
            and hidden == 16 * SIDE
        )
        return (shards_fast if fits else shards_any)(*arrays)

    placed = (
        P(("gx", "gy"), None, None),
        P(("gx", "gy"), None),
        P(),
        P(),
        P(("gx", "gy"), None),
        P(("gx", "gy"), None),
        P(("gx", "gy"), None),
        P(None, ("gx", "gy"), None),
        P(None, ("gx", "gy"), None),
        P(("gx", "gy")),
        P(("gx", "gy")),
        P(("gx", "gy")),
        P(("gx", "gy")),
        P(("gx", "gy"), None, None),
    )
    return jax.shard_map(
        shards,
        mesh=mesh,
        in_specs=placed,
        out_specs=(
            P(("gx", "gy"), None, None),
            P(("gx", "gy"), None, None),
            P(("gx", "gy"), None),
            P(("gx", "gy"), None),
            P(("gx", "gy"), None),
            P(None, ("gx", "gy"), None),
            P(None, ("gx", "gy"), None),
            P(("gx", "gy")),
            P(("gx", "gy")),
            P(("gx", "gy")),
            P(("gx", "gy")),
        ),
        check_vma=False,
    )
```
